32 devices in a mesh: group: 4 (over y, core), img: 8 (over z, x).
Axes of the slice: x: 2, y: 2, z: 4, core: 2. Of those that a mesh axis runs over, the one named last changes fastest.
Arguments:
- pixels: bfloat16 [32, 196, 8192], P(('group', 'img')), may hold values from -6 to 6
- band_mask: int32 [32, 32], P(('group', 'img')), may hold values from 0 to 1, as said below
- wavelength: int32 [4, 32], replicated, may hold values from 400 to 2499
- owner_order: int32 [7520], replicated, may hold values from 0 to 7519, as said below
- rest_weight: float32 [60160, 128], P(('group', 'img')), may hold values from -4 to 4, as said below
- rest_moment1: float32 [60160, 128], P(('group', 'img')), may hold values from -512 to 512
- rest_moment2: float32 [60160, 128], P(('group', 'img')), may hold values from 2090 to 8362
- fc_weight: float32 [128, 196608], P('group', 'img'), may hold values from -0.005859375 to 0.005859375
- fc_moment1: float32 [128, 196608], P('group', 'img'), may hold values from -2560 to 2560
- fc_moment2: float32 [128, 196608], P('group', 'img'), may hold values from 50176 to 200704
- cotangent: bfloat16 [6272, 768], P(('group', 'img')), may hold values from -6 to 6
Outputs:
- block_out: bfloat16 [6272, 768], P(('group', 'img'))
- pixel_grad: bfloat16 [32, 196, 8192], P(('group', 'img'))
- rest_new: float32 [60160, 128], P(('group', 'img'))
- rest_first: float32 [60160, 128], P(('group', 'img'))
- rest_second: float32 [60160, 128], P(('group', 'img'))
- fc_new: float32 [128, 196608], P('group', 'img')
- fc_first: float32 [128, 196608], P('group', 'img')
- fc_second: float32 [128, 196608], P('group', 'img')
The draws below stay inside these ranges and needn't reach their ends.
Inputs may be any that keep to these rules, and one draw needn't show every extreme that they name: `band_mask`: every image has 2 to 32 present bands, and some image has all 32. `owner_order`: A permutation of the packed blocks. `rest_weight`: in the order given by owner_order; padding entries are zero and gains lie near 1.
All inputs are finite; a program needn't handle non-finite values.
Results may differ from the reference program's by a relative error of at most 0.019.
Values may be sent and summed in bfloat16 or wider, within the bound.
A program may use at most 320 MiB of HBM per device.

```python
import math
import jax
import jax.numpy as jnp
from jax import lax

D = 768
HEADS = 12
HD = 64
HID = 3072
E = 128
HH = 4
HFF = 2048
PATCH = 256
S = 196
NB = 32
STEP = 5
IMAGES = 32
TOKENS = 6272
R_ROWS = 60160
RBLK = 7520
N_GROUP = 4


def owner_blocks(key):
    return jax.random.permutation(jax.random.fold_in(key, 7), RBLK).astype(jnp.int32)


def draw_owner_order(key, part):
    return owner_blocks(key)


def draw_band_mask(key, part):
    key = jax.random.fold_in(key, 11)
    count_key, order_key = jax.random.split(key)
    counts = jax.random.randint(count_key, (IMAGES,), 2, NB + 1)
    counts = counts.at[0].set(NB)
    band_ranks = jax.vmap(lambda row_key: jax.random.permutation(row_key, NB))(jax.random.split(order_key, IMAGES))
    return (band_ranks < counts[:, None]).astype(jnp.int32)


def draw_rest_weight(key, part):
    block_order = owner_blocks(key)
    key = jax.random.fold_in(key, 13)
    segments = [(3 * D * D, D ** (-0.5), 0.0), (D * D, 8.0 * D ** (-0.5), 0.0), (D * HID, D ** (-0.5), 0.0), (HID * D, HID ** (-0.5), 0.0), (E * E, 2.0 * E ** (-0.5), 0.0), (E * E, 2.0 * E ** (-0.5), 0.0), (E * E, E ** (-0.5), 0.0), (E * E, 3.0 * E ** (-0.5), 0.0), (E * HFF, E ** (-0.5), 0.0), (HFF * E, HFF ** (-0.5), 0.0), (D, 0.1, 1.0), (D, 0.1, 0.0), (D, 0.1, 1.0), (D, 0.1, 0.0), (D, 0.3, 0.0), (E, 0.1, 1.0), (E, 0.1, 0.0), (E, 0.1, 1.0), (E, 0.1, 0.0)]
    scales = jnp.concatenate([jnp.full((entry_size,), scale_val, jnp.float32) for entry_size, scale_val, center_val in segments])
    centers = jnp.concatenate([jnp.full((entry_size,), center_val, jnp.float32) for entry_size, scale_val, center_val in segments])
    used = scales.shape[0]
    noise_vals = jnp.clip(jax.random.normal(key, (used,), jnp.float32), -4.0, 4.0)
    values = centers + scales * noise_vals
    values = jnp.concatenate([values, jnp.zeros((R_ROWS * 128 - used,), jnp.float32)])
    return values.reshape(RBLK, 8, 128)[block_order].reshape(R_ROWS, 128)


def place_ends(array, key, low, high):
    longest = array.shape.index(max(array.shape))
    spots = []
    for shift in (0, 1):
        where = [jax.random.randint(jax.random.fold_in(key, axis), (), 0, length) for axis, length in enumerate(array.shape)]
        where[longest] = (where[longest] + shift) % array.shape[longest]
        spots.append(tuple(where))
    return array.at[spots[0]].set(low).at[spots[1]].set(high)


def steps_of(key, dims, pieces, smallest, top_value):
    def one(axis_at, blocks):
        draws = jax.random.uniform(jax.random.fold_in(jax.random.fold_in(key, 6), axis_at), (blocks,), jnp.float32, smallest / len(pieces), top_value / len(pieces))
        return jnp.repeat(jnp.exp(draws), dims[axis_at] // blocks).reshape((-1,) + (1,) * (len(dims) - axis_at - 1))

    loudness = one(*pieces[0])
    for cut in pieces[1:]:
        loudness = loudness * one(*cut)
    return loudness


def noise(rng, dims, deviation, limit, cuts=(), kind=jnp.bfloat16):
    values = deviation * jax.random.normal(rng, dims, jnp.float32)
    if cuts:
        values = values * steps_of(rng, dims, cuts, -0.22, 0.18)
    return jnp.clip(values, -limit, limit).astype(kind)


def setup_inputs(seed: int = 0) -> dict:
    key_list = jax.random.split(jax.random.key(seed), 12)
    pixels = noise(key_list[0], (IMAGES, S, NB * PATCH), 1.0, 6.0, ((0, 32),))
    band_mask = draw_band_mask(jax.random.fold_in(key_list[11], 71), 0)
    wavelength = place_ends(jax.random.randint(key_list[2], (N_GROUP, NB), 400, 2500), jax.random.fold_in(key_list[2], 1), 400, 2499).astype(jnp.int32)
    owner_order = draw_owner_order(jax.random.fold_in(key_list[11], 71), 0)
    rest_weight = draw_rest_weight(jax.random.fold_in(key_list[11], 71), 0)
    rest_moment1 = noise(key_list[5], (R_ROWS, 128), (TOKENS ** 0.5), 512.0, ((0, 32),), jnp.float32)
    rest_moment2 = jnp.clip(jnp.exp(math.log(8362.0) - 1.3865336 * jax.random.uniform(key_list[6], (R_ROWS, 128), jnp.float32) ** steps_of(key_list[6], (R_ROWS, 128), ((0, 32),), -0.2, 0.2)), 2090.0, 8362.0)
    fc_weight = noise(key_list[7], (E, D * PATCH), (E * PATCH * NB) ** -0.5, 0.005859375, ((0, 4), (1, 8)), jnp.float32)
    fc_moment1 = noise(key_list[8], (E, D * PATCH), ((NB * TOKENS) ** 0.5), 2560.0, ((0, 4), (1, 8)), jnp.float32)
    fc_moment2 = jnp.clip(jnp.exp(math.log(200704.0) - 1.3862944 * jax.random.uniform(key_list[9], (E, D * PATCH), jnp.float32) ** steps_of(key_list[9], (E, D * PATCH), ((0, 4), (1, 8)), -0.2, 0.2)), 50176.0, 200704.0)
    cotangent = noise(key_list[10], (TOKENS, D), 1.0, 6.0, ((0, 32),))
    return dict(pixels=pixels, band_mask=band_mask, wavelength=wavelength, owner_order=owner_order, rest_weight=rest_weight, rest_moment1=rest_moment1, rest_moment2=rest_moment2, fc_weight=fc_weight, fc_moment1=fc_moment1, fc_moment2=fc_moment2, cotangent=cotangent)


beta_one = 0.5
beta_two = 0.75
decay_rate = 0.05
epsilon_add = 1e-08
rest_rate = 0.02

@jax.custom_vjp
def low(v):
    return lax.optimization_barrier(v.astype(jnp.bfloat16)).astype(jnp.float32)

@jax.custom_vjp
def low_back(v):
    return v

def low_keep(v):
    return (low(v), None)

def low_pass(kept, grad):
    return (grad,)

def back_keep(v):
    return (v, None)

def back_low(kept, grad):
    return (low(grad),)
low.defvjp(low_keep, low_pass)
low_back.defvjp(back_keep, back_low)

def layout():
    return [('w_qkv', (D, 3 * D)), ('w_out', (D, D)), ('w_up', (D, HID)), ('w_down', (HID, D)), ('h_query', (E, E)), ('h_key', (E, E)), ('h_value', (E, E)), ('h_out', (E, E)), ('h_ffin', (E, HFF)), ('h_ffout', (HFF, E)), ('ln1_gain', (D,)), ('ln1_shift', (D,)), ('ln2_gain', (D,)), ('ln2_shift', (D,)), ('patch_bias', (D,)), ('hn1_gain', (E,)), ('hn1_shift', (E,)), ('hn2_gain', (E,)), ('hn2_shift', (E,))]

def unpack(packed):
    params = {}
    offset = 0
    for entry_name, extent in layout():
        entry_size = math.prod(extent)
        params[entry_name] = packed[offset:offset + entry_size].reshape(extent)
        offset += entry_size
    return params

def layer_norm(values, gain, shift):
    center = values - lax.optimization_barrier(jnp.mean(values, axis=-1, keepdims=True))
    spread = lax.optimization_barrier(jnp.mean(center * center, axis=-1, keepdims=True))
    return center * lax.rsqrt(spread + 1e-06) * gain + shift

def embed_waves(wavelength):
    half_width = E // 2
    frequency = jnp.exp(-math.log(10000.0) * jnp.arange(half_width, dtype=jnp.float32) / half_width)
    angles = wavelength.astype(jnp.float32)[..., None] * frequency
    return jnp.concatenate([jnp.sin(angles), jnp.cos(angles)], axis=-1)

def hyper_layer(embedded, params):
    highest = lax.Precision.HIGHEST
    groups = embedded.shape[0]
    head_size = E // HH
    queries = jnp.einsum('gbe,ef->gbf', embedded, params['h_query'], precision=highest).reshape(groups, NB, HH, head_size)
    keys_h = jnp.einsum('gbe,ef->gbf', embedded, params['h_key'], precision=highest).reshape(groups, NB, HH, head_size)
    values_h = jnp.einsum('gbe,ef->gbf', embedded, params['h_value'], precision=highest).reshape(groups, NB, HH, head_size)
    scores = jnp.einsum('gbhc,gthc->ghbt', queries, keys_h, precision=highest) * head_size ** (-0.5)
    softmax_w = jax.nn.softmax(scores, axis=-1)
    mixed = jnp.einsum('ghbt,gthc->gbhc', softmax_w, values_h, precision=highest).reshape(groups, NB, E)
    attended = jnp.einsum('gbe,ef->gbf', mixed, params['h_out'], precision=highest)
    first_norm = layer_norm(embedded + attended, params['hn1_gain'], params['hn1_shift'])
    inner = jax.nn.gelu(jnp.einsum('gbe,ef->gbf', first_norm, params['h_ffin'], precision=highest), approximate=False)
    outer = jnp.einsum('gbf,fe->gbe', inner, params['h_ffout'], precision=highest)
    second_norm = layer_norm(first_norm + outer, params['hn2_gain'], params['hn2_shift'])
    return second_norm + embedded

def block(stream, params):
    highest = lax.Precision.HIGHEST
    seq_len = stream.shape[0]
    first_norm = low(layer_norm(stream, params['ln1_gain'], params['ln1_shift']))
    qkv_joint = low_back(low(jnp.dot(first_norm, params['w_qkv'], precision=highest)))
    queries = qkv_joint[:, :D].reshape(seq_len, HEADS, HD)
    keys_h = qkv_joint[:, D:2 * D].reshape(seq_len, HEADS, HD)
    values_h = qkv_joint[:, 2 * D:].reshape(seq_len, HEADS, HD)
    scores = low_back(jnp.einsum('shd,thd->hst', queries, keys_h, precision=highest) * HD ** (-0.5))
    softmax_w = low(jax.nn.softmax(scores, axis=-1))
    attended = low_back(low(jnp.einsum('hst,thd->shd', softmax_w, values_h, precision=highest).reshape(seq_len, D)))
    middle = stream + low_back(jnp.dot(attended, params['w_out'], precision=highest))
    second_norm = low(layer_norm(middle, params['ln2_gain'], params['ln2_shift']))
    hidden = low_back(jnp.dot(second_norm, params['w_up'], precision=highest))
    activated = low(jax.nn.gelu(hidden, approximate=False))
    return middle + low_back(jnp.dot(activated, params['w_down'], precision=highest))

def forward(pixels, mask_f, wavelength, rest_flat, fc_master):
    highest = lax.Precision.HIGHEST
    params = unpack(low(rest_flat))
    shaped = low(hyper_layer(embed_waves(wavelength), params))
    kernel_master = low(fc_master).reshape(E, D, PATCH)
    kernels = jnp.einsum('gbk,kdp->gdbp', shaped, kernel_master, precision=highest).reshape(N_GROUP, D, NB * PATCH)
    kernels = low_back(low(kernels))
    per_group = IMAGES // N_GROUP
    group_of = jnp.arange(IMAGES, dtype=jnp.int32) // per_group

    def one_image(carry, item):
        image, present, group_id = item
        masked = (image.astype(jnp.float32).reshape(S, NB, PATCH) * present[None, :, None]).reshape(S, NB * PATCH)
        kernel = lax.dynamic_index_in_dim(kernels, group_id, 0, keepdims=False)
        linear = low_back(lax.dot_general(masked, kernel, (((1,), (1,)), ((), ())), precision=highest))
        return (carry, block(linear + params['patch_bias'], params))
    unused, outputs = lax.scan(jax.checkpoint(one_image), jnp.zeros((), jnp.float32), (pixels, mask_f, group_of))
    return outputs

def adamw_step(weight, moment_one, moment_two, grad, rate):
    first = beta_one * moment_one + (1.0 - beta_one) * grad
    second = beta_two * moment_two + (1.0 - beta_two) * grad * grad
    fix_one = 1.0 - beta_one ** STEP
    fix_two = 1.0 - beta_two ** STEP
    update = first / fix_one / (jnp.sqrt(second / fix_two) + epsilon_add) + decay_rate * weight
    return (weight - rate * update, first, second)

def reference(pixels, band_mask, wavelength, owner_order, rest_weight, rest_moment1, rest_moment2, fc_weight, fc_moment1, fc_moment2, cotangent):
    kernel_rate = float(E * PATCH * NB) ** (-0.5)
    inverse = jnp.argsort(owner_order).astype(jnp.int32)
    rest_nat = rest_weight.reshape(-1, 8, 128)[inverse].reshape(-1)
    mask_f = band_mask.astype(jnp.float32)

    def run(pixel_in, rest_flat, fc_master):
        return forward(pixel_in, mask_f, wavelength, rest_flat, fc_master)
    outputs, pullback = jax.vjp(run, pixels, rest_nat, fc_weight)
    pixel_grad, rest_grad_nat, fc_grad = pullback(cotangent.astype(jnp.float32).reshape(IMAGES, S, D))
    rest_grad = rest_grad_nat.reshape(-1, 8, 128)[owner_order].reshape(rest_weight.shape)
    rest_new, rest_first, rest_second = adamw_step(rest_weight, rest_moment1, rest_moment2, rest_grad, rest_rate)
    fc_new, fc_first, fc_second = adamw_step(fc_weight, fc_moment1, fc_moment2, fc_grad, kernel_rate)
    block_out = outputs.reshape(TOKENS, D).astype(jnp.bfloat16)
    return (block_out, pixel_grad.astype(jnp.bfloat16), rest_new, rest_first, rest_second, fc_new, fc_first, fc_second)
```

```python
import functools
import math

import jax
import jax.numpy as jnp
from jax import lax
from jax.experimental import pallas as pl
from jax.experimental.pallas import tpu as pltpu
from jax.sharding import PartitionSpec as P

MESH = pl.DeviceIdType.MESH

D = 768
HEADS = 12
HD = 64
HID = 3072
E = 128
HH = 4
HFF = 2048
PATCH = 256
NB = 32
STEP = 5


beta_one = 0.5
beta_two = 0.75
decay_rate = 0.05
epsilon_add = 1e-08
rest_rate = 0.02


def layout():
    return [
        ("w_qkv", (D, 3 * D)),
        ("w_out", (D, D)),
        ("w_up", (D, HID)),
        ("w_down", (HID, D)),
        ("h_query", (E, E)),
        ("h_key", (E, E)),
        ("h_value", (E, E)),
        ("h_out", (E, E)),
        ("h_ffin", (E, HFF)),
        ("h_ffout", (HFF, E)),
        ("ln1_gain", (D,)),
        ("ln1_shift", (D,)),
        ("ln2_gain", (D,)),
        ("ln2_shift", (D,)),
        ("patch_bias", (D,)),
        ("hn1_gain", (E,)),
        ("hn1_shift", (E,)),
        ("hn2_gain", (E,)),
        ("hn2_shift", (E,)),
    ]


def matrices():
    listed, at = [], 0
    for name, extent in layout():
        if len(extent) == 2:
            listed.append((name, extent[0], extent[1], at))
        at += math.prod(extent) // 128
    return listed


def vector_rows():
    first = sum(math.prod(extent) // 128 for _, extent in layout() if len(extent) == 2)
    count = sum(math.prod(extent) // 128 for _, extent in layout() if len(extent) == 1)
    return first, -(-count // 8) * 8


def spread_kernel(order_ref, low_ref, *refs):
    outs, linear = refs[:-1], refs[-1]
    step = pl.program_id(0)
    rows = low_ref.shape[0]

    def two(j, carry):
        pair = low_ref[pl.ds(pl.multiple_of(j * 16, 16), 16), :].astype(jnp.float32)
        for half in range(2):
            block = order_ref[step * (rows // 8) + j * 2 + half]
            linear[pl.ds(pl.multiple_of(block * 8, 8), 8), :] = pair[half * 8 : half * 8 + 8]
        return carry

    lax.fori_loop(0, rows // 16, two, 0, unroll=8)

    @pl.when(step == pl.num_programs(0) - 1)
    def _():
        for (name, height, width, first), out in zip(matrices(), outs):
            lanes = width // 128

            def some(j, carry, out=out, lanes=lanes, first=first):
                top = pl.multiple_of(j * 128, 128)
                for lane in range(lanes):
                    part = linear[pl.ds(first + top * lanes + lane, 128, stride=lanes), :]
                    out[pl.ds(top, 128), lane * 128 : lane * 128 + 128] = part.astype(out.dtype)
                return carry

            lax.fori_loop(0, height // 128, some, 0)
        first, count = vector_rows()
        outs[-1][...] = linear[first : first + count, :]


def spread_packed(gathered, slots, blocks):
    shards, rows = gathered.shape[0], gathered.shape[1]
    shapes = [
        jax.ShapeDtypeStruct((height, width), jnp.bfloat16 if name.startswith("w_") else jnp.float32)
        for name, height, width, first in matrices()
    ]
    shapes.append(jax.ShapeDtypeStruct((vector_rows()[1], 128), jnp.float32))
    return pl.pallas_call(
        spread_kernel,
        out_shape=shapes,
        grid_spec=pltpu.PrefetchScalarGridSpec(
            num_scalar_prefetch=1,
            grid=(shards,),
            in_specs=[pl.BlockSpec((None, rows, 128), lambda s, order: (s, 0, 0))],
            out_specs=[pl.BlockSpec(shape.shape, lambda s, order: (0, 0), pipeline_mode=pl.Buffered(1)) for shape in shapes],
            scratch_shapes=[pltpu.VMEM(((blocks + 1) * 8, 128), jnp.float32)],
        ),
        compiler_params=pltpu.CompilerParams(vmem_limit_bytes=60 << 20),
        name="spread_packed",
    )(slots, gathered)


def collect_kernel(order_ref, *refs):
    ins, low_ref, linear = refs[:-2], refs[-2], refs[-1]
    step = pl.program_id(0)
    rows = low_ref.shape[0]

    @pl.when(step == 0)
    def _():
        for (name, height, width, first), given in zip(matrices(), ins):
            lanes = width // 128

            def some(j, carry, given=given, lanes=lanes, first=first):
                top = pl.multiple_of(j * 128, 128)
                for lane in range(lanes):
                    part = given[pl.ds(top, 128), lane * 128 : lane * 128 + 128]
                    linear[pl.ds(first + top * lanes + lane, 128, stride=lanes), :] = part.astype(jnp.float32)
                return carry

            lax.fori_loop(0, height // 128, some, 0)
        first, count = vector_rows()
        linear[first : first + count, :] = ins[-1][...]
        rest = linear.shape[0] - first - count
        linear[first + count :, :] = jnp.zeros((rest, 128), jnp.float32)

    def two(j, carry):
        parts = []
        for half in range(2):
            block = order_ref[step * (rows // 8) + j * 2 + half]
            parts.append(linear[pl.ds(pl.multiple_of(block * 8, 8), 8), :])
        low_ref[pl.ds(pl.multiple_of(j * 16, 16), 16), :] = jnp.concatenate(parts, axis=0).astype(low_ref.dtype)
        return carry

    lax.fori_loop(0, rows // 16, two, 0, unroll=8)


def collect_packed(grads, slots, blocks, shards, rows):
    return pl.pallas_call(
        collect_kernel,
        out_shape=jax.ShapeDtypeStruct((shards, rows, 128), jnp.bfloat16),
        grid_spec=pltpu.PrefetchScalarGridSpec(
            num_scalar_prefetch=1,
            grid=(shards,),
            in_specs=[pl.BlockSpec(grad.shape, lambda s, order: (0, 0), pipeline_mode=pl.Buffered(1)) for grad in grads],
            out_specs=pl.BlockSpec((None, rows, 128), lambda s, order: (s, 0, 0)),
            scratch_shapes=[pltpu.VMEM(((blocks + 1) * 8, 128), jnp.float32)],
        ),
        compiler_params=pltpu.CompilerParams(vmem_limit_bytes=60 << 20),
        name="collect_packed",
    )(slots, *grads)


def layer_norm(values, gain, shift):
    center = values - jnp.mean(values, axis=-1, keepdims=True)
    spread = jnp.mean(center * center, axis=-1, keepdims=True)
    return center * lax.rsqrt(spread + 1e-06) * gain + shift


def embed_waves(wavelength):
    half_width = E // 2
    frequency = jnp.exp(-math.log(10000.0) * jnp.arange(half_width, dtype=jnp.float32) / half_width)
    angles = wavelength.astype(jnp.float32)[..., None] * frequency
    return jnp.concatenate([jnp.sin(angles), jnp.cos(angles)], axis=-1)


def hyper_layer(embedded, params):
    highest = lax.Precision.HIGHEST
    groups = embedded.shape[0]
    head_size = E // HH
    queries = jnp.einsum("gbe,ef->gbf", embedded, params["h_query"], precision=highest).reshape(
        groups, NB, HH, head_size
    )
    keys_h = jnp.einsum("gbe,ef->gbf", embedded, params["h_key"], precision=highest).reshape(
        groups, NB, HH, head_size
    )
    values_h = jnp.einsum("gbe,ef->gbf", embedded, params["h_value"], precision=highest).reshape(
        groups, NB, HH, head_size
    )
    scores = jnp.einsum("gbhc,gthc->ghbt", queries, keys_h, precision=highest) * head_size ** (-0.5)
    softmax_w = jax.nn.softmax(scores, axis=-1)
    mixed = jnp.einsum("ghbt,gthc->gbhc", softmax_w, values_h, precision=highest).reshape(
        groups, NB, E
    )
    attended = jnp.einsum("gbe,ef->gbf", mixed, params["h_out"], precision=highest)
    first_norm = layer_norm(embedded + attended, params["hn1_gain"], params["hn1_shift"])
    inner = jax.nn.gelu(
        jnp.einsum("gbe,ef->gbf", first_norm, params["h_ffin"], precision=highest),
        approximate=False,
    )
    outer = jnp.einsum("gbf,fe->gbe", inner, params["h_ffout"], precision=highest)
    second_norm = layer_norm(first_norm + outer, params["hn2_gain"], params["hn2_shift"])
    return second_norm + embedded


def tall(count):
    return -(-count // 16) * 16


def dot_nn(a, b):
    return lax.dot_general(a, b, (((1,), (0,)), ((), ())), preferred_element_type=jnp.float32)


def dot_nt(a, b):
    return lax.dot_general(a, b, (((1,), (1,)), ((), ())), preferred_element_type=jnp.float32)


def dot_tn(a, b):
    return lax.dot_general(a, b, (((0,), (0,)), ((), ())), preferred_element_type=jnp.float32)


def block_kernel(stream_ref, up_ref, vec_ref, wqkv_hbm, wout_hbm, wup_hbm, wdown_hbm,
                 out_ref, low_ref, gvec_ref, gqkv_hbm, gout_hbm, gup_hbm, gdown_hbm,
                 wqkv, wout, wup, wdown, gqkv, gout, gup, gdown,
                 xs, ups, up_low, norm_one, qkv, att, probs, mid, norm_two, acc, hid_low, datt, dqkv, in_sem, out_sem):
    f32, bf16 = jnp.float32, jnp.bfloat16
    seq = stream_ref.shape[0]
    rows = xs.shape[0]
    loads = [
        pltpu.make_async_copy(src, dst, in_sem.at[j])
        for j, (src, dst) in enumerate(((wqkv_hbm, wqkv), (wout_hbm, wout), (wup_hbm, wup), (wdown_hbm, wdown)))
    ]
    for load in loads:
        load.start()
    stores = [
        pltpu.make_async_copy(src, dst, out_sem.at[j])
        for j, (src, dst) in enumerate(((gqkv, gqkv_hbm), (gout, gout_hbm), (gup, gup_hbm), (gdown, gdown_hbm)))
    ]
    gain_one, shift_one = vec_ref[0:1, :], vec_ref[1:2, :]
    gain_two, shift_two = vec_ref[2:3, :], vec_ref[3:4, :]
    xs[...] = jnp.zeros_like(xs)
    xs[0:seq, :] = stream_ref[...] + vec_ref[4:5, :]
    ups[...] = jnp.zeros_like(ups)
    ups[0:seq, :] = up_ref[...].astype(f32)
    up_low[...] = ups[...].astype(bf16)

    def normed(values):
        center = values - jnp.mean(values, axis=-1, keepdims=True)
        scale = lax.rsqrt(jnp.mean(center * center, axis=-1, keepdims=True) + 1e-06)
        return center * scale, scale

    def normed_back(grad, unit, scale, gain):
        inner = grad * gain
        return scale * (
            inner
            - jnp.mean(inner, axis=-1, keepdims=True)
            - unit * jnp.mean(inner * unit, axis=-1, keepdims=True)
        )

    unit, scale = normed(xs[...])
    norm_one[...] = (unit * gain_one + shift_one).astype(bf16)
    loads[0].wait()

    def tile(j, size=D):
        return pl.ds(pl.multiple_of(j * size, size), size)

    def each(count, body):
        lax.fori_loop(0, count, lambda j, carry: (body(j), carry)[1], 0)

    def qkv_part(j):
        qkv[:, tile(j)] = dot_nn(norm_one[...], wqkv[:, tile(j)]).astype(bf16)

    each(3, qkv_part)
    inside = lax.broadcasted_iota(jnp.int32, (rows, rows), 1) < seq

    def heads(p):
        pair = [qkv[:, pl.ds(pl.multiple_of(j * D + p * 128, 128), 128)] for j in range(3)]
        outs = []
        for h in range(2):
            query, key, value = (part[:, h * HD : h * HD + HD] for part in pair)
            scores = jnp.where(inside, dot_nt(query, key) * (HD**-0.5), -1e30)
            weight = jnp.exp(scores - jnp.max(scores, axis=-1, keepdims=True))
            weight = weight / jnp.sum(weight, axis=-1, keepdims=True)
            probs[p * 2 + h] = weight
            outs.append(dot_nn(weight.astype(bf16), value))
        att[:, pl.ds(pl.multiple_of(p * 128, 128), 128)] = jnp.concatenate(outs, axis=1).astype(bf16)

    each(HEADS // 2, heads)
    loads[1].wait()
    mid[...] = xs[...] + dot_nn(att[...], wout[...])
    unit, scale = normed(mid[...])
    norm_two[...] = (unit * gain_two + shift_two).astype(bf16)
    loads[2].wait()
    loads[3].wait()
    acc[...] = jnp.zeros_like(acc)

    def hidden_part(j):
        hidden = dot_nn(norm_two[...], wup[:, tile(j)])
        half = 0.5 * (1.0 + lax.erf(hidden * (0.5**0.5)))
        active = (hidden * half).astype(bf16)
        slope = half + hidden * jnp.exp(-0.5 * hidden * hidden) * (2.0 * math.pi) ** -0.5
        mid[...] += dot_nn(active, wdown[tile(j), :])
        gdown[tile(j), :] = dot_tn(active, up_low[...]).astype(bf16)
        grad_hidden = (dot_nt(up_low[...], wdown[tile(j), :]) * slope).astype(bf16)
        gup[:, tile(j)] = dot_tn(norm_two[...], grad_hidden).astype(bf16)
        acc[...] += dot_nt(grad_hidden, wup[:, tile(j)])

    kept_unit, kept_scale = unit, scale
    hid_low[...] = kept_unit
    each(HID // D, hidden_part)
    stores[2].start()
    stores[3].start()
    out_ref[...] = mid[0:seq, :].astype(bf16)
    grad = acc[...]
    unit = hid_low[...]
    gvec_ref[...] = jnp.zeros_like(gvec_ref)
    gvec_ref[2:3, :] = jnp.sum(grad * unit, axis=0, keepdims=True)
    gvec_ref[3:4, :] = jnp.sum(grad, axis=0, keepdims=True)
    ups[...] += normed_back(grad, unit, kept_scale, gain_two)
    up_low[...] = ups[...].astype(bf16)
    gout[...] = dot_tn(att[...], up_low[...]).astype(bf16)
    stores[1].start()
    datt[...] = dot_nt(up_low[...], wout[...]).astype(bf16)

    def heads_back(p):
        pair = [qkv[:, pl.ds(pl.multiple_of(j * D + p * 128, 128), 128)] for j in range(3)]
        grad_pair = datt[:, pl.ds(pl.multiple_of(p * 128, 128), 128)]
        grads = [[], [], []]
        for h in range(2):
            query, key, value = (part[:, h * HD : h * HD + HD] for part in pair)
            grad_out = grad_pair[:, h * HD : h * HD + HD]
            weight = probs[p * 2 + h]
            grad_weight = dot_nt(grad_out, value)
            grads[2].append(dot_tn(weight.astype(bf16), grad_out))
            grad_score = weight * (grad_weight - jnp.sum(weight * grad_weight, axis=-1, keepdims=True))
            grad_score = grad_score.astype(bf16)
            grads[0].append(dot_nn(grad_score, key) * (HD**-0.5))
            grads[1].append(dot_tn(grad_score, query) * (HD**-0.5))
        for j in range(3):
            dqkv[:, pl.ds(pl.multiple_of(j * D + p * 128, 128), 128)] = jnp.concatenate(grads[j], axis=1).astype(bf16)

    each(HEADS // 2, heads_back)
    acc[...] = jnp.zeros_like(acc)

    def qkv_back(j):
        gqkv[:, tile(j)] = dot_tn(norm_one[...], dqkv[:, tile(j)]).astype(bf16)
        acc[...] += dot_nt(dqkv[:, tile(j)], wqkv[:, tile(j)])

    each(3, qkv_back)
    stores[0].start()
    unit, scale = normed(xs[...])
    grad = acc[...]
    gvec_ref[0:1, :] = jnp.sum(grad * unit, axis=0, keepdims=True)
    gvec_ref[1:2, :] = jnp.sum(grad, axis=0, keepdims=True)
    total = ups[...] + normed_back(grad, unit, scale, gain_one)
    gvec_ref[4:5, :] = jnp.sum(total, axis=0, keepdims=True)
    low_ref[...] = total.astype(bf16)
    for store in stores:
        store.wait()


def block_pass(stream, upstream, vectors, wqkv, wout, wup, wdown):
    f32, bf16 = jnp.float32, jnp.bfloat16
    seq = stream.shape[0]
    rows = tall(seq)
    whole = pl.BlockSpec(memory_space=pltpu.VMEM)
    far = pl.BlockSpec(memory_space=pl.ANY)
    mats = [wqkv, wout, wup, wdown]
    kept = [pltpu.VMEM(mat.shape, bf16) for mat in mats]
    dma = pltpu.SemaphoreType.DMA
    return pl.pallas_call(
        block_kernel,
        out_shape=[
            jax.ShapeDtypeStruct((seq, D), bf16),
            jax.ShapeDtypeStruct((rows, D), bf16),
            jax.ShapeDtypeStruct((8, D), f32),
        ]
        + [jax.ShapeDtypeStruct(mat.shape, bf16) for mat in mats],
        in_specs=[whole] * 3 + [far] * 4,
        out_specs=[whole] * 3 + [far] * 4,
        scratch_shapes=kept
        + kept
        + [
            pltpu.VMEM((rows, D), f32),
            pltpu.VMEM((rows, D), f32),
            pltpu.VMEM((rows, D), bf16),
            pltpu.VMEM((rows, D), bf16),
            pltpu.VMEM((rows, 3 * D), bf16),
            pltpu.VMEM((rows, D), bf16),
            pltpu.VMEM((HEADS, rows, rows), f32),
            pltpu.VMEM((rows, D), f32),
            pltpu.VMEM((rows, D), bf16),
            pltpu.VMEM((rows, D), f32),
            pltpu.VMEM((rows, D), f32),
            pltpu.VMEM((rows, D), bf16),
            pltpu.VMEM((rows, 3 * D), bf16),
            dma((4,)),
            dma((4,)),
        ],
        compiler_params=pltpu.CompilerParams(vmem_limit_bytes=60 << 20),
        cost_estimate=pl.CostEstimate(flops=8_400_000_000, bytes_accessed=30_000_000, transcendentals=2_000_000),
        name="block_pass",
    )(stream, upstream, vectors, *mats)


def adamw_step(weight, moment_one, moment_two, grad, rate):
    first = beta_one * moment_one + (1.0 - beta_one) * grad
    second = beta_two * moment_two + (1.0 - beta_two) * grad * grad
    fix_one = 1.0 - beta_one**STEP
    fix_two = 1.0 - beta_two**STEP
    update = first / fix_one / (jnp.sqrt(second / fix_two) + epsilon_add) + decay_rate * weight
    return (weight - rate * update, first, second)


NC = 8


def dims_step(count):
    return 16 if count % 16 == 0 else count


def make_kernel(shaped_ref, master_ref, kernel_ref, turned):
    dims = kernel_ref.shape[0]
    for dim in range(dims):
        part = dot_nn(shaped_ref[...], master_ref[:, dim * PATCH : (dim + 1) * PATCH])
        turned[pl.ds(dim, NB, stride=dims), :] = part[:, :128]
        turned[pl.ds(NB * dims + dim, NB, stride=dims), :] = part[:, 128:]
    for band in range(NB):
        for half in range(2):
            row = half * NB * dims + band * dims
            lane = band * PATCH + half * 128
            kernel_ref[:, lane : lane + 128] = turned[row : row + dims, :].astype(kernel_ref.dtype)


def make_kernels(shaped, master):
    dims = master.shape[1] // PATCH
    step = dims_step(dims)
    return pl.pallas_call(
        make_kernel,
        out_shape=jax.ShapeDtypeStruct((dims, NB * PATCH), jnp.bfloat16),
        grid=(dims // step,),
        in_specs=[
            pl.BlockSpec(shaped.shape, lambda j: (0, 0)),
            pl.BlockSpec((E, step * PATCH), lambda j: (0, j)),
        ],
        out_specs=pl.BlockSpec((step, NB * PATCH), lambda j: (j, 0)),
        scratch_shapes=[pltpu.VMEM((2 * NB * step, 128), jnp.float32)],
        compiler_params=pltpu.CompilerParams(vmem_limit_bytes=60 << 20),
        name="make_kernels",
    )(shaped, master)


def embed_kernel(pixel_ref, mask_ref, kernel_ref, stream_ref):
    masked = pixel_ref[...] * mask_ref[...].astype(jnp.bfloat16)
    part = dot_nt(masked, kernel_ref[...])

    @pl.when(pl.program_id(0) == 0)
    def _():
        stream_ref[...] = part

    @pl.when(pl.program_id(0) > 0)
    def _():
        stream_ref[...] += part


def embed_patches(pixels, mask, kernels):
    seq, width = pixels.shape[1], pixels.shape[2]
    cut = 1024
    return pl.pallas_call(
        embed_kernel,
        out_shape=jax.ShapeDtypeStruct((seq, D), jnp.float32),
        grid=(width // cut,),
        in_specs=[
            pl.BlockSpec((None, seq, cut), lambda j: (0, 0, j)),
            pl.BlockSpec((1, cut), lambda j: (0, j)),
            pl.BlockSpec((D, cut), lambda j: (0, j)),
        ],
        out_specs=pl.BlockSpec((seq, D), lambda j: (0, 0)),
        compiler_params=pltpu.CompilerParams(vmem_limit_bytes=60 << 20),
        name="embed_patches",
    )(pixels, mask, kernels)


def unembed_kernel(pixel_ref, mask_ref, kernel_ref, low_ref, back_ref, grad_ref, masked):
    seq = pixel_ref.shape[0]
    mask = mask_ref[...]
    masked[...] = jnp.zeros_like(masked)
    masked[0:seq, :] = pixel_ref[...].astype(jnp.float32) * mask
    back_ref[...] = (dot_nn(low_ref[...], kernel_ref[...])[0:seq] * mask).astype(back_ref.dtype)
    grad_ref[...] = dot_tn(low_ref[...], masked[...].astype(jnp.bfloat16)).astype(grad_ref.dtype)


def unembed_patches(pixels, mask, kernels, low):
    seq, width = pixels.shape[1], pixels.shape[2]
    cut = 1024
    return pl.pallas_call(
        unembed_kernel,
        out_shape=[
            jax.ShapeDtypeStruct(pixels.shape, jnp.bfloat16),
            jax.ShapeDtypeStruct((D, width), jnp.bfloat16),
        ],
        grid=(width // cut,),
        in_specs=[
            pl.BlockSpec((None, seq, cut), lambda j: (0, 0, j)),
            pl.BlockSpec((1, cut), lambda j: (0, j)),
            pl.BlockSpec((D, cut), lambda j: (0, j)),
            pl.BlockSpec(low.shape, lambda j: (0, 0)),
        ],
        out_specs=[
            pl.BlockSpec((None, seq, cut), lambda j: (0, 0, j)),
            pl.BlockSpec((D, cut), lambda j: (0, j)),
        ],
        scratch_shapes=[pltpu.VMEM((low.shape[0], cut), jnp.float32)],
        compiler_params=pltpu.CompilerParams(vmem_limit_bytes=60 << 20),
        name="unembed_patches",
    )(pixels, mask, kernels, low)


def master_kernel(rate, grad_ref, shaped_ref, weight_ref, one_ref, two_ref, new_ref, first_ref, second_ref, back_ref, turned):
    groups, dims = grad_ref.shape[0], grad_ref.shape[1]
    bands = groups * NB
    for group in range(groups):
        for band in range(NB):
            for half in range(2):
                row = half * bands * dims + (group * NB + band) * dims
                lane = band * PATCH + half * 128
                turned[row : row + dims, :] = grad_ref[group, :, lane : lane + 128].astype(jnp.float32)
    total = jnp.zeros(back_ref.shape, jnp.float32)
    for dim in range(dims):
        part = jnp.concatenate(
            [turned[pl.ds(half * bands * dims + dim, bands, stride=dims), :] for half in range(2)], axis=1
        ).astype(jnp.bfloat16)
        lanes = slice(dim * PATCH, (dim + 1) * PATCH)
        weight = weight_ref[:, lanes]
        total += dot_nt(part, weight.astype(jnp.bfloat16))
        grad = dot_tn(shaped_ref[...], part)
        new_ref[:, lanes], first_ref[:, lanes], second_ref[:, lanes] = adamw_step(
            weight, one_ref[:, lanes], two_ref[:, lanes], grad, rate
        )

    @pl.when(pl.program_id(0) == 0)
    def _():
        back_ref[...] = total

    @pl.when(pl.program_id(0) > 0)
    def _():
        back_ref[...] += total


def master_update(grads, shaped, weight, one, two, rate):
    groups, dims = grads.shape[0], grads.shape[1]
    step = dims_step(dims)
    columns = pl.BlockSpec((weight.shape[0], step * PATCH), lambda j: (0, j))
    like = jax.ShapeDtypeStruct(weight.shape, jnp.float32)
    return pl.pallas_call(
        functools.partial(master_kernel, rate),
        out_shape=[like, like, like, jax.ShapeDtypeStruct(shaped.shape, jnp.float32)],
        grid=(dims // step,),
        in_specs=[
            pl.BlockSpec((groups, step, NB * PATCH), lambda j: (0, j, 0)),
            pl.BlockSpec(shaped.shape, lambda j: (0, 0)),
            columns,
            columns,
            columns,
        ],
        out_specs=[columns, columns, columns, pl.BlockSpec(shaped.shape, lambda j: (0, 0))],
        scratch_shapes=[pltpu.VMEM((2 * groups * NB * step, 128), jnp.float32)],
        compiler_params=pltpu.CompilerParams(vmem_limit_bytes=60 << 20),
        name="master_update",
    )(grads, shaped, weight, one, two)


def spot():
    group = lax.axis_index("group")
    image = lax.axis_index("img")
    return group // 2, group % 2, image // 2, image % 2


def place(y, c, z, x):
    return (y * 2 + c, z * 2 + x)


def partners():
    y, c, z, x = spot()
    x2, y2 = x + (1 - c) * (1 - 2 * x), y + c * (1 - 2 * y)
    x3, y3 = x + c * (1 - 2 * x), y + (1 - c) * (1 - 2 * y)
    around = [place(y, c, (z + d) % 4, x) for d in (1, 2, 3)]
    return (x2, y2), (x3, y3), around, place(y2, c, z, x2), place(y3, c, z, x3), place(y, 1 - c, z, x)


def greet(peers):
    barrier = pltpu.get_barrier_semaphore()
    for peer in peers:
        pl.semaphore_signal(barrier, inc=1, device_id=peer, device_id_type=MESH)
    pl.semaphore_wait(barrier, len(peers))


def gather_kernel(own_ref, all_ref, local_sem, line_send, line_recv, group_send, group_recv, twin_send, twin_recv):
    y, c, z, x = spot()
    (x2, y2), (x3, y3), around, second, third, twin = partners()
    rows = own_ref.shape[0] // NC

    def cut(k):
        return pl.ds(k * rows, rows)

    def remote(src, dst, send_sem, recv_sem, target):
        return pltpu.make_async_remote_copy(
            src_ref=src, dst_ref=dst, send_sem=send_sem, recv_sem=recv_sem, device_id=target, device_id_type=MESH
        )

    def along(d, k):
        return remote(own_ref.at[cut(k)], all_ref.at[y, c, z, x, cut(k)], line_send.at[d - 1, k], line_recv.at[d - 1, k], around[d - 1])

    def along_in(d, k):
        return remote(own_ref.at[cut(k)], all_ref.at[y, c, (z + 4 - d) % 4, x, cut(k)], line_send.at[d - 1, k], line_recv.at[d - 1, k], around[d - 1])

    def square(core, j):
        yy, xx = ((y, x), (y2, x2), (y3, x3), (1 - y, 1 - x))[j]
        return all_ref.at[yy, core, :, xx]

    def hop(j, to, k, slot, landing):
        part = square(c, j).at[:, cut(k)]
        return remote(part, part, group_send.at[slot, k], group_recv.at[landing, k], to)

    def hop_in(landing, k):
        part = square(c, landing).at[:, cut(k)]
        return remote(part, part, group_send.at[0, k], group_recv.at[landing, k], twin)

    def share(j, k):
        part = square(c, j).at[:, cut(k)]
        yy, xx = ((y, x), (y2, x2), (y3, x3), (1 - y, 1 - x))[j]
        landing = (0, 2, 1, 3)[j]
        return remote(part, part, twin_send.at[j, k], twin_recv.at[landing, k], twin)

    def share_in(landing, k):
        yy, xx = ((y, x), (y2, x2), (y3, x3), (1 - y, 1 - x))[landing]
        part = all_ref.at[yy, 1 - c, :, xx, cut(k)]
        return remote(part, part, twin_send.at[0, k], twin_recv.at[landing, k], twin)

    keep = pltpu.make_async_copy(own_ref, all_ref.at[y, c, z, x], local_sem)
    keep.start()
    greet(around + [second, third, twin])
    for k in range(NC):
        for d in (1, 2, 3):
            along(d, k).start()
    keep.wait()
    for step in range(NC + 2):
        k = step
        if k < NC:
            for d in (1, 2, 3):
                along_in(d, k).wait_recv()
            hop(0, third, k, 0, 2).start()
            hop(0, second, k, 1, 1).start()
            share(0, k).start()
        k = step - 1
        if 0 <= k < NC:
            hop_in(1, k).wait_recv()
            hop(1, third, k, 2, 3).start()
            share(1, k).start()
        k = step - 2
        if 0 <= k < NC:
            hop_in(2, k).wait_recv()
            share(2, k).start()
            hop_in(3, k).wait_recv()
            share(3, k).start()
    for k in range(NC):
        for d in (1, 2, 3):
            along(d, k).wait_send()
        hop(0, third, k, 0, 2).wait_send()
        hop(0, second, k, 1, 1).wait_send()
        hop(1, third, k, 2, 3).wait_send()
        for j in range(4):
            share(j, k).wait_send()
            share_in(j, k).wait_recv()


def gather_packed(own):
    rows = own.shape[0]
    dma = pltpu.SemaphoreType.DMA
    return pl.pallas_call(
        gather_kernel,
        out_shape=jax.ShapeDtypeStruct((2, 2, 4, 2, rows, 128), own.dtype),
        in_specs=[pl.BlockSpec(memory_space=pl.ANY)],
        out_specs=pl.BlockSpec(memory_space=pl.ANY),
        scratch_shapes=[dma, dma((3, NC)), dma((3, NC)), dma((3, NC)), dma((4, NC)), dma((4, NC)), dma((4, NC))],
        compiler_params=pltpu.CompilerParams(collective_id=0, has_side_effects=True, vmem_limit_bytes=60 << 20),
        name="gather_packed",
    )(own)


def reduce_kernel(part_ref, sum_ref, own, twin_in, third_in, second_in, line_in, load_sem, twin_send, twin_recv, third_send, third_recv, second_send, second_recv, line_send, line_recv):
    f32, bf16 = jnp.float32, jnp.bfloat16
    y, c, z, x = spot()
    (x2, y2), (x3, y3), around, second, third, twin = partners()
    rows = sum_ref.shape[0] // NC

    def cut(k):
        return pl.ds(k * rows, rows)

    def remote(src, dst, send_sem, recv_sem, target):
        return pltpu.make_async_remote_copy(
            src_ref=src, dst_ref=dst, send_sem=send_sem, recv_sem=recv_sem, device_id=target, device_id_type=MESH
        )

    spots = ((1 - y, 1 - x), (y3, x3), (y2, x2), (y, x))
    turned = ((1 - y, 1 - x), (y2, x2), (y3, x3), (y, x))

    def load(j, k):
        yy, xx = spots[j]
        return pltpu.make_async_copy(part_ref.at[yy, c, :, xx, cut(k)], own.at[j, :, cut(k)], load_sem.at[j, k])

    def swap(j, k):
        yy, xx = turned[j]
        return remote(part_ref.at[yy, 1 - c, :, xx, cut(k)], twin_in.at[j, :, cut(k)], twin_send.at[j, k], twin_recv.at[j, k], twin)

    def to_third(j, k):
        return remote(own.at[j, :, cut(k)], third_in.at[j, :, cut(k)], third_send.at[j, k], third_recv.at[j, k], third)

    def to_second(k):
        return remote(own.at[2, :, cut(k)], second_in.at[:, cut(k)], second_send.at[k], second_recv.at[k], second)

    def to_line(d, k):
        return remote(own.at[3, (z + d) % 4, cut(k)], line_in.at[d - 1, cut(k)], line_send.at[d - 1, k], line_recv.at[d - 1, k], around[d - 1])

    for k in range(NC):
        for j in range(4):
            load(j, k).start()
    greet(around + [second, third, twin])
    for k in range(NC):
        for j in range(4):
            swap(j, k).start()

    def pair(j, k):
        load(j, k).wait()
        swap(j, k).wait_recv()
        return own[j, :, cut(k)].astype(f32) + twin_in[j, :, cut(k)].astype(f32)

    for step in range(NC + 3):
        k = step
        if k < NC:
            for j in (0, 1):
                own[j, :, cut(k)] = pair(j, k).astype(bf16)
                to_third(j, k).start()
        k = step - 1
        if 0 <= k < NC:
            held = pair(2, k)
            to_third(0, k).wait_recv()
            own[2, :, cut(k)] = (held + third_in[0, :, cut(k)].astype(f32)).astype(bf16)
            to_second(k).start()
        k = step - 2
        if 0 <= k < NC:
            held = pair(3, k)
            to_third(1, k).wait_recv()
            to_second(k).wait_recv()
            held += third_in[1, :, cut(k)].astype(f32) + second_in[:, cut(k)].astype(f32)
            own[3, :, cut(k)] = held.astype(bf16)
            for d in (1, 2, 3):
                to_line(d, k).start()
        k = step - 3
        if 0 <= k < NC:
            total = own[3, z, cut(k)].astype(f32)
            for d in (1, 2, 3):
                to_line(d, k).wait_recv()
                total += line_in[d - 1, cut(k)].astype(f32)
            sum_ref[cut(k)] = total
    for k in range(NC):
        for j in range(4):
            swap(j, k).wait_send()
        for j in (0, 1):
            to_third(j, k).wait_send()
        to_second(k).wait_send()
        for d in (1, 2, 3):
            to_line(d, k).wait_send()


def reduce_packed(part):
    rows = part.shape[-2]
    bf16 = jnp.bfloat16
    dma = pltpu.SemaphoreType.DMA
    return pl.pallas_call(
        reduce_kernel,
        out_shape=jax.ShapeDtypeStruct((rows, 128), jnp.float32),
        in_specs=[pl.BlockSpec(memory_space=pl.ANY)],
        out_specs=pl.BlockSpec(memory_space=pltpu.VMEM),
        scratch_shapes=[
            pltpu.VMEM((4, 4, rows, 128), bf16),
            pltpu.VMEM((4, 4, rows, 128), bf16),
            pltpu.VMEM((2, 4, rows, 128), bf16),
            pltpu.VMEM((4, rows, 128), bf16),
            pltpu.VMEM((3, rows, 128), bf16),
            dma((4, NC)), dma((4, NC)), dma((4, NC)), dma((2, NC)), dma((2, NC)), dma((NC,)), dma((NC,)), dma((3, NC)), dma((3, NC)),
        ],
        compiler_params=pltpu.CompilerParams(collective_id=1, has_side_effects=True, vmem_limit_bytes=56 << 20),
        name="reduce_packed",
    )(part)


def on_device(
    pixels,
    band_mask,
    wavelength,
    owner_order,
    rest_weight,
    rest_moment1,
    rest_moment2,
    fc_weight,
    fc_moment1,
    fc_moment2,
    cotangent,
):
    f32 = jnp.float32
    bf16 = jnp.bfloat16
    kernel_rate = float(E * PATCH * NB) ** (-0.5)
    groups = lax.axis_size("group")
    own_rows = rest_weight.shape[0]
    own_blocks = own_rows // 8
    fits = lax.axis_size("group") == 4 and lax.axis_size("img") == 8
    extra = -own_rows % 128
    slot_blocks = (own_rows + extra) // 8
    rest_low = jnp.pad(rest_weight.astype(bf16), ((0, extra), (0, 0)))
    if fits:
        gathered = gather_packed(rest_low)
    else:
        gathered = lax.all_gather(rest_low, ("group", "img"), axis=0, tiled=True)
    shards = gathered.size // ((own_rows + extra) * 128)
    gathered = gathered.reshape(shards, own_rows + extra, 128)
    total_blocks = owner_order.shape[0]
    slots = jnp.pad(
        owner_order.reshape(shards, own_blocks),
        ((0, 0), (0, slot_blocks - own_blocks)),
        constant_values=total_blocks,
    ).reshape(-1)
    unpacked = spread_packed(gathered, slots, total_blocks)
    weights = {entry[0]: matrix for entry, matrix in zip(matrices(), unpacked)}
    vectors = unpacked[-1].reshape(-1)
    at = 0
    for entry_name, extent in layout():
        if len(extent) == 1:
            weights[entry_name] = vectors[at : at + extent[0]]
            at += extent[0]
    block_vectors = jnp.pad(vectors[: 5 * D].reshape(5, D), ((0, 3), (0, 0)))
    hyper_names = [
        "h_query",
        "h_key",
        "h_value",
        "h_out",
        "h_ffin",
        "h_ffout",
        "hn1_gain",
        "hn1_shift",
        "hn2_gain",
        "hn2_shift",
    ]
    hyper_params = {entry_name: weights[entry_name].astype(f32) for entry_name in hyper_names}
    embedded = embed_waves(wavelength)

    def hyper_run(params_in):
        return hyper_layer(embedded, params_in)

    shaped, hyper_pull = jax.vjp(hyper_run, hyper_params)
    shaped_low = shaped.astype(bf16)
    band_width = E // groups
    group_id = lax.axis_index("group")
    own_shaped = lax.dynamic_slice_in_dim(shaped_low, group_id * band_width, band_width, 2)
    master = lax.all_gather(fc_weight.astype(bf16), "group", axis=0, tiled=True)
    group_shaped = lax.dynamic_index_in_dim(shaped_low, group_id, 0, keepdims=False)
    kernel_low = make_kernels(group_shaped, master)
    mask = jnp.repeat(band_mask.astype(f32), PATCH, axis=1)
    kernel_all = lax.all_gather(kernel_low, "img", axis=0, tiled=True)
    stream = embed_patches(pixels, mask, kernel_all)
    block_out, grad_low, block_vectors, *block_grads = block_pass(
        stream, cotangent, block_vectors, *(weights[entry[0]] for entry in matrices()[:4])
    )
    pixel_grad, kernel_grad = unembed_patches(pixels, mask, kernel_all, grad_low)
    kernel_grad_low = lax.psum_scatter(kernel_grad, "img", scatter_dimension=0, tiled=True)
    all_groups = lax.all_gather(kernel_grad_low[None], "group", axis=0, tiled=True)
    fc_new, fc_first, fc_second, shaped_part = master_update(
        all_groups,
        own_shaped.reshape(groups * NB, band_width),
        fc_weight,
        fc_moment1,
        fc_moment2,
        kernel_rate,
    )
    grad_shaped = lax.dynamic_update_slice_in_dim(
        jnp.zeros((groups, NB, E), f32),
        shaped_part.reshape(groups, NB, band_width),
        group_id * band_width,
        2,
    )
    (hyper_grads,) = hyper_pull(grad_shaped)
    given = list(block_grads) + [hyper_grads[entry[0]] for entry in matrices()[4:]]
    pieces = [block_vectors[:5].reshape(-1)]
    pieces += [hyper_grads[name] for name, extent in layout() if extent == (E,)]
    pieces.append(jnp.zeros((vector_rows()[1] * 128 - at,), f32))
    given.append(jnp.concatenate(pieces).reshape(-1, 128))
    joint_term = collect_packed(given, slots, total_blocks, shards, own_rows + extra)
    if fits:
        rest_grad = reduce_packed(joint_term.reshape(2, 2, 4, 2, own_rows + extra, 128))
    else:
        rest_grad = lax.psum_scatter(
            joint_term, ("group", "img"), scatter_dimension=0, tiled=False
        ).astype(f32)
    rest_grad = rest_grad[:own_rows]
    rest_new, rest_first, rest_second = adamw_step(
        rest_weight, rest_moment1, rest_moment2, rest_grad, rest_rate
    )
    return (block_out, pixel_grad, rest_new, rest_first, rest_second, fc_new, fc_first, fc_second)


def solution(mesh):
    placed = (
        P(("group", "img"), None, None),
        P(("group", "img"), None),
        P(),
        P(),
        P(("group", "img"), None),
        P(("group", "img"), None),
        P(("group", "img"), None),
        P("group", "img"),
        P("group", "img"),
        P("group", "img"),
        P(("group", "img"), None),
    )
    return jax.shard_map(
        on_device,
        mesh=mesh,
        in_specs=placed,
        out_specs=(
            P(("group", "img"), None),
            P(("group", "img"), None, None),
            P(("group", "img"), None),
            P(("group", "img"), None),
            P(("group", "img"), None),
            P("group", "img"),
            P("group", "img"),
            P("group", "img"),
        ),
        check_vma=False,
    )
```

```python
import functools
import math

import jax
import jax.numpy as jnp
from jax import lax
from jax.experimental import pallas as pl
from jax.experimental.pallas import tpu as pltpu
from jax.sharding import PartitionSpec as P

MESH = pl.DeviceIdType.MESH

D = 768
HEADS = 12
HD = 64
HID = 3072
E = 128
HH = 4
HFF = 2048
PATCH = 256
NB = 32
STEP = 5


beta_one = 0.5
beta_two = 0.75
decay_rate = 0.05
epsilon_add = 1e-08
rest_rate = 0.02


def layout():
    return [
        ("w_qkv", (D, 3 * D)),
        ("w_out", (D, D)),
        ("w_up", (D, HID)),
        ("w_down", (HID, D)),
        ("h_query", (E, E)),
        ("h_key", (E, E)),
        ("h_value", (E, E)),
        ("h_out", (E, E)),
        ("h_ffin", (E, HFF)),
        ("h_ffout", (HFF, E)),
        ("ln1_gain", (D,)),
        ("ln1_shift", (D,)),
        ("ln2_gain", (D,)),
        ("ln2_shift", (D,)),
        ("patch_bias", (D,)),
        ("hn1_gain", (E,)),
        ("hn1_shift", (E,)),
        ("hn2_gain", (E,)),
        ("hn2_shift", (E,)),
    ]


def matrices():
    listed, at = [], 0
    for name, extent in layout():
        if len(extent) == 2:
            listed.append((name, extent[0], extent[1], at))
        at += math.prod(extent) // 128
    return listed


def vector_rows():
    first = sum(math.prod(extent) // 128 for _, extent in layout() if len(extent) == 2)
    count = sum(math.prod(extent) // 128 for _, extent in layout() if len(extent) == 1)
    return first, -(-count // 8) * 8


def spread_kernel(order_ref, low_ref, *refs):
    outs, linear = refs[:-1], refs[-1]
    step = pl.program_id(0)
    rows = low_ref.shape[0]

    def two(j, carry):
        pair = low_ref[pl.ds(pl.multiple_of(j * 16, 16), 16), :].astype(jnp.float32)
        for half in range(2):
            block = order_ref[step * (rows // 8) + j * 2 + half]
            linear[pl.ds(pl.multiple_of(block * 8, 8), 8), :] = pair[half * 8 : half * 8 + 8]
        return carry

    lax.fori_loop(0, rows // 16, two, 0, unroll=8)

    @pl.when(step == pl.num_programs(0) - 1)
    def _():
        for (name, height, width, first), out in zip(matrices(), outs):
            lanes = width // 128

            def some(j, carry, out=out, lanes=lanes, first=first):
                top = pl.multiple_of(j * 128, 128)
                for lane in range(lanes):
                    part = linear[pl.ds(first + top * lanes + lane, 128, stride=lanes), :]
                    out[pl.ds(top, 128), lane * 128 : lane * 128 + 128] = part.astype(out.dtype)
                return carry

            lax.fori_loop(0, height // 128, some, 0)
        first, count = vector_rows()
        outs[-1][...] = linear[first : first + count, :]


def spread_packed(gathered, slots, blocks):
    shards, rows = gathered.shape[0], gathered.shape[1]
    shapes = [
        jax.ShapeDtypeStruct((height, width), jnp.bfloat16 if name.startswith("w_") else jnp.float32)
        for name, height, width, first in matrices()
    ]
    shapes.append(jax.ShapeDtypeStruct((vector_rows()[1], 128), jnp.float32))
    return pl.pallas_call(
        spread_kernel,
        out_shape=shapes,
        grid_spec=pltpu.PrefetchScalarGridSpec(
            num_scalar_prefetch=1,
            grid=(shards,),
            in_specs=[pl.BlockSpec((None, rows, 128), lambda s, order: (s, 0, 0))],
            out_specs=[pl.BlockSpec(shape.shape, lambda s, order: (0, 0), pipeline_mode=pl.Buffered(1)) for shape in shapes],
            scratch_shapes=[pltpu.VMEM(((blocks + 1) * 8, 128), jnp.float32)],
        ),
        compiler_params=pltpu.CompilerParams(vmem_limit_bytes=60 << 20),
        name="spread_packed",
    )(slots, gathered)


def collect_kernel(order_ref, *refs):
    ins, low_ref, linear = refs[:-2], refs[-2], refs[-1]
    step = pl.program_id(0)
    rows = low_ref.shape[0]

    @pl.when(step == 0)
    def _():
        for (name, height, width, first), given in zip(matrices(), ins):
            lanes = width // 128

            def some(j, carry, given=given, lanes=lanes, first=first):
                top = pl.multiple_of(j * 128, 128)
                for lane in range(lanes):
                    part = given[pl.ds(top, 128), lane * 128 : lane * 128 + 128]
                    linear[pl.ds(first + top * lanes + lane, 128, stride=lanes), :] = part.astype(jnp.float32)
                return carry

            lax.fori_loop(0, height // 128, some, 0)
        first, count = vector_rows()
        linear[first : first + count, :] = ins[-1][...]
        rest = linear.shape[0] - first - count
        linear[first + count :, :] = jnp.zeros((rest, 128), jnp.float32)

    def two(j, carry):
        parts = []
        for half in range(2):
            block = order_ref[step * (rows // 8) + j * 2 + half]
            parts.append(linear[pl.ds(pl.multiple_of(block * 8, 8), 8), :])
        low_ref[pl.ds(pl.multiple_of(j * 16, 16), 16), :] = jnp.concatenate(parts, axis=0).astype(low_ref.dtype)
        return carry

    lax.fori_loop(0, rows // 16, two, 0, unroll=8)


def collect_packed(grads, slots, blocks, shards, rows):
    return pl.pallas_call(
        collect_kernel,
        out_shape=jax.ShapeDtypeStruct((shards, rows, 128), jnp.bfloat16),
        grid_spec=pltpu.PrefetchScalarGridSpec(
            num_scalar_prefetch=1,
            grid=(shards,),
            in_specs=[pl.BlockSpec(grad.shape, lambda s, order: (0, 0), pipeline_mode=pl.Buffered(1)) for grad in grads],
            out_specs=pl.BlockSpec((None, rows, 128), lambda s, order: (s, 0, 0)),
            scratch_shapes=[pltpu.VMEM(((blocks + 1) * 8, 128), jnp.float32)],
        ),
        compiler_params=pltpu.CompilerParams(vmem_limit_bytes=60 << 20),
        name="collect_packed",
    )(slots, *grads)


def layer_norm(values, gain, shift):
    center = values - jnp.mean(values, axis=-1, keepdims=True)
    spread = jnp.mean(center * center, axis=-1, keepdims=True)
    return center * lax.rsqrt(spread + 1e-06) * gain + shift


def embed_waves(wavelength):
    half_width = E // 2
    frequency = jnp.exp(-math.log(10000.0) * jnp.arange(half_width, dtype=jnp.float32) / half_width)
    angles = wavelength.astype(jnp.float32)[..., None] * frequency
    return jnp.concatenate([jnp.sin(angles), jnp.cos(angles)], axis=-1)


def hyper_layer(embedded, params):
    highest = lax.Precision.HIGHEST
    groups = embedded.shape[0]
    head_size = E // HH
    queries = jnp.einsum("gbe,ef->gbf", embedded, params["h_query"], precision=highest).reshape(
        groups, NB, HH, head_size
    )
    keys_h = jnp.einsum("gbe,ef->gbf", embedded, params["h_key"], precision=highest).reshape(
        groups, NB, HH, head_size
    )
    values_h = jnp.einsum("gbe,ef->gbf", embedded, params["h_value"], precision=highest).reshape(
        groups, NB, HH, head_size
    )
    scores = jnp.einsum("gbhc,gthc->ghbt", queries, keys_h, precision=highest) * head_size ** (-0.5)
    softmax_w = jax.nn.softmax(scores, axis=-1)
    mixed = jnp.einsum("ghbt,gthc->gbhc", softmax_w, values_h, precision=highest).reshape(
        groups, NB, E
    )
    attended = jnp.einsum("gbe,ef->gbf", mixed, params["h_out"], precision=highest)
    first_norm = layer_norm(embedded + attended, params["hn1_gain"], params["hn1_shift"])
    inner = jax.nn.gelu(
        jnp.einsum("gbe,ef->gbf", first_norm, params["h_ffin"], precision=highest),
        approximate=False,
    )
    outer = jnp.einsum("gbf,fe->gbe", inner, params["h_ffout"], precision=highest)
    second_norm = layer_norm(first_norm + outer, params["hn2_gain"], params["hn2_shift"])
    return second_norm + embedded


def tall(count):
    return -(-count // 16) * 16


def dot_nn(a, b):
    return lax.dot_general(a, b, (((1,), (0,)), ((), ())), preferred_element_type=jnp.float32)


def dot_nt(a, b):
    return lax.dot_general(a, b, (((1,), (1,)), ((), ())), preferred_element_type=jnp.float32)


def dot_tn(a, b):
    return lax.dot_general(a, b, (((0,), (0,)), ((), ())), preferred_element_type=jnp.float32)


def block_kernel(stream_ref, up_ref, vec_ref, wqkv_hbm, wout_hbm, wup_hbm, wdown_hbm,
                 out_ref, low_ref, gvec_ref, gqkv_hbm, gout_hbm, gup_hbm, gdown_hbm,
                 wqkv, wout, wup, wdown, gqkv, gout, gup, gdown,
                 xs, ups, up_low, norm_one, qkv, att, probs, mid, norm_two, acc, hid_low, datt, dqkv, in_sem, out_sem):
    f32, bf16 = jnp.float32, jnp.bfloat16
    seq = stream_ref.shape[0]
    rows = xs.shape[0]
    loads = [
        pltpu.make_async_copy(src, dst, in_sem.at[j])
        for j, (src, dst) in enumerate(((wqkv_hbm, wqkv), (wout_hbm, wout), (wup_hbm, wup), (wdown_hbm, wdown)))
    ]
    for load in loads:
        load.start()
    stores = [
        pltpu.make_async_copy(src, dst, out_sem.at[j])
        for j, (src, dst) in enumerate(((gqkv, gqkv_hbm), (gout, gout_hbm), (gup, gup_hbm), (gdown, gdown_hbm)))
    ]
    gain_one, shift_one = vec_ref[0:1, :], vec_ref[1:2, :]
    gain_two, shift_two = vec_ref[2:3, :], vec_ref[3:4, :]
    xs[...] = jnp.zeros_like(xs)
    xs[0:seq, :] = stream_ref[...] + vec_ref[4:5, :]
    ups[...] = jnp.zeros_like(ups)
    ups[0:seq, :] = up_ref[...].astype(f32)
    up_low[...] = ups[...].astype(bf16)

    def normed(values):
        center = values - jnp.mean(values, axis=-1, keepdims=True)
        scale = lax.rsqrt(jnp.mean(center * center, axis=-1, keepdims=True) + 1e-06)
        return center * scale, scale

    def normed_back(grad, unit, scale, gain):
        inner = grad * gain
        return scale * (
            inner
            - jnp.mean(inner, axis=-1, keepdims=True)
            - unit * jnp.mean(inner * unit, axis=-1, keepdims=True)
        )

    unit, scale = normed(xs[...])
    norm_one[...] = (unit * gain_one + shift_one).astype(bf16)
    loads[0].wait()

    def tile(j, size=D):
        return pl.ds(pl.multiple_of(j * size, size), size)

    def each(count, body):
        lax.fori_loop(0, count, lambda j, carry: (body(j), carry)[1], 0)

    def qkv_part(j):
        qkv[:, tile(j)] = dot_nn(norm_one[...], wqkv[:, tile(j)]).astype(bf16)

    each(3, qkv_part)
    inside = lax.broadcasted_iota(jnp.int32, (rows, rows), 1) < seq

    def heads(p):
        pair = [qkv[:, pl.ds(pl.multiple_of(j * D + p * 128, 128), 128)] for j in range(3)]
        outs = []
        for h in range(2):
            query, key, value = (part[:, h * HD : h * HD + HD] for part in pair)
            scores = jnp.where(inside, dot_nt(query, key) * (HD**-0.5), -1e30)
            weight = jnp.exp(scores - jnp.max(scores, axis=-1, keepdims=True))
            weight = weight / jnp.sum(weight, axis=-1, keepdims=True)
            probs[p * 2 + h] = weight
            outs.append(dot_nn(weight.astype(bf16), value))
        att[:, pl.ds(pl.multiple_of(p * 128, 128), 128)] = jnp.concatenate(outs, axis=1).astype(bf16)

    each(HEADS // 2, heads)
    loads[1].wait()
    mid[...] = xs[...] + dot_nn(att[...], wout[...])
    unit, scale = normed(mid[...])
    norm_two[...] = (unit * gain_two + shift_two).astype(bf16)
    loads[2].wait()
    loads[3].wait()
    acc[...] = jnp.zeros_like(acc)

    def hidden_part(j):
        hidden = dot_nn(norm_two[...], wup[:, tile(j)])
        half = 0.5 * (1.0 + lax.erf(hidden * (0.5**0.5)))
        active = (hidden * half).astype(bf16)
        slope = half + hidden * jnp.exp(-0.5 * hidden * hidden) * (2.0 * math.pi) ** -0.5
        mid[...] += dot_nn(active, wdown[tile(j), :])
        gdown[tile(j), :] = dot_tn(active, up_low[...]).astype(bf16)
        grad_hidden = (dot_nt(up_low[...], wdown[tile(j), :]) * slope).astype(bf16)
        gup[:, tile(j)] = dot_tn(norm_two[...], grad_hidden).astype(bf16)
        acc[...] += dot_nt(grad_hidden, wup[:, tile(j)])

    kept_unit, kept_scale = unit, scale
    hid_low[...] = kept_unit
    each(HID // D, hidden_part)
    stores[2].start()
    stores[3].start()
    out_ref[...] = mid[0:seq, :].astype(bf16)
    grad = acc[...]
    unit = hid_low[...]
    gvec_ref[...] = jnp.zeros_like(gvec_ref)
    gvec_ref[2:3, :] = jnp.sum(grad * unit, axis=0, keepdims=True)
    gvec_ref[3:4, :] = jnp.sum(grad, axis=0, keepdims=True)
    ups[...] += normed_back(grad, unit, kept_scale, gain_two)
    up_low[...] = ups[...].astype(bf16)
    gout[...] = dot_tn(att[...], up_low[...]).astype(bf16)
    stores[1].start()
    datt[...] = dot_nt(up_low[...], wout[...]).astype(bf16)

    def heads_back(p):
        pair = [qkv[:, pl.ds(pl.multiple_of(j * D + p * 128, 128), 128)] for j in range(3)]
        grad_pair = datt[:, pl.ds(pl.multiple_of(p * 128, 128), 128)]
        grads = [[], [], []]
        for h in range(2):
            query, key, value = (part[:, h * HD : h * HD + HD] for part in pair)
            grad_out = grad_pair[:, h * HD : h * HD + HD]
            weight = probs[p * 2 + h]
            grad_weight = dot_nt(grad_out, value)
            grads[2].append(dot_tn(weight.astype(bf16), grad_out))
            grad_score = weight * (grad_weight - jnp.sum(weight * grad_weight, axis=-1, keepdims=True))
            grad_score = grad_score.astype(bf16)
            grads[0].append(dot_nn(grad_score, key) * (HD**-0.5))
            grads[1].append(dot_tn(grad_score, query) * (HD**-0.5))
        for j in range(3):
            dqkv[:, pl.ds(pl.multiple_of(j * D + p * 128, 128), 128)] = jnp.concatenate(grads[j], axis=1).astype(bf16)

    each(HEADS // 2, heads_back)
    acc[...] = jnp.zeros_like(acc)

    def qkv_back(j):
        gqkv[:, tile(j)] = dot_tn(norm_one[...], dqkv[:, tile(j)]).astype(bf16)
        acc[...] += dot_nt(dqkv[:, tile(j)], wqkv[:, tile(j)])

    each(3, qkv_back)
    stores[0].start()
    unit, scale = normed(xs[...])
    grad = acc[...]
    gvec_ref[0:1, :] = jnp.sum(grad * unit, axis=0, keepdims=True)
    gvec_ref[1:2, :] = jnp.sum(grad, axis=0, keepdims=True)
    total = ups[...] + normed_back(grad, unit, scale, gain_one)
    gvec_ref[4:5, :] = jnp.sum(total, axis=0, keepdims=True)
    low_ref[...] = total.astype(bf16)
    for store in stores:
        store.wait()


def block_pass(stream, upstream, vectors, wqkv, wout, wup, wdown):
    f32, bf16 = jnp.float32, jnp.bfloat16
    seq = stream.shape[0]
    rows = tall(seq)
    whole = pl.BlockSpec(memory_space=pltpu.VMEM)
    far = pl.BlockSpec(memory_space=pl.ANY)
    mats = [wqkv, wout, wup, wdown]
    kept = [pltpu.VMEM(mat.shape, bf16) for mat in mats]
    dma = pltpu.SemaphoreType.DMA
    return pl.pallas_call(
        block_kernel,
        out_shape=[
            jax.ShapeDtypeStruct((seq, D), bf16),
            jax.ShapeDtypeStruct((rows, D), bf16),
            jax.ShapeDtypeStruct((8, D), f32),
        ]
        + [jax.ShapeDtypeStruct(mat.shape, bf16) for mat in mats],
        in_specs=[whole] * 3 + [far] * 4,
        out_specs=[whole] * 3 + [far] * 4,
        scratch_shapes=kept
        + kept
        + [
            pltpu.VMEM((rows, D), f32),
            pltpu.VMEM((rows, D), f32),
            pltpu.VMEM((rows, D), bf16),
            pltpu.VMEM((rows, D), bf16),
            pltpu.VMEM((rows, 3 * D), bf16),
            pltpu.VMEM((rows, D), bf16),
            pltpu.VMEM((HEADS, rows, rows), f32),
            pltpu.VMEM((rows, D), f32),
            pltpu.VMEM((rows, D), bf16),
            pltpu.VMEM((rows, D), f32),
            pltpu.VMEM((rows, D), f32),
            pltpu.VMEM((rows, D), bf16),
            pltpu.VMEM((rows, 3 * D), bf16),
            dma((4,)),
            dma((4,)),
        ],
        compiler_params=pltpu.CompilerParams(vmem_limit_bytes=60 << 20),
        cost_estimate=pl.CostEstimate(flops=8_400_000_000, bytes_accessed=30_000_000, transcendentals=2_000_000),
        name="block_pass",
    )(stream, upstream, vectors, *mats)


def adamw_step(weight, moment_one, moment_two, grad, rate):
    first = beta_one * moment_one + (1.0 - beta_one) * grad
    second = beta_two * moment_two + (1.0 - beta_two) * grad * grad
    fix_one = 1.0 - beta_one**STEP
    fix_two = 1.0 - beta_two**STEP
    update = first / fix_one / (jnp.sqrt(second / fix_two) + epsilon_add) + decay_rate * weight
    return (weight - rate * update, first, second)


NC = 8


def dims_step(count):
    return 16 if count % 16 == 0 else count


def make_kernel(shaped_ref, master_ref, kernel_ref, turned):
    dims = kernel_ref.shape[0]
    for dim in range(dims):
        part = dot_nn(shaped_ref[...], master_ref[:, dim * PATCH : (dim + 1) * PATCH])
        turned[pl.ds(dim, NB, stride=dims), :] = part[:, :128]
        turned[pl.ds(NB * dims + dim, NB, stride=dims), :] = part[:, 128:]
    for band in range(NB):
        for half in range(2):
            row = half * NB * dims + band * dims
            lane = band * PATCH + half * 128
            kernel_ref[:, lane : lane + 128] = turned[row : row + dims, :].astype(kernel_ref.dtype)


def make_kernels(shaped, master):
    dims = master.shape[1] // PATCH
    step = dims_step(dims)
    return pl.pallas_call(
        make_kernel,
        out_shape=jax.ShapeDtypeStruct((dims, NB * PATCH), jnp.bfloat16),
        grid=(dims // step,),
        in_specs=[
            pl.BlockSpec(shaped.shape, lambda j: (0, 0)),
            pl.BlockSpec((E, step * PATCH), lambda j: (0, j)),
        ],
        out_specs=pl.BlockSpec((step, NB * PATCH), lambda j: (j, 0)),
        scratch_shapes=[pltpu.VMEM((2 * NB * step, 128), jnp.float32)],
        compiler_params=pltpu.CompilerParams(vmem_limit_bytes=60 << 20),
        name="make_kernels",
    )(shaped, master)


def embed_kernel(pixel_ref, mask_ref, kernel_ref, stream_ref):
    masked = pixel_ref[...] * mask_ref[...].astype(jnp.bfloat16)
    part = dot_nt(masked, kernel_ref[...])

    @pl.when(pl.program_id(0) == 0)
    def _():
        stream_ref[...] = part

    @pl.when(pl.program_id(0) > 0)
    def _():
        stream_ref[...] += part


def embed_patches(pixels, mask, kernels):
    seq, width = pixels.shape[1], pixels.shape[2]
    cut = 1024
    return pl.pallas_call(
        embed_kernel,
        out_shape=jax.ShapeDtypeStruct((seq, D), jnp.float32),
        grid=(width // cut,),
        in_specs=[
            pl.BlockSpec((None, seq, cut), lambda j: (0, 0, j)),
            pl.BlockSpec((1, cut), lambda j: (0, j)),
            pl.BlockSpec((D, cut), lambda j: (0, j)),
        ],
        out_specs=pl.BlockSpec((seq, D), lambda j: (0, 0)),
        compiler_params=pltpu.CompilerParams(vmem_limit_bytes=60 << 20),
        name="embed_patches",
    )(pixels, mask, kernels)


def unembed_kernel(pixel_ref, mask_ref, kernel_ref, low_ref, back_ref, grad_ref, masked):
    seq = pixel_ref.shape[0]
    mask = mask_ref[...]
    masked[...] = jnp.zeros_like(masked)
    masked[0:seq, :] = pixel_ref[...].astype(jnp.float32) * mask
    back_ref[...] = (dot_nn(low_ref[...], kernel_ref[...])[0:seq] * mask).astype(back_ref.dtype)
    grad_ref[...] = dot_tn(low_ref[...], masked[...].astype(jnp.bfloat16)).astype(grad_ref.dtype)


def unembed_patches(pixels, mask, kernels, low):
    seq, width = pixels.shape[1], pixels.shape[2]
    cut = 1024
    return pl.pallas_call(
        unembed_kernel,
        out_shape=[
            jax.ShapeDtypeStruct(pixels.shape, jnp.bfloat16),
            jax.ShapeDtypeStruct((D, width), jnp.bfloat16),
        ],
        grid=(width // cut,),
        in_specs=[
            pl.BlockSpec((None, seq, cut), lambda j: (0, 0, j)),
            pl.BlockSpec((1, cut), lambda j: (0, j)),
            pl.BlockSpec((D, cut), lambda j: (0, j)),
            pl.BlockSpec(low.shape, lambda j: (0, 0)),
        ],
        out_specs=[
            pl.BlockSpec((None, seq, cut), lambda j: (0, 0, j)),
            pl.BlockSpec((D, cut), lambda j: (0, j)),
        ],
        scratch_shapes=[pltpu.VMEM((low.shape[0], cut), jnp.float32)],
        compiler_params=pltpu.CompilerParams(vmem_limit_bytes=60 << 20),
        name="unembed_patches",
    )(pixels, mask, kernels, low)


def master_kernel(rate, grad_ref, shaped_ref, weight_ref, one_ref, two_ref, new_ref, first_ref, second_ref, back_ref, turned):
    groups, dims = grad_ref.shape[0], grad_ref.shape[1]
    bands = groups * NB
    for group in range(groups):
        for band in range(NB):
            for half in range(2):
                row = half * bands * dims + (group * NB + band) * dims
                lane = band * PATCH + half * 128
                turned[row : row + dims, :] = grad_ref[group, :, lane : lane + 128].astype(jnp.float32)
    total = jnp.zeros(back_ref.shape, jnp.float32)
    for dim in range(dims):
        part = jnp.concatenate(
            [turned[pl.ds(half * bands * dims + dim, bands, stride=dims), :] for half in range(2)], axis=1
        ).astype(jnp.bfloat16)
        lanes = slice(dim * PATCH, (dim + 1) * PATCH)
        weight = weight_ref[:, lanes]
        total += dot_nt(part, weight.astype(jnp.bfloat16))
        grad = dot_tn(shaped_ref[...], part)
        new_ref[:, lanes], first_ref[:, lanes], second_ref[:, lanes] = adamw_step(
            weight, one_ref[:, lanes], two_ref[:, lanes], grad, rate
        )

    @pl.when(pl.program_id(0) == 0)
    def _():
        back_ref[...] = total

    @pl.when(pl.program_id(0) > 0)
    def _():
        back_ref[...] += total


def master_update(grads, shaped, weight, one, two, rate):
    groups, dims = grads.shape[0], grads.shape[1]
    step = dims_step(dims)
    columns = pl.BlockSpec((weight.shape[0], step * PATCH), lambda j: (0, j))
    like = jax.ShapeDtypeStruct(weight.shape, jnp.float32)
    return pl.pallas_call(
        functools.partial(master_kernel, rate),
        out_shape=[like, like, like, jax.ShapeDtypeStruct(shaped.shape, jnp.float32)],
        grid=(dims // step,),
        in_specs=[
            pl.BlockSpec((groups, step, NB * PATCH), lambda j: (0, j, 0)),
            pl.BlockSpec(shaped.shape, lambda j: (0, 0)),
            columns,
            columns,
            columns,
        ],
        out_specs=[columns, columns, columns, pl.BlockSpec(shaped.shape, lambda j: (0, 0))],
        scratch_shapes=[pltpu.VMEM((2 * groups * NB * step, 128), jnp.float32)],
        compiler_params=pltpu.CompilerParams(vmem_limit_bytes=60 << 20),
        name="master_update",
    )(grads, shaped, weight, one, two)


def spot():
    group = lax.axis_index("group")
    image = lax.axis_index("img")
    return group // 2, group % 2, image // 2, image % 2


def place(y, c, z, x):
    return (y * 2 + c, z * 2 + x)


def partners():
    y, c, z, x = spot()
    x2, y2 = x + (1 - c) * (1 - 2 * x), y + c * (1 - 2 * y)
    x3, y3 = x + c * (1 - 2 * x), y + (1 - c) * (1 - 2 * y)
    around = [place(y, c, (z + d) % 4, x) for d in (1, 2, 3)]
    return (x2, y2), (x3, y3), around, place(y2, c, z, x2), place(y3, c, z, x3), place(y, 1 - c, z, x)


def greet(peers):
    barrier = pltpu.get_barrier_semaphore()
    for peer in peers:
        pl.semaphore_signal(barrier, inc=1, device_id=peer, device_id_type=MESH)
    pl.semaphore_wait(barrier, len(peers))


def gather_kernel(own_ref, all_ref, local_sem, line_send, line_recv, group_send, group_recv, twin_send, twin_recv):
    y, c, z, x = spot()
    (x2, y2), (x3, y3), around, second, third, twin = partners()
    rows = own_ref.shape[0] // NC

    def cut(k):
        return pl.ds(k * rows, rows)

    def remote(src, dst, send_sem, recv_sem, target):
        return pltpu.make_async_remote_copy(
            src_ref=src, dst_ref=dst, send_sem=send_sem, recv_sem=recv_sem, device_id=target, device_id_type=MESH
        )

    def along(d, k):
        return remote(own_ref.at[cut(k)], all_ref.at[y, c, z, x, cut(k)], line_send.at[d - 1, k], line_recv.at[d - 1, k], around[d - 1])

    def along_in(d, k):
        return remote(own_ref.at[cut(k)], all_ref.at[y, c, (z + 4 - d) % 4, x, cut(k)], line_send.at[d - 1, k], line_recv.at[d - 1, k], around[d - 1])

    def square(core, j):
        yy, xx = ((y, x), (y2, x2), (y3, x3), (1 - y, 1 - x))[j]
        return all_ref.at[yy, core, :, xx]

    def hop(j, to, k, slot, landing):
        part = square(c, j).at[:, cut(k)]
        return remote(part, part, group_send.at[slot, k], group_recv.at[landing, k], to)

    def hop_in(landing, k):
        part = square(c, landing).at[:, cut(k)]
        return remote(part, part, group_send.at[0, k], group_recv.at[landing, k], twin)

    def share(j, k):
        part = square(c, j).at[:, cut(k)]
        yy, xx = ((y, x), (y2, x2), (y3, x3), (1 - y, 1 - x))[j]
        landing = (0, 2, 1, 3)[j]
        return remote(part, part, twin_send.at[j, k], twin_recv.at[landing, k], twin)

    def share_in(landing, k):
        yy, xx = ((y, x), (y2, x2), (y3, x3), (1 - y, 1 - x))[landing]
        part = all_ref.at[yy, 1 - c, :, xx, cut(k)]
        return remote(part, part, twin_send.at[0, k], twin_recv.at[landing, k], twin)

    keep = pltpu.make_async_copy(own_ref, all_ref.at[y, c, z, x], local_sem)
    keep.start()
    greet(around + [second, third, twin])
    for k in range(NC):
        for d in (1, 2, 3):
            along(d, k).start()
    keep.wait()
    for step in range(NC + 2):
        k = step
        if k < NC:
            for d in (1, 2, 3):
                along_in(d, k).wait_recv()
            hop(0, third, k, 0, 2).start()
            hop(0, second, k, 1, 1).start()
            share(0, k).start()
        k = step - 1
        if 0 <= k < NC:
            hop_in(1, k).wait_recv()
            hop(1, third, k, 2, 3).start()
            share(1, k).start()
        k = step - 2
        if 0 <= k < NC:
            hop_in(2, k).wait_recv()
            share(2, k).start()
            hop_in(3, k).wait_recv()
            share(3, k).start()
    for k in range(NC):
        for d in (1, 2, 3):
            along(d, k).wait_send()
        hop(0, third, k, 0, 2).wait_send()
        hop(0, second, k, 1, 1).wait_send()
        hop(1, third, k, 2, 3).wait_send()
        for j in range(4):
            share(j, k).wait_send()
            share_in(j, k).wait_recv()


def gather_packed(own):
    rows = own.shape[0]
    dma = pltpu.SemaphoreType.DMA
    return pl.pallas_call(
        gather_kernel,
        out_shape=jax.ShapeDtypeStruct((2, 2, 4, 2, rows, 128), own.dtype),
        in_specs=[pl.BlockSpec(memory_space=pl.ANY)],
        out_specs=pl.BlockSpec(memory_space=pl.ANY),
        scratch_shapes=[dma, dma((3, NC)), dma((3, NC)), dma((3, NC)), dma((4, NC)), dma((4, NC)), dma((4, NC))],
        compiler_params=pltpu.CompilerParams(collective_id=0, has_side_effects=True, vmem_limit_bytes=60 << 20),
        name="gather_packed",
    )(own)


def reduce_kernel(part_ref, sum_ref, own, twin_in, third_in, second_in, line_in, load_sem, twin_send, twin_recv, third_send, third_recv, second_send, second_recv, line_send, line_recv):
    f32, bf16 = jnp.float32, jnp.bfloat16
    y, c, z, x = spot()
    (x2, y2), (x3, y3), around, second, third, twin = partners()
    rows = sum_ref.shape[0] // NC

    def cut(k):
        return pl.ds(k * rows, rows)

    def remote(src, dst, send_sem, recv_sem, target):
        return pltpu.make_async_remote_copy(
            src_ref=src, dst_ref=dst, send_sem=send_sem, recv_sem=recv_sem, device_id=target, device_id_type=MESH
        )

    spots = ((1 - y, 1 - x), (y3, x3), (y2, x2), (y, x))
    turned = ((1 - y, 1 - x), (y2, x2), (y3, x3), (y, x))

    def load(j, k):
        yy, xx = spots[j]
        return pltpu.make_async_copy(part_ref.at[yy, c, :, xx, cut(k)], own.at[j, :, cut(k)], load_sem.at[j, k])

    def swap(j, k):
        yy, xx = turned[j]
        return remote(part_ref.at[yy, 1 - c, :, xx, cut(k)], twin_in.at[j, :, cut(k)], twin_send.at[j, k], twin_recv.at[j, k], twin)

    def to_third(j, k):
        return remote(own.at[j, :, cut(k)], third_in.at[j, :, cut(k)], third_send.at[j, k], third_recv.at[j, k], third)

    def to_second(k):
        return remote(own.at[2, :, cut(k)], second_in.at[:, cut(k)], second_send.at[k], second_recv.at[k], second)

    def to_line(d, k):
        return remote(own.at[3, (z + d) % 4, cut(k)], line_in.at[d - 1, cut(k)], line_send.at[d - 1, k], line_recv.at[d - 1, k], around[d - 1])

    for k in range(NC):
        for j in range(4):
            load(j, k).start()
    greet(around + [second, third, twin])
    for k in range(NC):
        for j in range(4):
            swap(j, k).start()

    def pair(j, k):
        load(j, k).wait()
        swap(j, k).wait_recv()
        return own[j, :, cut(k)].astype(f32) + twin_in[j, :, cut(k)].astype(f32)

    for step in range(NC + 3):
        k = step
        if k < NC:
            for j in (0, 1):
                own[j, :, cut(k)] = pair(j, k).astype(bf16)
                to_third(j, k).start()
        k = step - 1
        if 0 <= k < NC:
            held = pair(2, k)
            to_third(0, k).wait_recv()
            own[2, :, cut(k)] = (held + third_in[0, :, cut(k)].astype(f32)).astype(bf16)
            to_second(k).start()
        k = step - 2
        if 0 <= k < NC:
            held = pair(3, k)
            to_third(1, k).wait_recv()
            to_second(k).wait_recv()
            held += third_in[1, :, cut(k)].astype(f32) + second_in[:, cut(k)].astype(f32)
            own[3, :, cut(k)] = held.astype(bf16)
            for d in (1, 2, 3):
                to_line(d, k).start()
        k = step - 3
        if 0 <= k < NC:
            total = own[3, z, cut(k)].astype(f32)
            for d in (1, 2, 3):
                to_line(d, k).wait_recv()
                total += line_in[d - 1, cut(k)].astype(f32)
            sum_ref[cut(k)] = total
    for k in range(NC):
        for j in range(4):
            swap(j, k).wait_send()
        for j in (0, 1):
            to_third(j, k).wait_send()
        to_second(k).wait_send()
        for d in (1, 2, 3):
            to_line(d, k).wait_send()


def reduce_packed(part):
    rows = part.shape[-2]
    bf16 = jnp.bfloat16
    dma = pltpu.SemaphoreType.DMA
    return pl.pallas_call(
        reduce_kernel,
        out_shape=jax.ShapeDtypeStruct((rows, 128), jnp.float32),
        in_specs=[pl.BlockSpec(memory_space=pl.ANY)],
        out_specs=pl.BlockSpec(memory_space=pltpu.VMEM),
        scratch_shapes=[
            pltpu.VMEM((4, 4, rows, 128), bf16),
            pltpu.VMEM((4, 4, rows, 128), bf16),
            pltpu.VMEM((2, 4, rows, 128), bf16),
            pltpu.VMEM((4, rows, 128), bf16),
            pltpu.VMEM((3, rows, 128), bf16),
            dma((4, NC)), dma((4, NC)), dma((4, NC)), dma((2, NC)), dma((2, NC)), dma((NC,)), dma((NC,)), dma((3, NC)), dma((3, NC)),
        ],
        compiler_params=pltpu.CompilerParams(collective_id=1, has_side_effects=True, vmem_limit_bytes=56 << 20),
        name="reduce_packed",
    )(part)


CHUNK = 16


def over_x(k):
    return k % 2 == 0


def quad_peers():
    y, c, z, x = spot()
    low = z % 2
    side = place(y, c, z, 1 - x)
    along = place(y, c, z + 1 - 2 * low, x)
    twin = place(y, 1 - c, z, x)
    partner = place(y, 1 - c, (z + 2) % 4, x)
    moved = (c + z // 2) % 2 == 1
    return y, c, z, x, low, side, along, twin, partner, moved


def swap_images(value):
    pairs = []
    for y in range(2):
        for c in range(2):
            for z in range(4):
                for x in range(2):
                    other = (1 - c, (z + 2) % 4) if c != z // 2 else (c, z)
                    pairs.append((((y * 2 + c) * 4 + z) * 2 + x, ((y * 2 + other[0]) * 4 + other[1]) * 2 + x))
    return lax.ppermute(value, ("group", "img"), pairs)


def remote(src, dst, send_sem, recv_sem, target):
    return pltpu.make_async_remote_copy(
        src_ref=src, dst_ref=dst, send_sem=send_sem, recv_sem=recv_sem, device_id=target, device_id_type=MESH
    )


def share_kernel(made_ref, all_ref, keep_sem, swap_send, swap_recv, side_send, side_recv, along_send, along_recv, far_send, far_recv, twin_send, twin_recv):
    y, c, z, x, low, side, along, twin, partner, moved = quad_peers()
    count = made_ref.shape[0] // CHUNK

    def cut(k):
        return pl.ds(k * CHUNK, CHUNK)

    def block(core, j, k):
        return all_ref.at[2 * core + (low + j // 2) % 2, (x + j % 2) % 2, cut(k)]

    def keep(k):
        return pltpu.make_async_copy(made_ref.at[cut(k)], block(c, 0, k), keep_sem.at[k])

    def swap(k):
        return remote(made_ref.at[cut(k)], block(1 - c, 0, k), swap_send.at[k], swap_recv.at[k], partner)

    def swap_in(k):
        return remote(made_ref.at[cut(k)], block(c, 0, k), swap_send.at[k], swap_recv.at[k], partner)

    def to_side(k):
        return remote(block(c, 0, k), block(c, 0, k), side_send.at[k], side_recv.at[k], side)

    def from_side(k):
        return remote(block(c, 1, k), block(c, 1, k), side_send.at[k], side_recv.at[k], side)

    def to_along(k):
        return remote(block(c, 0, k), block(c, 0, k), along_send.at[k], along_recv.at[k], along)

    def from_along(k):
        return remote(block(c, 2, k), block(c, 2, k), along_send.at[k], along_recv.at[k], along)

    def pass_on(k):
        j, to = (2, side) if over_x(k) else (1, along)
        return remote(block(c, j, k), block(c, j, k), far_send.at[k], far_recv.at[k], to)

    def from_far(k):
        return remote(block(c, 3, k), block(c, 3, k), far_send.at[k], far_recv.at[k], twin)

    def give(j, k):
        return remote(block(c, j, k), block(c, j, k), twin_send.at[j, k], twin_recv.at[j, k], twin)

    def given(j, k):
        return remote(block(1 - c, j, k), block(1 - c, j, k), twin_send.at[j, k], twin_recv.at[j, k], twin)

    @pl.when(jnp.logical_not(moved))
    def _():
        for k in range(count):
            keep(k).start()

    greet([side, along, twin, partner])

    @pl.when(moved)
    def _():
        for k in range(count):
            swap(k).start()

    for step in range(count + 2):
        k = step
        if k < count:

            @pl.when(moved)
            def _(k=k):
                swap_in(k).wait_recv()

            @pl.when(jnp.logical_not(moved))
            def _(k=k):
                keep(k).wait()

            to_side(k).start()
            to_along(k).start()
            give(0, k).start()
        k = step - 1
        if 0 <= k < count:
            if over_x(k):
                from_along(k).wait_recv()
                pass_on(k).start()
                from_side(k).wait_recv()
            else:
                from_side(k).wait_recv()
                pass_on(k).start()
                from_along(k).wait_recv()
            give(1, k).start()
            give(2, k).start()
        k = step - 2
        if 0 <= k < count:
            from_far(k).wait_recv()
            give(3, k).start()

    @pl.when(moved)
    def _():
        for k in range(count):
            swap(k).wait_send()

    for k in range(count):
        to_side(k).wait_send()
        to_along(k).wait_send()
        pass_on(k).wait_send()
        for j in range(4):
            give(j, k).wait_send()
            given(j, k).wait_recv()


def share_kernels(made):
    dims, width = made.shape
    count = dims // CHUNK
    dma = pltpu.SemaphoreType.DMA
    shared = pl.pallas_call(
        share_kernel,
        out_shape=jax.ShapeDtypeStruct((4, 2, dims, width), made.dtype),
        in_specs=[pl.BlockSpec(memory_space=pl.ANY)],
        out_specs=pl.BlockSpec(memory_space=pl.ANY),
        scratch_shapes=[dma((count,))] * 9 + [dma((4, count))] * 2,
        compiler_params=pltpu.CompilerParams(collective_id=2, has_side_effects=True, vmem_limit_bytes=60 << 20),
        name="share_kernels",
    )(made)
    return shared.reshape(8 * dims, width)


def fold_kernel(part_ref, all_ref, own, twin_in, relay_in, side_in, along_in, load_sem, keep_sem, twin_send, twin_recv, relay_send, relay_recv,
                side_send, side_recv, along_send, along_recv, swap_send, swap_recv, group_send, group_recv, give_send, give_recv):
    f32, bf16 = jnp.float32, jnp.bfloat16
    y, c, z, x, low, side, along, twin, partner, moved = quad_peers()
    over = place(1 - y, c, z, x)
    count = all_ref.shape[2] // CHUNK

    def cut(k):
        return pl.ds(k * CHUNK, CHUNK)

    def part(core, j, k):
        return part_ref.at[2 * core + (low + j // 2) % 2, (x + j % 2) % 2, cut(k)]

    def load(j, k):
        return pltpu.make_async_copy(part(c, j, k), own.at[j, cut(k)], load_sem.at[j, k])

    def swap(j, k):
        return remote(part(1 - c, j, k), twin_in.at[j, cut(k)], twin_send.at[j, k], twin_recv.at[j, k], twin)

    def relay(k):
        return remote(own.at[3, cut(k)], relay_in.at[cut(k)], relay_send.at[k], relay_recv.at[k], along if over_x(k) else side)

    def to_side(k):
        return remote(own.at[1, cut(k)], side_in.at[cut(k)], side_send.at[k], side_recv.at[k], side)

    def to_along(k):
        return remote(own.at[2, cut(k)], along_in.at[cut(k)], along_send.at[k], along_recv.at[k], along)

    def keep(k):
        return pltpu.make_async_copy(own.at[0, cut(k)], all_ref.at[y, c, cut(k)], keep_sem.at[k])

    def move(k):
        return remote(own.at[0, cut(k)], all_ref.at[y, 1 - c, cut(k)], swap_send.at[k], swap_recv.at[k], partner)

    def moved_in(k):
        return remote(own.at[0, cut(k)], all_ref.at[y, c, cut(k)], swap_send.at[k], swap_recv.at[k], partner)

    def cross(k):
        return remote(all_ref.at[y, c, cut(k)], all_ref.at[y, c, cut(k)], group_send.at[k], group_recv.at[k], over)

    def crossed(k):
        return remote(all_ref.at[1 - y, c, cut(k)], all_ref.at[1 - y, c, cut(k)], group_send.at[k], group_recv.at[k], over)

    def give(j, k):
        here = all_ref.at[(y + j) % 2, c, cut(k)]
        return remote(here, here, give_send.at[j, k], give_recv.at[j, k], twin)

    def given(j, k):
        here = all_ref.at[(y + j) % 2, 1 - c, cut(k)]
        return remote(here, here, give_send.at[j, k], give_recv.at[j, k], twin)

    def pair(j, k):
        load(j, k).wait()
        swap(j, k).wait_recv()
        return own[j, cut(k)].astype(f32) + twin_in[j, cut(k)].astype(f32)

    for k in range(count):
        for j in (3, 1, 2, 0):
            load(j, k).start()
    greet([side, along, twin, partner, over])
    for k in range(count):
        for j in (3, 1, 2, 0):
            swap(j, k).start()

    for step in range(count + 4):
        k = step
        if k < count:
            own[3, cut(k)] = pair(3, k).astype(bf16)
            relay(k).start()
        k = step - 1
        if 0 <= k < count:
            first, second = (to_along, to_side) if over_x(k) else (to_side, to_along)
            plain, summed = (2, 1) if over_x(k) else (1, 2)
            own[plain, cut(k)] = pair(plain, k).astype(bf16)
            first(k).start()
            held = pair(summed, k)
            relay(k).wait_recv()
            own[summed, cut(k)] = (held + relay_in[cut(k)].astype(f32)).astype(bf16)
            second(k).start()
        k = step - 2
        if 0 <= k < count:
            held = pair(0, k)
            to_side(k).wait_recv()
            to_along(k).wait_recv()
            held += side_in[cut(k)].astype(f32) + along_in[cut(k)].astype(f32)
            own[0, cut(k)] = held.astype(bf16)

            @pl.when(moved)
            def _(k=k):
                move(k).start()

            @pl.when(jnp.logical_not(moved))
            def _(k=k):
                keep(k).start()

        k = step - 3
        if 0 <= k < count:

            @pl.when(moved)
            def _(k=k):
                moved_in(k).wait_recv()

            @pl.when(jnp.logical_not(moved))
            def _(k=k):
                keep(k).wait()

            cross(k).start()
            give(0, k).start()
        k = step - 4
        if 0 <= k < count:
            crossed(k).wait_recv()
            give(1, k).start()

    @pl.when(moved)
    def _():
        for k in range(count):
            move(k).wait_send()

    for k in range(count):
        for j in range(4):
            swap(j, k).wait_send()
        relay(k).wait_send()
        to_side(k).wait_send()
        to_along(k).wait_send()
        cross(k).wait_send()
        for j in range(2):
            give(j, k).wait_send()
            given(j, k).wait_recv()


def fold_kernels(part):
    width = part.shape[1]
    dims = part.shape[0] // 8
    count = dims // CHUNK
    bf16 = jnp.bfloat16
    dma = pltpu.SemaphoreType.DMA
    folded = pl.pallas_call(
        fold_kernel,
        out_shape=jax.ShapeDtypeStruct((2, 2, dims, width), bf16),
        in_specs=[pl.BlockSpec(memory_space=pl.ANY)],
        out_specs=pl.BlockSpec(memory_space=pl.ANY),
        scratch_shapes=[
            pltpu.VMEM((4, dims, width), bf16),
            pltpu.VMEM((4, dims, width), bf16),
            pltpu.VMEM((dims, width), bf16),
            pltpu.VMEM((dims, width), bf16),
            pltpu.VMEM((dims, width), bf16),
            dma((4, count)),
            dma((count,)),
            dma((4, count)),
            dma((4, count)),
        ]
        + [dma((count,))] * 10
        + [dma((2, count))] * 2,
        compiler_params=pltpu.CompilerParams(collective_id=3, has_side_effects=True, vmem_limit_bytes=60 << 20),
        name="fold_kernels",
    )(part.reshape(4, 2, dims, width))
    return folded.reshape(4, dims, width)


def on_device(
    pixels,
    band_mask,
    wavelength,
    owner_order,
    rest_weight,
    rest_moment1,
    rest_moment2,
    fc_weight,
    fc_moment1,
    fc_moment2,
    cotangent,
):
    f32 = jnp.float32
    bf16 = jnp.bfloat16
    kernel_rate = float(E * PATCH * NB) ** (-0.5)
    groups = lax.axis_size("group")
    own_rows = rest_weight.shape[0]
    own_blocks = own_rows // 8
    fits = lax.axis_size("group") == 4 and lax.axis_size("img") == 8
    extra = -own_rows % 128
    slot_blocks = (own_rows + extra) // 8
    mask = band_mask.astype(f32)
    low_weight = fc_weight.astype(bf16)
    rest_low = jnp.pad(rest_weight.astype(bf16), ((0, extra), (0, 0)))
    if fits:
        gathered = gather_packed(rest_low)
        gathered, pixels, cotangent, mask, low_weight = lax.optimization_barrier(
            (gathered, pixels, cotangent, mask, low_weight)
        )
        pixels, cotangent, mask = swap_images(pixels), swap_images(cotangent), swap_images(mask)
    else:
        gathered = lax.all_gather(rest_low, ("group", "img"), axis=0, tiled=True)
    shards = gathered.size // ((own_rows + extra) * 128)
    gathered = gathered.reshape(shards, own_rows + extra, 128)
    total_blocks = owner_order.shape[0]
    slots = jnp.pad(
        owner_order.reshape(shards, own_blocks),
        ((0, 0), (0, slot_blocks - own_blocks)),
        constant_values=total_blocks,
    ).reshape(-1)
    unpacked = spread_packed(gathered, slots, total_blocks)
    weights = {entry[0]: matrix for entry, matrix in zip(matrices(), unpacked)}
    vectors = unpacked[-1].reshape(-1)
    at = 0
    for entry_name, extent in layout():
        if len(extent) == 1:
            weights[entry_name] = vectors[at : at + extent[0]]
            at += extent[0]
    block_vectors = jnp.pad(vectors[: 5 * D].reshape(5, D), ((0, 3), (0, 0)))
    hyper_names = [
        "h_query",
        "h_key",
        "h_value",
        "h_out",
        "h_ffin",
        "h_ffout",
        "hn1_gain",
        "hn1_shift",
        "hn2_gain",
        "hn2_shift",
    ]
    hyper_params = {entry_name: weights[entry_name].astype(f32) for entry_name in hyper_names}
    embedded = embed_waves(wavelength)

    def hyper_run(params_in):
        return hyper_layer(embedded, params_in)

    shaped, hyper_pull = jax.vjp(hyper_run, hyper_params)
    shaped_low = shaped.astype(bf16)
    band_width = E // groups
    group_id = lax.axis_index("group")
    own_shaped = lax.dynamic_slice_in_dim(shaped_low, group_id * band_width, band_width, 2)
    master = lax.all_gather(low_weight, "group", axis=0, tiled=True)
    group_shaped = lax.dynamic_index_in_dim(shaped_low, group_id, 0, keepdims=False)
    kernel_low = make_kernels(group_shaped, master)
    mask = jnp.repeat(mask, PATCH, axis=1)
    if fits:
        kernel_all = share_kernels(kernel_low)
    else:
        kernel_all = lax.all_gather(kernel_low, "img", axis=0, tiled=True)
    stream = embed_patches(pixels, mask, kernel_all)
    block_out, grad_low, block_vectors, *block_grads = block_pass(
        stream, cotangent, block_vectors, *(weights[entry[0]] for entry in matrices()[:4])
    )
    pixel_grad, kernel_grad = unembed_patches(pixels, mask, kernel_all, grad_low)
    if fits:
        block_out, pixel_grad = swap_images(block_out), swap_images(pixel_grad)
        all_groups = fold_kernels(kernel_grad)
    else:
        kernel_grad_low = lax.psum_scatter(kernel_grad, "img", scatter_dimension=0, tiled=True)
        all_groups = lax.all_gather(kernel_grad_low[None], "group", axis=0, tiled=True)
    fc_new, fc_first, fc_second, shaped_part = master_update(
        all_groups,
        own_shaped.reshape(groups * NB, band_width),
        fc_weight,
        fc_moment1,
        fc_moment2,
        kernel_rate,
    )
    grad_shaped = lax.dynamic_update_slice_in_dim(
        jnp.zeros((groups, NB, E), f32),
        shaped_part.reshape(groups, NB, band_width),
        group_id * band_width,
        2,
    )
    (hyper_grads,) = hyper_pull(grad_shaped)
    given = list(block_grads) + [hyper_grads[entry[0]] for entry in matrices()[4:]]
    pieces = [block_vectors[:5].reshape(-1)]
    pieces += [hyper_grads[name] for name, extent in layout() if extent == (E,)]
    pieces.append(jnp.zeros((vector_rows()[1] * 128 - at,), f32))
    given.append(jnp.concatenate(pieces).reshape(-1, 128))
    joint_term = collect_packed(given, slots, total_blocks, shards, own_rows + extra)
    if fits:
        rest_grad = reduce_packed(joint_term.reshape(2, 2, 4, 2, own_rows + extra, 128))
    else:
        rest_grad = lax.psum_scatter(
            joint_term, ("group", "img"), scatter_dimension=0, tiled=False
        ).astype(f32)
    rest_grad = rest_grad[:own_rows]
    rest_new, rest_first, rest_second = adamw_step(
        rest_weight, rest_moment1, rest_moment2, rest_grad, rest_rate
    )
    return (block_out, pixel_grad, rest_new, rest_first, rest_second, fc_new, fc_first, fc_second)


def solution(mesh):
    placed = (
        P(("group", "img"), None, None),
        P(("group", "img"), None),
        P(),
        P(),
        P(("group", "img"), None),
        P(("group", "img"), None),
        P(("group", "img"), None),
        P("group", "img"),
        P("group", "img"),
        P("group", "img"),
        P(("group", "img"), None),
    )
    return jax.shard_map(
        on_device,
        mesh=mesh,
        in_specs=placed,
        out_specs=(
            P(("group", "img"), None),
            P(("group", "img"), None, None),
            P(("group", "img"), None),
            P(("group", "img"), None),
            P(("group", "img"), None),
            P("group", "img"),
            P("group", "img"),
            P("group", "img"),
        ),
        check_vma=False,
    )
```

```python
import functools
import math

import jax
import jax.numpy as jnp
from jax import lax
from jax.experimental import pallas as pl
from jax.experimental.pallas import tpu as pltpu
from jax.sharding import PartitionSpec as P

MESH = pl.DeviceIdType.MESH

D = 768
HEADS = 12
HD = 64
HID = 3072
E = 128
HH = 4
HFF = 2048
PATCH = 256
NB = 32
STEP = 5


beta_one = 0.5
beta_two = 0.75
decay_rate = 0.05
epsilon_add = 1e-08
rest_rate = 0.02


def layout():
    return [
        ("w_qkv", (D, 3 * D)),
        ("w_out", (D, D)),
        ("w_up", (D, HID)),
        ("w_down", (HID, D)),
        ("h_query", (E, E)),
        ("h_key", (E, E)),
        ("h_value", (E, E)),
        ("h_out", (E, E)),
        ("h_ffin", (E, HFF)),
        ("h_ffout", (HFF, E)),
        ("ln1_gain", (D,)),
        ("ln1_shift", (D,)),
        ("ln2_gain", (D,)),
        ("ln2_shift", (D,)),
        ("patch_bias", (D,)),
        ("hn1_gain", (E,)),
        ("hn1_shift", (E,)),
        ("hn2_gain", (E,)),
        ("hn2_shift", (E,)),
    ]


def matrices():
    listed, at = [], 0
    for name, extent in layout():
        if len(extent) == 2:
            listed.append((name, extent[0], extent[1], at))
        at += math.prod(extent) // 128
    return listed


def vector_places():
    listed, at = [], 0
    rows = [0, 0]
    for name, extent in layout():
        if len(extent) == 1:
            kind = 0 if extent[0] == D else 1
            for j in range(extent[0] // 128):
                listed.append((at + j, kind, rows[kind], j * 128))
            rows[kind] += 1
        at += math.prod(extent) // 128
    return listed


def spread_kernel(order_ref, low_ref, *refs):
    outs, linear = refs[:-1], refs[-1]
    step = pl.program_id(0)
    rows = low_ref.shape[0]

    def two(j, carry):
        pair = low_ref[pl.ds(pl.multiple_of(j * 16, 16), 16), :].astype(jnp.float32)
        for half in range(2):
            block = order_ref[step * (rows // 8) + j * 2 + half]
            linear[pl.ds(pl.multiple_of(block * 8, 8), 8), :] = pair[half * 8 : half * 8 + 8]
        return carry

    lax.fori_loop(0, rows // 16, two, 0, unroll=8)

    @pl.when(step == pl.num_programs(0) - 1)
    def _():
        for (name, height, width, first), out in zip(matrices(), outs):
            lanes = width // 128

            def some(j, carry, out=out, lanes=lanes, first=first):
                top = pl.multiple_of(j * 128, 128)
                for lane in range(lanes):
                    part = linear[pl.ds(first + top * lanes + lane, 128, stride=lanes), :]
                    out[pl.ds(top, 128), lane * 128 : lane * 128 + 128] = part.astype(out.dtype)
                return carry

            lax.fori_loop(0, height // 128, some, 0)
        for out in outs[-2:]:
            out[...] = jnp.zeros_like(out)
        for row, kind, top, lane in vector_places():
            outs[kind - 2][top : top + 1, lane : lane + 128] = linear[row : row + 1, :]


def spread_packed(gathered, slots, blocks):
    shards, rows = gathered.shape[0], gathered.shape[1]
    shapes = [
        jax.ShapeDtypeStruct((height, width), jnp.bfloat16 if name.startswith("w_") else jnp.float32)
        for name, height, width, first in matrices()
    ]
    shapes += [jax.ShapeDtypeStruct((8, D), jnp.float32), jax.ShapeDtypeStruct((8, E), jnp.float32)]
    return pl.pallas_call(
        spread_kernel,
        out_shape=shapes,
        grid_spec=pltpu.PrefetchScalarGridSpec(
            num_scalar_prefetch=1,
            grid=(shards,),
            in_specs=[pl.BlockSpec((None, rows, 128), lambda s, order: (s, 0, 0))],
            out_specs=[pl.BlockSpec(shape.shape, lambda s, order: (0, 0), pipeline_mode=pl.Buffered(1)) for shape in shapes],
            scratch_shapes=[pltpu.VMEM(((blocks + 1) * 8, 128), jnp.float32)],
        ),
        compiler_params=pltpu.CompilerParams(vmem_limit_bytes=60 << 20),
        name="spread_packed",
    )(slots, gathered)


def collect_kernel(order_ref, *refs):
    ins, low_ref, linear = refs[:-2], refs[-2], refs[-1]
    step = pl.program_id(0)
    rows = low_ref.shape[0]

    @pl.when(step == 0)
    def _():
        for (name, height, width, first), given in zip(matrices(), ins):
            lanes = width // 128

            def some(j, carry, given=given, lanes=lanes, first=first):
                top = pl.multiple_of(j * 128, 128)
                for lane in range(lanes):
                    part = given[pl.ds(top, 128), lane * 128 : lane * 128 + 128]
                    linear[pl.ds(first + top * lanes + lane, 128, stride=lanes), :] = part.astype(jnp.float32)
                return carry

            lax.fori_loop(0, height // 128, some, 0)
        first = vector_places()[0][0]
        linear[first:, :] = jnp.zeros((linear.shape[0] - first, 128), jnp.float32)
        for row, kind, top, lane in vector_places():
            linear[row : row + 1, :] = ins[kind - 2][top : top + 1, lane : lane + 128]

    def two(j, carry):
        parts = []
        for half in range(2):
            block = order_ref[step * (rows // 8) + j * 2 + half]
            parts.append(linear[pl.ds(pl.multiple_of(block * 8, 8), 8), :])
        low_ref[pl.ds(pl.multiple_of(j * 16, 16), 16), :] = jnp.concatenate(parts, axis=0).astype(low_ref.dtype)
        return carry

    lax.fori_loop(0, rows // 16, two, 0, unroll=8)


def collect_packed(grads, slots, blocks, shards, rows):
    return pl.pallas_call(
        collect_kernel,
        out_shape=jax.ShapeDtypeStruct((shards, rows, 128), jnp.bfloat16),
        grid_spec=pltpu.PrefetchScalarGridSpec(
            num_scalar_prefetch=1,
            grid=(shards,),
            in_specs=[pl.BlockSpec(grad.shape, lambda s, order: (0, 0), pipeline_mode=pl.Buffered(1)) for grad in grads],
            out_specs=pl.BlockSpec((None, rows, 128), lambda s, order: (s, 0, 0)),
            scratch_shapes=[pltpu.VMEM(((blocks + 1) * 8, 128), jnp.float32)],
        ),
        compiler_params=pltpu.CompilerParams(vmem_limit_bytes=60 << 20),
        name="collect_packed",
    )(slots, *grads)


def embed_waves(wavelength):
    half_width = E // 2
    frequency = jnp.exp(-math.log(10000.0) * jnp.arange(half_width, dtype=jnp.float32) / half_width)
    angles = wavelength.astype(jnp.float32)[..., None] * frequency
    return jnp.concatenate([jnp.sin(angles), jnp.cos(angles)], axis=-1)


def exact(a, b, left, right):
    return lax.dot_general(
        a, b, (((left,), (right,)), ((), ())), precision=lax.Precision.HIGHEST, preferred_element_type=jnp.float32
    )


def unit_scale(values):
    center = values - jnp.mean(values, axis=-1, keepdims=True)
    scale = lax.rsqrt(jnp.mean(center * center, axis=-1, keepdims=True) + 1e-06)
    return center * scale, scale


def unit_back(grad, unit, scale, gain):
    inner = grad * gain
    return scale * (
        inner - jnp.mean(inner, axis=-1, keepdims=True) - unit * jnp.mean(inner * unit, axis=-1, keepdims=True)
    )


def wave_kernel(embed_ref, wq_ref, wk_ref, wv_ref, wo_ref, win_ref, wout_ref, vec_ref, shaped_ref, own_ref, kept_ref, slope_ref):
    rows = embed_ref.shape[0]
    groups = rows // NB
    embedded = embed_ref[...]
    queries = exact(embedded, wq_ref[...], 1, 0)
    keys = exact(embedded, wk_ref[...], 1, 0)
    values = exact(embedded, wv_ref[...], 1, 0)
    size = E // HH
    across = lax.broadcasted_iota(jnp.int32, (rows, rows), 0) // NB == lax.broadcasted_iota(jnp.int32, (rows, rows), 1) // NB
    mixed = []
    for head in range(HH):
        lanes = slice(head * size, head * size + size)
        scores = exact(queries[:, lanes], keys[:, lanes], 1, 1) * size**-0.5
        scores = jnp.where(across, scores, -1e30)
        weight = jnp.exp(scores - jnp.max(scores, axis=-1, keepdims=True))
        weight = weight / jnp.sum(weight, axis=-1, keepdims=True)
        kept_ref[head] = weight
        mixed.append(exact(weight, values[:, lanes], 1, 0))
    mixed = jnp.concatenate(mixed, axis=1)
    unit_one, scale_one = unit_scale(embedded + exact(mixed, wo_ref[...], 1, 0))
    first = unit_one * vec_ref[0:1, :] + vec_ref[1:2, :]
    inner = exact(first, win_ref[...], 1, 0)
    half = 0.5 * (1.0 + lax.erf(inner * 0.5**0.5))
    slope_ref[0] = inner * half
    slope_ref[1] = half + inner * jnp.exp(-0.5 * inner * inner) * (2.0 * math.pi) ** -0.5
    unit_two, scale_two = unit_scale(first + exact(inner * half, wout_ref[...], 1, 0))
    shaped = (unit_two * vec_ref[2:3, :] + vec_ref[3:4, :] + embedded).astype(jnp.bfloat16)
    for j, part in enumerate((queries, keys, values, mixed, unit_one, unit_two)):
        kept_ref[HH + j] = part
    kept_ref[HH + 6] = jnp.broadcast_to(scale_one, (rows, E))
    kept_ref[HH + 7] = jnp.broadcast_to(scale_two, (rows, E))
    shaped_ref[...] = shaped
    wide = shaped.astype(jnp.float32)
    width = E // groups
    group = lax.axis_index("group")
    own = jnp.zeros((rows, width), jnp.float32)
    for j in range(groups):
        own = jnp.where(group == j, wide[:, j * width : (j + 1) * width], own)
    own_ref[...] = own.astype(jnp.bfloat16)


def wave_layer(embedded, mats, vectors):
    rows = embedded.shape[0]
    groups = rows // NB
    f32, bf16 = jnp.float32, jnp.bfloat16
    return pl.pallas_call(
        wave_kernel,
        out_shape=[
            jax.ShapeDtypeStruct((rows, E), bf16),
            jax.ShapeDtypeStruct((rows, E // groups), bf16),
            jax.ShapeDtypeStruct((HH + 8, rows, E), f32),
            jax.ShapeDtypeStruct((2, rows, HFF), f32),
        ],
        compiler_params=pltpu.CompilerParams(vmem_limit_bytes=60 << 20),
        name="wave_layer",
    )(embedded, *mats, vectors)


def wave_back_kernel(part_ref, embed_ref, kept_ref, slope_ref, wq_ref, wk_ref, wv_ref, wo_ref, win_ref, wout_ref, vec_ref,
                     gq_ref, gk_ref, gv_ref, go_ref, gin_ref, gout_ref, gvec_ref):
    rows = embed_ref.shape[0]
    groups = rows // NB
    width = E // groups
    size = E // HH
    group = lax.axis_index("group")
    spread = jnp.concatenate([part_ref[...]] * groups, axis=1)
    lane = lax.broadcasted_iota(jnp.int32, (rows, E), 1) // width
    grad = jnp.where(lane == group, spread, 0.0)
    embedded = embed_ref[...]
    queries, keys, values, mixed, unit_one, unit_two, scale_one, scale_two = (kept_ref[HH + j] for j in range(8))
    gvec_ref[...] = jnp.zeros_like(gvec_ref)
    gvec_ref[2:3, :] = jnp.sum(grad * unit_two, axis=0, keepdims=True)
    gvec_ref[3:4, :] = jnp.sum(grad, axis=0, keepdims=True)
    grad = unit_back(grad, unit_two, scale_two, vec_ref[2:3, :])
    gout_ref[...] = exact(slope_ref[0], grad, 0, 0)
    inner = exact(grad, wout_ref[...], 1, 1) * slope_ref[1]
    first = unit_one * vec_ref[0:1, :] + vec_ref[1:2, :]
    gin_ref[...] = exact(first, inner, 0, 0)
    grad = grad + exact(inner, win_ref[...], 1, 1)
    gvec_ref[0:1, :] = jnp.sum(grad * unit_one, axis=0, keepdims=True)
    gvec_ref[1:2, :] = jnp.sum(grad, axis=0, keepdims=True)
    grad = unit_back(grad, unit_one, scale_one, vec_ref[0:1, :])
    go_ref[...] = exact(mixed, grad, 0, 0)
    grad = exact(grad, wo_ref[...], 1, 1)
    parts = [[], [], []]
    for head in range(HH):
        lanes = slice(head * size, head * size + size)
        weight = kept_ref[head]
        grad_weight = exact(grad[:, lanes], values[:, lanes], 1, 1)
        parts[2].append(exact(weight, grad[:, lanes], 0, 0))
        score = weight * (grad_weight - jnp.sum(weight * grad_weight, axis=-1, keepdims=True)) * size**-0.5
        parts[0].append(exact(score, keys[:, lanes], 1, 0))
        parts[1].append(exact(score, queries[:, lanes], 0, 0))
    for out, part in zip((gq_ref, gk_ref, gv_ref), parts):
        out[...] = exact(embedded, jnp.concatenate(part, axis=1), 0, 0)


def wave_back(part, embedded, kept, slope, mats, vectors):
    f32 = jnp.float32
    return pl.pallas_call(
        wave_back_kernel,
        out_shape=[jax.ShapeDtypeStruct(mat.shape, f32) for mat in mats] + [jax.ShapeDtypeStruct((8, E), f32)],
        compiler_params=pltpu.CompilerParams(vmem_limit_bytes=60 << 20),
        name="wave_back",
    )(part, embedded, kept, slope, *mats, vectors)


def tall(count):
    return -(-count // 16) * 16


def dot_nn(a, b):
    return lax.dot_general(a, b, (((1,), (0,)), ((), ())), preferred_element_type=jnp.float32)


def dot_nt(a, b):
    return lax.dot_general(a, b, (((1,), (1,)), ((), ())), preferred_element_type=jnp.float32)


def dot_tn(a, b):
    return lax.dot_general(a, b, (((0,), (0,)), ((), ())), preferred_element_type=jnp.float32)


def block_kernel(stream_ref, up_ref, vec_ref, wqkv_hbm, wout_hbm, wup_hbm, wdown_hbm,
                 out_ref, low_ref, gvec_ref, gqkv_hbm, gout_hbm, gup_hbm, gdown_hbm,
                 wqkv, wout, wup, wdown, gqkv, gout, gup, gdown,
                 xs, ups, up_low, norm_one, qkv, att, probs, mid, norm_two, acc, hid_low, datt, dqkv, in_sem, out_sem):
    f32, bf16 = jnp.float32, jnp.bfloat16
    seq = stream_ref.shape[0]
    rows = xs.shape[0]
    loads = [
        pltpu.make_async_copy(src, dst, in_sem.at[j])
        for j, (src, dst) in enumerate(((wqkv_hbm, wqkv), (wout_hbm, wout), (wup_hbm, wup), (wdown_hbm, wdown)))
    ]
    for load in loads:
        load.start()
    stores = [
        pltpu.make_async_copy(src, dst, out_sem.at[j])
        for j, (src, dst) in enumerate(((gqkv, gqkv_hbm), (gout, gout_hbm), (gup, gup_hbm), (gdown, gdown_hbm)))
    ]
    gain_one, shift_one = vec_ref[0:1, :], vec_ref[1:2, :]
    gain_two, shift_two = vec_ref[2:3, :], vec_ref[3:4, :]
    xs[...] = jnp.zeros_like(xs)
    xs[0:seq, :] = stream_ref[...] + vec_ref[4:5, :]
    ups[...] = jnp.zeros_like(ups)
    ups[0:seq, :] = up_ref[...].astype(f32)
    up_low[...] = ups[...].astype(bf16)

    def normed(values):
        center = values - jnp.mean(values, axis=-1, keepdims=True)
        scale = lax.rsqrt(jnp.mean(center * center, axis=-1, keepdims=True) + 1e-06)
        return center * scale, scale

    def normed_back(grad, unit, scale, gain):
        inner = grad * gain
        return scale * (
            inner
            - jnp.mean(inner, axis=-1, keepdims=True)
            - unit * jnp.mean(inner * unit, axis=-1, keepdims=True)
        )

    unit, scale = normed(xs[...])
    norm_one[...] = (unit * gain_one + shift_one).astype(bf16)
    loads[0].wait()

    def tile(j, size=D):
        return pl.ds(pl.multiple_of(j * size, size), size)

    def each(count, body):
        lax.fori_loop(0, count, lambda j, carry: (body(j), carry)[1], 0)

    def qkv_part(j):
        qkv[:, tile(j)] = dot_nn(norm_one[...], wqkv[:, tile(j)]).astype(bf16)

    each(3, qkv_part)
    inside = lax.broadcasted_iota(jnp.int32, (rows, rows), 1) < seq

    def heads(p):
        pair = [qkv[:, pl.ds(pl.multiple_of(j * D + p * 128, 128), 128)] for j in range(3)]
        outs = []
        for h in range(2):
            query, key, value = (part[:, h * HD : h * HD + HD] for part in pair)
            scores = jnp.where(inside, dot_nt(query, key) * (HD**-0.5), -1e30)
            weight = jnp.exp(scores - jnp.max(scores, axis=-1, keepdims=True))
            weight = weight / jnp.sum(weight, axis=-1, keepdims=True)
            probs[p * 2 + h] = weight
            outs.append(dot_nn(weight.astype(bf16), value))
        att[:, pl.ds(pl.multiple_of(p * 128, 128), 128)] = jnp.concatenate(outs, axis=1).astype(bf16)

    each(HEADS // 2, heads)
    loads[1].wait()
    mid[...] = xs[...] + dot_nn(att[...], wout[...])
    unit, scale = normed(mid[...])
    norm_two[...] = (unit * gain_two + shift_two).astype(bf16)
    loads[2].wait()
    loads[3].wait()
    acc[...] = jnp.zeros_like(acc)

    def hidden_part(j):
        hidden = dot_nn(norm_two[...], wup[:, tile(j)])
        half = 0.5 * (1.0 + lax.erf(hidden * (0.5**0.5)))
        active = (hidden * half).astype(bf16)
        slope = half + hidden * jnp.exp(-0.5 * hidden * hidden) * (2.0 * math.pi) ** -0.5
        mid[...] += dot_nn(active, wdown[tile(j), :])
        gdown[tile(j), :] = dot_tn(active, up_low[...]).astype(bf16)
        grad_hidden = (dot_nt(up_low[...], wdown[tile(j), :]) * slope).astype(bf16)
        gup[:, tile(j)] = dot_tn(norm_two[...], grad_hidden).astype(bf16)
        acc[...] += dot_nt(grad_hidden, wup[:, tile(j)])

    kept_unit, kept_scale = unit, scale
    hid_low[...] = kept_unit
    each(HID // D, hidden_part)
    stores[2].start()
    stores[3].start()
    out_ref[...] = mid[0:seq, :].astype(bf16)
    grad = acc[...]
    unit = hid_low[...]
    gvec_ref[...] = jnp.zeros_like(gvec_ref)
    gvec_ref[2:3, :] = jnp.sum(grad * unit, axis=0, keepdims=True)
    gvec_ref[3:4, :] = jnp.sum(grad, axis=0, keepdims=True)
    ups[...] += normed_back(grad, unit, kept_scale, gain_two)
    up_low[...] = ups[...].astype(bf16)
    gout[...] = dot_tn(att[...], up_low[...]).astype(bf16)
    stores[1].start()
    datt[...] = dot_nt(up_low[...], wout[...]).astype(bf16)

    def heads_back(p):
        pair = [qkv[:, pl.ds(pl.multiple_of(j * D + p * 128, 128), 128)] for j in range(3)]
        grad_pair = datt[:, pl.ds(pl.multiple_of(p * 128, 128), 128)]
        grads = [[], [], []]
        for h in range(2):
            query, key, value = (part[:, h * HD : h * HD + HD] for part in pair)
            grad_out = grad_pair[:, h * HD : h * HD + HD]
            weight = probs[p * 2 + h]
            grad_weight = dot_nt(grad_out, value)
            grads[2].append(dot_tn(weight.astype(bf16), grad_out))
            grad_score = weight * (grad_weight - jnp.sum(weight * grad_weight, axis=-1, keepdims=True))
            grad_score = grad_score.astype(bf16)
            grads[0].append(dot_nn(grad_score, key) * (HD**-0.5))
            grads[1].append(dot_tn(grad_score, query) * (HD**-0.5))
        for j in range(3):
            dqkv[:, pl.ds(pl.multiple_of(j * D + p * 128, 128), 128)] = jnp.concatenate(grads[j], axis=1).astype(bf16)

    each(HEADS // 2, heads_back)
    acc[...] = jnp.zeros_like(acc)

    def qkv_back(j):
        gqkv[:, tile(j)] = dot_tn(norm_one[...], dqkv[:, tile(j)]).astype(bf16)
        acc[...] += dot_nt(dqkv[:, tile(j)], wqkv[:, tile(j)])

    each(3, qkv_back)
    stores[0].start()
    unit, scale = normed(xs[...])
    grad = acc[...]
    gvec_ref[0:1, :] = jnp.sum(grad * unit, axis=0, keepdims=True)
    gvec_ref[1:2, :] = jnp.sum(grad, axis=0, keepdims=True)
    total = ups[...] + normed_back(grad, unit, scale, gain_one)
    gvec_ref[4:5, :] = jnp.sum(total, axis=0, keepdims=True)
    low_ref[...] = total.astype(bf16)
    for store in stores:
        store.wait()


def block_pass(stream, upstream, vectors, wqkv, wout, wup, wdown):
    f32, bf16 = jnp.float32, jnp.bfloat16
    seq = stream.shape[0]
    rows = tall(seq)
    whole = pl.BlockSpec(memory_space=pltpu.VMEM)
    far = pl.BlockSpec(memory_space=pl.ANY)
    mats = [wqkv, wout, wup, wdown]
    kept = [pltpu.VMEM(mat.shape, bf16) for mat in mats]
    dma = pltpu.SemaphoreType.DMA
    return pl.pallas_call(
        block_kernel,
        out_shape=[
            jax.ShapeDtypeStruct((seq, D), bf16),
            jax.ShapeDtypeStruct((rows, D), bf16),
            jax.ShapeDtypeStruct((8, D), f32),
        ]
        + [jax.ShapeDtypeStruct(mat.shape, bf16) for mat in mats],
        in_specs=[whole] * 3 + [far] * 4,
        out_specs=[whole] * 3 + [far] * 4,
        scratch_shapes=kept
        + kept
        + [
            pltpu.VMEM((rows, D), f32),
            pltpu.VMEM((rows, D), f32),
            pltpu.VMEM((rows, D), bf16),
            pltpu.VMEM((rows, D), bf16),
            pltpu.VMEM((rows, 3 * D), bf16),
            pltpu.VMEM((rows, D), bf16),
            pltpu.VMEM((HEADS, rows, rows), f32),
            pltpu.VMEM((rows, D), f32),
            pltpu.VMEM((rows, D), bf16),
            pltpu.VMEM((rows, D), f32),
            pltpu.VMEM((rows, D), f32),
            pltpu.VMEM((rows, D), bf16),
            pltpu.VMEM((rows, 3 * D), bf16),
            dma((4,)),
            dma((4,)),
        ],
        compiler_params=pltpu.CompilerParams(vmem_limit_bytes=60 << 20),
        cost_estimate=pl.CostEstimate(flops=8_400_000_000, bytes_accessed=30_000_000, transcendentals=2_000_000),
        name="block_pass",
    )(stream, upstream, vectors, *mats)


def adamw_step(weight, moment_one, moment_two, grad, rate):
    first = beta_one * moment_one + (1.0 - beta_one) * grad
    second = beta_two * moment_two + (1.0 - beta_two) * grad * grad
    fix_one = 1.0 - beta_one**STEP
    fix_two = 1.0 - beta_two**STEP
    update = first / fix_one / (jnp.sqrt(second / fix_two) + epsilon_add) + decay_rate * weight
    return (weight - rate * update, first, second)


NC = 15


def dims_step(count):
    return 16 if count % 16 == 0 else count


def make_kernel(shaped_ref, master_ref, kernel_ref, turned):
    dims = kernel_ref.shape[0]
    shaped = shaped_ref[pl.ds(pl.multiple_of(lax.axis_index("group") * NB, NB), NB), :]
    for dim in range(dims):
        part = dot_nn(shaped, master_ref[:, dim * PATCH : (dim + 1) * PATCH])
        turned[pl.ds(dim, NB, stride=dims), :] = part[:, :128]
        turned[pl.ds(NB * dims + dim, NB, stride=dims), :] = part[:, 128:]
    for band in range(NB):
        for half in range(2):
            row = half * NB * dims + band * dims
            lane = band * PATCH + half * 128
            kernel_ref[:, lane : lane + 128] = turned[row : row + dims, :].astype(kernel_ref.dtype)


def make_kernels(shaped, master):
    dims = master.shape[1] // PATCH
    step = dims_step(dims)
    return pl.pallas_call(
        make_kernel,
        out_shape=jax.ShapeDtypeStruct((dims, NB * PATCH), jnp.bfloat16),
        grid=(dims // step,),
        in_specs=[
            pl.BlockSpec(shaped.shape, lambda j: (0, 0)),
            pl.BlockSpec((E, step * PATCH), lambda j: (0, j)),
        ],
        out_specs=pl.BlockSpec((step, NB * PATCH), lambda j: (j, 0)),
        scratch_shapes=[pltpu.VMEM((2 * NB * step, 128), jnp.float32)],
        compiler_params=pltpu.CompilerParams(vmem_limit_bytes=60 << 20),
        name="make_kernels",
    )(shaped, master)


def embed_kernel(pixel_ref, mask_ref, kernel_ref, stream_ref):
    masked = pixel_ref[...] * mask_ref[...].astype(jnp.bfloat16)
    part = dot_nt(masked, kernel_ref[...])

    @pl.when(pl.program_id(0) == 0)
    def _():
        stream_ref[...] = part

    @pl.when(pl.program_id(0) > 0)
    def _():
        stream_ref[...] += part


def embed_patches(pixels, mask, kernels):
    seq, width = pixels.shape[1], pixels.shape[2]
    cut = 1024
    return pl.pallas_call(
        embed_kernel,
        out_shape=jax.ShapeDtypeStruct((seq, D), jnp.float32),
        grid=(width // cut,),
        in_specs=[
            pl.BlockSpec((None, seq, cut), lambda j: (0, 0, j)),
            pl.BlockSpec((1, cut), lambda j: (0, j)),
            pl.BlockSpec((D, cut), lambda j: (0, j)),
        ],
        out_specs=pl.BlockSpec((seq, D), lambda j: (0, 0)),
        compiler_params=pltpu.CompilerParams(vmem_limit_bytes=60 << 20),
        name="embed_patches",
    )(pixels, mask, kernels)


def unembed_kernel(pixel_ref, mask_ref, kernel_ref, low_ref, back_ref, grad_ref, masked):
    seq = pixel_ref.shape[0]
    mask = mask_ref[...]
    masked[...] = jnp.zeros_like(masked)
    masked[0:seq, :] = pixel_ref[...].astype(jnp.float32) * mask
    back_ref[...] = (dot_nn(low_ref[...], kernel_ref[...])[0:seq] * mask).astype(back_ref.dtype)
    grad_ref[...] = dot_tn(low_ref[...], masked[...].astype(jnp.bfloat16)).astype(grad_ref.dtype)


def unembed_patches(pixels, mask, kernels, low):
    seq, width = pixels.shape[1], pixels.shape[2]
    cut = 1024
    return pl.pallas_call(
        unembed_kernel,
        out_shape=[
            jax.ShapeDtypeStruct(pixels.shape, jnp.bfloat16),
            jax.ShapeDtypeStruct((D, width), jnp.bfloat16),
        ],
        grid=(width // cut,),
        in_specs=[
            pl.BlockSpec((None, seq, cut), lambda j: (0, 0, j)),
            pl.BlockSpec((1, cut), lambda j: (0, j)),
            pl.BlockSpec((D, cut), lambda j: (0, j)),
            pl.BlockSpec(low.shape, lambda j: (0, 0)),
        ],
        out_specs=[
            pl.BlockSpec((None, seq, cut), lambda j: (0, 0, j)),
            pl.BlockSpec((D, cut), lambda j: (0, j)),
        ],
        scratch_shapes=[pltpu.VMEM((low.shape[0], cut), jnp.float32)],
        compiler_params=pltpu.CompilerParams(vmem_limit_bytes=60 << 20),
        name="unembed_patches",
    )(pixels, mask, kernels, low)


def master_kernel(rate, grad_ref, shaped_ref, weight_ref, one_ref, two_ref, new_ref, first_ref, second_ref, back_ref, turned):
    groups, dims = grad_ref.shape[0], grad_ref.shape[1]
    bands = groups * NB
    for group in range(groups):
        for band in range(NB):
            for half in range(2):
                row = half * bands * dims + (group * NB + band) * dims
                lane = band * PATCH + half * 128
                turned[row : row + dims, :] = grad_ref[group, :, lane : lane + 128].astype(jnp.float32)
    total = jnp.zeros(back_ref.shape, jnp.float32)
    for dim in range(dims):
        part = jnp.concatenate(
            [turned[pl.ds(half * bands * dims + dim, bands, stride=dims), :] for half in range(2)], axis=1
        ).astype(jnp.bfloat16)
        lanes = slice(dim * PATCH, (dim + 1) * PATCH)
        weight = weight_ref[:, lanes]
        total += dot_nt(part, weight.astype(jnp.bfloat16))
        grad = dot_tn(shaped_ref[...], part)
        new_ref[:, lanes], first_ref[:, lanes], second_ref[:, lanes] = adamw_step(
            weight, one_ref[:, lanes], two_ref[:, lanes], grad, rate
        )

    @pl.when(pl.program_id(0) == 0)
    def _():
        back_ref[...] = total

    @pl.when(pl.program_id(0) > 0)
    def _():
        back_ref[...] += total


def master_update(grads, shaped, weight, one, two, rate):
    groups, dims = grads.shape[0], grads.shape[1]
    step = dims_step(dims)
    columns = pl.BlockSpec((weight.shape[0], step * PATCH), lambda j: (0, j))
    like = jax.ShapeDtypeStruct(weight.shape, jnp.float32)
    return pl.pallas_call(
        functools.partial(master_kernel, rate),
        out_shape=[like, like, like, jax.ShapeDtypeStruct(shaped.shape, jnp.float32)],
        grid=(dims // step,),
        in_specs=[
            pl.BlockSpec((groups, step, NB * PATCH), lambda j: (0, j, 0)),
            pl.BlockSpec(shaped.shape, lambda j: (0, 0)),
            columns,
            columns,
            columns,
        ],
        out_specs=[columns, columns, columns, pl.BlockSpec(shaped.shape, lambda j: (0, 0))],
        scratch_shapes=[pltpu.VMEM((2 * groups * NB * step, 128), jnp.float32)],
        compiler_params=pltpu.CompilerParams(vmem_limit_bytes=60 << 20),
        name="master_update",
    )(grads, shaped, weight, one, two)


def spot():
    group = lax.axis_index("group")
    image = lax.axis_index("img")
    return group // 2, group % 2, image // 2, image % 2


def place(y, c, z, x):
    return (y * 2 + c, z * 2 + x)


def partners():
    y, c, z, x = spot()
    x2, y2 = x + (1 - c) * (1 - 2 * x), y + c * (1 - 2 * y)
    x3, y3 = x + c * (1 - 2 * x), y + (1 - c) * (1 - 2 * y)
    around = [place(y, c, (z + d) % 4, x) for d in (1, 2, 3)]
    return (x2, y2), (x3, y3), around, place(y2, c, z, x2), place(y3, c, z, x3), place(y, 1 - c, z, x)


def greet(peers):
    barrier = pltpu.get_barrier_semaphore()
    for peer in peers:
        pl.semaphore_signal(barrier, inc=1, device_id=peer, device_id_type=MESH)
    pl.semaphore_wait(barrier, len(peers))


def gather_kernel(own_ref, all_ref, local_sem, line_send, line_recv, group_send, group_recv, twin_send, twin_recv):
    y, c, z, x = spot()
    (x2, y2), (x3, y3), around, second, third, twin = partners()
    rows = own_ref.shape[0] // NC

    def cut(k):
        return pl.ds(k * rows, rows)

    def remote(src, dst, send_sem, recv_sem, target):
        return pltpu.make_async_remote_copy(
            src_ref=src, dst_ref=dst, send_sem=send_sem, recv_sem=recv_sem, device_id=target, device_id_type=MESH
        )

    def along(d, k):
        return remote(own_ref.at[cut(k)], all_ref.at[y, c, z, x, cut(k)], line_send.at[d - 1, k], line_recv.at[d - 1, k], around[d - 1])

    def along_in(d, k):
        return remote(own_ref.at[cut(k)], all_ref.at[y, c, (z + 4 - d) % 4, x, cut(k)], line_send.at[d - 1, k], line_recv.at[d - 1, k], around[d - 1])

    def square(core, j):
        yy, xx = ((y, x), (y2, x2), (y3, x3), (1 - y, 1 - x))[j]
        return all_ref.at[yy, core, :, xx]

    def hop(j, to, k, slot, landing):
        part = square(c, j).at[:, cut(k)]
        return remote(part, part, group_send.at[slot, k], group_recv.at[landing, k], to)

    def hop_in(landing, k):
        part = square(c, landing).at[:, cut(k)]
        return remote(part, part, group_send.at[0, k], group_recv.at[landing, k], twin)

    def share(j, k):
        part = square(c, j).at[:, cut(k)]
        yy, xx = ((y, x), (y2, x2), (y3, x3), (1 - y, 1 - x))[j]
        landing = (0, 2, 1, 3)[j]
        return remote(part, part, twin_send.at[j, k], twin_recv.at[landing, k], twin)

    def share_in(landing, k):
        yy, xx = ((y, x), (y2, x2), (y3, x3), (1 - y, 1 - x))[landing]
        part = all_ref.at[yy, 1 - c, :, xx, cut(k)]
        return remote(part, part, twin_send.at[0, k], twin_recv.at[landing, k], twin)

    keep = pltpu.make_async_copy(own_ref, all_ref.at[y, c, z, x], local_sem)
    keep.start()
    greet(around + [second, third, twin])
    for k in range(NC):
        for d in (1, 2, 3):
            along(d, k).start()
    keep.wait()
    for step in range(NC + 2):
        k = step
        if k < NC:
            for d in (1, 2, 3):
                along_in(d, k).wait_recv()
            hop(0, third, k, 0, 2).start()
            hop(0, second, k, 1, 1).start()
            share(0, k).start()
        k = step - 1
        if 0 <= k < NC:
            hop_in(1, k).wait_recv()
            hop(1, third, k, 2, 3).start()
            share(1, k).start()
        k = step - 2
        if 0 <= k < NC:
            hop_in(2, k).wait_recv()
            share(2, k).start()
            hop_in(3, k).wait_recv()
            share(3, k).start()
    for k in range(NC):
        for d in (1, 2, 3):
            along(d, k).wait_send()
        hop(0, third, k, 0, 2).wait_send()
        hop(0, second, k, 1, 1).wait_send()
        hop(1, third, k, 2, 3).wait_send()
        for j in range(4):
            share(j, k).wait_send()
            share_in(j, k).wait_recv()


def gather_packed(own):
    rows = own.shape[0]
    dma = pltpu.SemaphoreType.DMA
    return pl.pallas_call(
        gather_kernel,
        out_shape=jax.ShapeDtypeStruct((2, 2, 4, 2, rows, 128), own.dtype),
        in_specs=[pl.BlockSpec(memory_space=pltpu.VMEM)],
        out_specs=pl.BlockSpec(memory_space=pl.ANY),
        scratch_shapes=[dma, dma((3, NC)), dma((3, NC)), dma((3, NC)), dma((4, NC)), dma((4, NC)), dma((4, NC))],
        compiler_params=pltpu.CompilerParams(collective_id=0, has_side_effects=True, vmem_limit_bytes=60 << 20),
        name="gather_packed",
    )(own)


def reduce_kernel(part_ref, sum_ref, own, twin_in, third_in, second_in, line_in, load_sem, twin_send, twin_recv, third_send, third_recv, second_send, second_recv, line_send, line_recv):
    f32, bf16 = jnp.float32, jnp.bfloat16
    y, c, z, x = spot()
    (x2, y2), (x3, y3), around, second, third, twin = partners()
    rows = sum_ref.shape[0] // NC

    def cut(k):
        return pl.ds(k * rows, rows)

    def remote(src, dst, send_sem, recv_sem, target):
        return pltpu.make_async_remote_copy(
            src_ref=src, dst_ref=dst, send_sem=send_sem, recv_sem=recv_sem, device_id=target, device_id_type=MESH
        )

    spots = ((1 - y, 1 - x), (y3, x3), (y2, x2), (y, x))
    turned = ((1 - y, 1 - x), (y2, x2), (y3, x3), (y, x))

    def load(j, k):
        yy, xx = spots[j]
        return pltpu.make_async_copy(part_ref.at[yy, c, :, xx, cut(k)], own.at[j, :, cut(k)], load_sem.at[j, k])

    def swap(j, k):
        yy, xx = turned[j]
        return remote(part_ref.at[yy, 1 - c, :, xx, cut(k)], twin_in.at[j, :, cut(k)], twin_send.at[j, k], twin_recv.at[j, k], twin)

    def to_third(j, k):
        return remote(own.at[j, :, cut(k)], third_in.at[j, :, cut(k)], third_send.at[j, k], third_recv.at[j, k], third)

    def to_second(k):
        return remote(own.at[2, :, cut(k)], second_in.at[:, cut(k)], second_send.at[k], second_recv.at[k], second)

    def to_line(d, k):
        return remote(own.at[3, (z + d) % 4, cut(k)], line_in.at[d - 1, cut(k)], line_send.at[d - 1, k], line_recv.at[d - 1, k], around[d - 1])

    for k in range(NC):
        for j in range(4):
            load(j, k).start()
    greet(around + [second, third, twin])
    for k in range(NC):
        for j in range(4):
            swap(j, k).start()

    def pair(j, k):
        load(j, k).wait()
        swap(j, k).wait_recv()
        return own[j, :, cut(k)].astype(f32) + twin_in[j, :, cut(k)].astype(f32)

    for step in range(NC + 3):
        k = step
        if k < NC:
            for j in (0, 1):
                own[j, :, cut(k)] = pair(j, k).astype(bf16)
                to_third(j, k).start()
        k = step - 1
        if 0 <= k < NC:
            held = pair(2, k)
            to_third(0, k).wait_recv()
            own[2, :, cut(k)] = (held + third_in[0, :, cut(k)].astype(f32)).astype(bf16)
            to_second(k).start()
        k = step - 2
        if 0 <= k < NC:
            held = pair(3, k)
            to_third(1, k).wait_recv()
            to_second(k).wait_recv()
            held += third_in[1, :, cut(k)].astype(f32) + second_in[:, cut(k)].astype(f32)
            own[3, :, cut(k)] = held.astype(bf16)
            for d in (1, 2, 3):
                to_line(d, k).start()
        k = step - 3
        if 0 <= k < NC:
            total = own[3, z, cut(k)].astype(f32)
            for d in (1, 2, 3):
                to_line(d, k).wait_recv()
                total += line_in[d - 1, cut(k)].astype(f32)
            sum_ref[cut(k)] = total
    for k in range(NC):
        for j in range(4):
            swap(j, k).wait_send()
        for j in (0, 1):
            to_third(j, k).wait_send()
        to_second(k).wait_send()
        for d in (1, 2, 3):
            to_line(d, k).wait_send()


def reduce_packed(part):
    rows = part.shape[-2]
    bf16 = jnp.bfloat16
    dma = pltpu.SemaphoreType.DMA
    return pl.pallas_call(
        reduce_kernel,
        out_shape=jax.ShapeDtypeStruct((rows, 128), jnp.float32),
        in_specs=[pl.BlockSpec(memory_space=pl.ANY)],
        out_specs=pl.BlockSpec(memory_space=pltpu.VMEM),
        scratch_shapes=[
            pltpu.VMEM((4, 4, rows, 128), bf16),
            pltpu.VMEM((4, 4, rows, 128), bf16),
            pltpu.VMEM((2, 4, rows, 128), bf16),
            pltpu.VMEM((4, rows, 128), bf16),
            pltpu.VMEM((3, rows, 128), bf16),
            dma((4, NC)), dma((4, NC)), dma((4, NC)), dma((2, NC)), dma((2, NC)), dma((NC,)), dma((NC,)), dma((3, NC)), dma((3, NC)),
        ],
        compiler_params=pltpu.CompilerParams(collective_id=1, has_side_effects=True, vmem_limit_bytes=56 << 20),
        name="reduce_packed",
    )(part)


CHUNK = 16


def over_x(k):
    return k % 2 == 0


def quad_peers():
    y, c, z, x = spot()
    low = z % 2
    side = place(y, c, z, 1 - x)
    along = place(y, c, z + 1 - 2 * low, x)
    twin = place(y, 1 - c, z, x)
    partner = place(y, 1 - c, (z + 2) % 4, x)
    moved = (c + z // 2) % 2 == 1
    return y, c, z, x, low, side, along, twin, partner, moved


def swap_images(value):
    pairs = []
    for y in range(2):
        for c in range(2):
            for z in range(4):
                for x in range(2):
                    other = (1 - c, (z + 2) % 4) if c != z // 2 else (c, z)
                    pairs.append((((y * 2 + c) * 4 + z) * 2 + x, ((y * 2 + other[0]) * 4 + other[1]) * 2 + x))
    return lax.ppermute(value, ("group", "img"), pairs)


def remote(src, dst, send_sem, recv_sem, target):
    return pltpu.make_async_remote_copy(
        src_ref=src, dst_ref=dst, send_sem=send_sem, recv_sem=recv_sem, device_id=target, device_id_type=MESH
    )


def share_kernel(made_ref, all_ref, keep_sem, swap_send, swap_recv, side_send, side_recv, along_send, along_recv, far_send, far_recv, twin_send, twin_recv):
    y, c, z, x, low, side, along, twin, partner, moved = quad_peers()
    count = made_ref.shape[0] // CHUNK

    def cut(k):
        return pl.ds(k * CHUNK, CHUNK)

    def block(core, j, k):
        return all_ref.at[2 * core + (low + j // 2) % 2, (x + j % 2) % 2, cut(k)]

    def keep(k):
        return pltpu.make_async_copy(made_ref.at[cut(k)], block(c, 0, k), keep_sem.at[k])

    def swap(k):
        return remote(made_ref.at[cut(k)], block(1 - c, 0, k), swap_send.at[k], swap_recv.at[k], partner)

    def swap_in(k):
        return remote(made_ref.at[cut(k)], block(c, 0, k), swap_send.at[k], swap_recv.at[k], partner)

    def to_side(k):
        return remote(block(c, 0, k), block(c, 0, k), side_send.at[k], side_recv.at[k], side)

    def from_side(k):
        return remote(block(c, 1, k), block(c, 1, k), side_send.at[k], side_recv.at[k], side)

    def to_along(k):
        return remote(block(c, 0, k), block(c, 0, k), along_send.at[k], along_recv.at[k], along)

    def from_along(k):
        return remote(block(c, 2, k), block(c, 2, k), along_send.at[k], along_recv.at[k], along)

    def pass_on(k):
        j, to = (2, side) if over_x(k) else (1, along)
        return remote(block(c, j, k), block(c, j, k), far_send.at[k], far_recv.at[k], to)

    def from_far(k):
        return remote(block(c, 3, k), block(c, 3, k), far_send.at[k], far_recv.at[k], twin)

    def give(j, k):
        return remote(block(c, j, k), block(c, j, k), twin_send.at[j, k], twin_recv.at[j, k], twin)

    def given(j, k):
        return remote(block(1 - c, j, k), block(1 - c, j, k), twin_send.at[j, k], twin_recv.at[j, k], twin)

    @pl.when(jnp.logical_not(moved))
    def _():
        for k in range(count):
            keep(k).start()

    greet([side, along, twin, partner])

    @pl.when(moved)
    def _():
        for k in range(count):
            swap(k).start()

    for step in range(count + 2):
        k = step
        if k < count:

            @pl.when(moved)
            def _(k=k):
                swap_in(k).wait_recv()

            @pl.when(jnp.logical_not(moved))
            def _(k=k):
                keep(k).wait()

            to_side(k).start()
            to_along(k).start()
            give(0, k).start()
        k = step - 1
        if 0 <= k < count:
            if over_x(k):
                from_along(k).wait_recv()
                pass_on(k).start()
                from_side(k).wait_recv()
            else:
                from_side(k).wait_recv()
                pass_on(k).start()
                from_along(k).wait_recv()
            give(1, k).start()
            give(2, k).start()
        k = step - 2
        if 0 <= k < count:
            from_far(k).wait_recv()
            give(3, k).start()

    @pl.when(moved)
    def _():
        for k in range(count):
            swap(k).wait_send()

    for k in range(count):
        to_side(k).wait_send()
        to_along(k).wait_send()
        pass_on(k).wait_send()
        for j in range(4):
            give(j, k).wait_send()
            given(j, k).wait_recv()


def share_kernels(made):
    dims, width = made.shape
    count = dims // CHUNK
    dma = pltpu.SemaphoreType.DMA
    shared = pl.pallas_call(
        share_kernel,
        out_shape=jax.ShapeDtypeStruct((4, 2, dims, width), made.dtype),
        in_specs=[pl.BlockSpec(memory_space=pltpu.VMEM)],
        out_specs=pl.BlockSpec(memory_space=pl.ANY),
        scratch_shapes=[dma((count,))] * 9 + [dma((4, count))] * 2,
        compiler_params=pltpu.CompilerParams(collective_id=2, has_side_effects=True, vmem_limit_bytes=60 << 20),
        name="share_kernels",
    )(made)
    return shared.reshape(8 * dims, width)


def fold_kernel(part_ref, all_ref, own, twin_in, relay_in, side_in, along_in, load_sem, keep_sem, twin_send, twin_recv, relay_send, relay_recv,
                side_send, side_recv, along_send, along_recv, swap_send, swap_recv, group_send, group_recv, give_send, give_recv):
    f32, bf16 = jnp.float32, jnp.bfloat16
    y, c, z, x, low, side, along, twin, partner, moved = quad_peers()
    over = place(1 - y, c, z, x)
    count = all_ref.shape[2] // CHUNK

    def cut(k):
        return pl.ds(k * CHUNK, CHUNK)

    def part(core, j, k):
        return part_ref.at[2 * core + (low + j // 2) % 2, (x + j % 2) % 2, cut(k)]

    def load(j, k):
        return pltpu.make_async_copy(part(c, j, k), own.at[j, cut(k)], load_sem.at[j, k])

    def swap(j, k):
        return remote(part(1 - c, j, k), twin_in.at[j, cut(k)], twin_send.at[j, k], twin_recv.at[j, k], twin)

    def relay(k):
        return remote(own.at[3, cut(k)], relay_in.at[cut(k)], relay_send.at[k], relay_recv.at[k], along if over_x(k) else side)

    def to_side(k):
        return remote(own.at[1, cut(k)], side_in.at[cut(k)], side_send.at[k], side_recv.at[k], side)

    def to_along(k):
        return remote(own.at[2, cut(k)], along_in.at[cut(k)], along_send.at[k], along_recv.at[k], along)

    def keep(k):
        return pltpu.make_async_copy(own.at[0, cut(k)], all_ref.at[y, c, cut(k)], keep_sem.at[k])

    def move(k):
        return remote(own.at[0, cut(k)], all_ref.at[y, 1 - c, cut(k)], swap_send.at[k], swap_recv.at[k], partner)

    def moved_in(k):
        return remote(own.at[0, cut(k)], all_ref.at[y, c, cut(k)], swap_send.at[k], swap_recv.at[k], partner)

    def cross(k):
        return remote(all_ref.at[y, c, cut(k)], all_ref.at[y, c, cut(k)], group_send.at[k], group_recv.at[k], over)

    def crossed(k):
        return remote(all_ref.at[1 - y, c, cut(k)], all_ref.at[1 - y, c, cut(k)], group_send.at[k], group_recv.at[k], over)

    def give(j, k):
        here = all_ref.at[(y + j) % 2, c, cut(k)]
        return remote(here, here, give_send.at[j, k], give_recv.at[j, k], twin)

    def given(j, k):
        here = all_ref.at[(y + j) % 2, 1 - c, cut(k)]
        return remote(here, here, give_send.at[j, k], give_recv.at[j, k], twin)

    def pair(j, k):
        load(j, k).wait()
        swap(j, k).wait_recv()
        return own[j, cut(k)].astype(f32) + twin_in[j, cut(k)].astype(f32)

    for k in range(count):
        for j in (3, 1, 2, 0):
            load(j, k).start()
    greet([side, along, twin, partner, over])
    for k in range(count):
        for j in (3, 1, 2, 0):
            swap(j, k).start()

    for step in range(count + 4):
        k = step
        if k < count:
            own[3, cut(k)] = pair(3, k).astype(bf16)
            relay(k).start()
        k = step - 1
        if 0 <= k < count:
            first, second = (to_along, to_side) if over_x(k) else (to_side, to_along)
            plain, summed = (2, 1) if over_x(k) else (1, 2)
            own[plain, cut(k)] = pair(plain, k).astype(bf16)
            first(k).start()
            held = pair(summed, k)
            relay(k).wait_recv()
            own[summed, cut(k)] = (held + relay_in[cut(k)].astype(f32)).astype(bf16)
            second(k).start()
        k = step - 2
        if 0 <= k < count:
            held = pair(0, k)
            to_side(k).wait_recv()
            to_along(k).wait_recv()
            held += side_in[cut(k)].astype(f32) + along_in[cut(k)].astype(f32)
            own[0, cut(k)] = held.astype(bf16)

            @pl.when(moved)
            def _(k=k):
                move(k).start()

            @pl.when(jnp.logical_not(moved))
            def _(k=k):
                keep(k).start()

        k = step - 3
        if 0 <= k < count:

            @pl.when(moved)
            def _(k=k):
                moved_in(k).wait_recv()

            @pl.when(jnp.logical_not(moved))
            def _(k=k):
                keep(k).wait()

            cross(k).start()
            give(0, k).start()
        k = step - 4
        if 0 <= k < count:
            crossed(k).wait_recv()
            give(1, k).start()

    @pl.when(moved)
    def _():
        for k in range(count):
            move(k).wait_send()

    for k in range(count):
        for j in range(4):
            swap(j, k).wait_send()
        relay(k).wait_send()
        to_side(k).wait_send()
        to_along(k).wait_send()
        cross(k).wait_send()
        for j in range(2):
            give(j, k).wait_send()
            given(j, k).wait_recv()


def fold_kernels(part):
    width = part.shape[1]
    dims = part.shape[0] // 8
    count = dims // CHUNK
    bf16 = jnp.bfloat16
    dma = pltpu.SemaphoreType.DMA
    folded = pl.pallas_call(
        fold_kernel,
        out_shape=jax.ShapeDtypeStruct((2, 2, dims, width), bf16),
        in_specs=[pl.BlockSpec(memory_space=pl.ANY)],
        out_specs=pl.BlockSpec(memory_space=pl.ANY),
        scratch_shapes=[
            pltpu.VMEM((4, dims, width), bf16),
            pltpu.VMEM((4, dims, width), bf16),
            pltpu.VMEM((dims, width), bf16),
            pltpu.VMEM((dims, width), bf16),
            pltpu.VMEM((dims, width), bf16),
            dma((4, count)),
            dma((count,)),
            dma((4, count)),
            dma((4, count)),
        ]
        + [dma((count,))] * 10
        + [dma((2, count))] * 2,
        compiler_params=pltpu.CompilerParams(collective_id=3, has_side_effects=True, vmem_limit_bytes=60 << 20),
        name="fold_kernels",
    )(part.reshape(4, 2, dims, width))
    return folded.reshape(4, dims, width)


def on_device(
    pixels,
    band_mask,
    wavelength,
    owner_order,
    rest_weight,
    rest_moment1,
    rest_moment2,
    fc_weight,
    fc_moment1,
    fc_moment2,
    cotangent,
):
    f32 = jnp.float32
    bf16 = jnp.bfloat16
    kernel_rate = float(E * PATCH * NB) ** (-0.5)
    groups = lax.axis_size("group")
    own_rows = rest_weight.shape[0]
    own_blocks = own_rows // 8
    fits = lax.axis_size("group") == 4 and lax.axis_size("img") == 8
    extra = -own_rows % 128
    slot_blocks = (own_rows + extra) // 8
    mask = band_mask.astype(f32)
    low_weight = fc_weight.astype(bf16)
    rest_low = jnp.pad(rest_weight.astype(bf16), ((0, extra), (0, 0)))
    if fits:
        mask = swap_images(mask)
        gathered = gather_packed(rest_low)
        gathered, pixels, cotangent, low_weight = lax.optimization_barrier(
            (gathered, pixels, cotangent, low_weight)
        )
        pixels, cotangent = swap_images(pixels), swap_images(cotangent)
    else:
        gathered = lax.all_gather(rest_low, ("group", "img"), axis=0, tiled=True)
    shards = gathered.size // ((own_rows + extra) * 128)
    gathered = gathered.reshape(shards, own_rows + extra, 128)
    total_blocks = owner_order.shape[0]
    slots = jnp.pad(
        owner_order.reshape(shards, own_blocks),
        ((0, 0), (0, slot_blocks - own_blocks)),
        constant_values=total_blocks,
    ).reshape(-1)
    unpacked = spread_packed(gathered, slots, total_blocks)
    block_mats, wave_mats = unpacked[:4], unpacked[4:10]
    block_vectors, wave_vectors = unpacked[10:]
    embedded = embed_waves(wavelength).reshape(groups * NB, E)
    shaped_low, own_shaped, kept, slope = wave_layer(embedded, wave_mats, wave_vectors)
    master = lax.all_gather(low_weight, "group", axis=0, tiled=True)
    kernel_low = make_kernels(shaped_low, master)
    if fits:
        kernel_all, mask = lax.optimization_barrier((share_kernels(kernel_low), mask))
    else:
        kernel_all = lax.all_gather(kernel_low, "img", axis=0, tiled=True)
    mask = jnp.repeat(mask, PATCH, axis=1)
    stream = embed_patches(pixels, mask, kernel_all)
    block_out, grad_low, block_vectors, *block_grads = block_pass(
        stream, cotangent, block_vectors, *block_mats
    )
    pixel_grad, kernel_grad = unembed_patches(pixels, mask, kernel_all, grad_low)
    if fits:
        all_groups = fold_kernels(kernel_grad)
        all_groups, block_out, pixel_grad = lax.optimization_barrier((all_groups, block_out, pixel_grad))
        block_out, pixel_grad = swap_images(block_out), swap_images(pixel_grad)
    else:
        kernel_grad_low = lax.psum_scatter(kernel_grad, "img", scatter_dimension=0, tiled=True)
        all_groups = lax.all_gather(kernel_grad_low[None], "group", axis=0, tiled=True)
    fc_new, fc_first, fc_second, shaped_part = master_update(
        all_groups,
        own_shaped,
        fc_weight,
        fc_moment1,
        fc_moment2,
        kernel_rate,
    )
    *wave_grads, wave_vectors = wave_back(shaped_part, embedded, kept, slope, wave_mats, wave_vectors)
    given = [*block_grads, *wave_grads, block_vectors, wave_vectors]
    joint_term = collect_packed(given, slots, total_blocks, shards, own_rows + extra)
    if fits:
        rest_grad = reduce_packed(joint_term.reshape(2, 2, 4, 2, own_rows + extra, 128))
    else:
        rest_grad = lax.psum_scatter(
            joint_term, ("group", "img"), scatter_dimension=0, tiled=False
        ).astype(f32)
    rest_grad = rest_grad[:own_rows]
    rest_new, rest_first, rest_second = adamw_step(
        rest_weight, rest_moment1, rest_moment2, rest_grad, rest_rate
    )
    return (block_out, pixel_grad, rest_new, rest_first, rest_second, fc_new, fc_first, fc_second)


def solution(mesh):
    placed = (
        P(("group", "img"), None, None),
        P(("group", "img"), None),
        P(),
        P(),
        P(("group", "img"), None),
        P(("group", "img"), None),
        P(("group", "img"), None),
        P("group", "img"),
        P("group", "img"),
        P("group", "img"),
        P(("group", "img"), None),
    )
    return jax.shard_map(
        on_device,
        mesh=mesh,
        in_specs=placed,
        out_specs=(
            P(("group", "img"), None),
            P(("group", "img"), None, None),
            P(("group", "img"), None),
            P(("group", "img"), None),
            P(("group", "img"), None),
            P("group", "img"),
            P("group", "img"),
            P("group", "img"),
        ),
        check_vma=False,
    )
```

```python
import functools
import math

import jax
import jax.numpy as jnp
from jax import lax
from jax.experimental import pallas as pl
from jax.experimental.pallas import tpu as pltpu
from jax.sharding import PartitionSpec as P

MESH = pl.DeviceIdType.MESH

D = 768
HEADS = 12
HD = 64
HID = 3072
E = 128
HH = 4
HFF = 2048
PATCH = 256
NB = 32
STEP = 5


beta_one = 0.5
beta_two = 0.75
decay_rate = 0.05
epsilon_add = 1e-08
rest_rate = 0.02


def layout():
    return [
        ("w_qkv", (D, 3 * D)),
        ("w_out", (D, D)),
        ("w_up", (D, HID)),
        ("w_down", (HID, D)),
        ("h_query", (E, E)),
        ("h_key", (E, E)),
        ("h_value", (E, E)),
        ("h_out", (E, E)),
        ("h_ffin", (E, HFF)),
        ("h_ffout", (HFF, E)),
        ("ln1_gain", (D,)),
        ("ln1_shift", (D,)),
        ("ln2_gain", (D,)),
        ("ln2_shift", (D,)),
        ("patch_bias", (D,)),
        ("hn1_gain", (E,)),
        ("hn1_shift", (E,)),
        ("hn2_gain", (E,)),
        ("hn2_shift", (E,)),
    ]


def embed_waves(wavelength):
    half_width = E // 2
    frequency = jnp.exp(-math.log(10000.0) * jnp.arange(half_width, dtype=jnp.float32) / half_width)
    angles = wavelength.astype(jnp.float32)[..., None] * frequency
    return jnp.concatenate([jnp.sin(angles), jnp.cos(angles)], axis=-1)


def matrices():
    listed, at = [], 0
    for name, extent in layout():
        if len(extent) == 2:
            listed.append((name, extent[0], extent[1], at))
        at += math.prod(extent) // 128
    return listed


def vector_places():
    listed, at = [], 0
    rows = [0, 0]
    for name, extent in layout():
        if len(extent) == 1:
            kind = 0 if extent[0] == D else 1
            for j in range(extent[0] // 128):
                listed.append((at + j, kind, rows[kind], j * 128))
            rows[kind] += 1
        at += math.prod(extent) // 128
    return listed


def vector_shapes():
    return [jax.ShapeDtypeStruct((8, D), jnp.float32), jax.ShapeDtypeStruct((8, E), jnp.float32)]


def shards_a_step(shards, wanted):
    return wanted if shards % wanted == 0 else 1


def spread_kernel(order_ref, low_ref, *refs):
    big, small = matrices()[:4], matrices()[4:]
    far, outs, linear, kept, sem = refs[:4], refs[4:12], refs[12], refs[13:17], refs[17]
    step = pl.program_id(0)
    shards, rows = low_ref.shape[0], low_ref.shape[1]

    for shard in range(shards):

        def two(j, carry, shard=shard):
            pair = low_ref[shard, pl.ds(pl.multiple_of(j * 16, 16), 16), :].astype(jnp.float32)
            for half in range(2):
                block = order_ref[(step * shards + shard) * (rows // 8) + j * 2 + half]
                linear[pl.ds(pl.multiple_of(block * 8, 8), 8), :] = pair[half * 8 : half * 8 + 8]
            return carry

        lax.fori_loop(0, rows // 16, two, 0, unroll=8)

    @pl.when(step == pl.num_programs(0) - 1)
    def _():
        def relay(height, width, first, out):
            lanes = width // 128

            def some(j, carry):
                top = pl.multiple_of(j * 128, 128)
                for lane in range(lanes):
                    part = linear[pl.ds(first + top * lanes + lane, 128, stride=lanes), :]
                    out[pl.ds(top, 128), lane * 128 : lane * 128 + 128] = part.astype(out.dtype)
                return carry

            lax.fori_loop(0, height // 128, some, 0)

        copies = []
        for j, (name, height, width, first) in enumerate(big):
            relay(height, width, first, kept[j])
            copies.append(pltpu.make_async_copy(kept[j], far[j], sem.at[j]))
            copies[-1].start()
        for (name, height, width, first), out in zip(small, outs):
            relay(height, width, first, out)
        for out in outs[-2:]:
            out[...] = jnp.zeros_like(out)
        for row, kind, top, lane in vector_places():
            outs[kind - 2][top : top + 1, lane : lane + 128] = linear[row : row + 1, :]
        for copy in copies:
            copy.wait()


def spread_packed(gathered, slots, blocks):
    shards, rows = gathered.shape[0], gathered.shape[1]
    some = shards_a_step(shards, 4)
    big = [jax.ShapeDtypeStruct((height, width), jnp.bfloat16) for name, height, width, first in matrices()[:4]]
    small = [jax.ShapeDtypeStruct((height, width), jnp.float32) for name, height, width, first in matrices()[4:]]
    small += vector_shapes()
    return pl.pallas_call(
        spread_kernel,
        out_shape=big + small,
        grid_spec=pltpu.PrefetchScalarGridSpec(
            num_scalar_prefetch=1,
            grid=(shards // some,),
            in_specs=[pl.BlockSpec((some, rows, 128), lambda s, order: (s, 0, 0))],
            out_specs=[pl.BlockSpec(memory_space=pl.ANY) for shape in big]
            + [pl.BlockSpec(shape.shape, lambda s, order: (0, 0), pipeline_mode=pl.Buffered(1)) for shape in small],
            scratch_shapes=[pltpu.VMEM(((blocks + 1) * 8, 128), jnp.float32)]
            + [pltpu.VMEM(shape.shape, shape.dtype) for shape in big]
            + [pltpu.SemaphoreType.DMA((4,))],
        ),
        compiler_params=pltpu.CompilerParams(vmem_limit_bytes=60 << 20),
        name="spread_packed",
    )(slots, gathered)


def collect_kernel(order_ref, *refs):
    big, small = matrices()[:4], matrices()[4:]
    far, ins, low_ref, linear, kept, sem = refs[:4], refs[4:12], refs[12], refs[13], refs[14:18], refs[18]
    step = pl.program_id(0)
    shards, rows = low_ref.shape[0], low_ref.shape[1]

    @pl.when(step == 0)
    def _():
        copies = [pltpu.make_async_copy(far[j], kept[j], sem.at[j]) for j in range(4)]
        for copy in copies:
            copy.start()

        def relay(height, width, first, given):
            lanes = width // 128

            def some(j, carry):
                top = pl.multiple_of(j * 128, 128)
                for lane in range(lanes):
                    part = given[pl.ds(top, 128), lane * 128 : lane * 128 + 128]
                    linear[pl.ds(first + top * lanes + lane, 128, stride=lanes), :] = part.astype(jnp.float32)
                return carry

            lax.fori_loop(0, height // 128, some, 0)

        for (name, height, width, first), given in zip(small, ins):
            relay(height, width, first, given)
        first = vector_places()[0][0]
        linear[first:, :] = jnp.zeros((linear.shape[0] - first, 128), jnp.float32)
        for row, kind, top, lane in vector_places():
            linear[row : row + 1, :] = ins[kind - 2][top : top + 1, lane : lane + 128]
        for j, (name, height, width, first) in enumerate(big):
            copies[j].wait()
            relay(height, width, first, kept[j])

    for shard in range(shards):

        def two(j, carry, shard=shard):
            parts = []
            for half in range(2):
                block = order_ref[(step * shards + shard) * (rows // 8) + j * 2 + half]
                parts.append(linear[pl.ds(pl.multiple_of(block * 8, 8), 8), :])
            low_ref[shard, pl.ds(pl.multiple_of(j * 16, 16), 16), :] = jnp.concatenate(parts, axis=0).astype(low_ref.dtype)
            return carry

        lax.fori_loop(0, rows // 16, two, 0, unroll=20)


def collect_packed(grads, slots, blocks, shards, rows):
    some = shards_a_step(shards, 2)
    whole = [pl.BlockSpec(grad.shape, lambda s, order: (0, 0), pipeline_mode=pl.Buffered(1)) for grad in grads[4:]]
    return pl.pallas_call(
        collect_kernel,
        out_shape=jax.ShapeDtypeStruct((shards, rows, 128), jnp.bfloat16),
        grid_spec=pltpu.PrefetchScalarGridSpec(
            num_scalar_prefetch=1,
            grid=(shards // some,),
            in_specs=[pl.BlockSpec(memory_space=pl.ANY)] * 4 + whole,
            out_specs=pl.BlockSpec((some, rows, 128), lambda s, order: (s, 0, 0)),
            scratch_shapes=[pltpu.VMEM(((blocks + 1) * 8, 128), jnp.float32)]
            + [pltpu.VMEM(grad.shape, grad.dtype) for grad in grads[:4]]
            + [pltpu.SemaphoreType.DMA((4,))],
        ),
        compiler_params=pltpu.CompilerParams(vmem_limit_bytes=60 << 20),
        name="collect_packed",
    )(slots, *grads)


def exact(a, b, left, right):
    return lax.dot_general(
        a, b, (((left,), (right,)), ((), ())), precision=lax.Precision.HIGHEST, preferred_element_type=jnp.float32
    )


def unit_scale(values):
    center = values - jnp.mean(values, axis=-1, keepdims=True)
    scale = lax.rsqrt(jnp.mean(center * center, axis=-1, keepdims=True) + 1e-06)
    return center * scale, scale


def unit_back(grad, unit, scale, gain):
    inner = grad * gain
    return scale * (
        inner - jnp.mean(inner, axis=-1, keepdims=True) - unit * jnp.mean(inner * unit, axis=-1, keepdims=True)
    )


def wave_kernel(embed_ref, wq_ref, wk_ref, wv_ref, wo_ref, win_ref, wout_ref, vec_ref, shaped_ref, own_ref, kept_ref, slope_ref):
    rows = embed_ref.shape[0]
    groups = rows // NB
    embedded = embed_ref[...]
    queries = exact(embedded, wq_ref[...], 1, 0)
    keys = exact(embedded, wk_ref[...], 1, 0)
    values = exact(embedded, wv_ref[...], 1, 0)
    size = E // HH
    across = lax.broadcasted_iota(jnp.int32, (rows, rows), 0) // NB == lax.broadcasted_iota(jnp.int32, (rows, rows), 1) // NB
    mixed = []
    for head in range(HH):
        lanes = slice(head * size, head * size + size)
        scores = exact(queries[:, lanes], keys[:, lanes], 1, 1) * size**-0.5
        scores = jnp.where(across, scores, -1e30)
        weight = jnp.exp(scores - jnp.max(scores, axis=-1, keepdims=True))
        weight = weight / jnp.sum(weight, axis=-1, keepdims=True)
        kept_ref[head] = weight
        mixed.append(exact(weight, values[:, lanes], 1, 0))
    mixed = jnp.concatenate(mixed, axis=1)
    unit_one, scale_one = unit_scale(embedded + exact(mixed, wo_ref[...], 1, 0))
    first = unit_one * vec_ref[0:1, :] + vec_ref[1:2, :]
    inner = exact(first, win_ref[...], 1, 0)
    half = 0.5 * (1.0 + lax.erf(inner * 0.5**0.5))
    slope_ref[0] = inner * half
    slope_ref[1] = half + inner * jnp.exp(-0.5 * inner * inner) * (2.0 * math.pi) ** -0.5
    unit_two, scale_two = unit_scale(first + exact(inner * half, wout_ref[...], 1, 0))
    shaped = (unit_two * vec_ref[2:3, :] + vec_ref[3:4, :] + embedded).astype(jnp.bfloat16)
    for j, part in enumerate((queries, keys, values, mixed, unit_one, unit_two)):
        kept_ref[HH + j] = part
    kept_ref[HH + 6] = jnp.broadcast_to(scale_one, (rows, E))
    kept_ref[HH + 7] = jnp.broadcast_to(scale_two, (rows, E))
    shaped_ref[...] = shaped
    wide = shaped.astype(jnp.float32)
    width = E // groups
    group = lax.axis_index("group")
    own = jnp.zeros((rows, width), jnp.float32)
    for j in range(groups):
        own = jnp.where(group == j, wide[:, j * width : (j + 1) * width], own)
    own_ref[...] = own.astype(jnp.bfloat16)


def wave_layer(embedded, mats, vectors):
    rows = embedded.shape[0]
    groups = rows // NB
    f32, bf16 = jnp.float32, jnp.bfloat16
    return pl.pallas_call(
        wave_kernel,
        out_shape=[
            jax.ShapeDtypeStruct((rows, E), bf16),
            jax.ShapeDtypeStruct((rows, E // groups), bf16),
            jax.ShapeDtypeStruct((HH + 8, rows, E), f32),
            jax.ShapeDtypeStruct((2, rows, HFF), f32),
        ],
        compiler_params=pltpu.CompilerParams(vmem_limit_bytes=60 << 20),
        name="wave_layer",
    )(embedded, *mats, vectors)


def wave_back_kernel(part_ref, embed_ref, kept_ref, slope_ref, wq_ref, wk_ref, wv_ref, wo_ref, win_ref, wout_ref, vec_ref,
                     gq_ref, gk_ref, gv_ref, go_ref, gin_ref, gout_ref, gvec_ref):
    rows = embed_ref.shape[0]
    groups = rows // NB
    width = E // groups
    size = E // HH
    group = lax.axis_index("group")
    spread = jnp.concatenate([part_ref[...]] * groups, axis=1)
    lane = lax.broadcasted_iota(jnp.int32, (rows, E), 1) // width
    grad = jnp.where(lane == group, spread, 0.0)
    embedded = embed_ref[...]
    queries, keys, values, mixed, unit_one, unit_two, scale_one, scale_two = (kept_ref[HH + j] for j in range(8))
    gvec_ref[...] = jnp.zeros_like(gvec_ref)
    gvec_ref[2:3, :] = jnp.sum(grad * unit_two, axis=0, keepdims=True)
    gvec_ref[3:4, :] = jnp.sum(grad, axis=0, keepdims=True)
    grad = unit_back(grad, unit_two, scale_two, vec_ref[2:3, :])
    gout_ref[...] = exact(slope_ref[0], grad, 0, 0)
    inner = exact(grad, wout_ref[...], 1, 1) * slope_ref[1]
    first = unit_one * vec_ref[0:1, :] + vec_ref[1:2, :]
    gin_ref[...] = exact(first, inner, 0, 0)
    grad = grad + exact(inner, win_ref[...], 1, 1)
    gvec_ref[0:1, :] = jnp.sum(grad * unit_one, axis=0, keepdims=True)
    gvec_ref[1:2, :] = jnp.sum(grad, axis=0, keepdims=True)
    grad = unit_back(grad, unit_one, scale_one, vec_ref[0:1, :])
    go_ref[...] = exact(mixed, grad, 0, 0)
    grad = exact(grad, wo_ref[...], 1, 1)
    parts = [[], [], []]
    for head in range(HH):
        lanes = slice(head * size, head * size + size)
        weight = kept_ref[head]
        grad_weight = exact(grad[:, lanes], values[:, lanes], 1, 1)
        parts[2].append(exact(weight, grad[:, lanes], 0, 0))
        score = weight * (grad_weight - jnp.sum(weight * grad_weight, axis=-1, keepdims=True)) * size**-0.5
        parts[0].append(exact(score, keys[:, lanes], 1, 0))
        parts[1].append(exact(score, queries[:, lanes], 0, 0))
    for out, part in zip((gq_ref, gk_ref, gv_ref), parts):
        out[...] = exact(embedded, jnp.concatenate(part, axis=1), 0, 0)


def wave_back(part, embedded, kept, slope, mats, vectors):
    f32 = jnp.float32
    return pl.pallas_call(
        wave_back_kernel,
        out_shape=[jax.ShapeDtypeStruct(mat.shape, f32) for mat in mats] + [jax.ShapeDtypeStruct((8, E), f32)],
        compiler_params=pltpu.CompilerParams(vmem_limit_bytes=60 << 20),
        name="wave_back",
    )(part, embedded, kept, slope, *mats, vectors)


def tall(count):
    return -(-count // 16) * 16


def dot_nn(a, b):
    return lax.dot_general(a, b, (((1,), (0,)), ((), ())), preferred_element_type=jnp.float32)


def dot_nt(a, b):
    return lax.dot_general(a, b, (((1,), (1,)), ((), ())), preferred_element_type=jnp.float32)


def dot_tn(a, b):
    return lax.dot_general(a, b, (((0,), (0,)), ((), ())), preferred_element_type=jnp.float32)


def block_kernel(stream_ref, up_ref, vec_ref, wqkv_hbm, wout_hbm, wup_hbm, wdown_hbm,
                 out_ref, low_ref, gvec_ref, gqkv_hbm, gout_hbm, gup_hbm, gdown_hbm,
                 wqkv, wout, wup, wdown, gqkv, gout, gup, gdown,
                 xs, ups, up_low, norm_one, qkv, att, probs, mid, norm_two, acc, hid_low, datt, dqkv, in_sem, out_sem):
    f32, bf16 = jnp.float32, jnp.bfloat16
    seq = stream_ref.shape[0]
    rows = xs.shape[0]
    loads = [
        pltpu.make_async_copy(src, dst, in_sem.at[j])
        for j, (src, dst) in enumerate(((wqkv_hbm, wqkv), (wout_hbm, wout), (wup_hbm, wup), (wdown_hbm, wdown)))
    ]
    for load in loads:
        load.start()
    stores = [
        pltpu.make_async_copy(src, dst, out_sem.at[j])
        for j, (src, dst) in enumerate(((gqkv, gqkv_hbm), (gout, gout_hbm), (gup, gup_hbm), (gdown, gdown_hbm)))
    ]
    gain_one, shift_one = vec_ref[0:1, :], vec_ref[1:2, :]
    gain_two, shift_two = vec_ref[2:3, :], vec_ref[3:4, :]
    xs[...] = jnp.zeros_like(xs)
    xs[0:seq, :] = stream_ref[...] + vec_ref[4:5, :]
    ups[...] = jnp.zeros_like(ups)
    ups[0:seq, :] = up_ref[...].astype(f32)
    up_low[...] = ups[...].astype(bf16)

    def normed(values):
        center = values - jnp.mean(values, axis=-1, keepdims=True)
        scale = lax.rsqrt(jnp.mean(center * center, axis=-1, keepdims=True) + 1e-06)
        return center * scale, scale

    def normed_back(grad, unit, scale, gain):
        inner = grad * gain
        return scale * (
            inner
            - jnp.mean(inner, axis=-1, keepdims=True)
            - unit * jnp.mean(inner * unit, axis=-1, keepdims=True)
        )

    unit, scale = normed(xs[...])
    norm_one[...] = (unit * gain_one + shift_one).astype(bf16)
    loads[0].wait()

    def tile(j, size=D):
        return pl.ds(pl.multiple_of(j * size, size), size)

    def each(count, body):
        lax.fori_loop(0, count, lambda j, carry: (body(j), carry)[1], 0)

    def qkv_part(j):
        qkv[:, tile(j)] = dot_nn(norm_one[...], wqkv[:, tile(j)]).astype(bf16)

    each(3, qkv_part)
    inside = lax.broadcasted_iota(jnp.int32, (rows, rows), 1) < seq

    def heads(p):
        pair = [qkv[:, pl.ds(pl.multiple_of(j * D + p * 128, 128), 128)] for j in range(3)]
        outs = []
        for h in range(2):
            query, key, value = (part[:, h * HD : h * HD + HD] for part in pair)
            scores = jnp.where(inside, dot_nt(query, key) * (HD**-0.5), -1e30)
            weight = jnp.exp(scores - jnp.max(scores, axis=-1, keepdims=True))
            weight = weight / jnp.sum(weight, axis=-1, keepdims=True)
            probs[p * 2 + h] = weight
            outs.append(dot_nn(weight.astype(bf16), value))
        att[:, pl.ds(pl.multiple_of(p * 128, 128), 128)] = jnp.concatenate(outs, axis=1).astype(bf16)

    each(HEADS // 2, heads)
    loads[1].wait()
    mid[...] = xs[...] + dot_nn(att[...], wout[...])
    unit, scale = normed(mid[...])
    norm_two[...] = (unit * gain_two + shift_two).astype(bf16)
    loads[2].wait()
    loads[3].wait()
    acc[...] = jnp.zeros_like(acc)

    def hidden_part(j):
        hidden = dot_nn(norm_two[...], wup[:, tile(j)])
        half = 0.5 * (1.0 + lax.erf(hidden * (0.5**0.5)))
        active = (hidden * half).astype(bf16)
        slope = half + hidden * jnp.exp(-0.5 * hidden * hidden) * (2.0 * math.pi) ** -0.5
        mid[...] += dot_nn(active, wdown[tile(j), :])
        gdown[tile(j), :] = dot_tn(active, up_low[...]).astype(bf16)
        grad_hidden = (dot_nt(up_low[...], wdown[tile(j), :]) * slope).astype(bf16)
        gup[:, tile(j)] = dot_tn(norm_two[...], grad_hidden).astype(bf16)
        acc[...] += dot_nt(grad_hidden, wup[:, tile(j)])

    kept_unit, kept_scale = unit, scale
    hid_low[...] = kept_unit
    each(HID // D, hidden_part)
    stores[2].start()
    stores[3].start()
    out_ref[...] = mid[0:seq, :].astype(bf16)
    grad = acc[...]
    unit = hid_low[...]
    gvec_ref[...] = jnp.zeros_like(gvec_ref)
    gvec_ref[2:3, :] = jnp.sum(grad * unit, axis=0, keepdims=True)
    gvec_ref[3:4, :] = jnp.sum(grad, axis=0, keepdims=True)
    ups[...] += normed_back(grad, unit, kept_scale, gain_two)
    up_low[...] = ups[...].astype(bf16)
    gout[...] = dot_tn(att[...], up_low[...]).astype(bf16)
    stores[1].start()
    datt[...] = dot_nt(up_low[...], wout[...]).astype(bf16)

    def heads_back(p):
        pair = [qkv[:, pl.ds(pl.multiple_of(j * D + p * 128, 128), 128)] for j in range(3)]
        grad_pair = datt[:, pl.ds(pl.multiple_of(p * 128, 128), 128)]
        grads = [[], [], []]
        for h in range(2):
            query, key, value = (part[:, h * HD : h * HD + HD] for part in pair)
            grad_out = grad_pair[:, h * HD : h * HD + HD]
            weight = probs[p * 2 + h]
            grad_weight = dot_nt(grad_out, value)
            grads[2].append(dot_tn(weight.astype(bf16), grad_out))
            grad_score = weight * (grad_weight - jnp.sum(weight * grad_weight, axis=-1, keepdims=True))
            grad_score = grad_score.astype(bf16)
            grads[0].append(dot_nn(grad_score, key) * (HD**-0.5))
            grads[1].append(dot_tn(grad_score, query) * (HD**-0.5))
        for j in range(3):
            dqkv[:, pl.ds(pl.multiple_of(j * D + p * 128, 128), 128)] = jnp.concatenate(grads[j], axis=1).astype(bf16)

    each(HEADS // 2, heads_back)
    acc[...] = jnp.zeros_like(acc)

    def qkv_back(j):
        gqkv[:, tile(j)] = dot_tn(norm_one[...], dqkv[:, tile(j)]).astype(bf16)
        acc[...] += dot_nt(dqkv[:, tile(j)], wqkv[:, tile(j)])

    each(3, qkv_back)
    stores[0].start()
    unit, scale = normed(xs[...])
    grad = acc[...]
    gvec_ref[0:1, :] = jnp.sum(grad * unit, axis=0, keepdims=True)
    gvec_ref[1:2, :] = jnp.sum(grad, axis=0, keepdims=True)
    total = ups[...] + normed_back(grad, unit, scale, gain_one)
    gvec_ref[4:5, :] = jnp.sum(total, axis=0, keepdims=True)
    low_ref[...] = total.astype(bf16)
    for store in stores:
        store.wait()


def block_pass(stream, upstream, vectors, wqkv, wout, wup, wdown):
    f32, bf16 = jnp.float32, jnp.bfloat16
    seq = stream.shape[0]
    rows = tall(seq)
    whole = pl.BlockSpec(memory_space=pltpu.VMEM)
    far = pl.BlockSpec(memory_space=pl.ANY)
    mats = [wqkv, wout, wup, wdown]
    kept = [pltpu.VMEM(mat.shape, bf16) for mat in mats]
    dma = pltpu.SemaphoreType.DMA
    return pl.pallas_call(
        block_kernel,
        out_shape=[
            jax.ShapeDtypeStruct((seq, D), bf16),
            jax.ShapeDtypeStruct((rows, D), bf16),
            jax.ShapeDtypeStruct((8, D), f32),
        ]
        + [jax.ShapeDtypeStruct(mat.shape, bf16) for mat in mats],
        in_specs=[whole] * 3 + [far] * 4,
        out_specs=[whole] * 3 + [far] * 4,
        scratch_shapes=kept
        + kept
        + [
            pltpu.VMEM((rows, D), f32),
            pltpu.VMEM((rows, D), f32),
            pltpu.VMEM((rows, D), bf16),
            pltpu.VMEM((rows, D), bf16),
            pltpu.VMEM((rows, 3 * D), bf16),
            pltpu.VMEM((rows, D), bf16),
            pltpu.VMEM((HEADS, rows, rows), f32),
            pltpu.VMEM((rows, D), f32),
            pltpu.VMEM((rows, D), bf16),
            pltpu.VMEM((rows, D), f32),
            pltpu.VMEM((rows, D), f32),
            pltpu.VMEM((rows, D), bf16),
            pltpu.VMEM((rows, 3 * D), bf16),
            dma((4,)),
            dma((4,)),
        ],
        compiler_params=pltpu.CompilerParams(vmem_limit_bytes=60 << 20),
        cost_estimate=pl.CostEstimate(flops=8_400_000_000, bytes_accessed=30_000_000, transcendentals=2_000_000),
        name="block_pass",
    )(stream, upstream, vectors, *mats)


def adamw_step(weight, moment_one, moment_two, grad, rate):
    first = beta_one * moment_one + (1.0 - beta_one) * grad
    second = beta_two * moment_two + (1.0 - beta_two) * grad * grad
    fix_one = 1.0 - beta_one**STEP
    fix_two = 1.0 - beta_two**STEP
    update = first / fix_one / (jnp.sqrt(second / fix_two) + epsilon_add) + decay_rate * weight
    return (weight - rate * update, first, second)


NC = 15
HEAD = 96


def dims_step(count):
    return 16 if count % 16 == 0 else count


def make_kernel(shaped_ref, master_ref, kernel_ref, turned):
    dims = kernel_ref.shape[0]
    shaped = shaped_ref[pl.ds(pl.multiple_of(lax.axis_index("group") * NB, NB), NB), :]
    for dim in range(dims):
        part = dot_nn(shaped, master_ref[:, dim * PATCH : (dim + 1) * PATCH])
        turned[pl.ds(dim, NB, stride=dims), :] = part[:, :128]
        turned[pl.ds(NB * dims + dim, NB, stride=dims), :] = part[:, 128:]
    for band in range(NB):
        for half in range(2):
            row = half * NB * dims + band * dims
            lane = band * PATCH + half * 128
            kernel_ref[:, lane : lane + 128] = turned[row : row + dims, :].astype(kernel_ref.dtype)


def make_kernels(shaped, master):
    dims = master.shape[1] // PATCH
    step = dims_step(dims)
    return pl.pallas_call(
        make_kernel,
        out_shape=jax.ShapeDtypeStruct((dims, NB * PATCH), jnp.bfloat16),
        grid=(dims // step,),
        in_specs=[
            pl.BlockSpec(shaped.shape, lambda j: (0, 0)),
            pl.BlockSpec((E, step * PATCH), lambda j: (0, j)),
        ],
        out_specs=pl.BlockSpec((step, NB * PATCH), lambda j: (j, 0)),
        scratch_shapes=[pltpu.VMEM((2 * NB * step, 128), jnp.float32)],
        compiler_params=pltpu.CompilerParams(vmem_limit_bytes=60 << 20),
        name="make_kernels",
    )(shaped, master)


def embed_kernel(pixel_ref, mask_ref, kernel_ref, stream_ref):
    masked = pixel_ref[...] * mask_ref[...].astype(jnp.bfloat16)
    part = dot_nt(masked, kernel_ref[...])

    @pl.when(pl.program_id(0) == 0)
    def _():
        stream_ref[...] = part

    @pl.when(pl.program_id(0) > 0)
    def _():
        stream_ref[...] += part


def embed_patches(pixels, mask, kernels):
    seq, width = pixels.shape[1], pixels.shape[2]
    cut = 1024
    return pl.pallas_call(
        embed_kernel,
        out_shape=jax.ShapeDtypeStruct((seq, D), jnp.float32),
        grid=(width // cut,),
        in_specs=[
            pl.BlockSpec((None, seq, cut), lambda j: (0, 0, j)),
            pl.BlockSpec((1, cut), lambda j: (0, j)),
            pl.BlockSpec((D, cut), lambda j: (0, j)),
        ],
        out_specs=pl.BlockSpec((seq, D), lambda j: (0, 0)),
        compiler_params=pltpu.CompilerParams(vmem_limit_bytes=60 << 20),
        name="embed_patches",
    )(pixels, mask, kernels)


def unembed_kernel(masked_ref, mask_ref, kernel_ref, low_ref, back_ref, grad_ref):
    seq = back_ref.shape[0]
    back_ref[...] = (dot_nn(low_ref[...], kernel_ref[...])[0:seq] * mask_ref[...]).astype(back_ref.dtype)
    grad_ref[...] = dot_tn(low_ref[...], masked_ref[...]).astype(grad_ref.dtype)


def unembed_patches(masked, mask, kernels, low, seq):
    rows, width = masked.shape
    cut = 1024
    return pl.pallas_call(
        unembed_kernel,
        out_shape=[
            jax.ShapeDtypeStruct((1, seq, width), jnp.bfloat16),
            jax.ShapeDtypeStruct((D, width), jnp.bfloat16),
        ],
        grid=(width // cut,),
        in_specs=[
            pl.BlockSpec((rows, cut), lambda j: (0, j)),
            pl.BlockSpec((1, cut), lambda j: (0, j)),
            pl.BlockSpec((D, cut), lambda j: (0, j)),
            pl.BlockSpec(low.shape, lambda j: (0, 0)),
        ],
        out_specs=[
            pl.BlockSpec((None, seq, cut), lambda j: (0, 0, j)),
            pl.BlockSpec((D, cut), lambda j: (0, j)),
        ],
        compiler_params=pltpu.CompilerParams(vmem_limit_bytes=60 << 20),
        name="unembed_patches",
    )(masked, mask, kernels, low)


def master_kernel(rate, grad_ref, shaped_ref, weight_ref, one_ref, two_ref, new_ref, first_ref, second_ref, back_ref, turned):
    groups, dims = grad_ref.shape[0], grad_ref.shape[1]
    bands = groups * NB
    for group in range(groups):
        for band in range(NB):
            for half in range(2):
                row = half * bands * dims + (group * NB + band) * dims
                lane = band * PATCH + half * 128
                turned[row : row + dims, :] = grad_ref[group, :, lane : lane + 128].astype(jnp.float32)
    total = jnp.zeros(back_ref.shape, jnp.float32)
    for dim in range(dims):
        part = jnp.concatenate(
            [turned[pl.ds(half * bands * dims + dim, bands, stride=dims), :] for half in range(2)], axis=1
        ).astype(jnp.bfloat16)
        lanes = slice(dim * PATCH, (dim + 1) * PATCH)
        weight = weight_ref[:, lanes]
        total += dot_nt(part, weight.astype(jnp.bfloat16))
        grad = dot_tn(shaped_ref[...], part)
        new_ref[:, lanes], first_ref[:, lanes], second_ref[:, lanes] = adamw_step(
            weight, one_ref[:, lanes], two_ref[:, lanes], grad, rate
        )

    @pl.when(pl.program_id(0) == 0)
    def _():
        back_ref[...] = total

    @pl.when(pl.program_id(0) > 0)
    def _():
        back_ref[...] += total


def master_update(grads, shaped, weight, one, two, rate):
    groups, dims = grads.shape[0], grads.shape[1]
    step = dims_step(dims)
    columns = pl.BlockSpec((weight.shape[0], step * PATCH), lambda j: (0, j))
    like = jax.ShapeDtypeStruct(weight.shape, jnp.float32)
    return pl.pallas_call(
        functools.partial(master_kernel, rate),
        out_shape=[like, like, like, jax.ShapeDtypeStruct(shaped.shape, jnp.float32)],
        grid=(dims // step,),
        in_specs=[
            pl.BlockSpec((groups, step, NB * PATCH), lambda j: (0, j, 0)),
            pl.BlockSpec(shaped.shape, lambda j: (0, 0)),
            columns,
            columns,
            columns,
        ],
        out_specs=[columns, columns, columns, pl.BlockSpec(shaped.shape, lambda j: (0, 0))],
        scratch_shapes=[pltpu.VMEM((2 * groups * NB * step, 128), jnp.float32)],
        compiler_params=pltpu.CompilerParams(vmem_limit_bytes=60 << 20),
        name="master_update",
    )(grads, shaped, weight, one, two)


def spot():
    group = lax.axis_index("group")
    image = lax.axis_index("img")
    return group // 2, group % 2, image // 2, image % 2


def place(y, c, z, x):
    return (y * 2 + c, z * 2 + x)


def partners():
    y, c, z, x = spot()
    x2, y2 = x + (1 - c) * (1 - 2 * x), y + c * (1 - 2 * y)
    x3, y3 = x + c * (1 - 2 * x), y + (1 - c) * (1 - 2 * y)
    around = [place(y, c, (z + d) % 4, x) for d in (1, 2, 3)]
    return (x2, y2), (x3, y3), around, place(y2, c, z, x2), place(y3, c, z, x3), place(y, 1 - c, z, x)


def greet(peers):
    barrier = pltpu.get_barrier_semaphore()
    for peer in peers:
        pl.semaphore_signal(barrier, inc=1, device_id=peer, device_id_type=MESH)
    pl.semaphore_wait(barrier, len(peers))


def remote(src, dst, send_sem, recv_sem, target):
    return pltpu.make_async_remote_copy(
        src_ref=src, dst_ref=dst, send_sem=send_sem, recv_sem=recv_sem, device_id=target, device_id_type=MESH
    )


def gather_kernel(own_ref, pixel_ref, all_ref, head_ref, head_sem, local_sem, line_send, line_recv, group_send, group_recv, twin_send, twin_recv):
    y, c, z, x = spot()
    (x2, y2), (x3, y3), around, second, third, twin = partners()
    partner = place(y, 1 - c, (z + 2) % 4, x)
    moved = (c + z // 2) % 2 == 1
    rows = own_ref.shape[0] // NC

    def cut(k):
        return pl.ds(k * rows, rows)

    head = remote(pixel_ref.at[0, pl.ds(0, HEAD)], head_ref.at[0], head_sem.at[0], head_sem.at[1], partner)

    def along(d, k):
        return remote(own_ref.at[cut(k)], all_ref.at[y, c, z, x, cut(k)], line_send.at[d - 1, k], line_recv.at[d - 1, k], around[d - 1])

    def along_in(d, k):
        return remote(own_ref.at[cut(k)], all_ref.at[y, c, (z + 4 - d) % 4, x, cut(k)], line_send.at[d - 1, k], line_recv.at[d - 1, k], around[d - 1])

    def square(core, j):
        yy, xx = ((y, x), (y2, x2), (y3, x3), (1 - y, 1 - x))[j]
        return all_ref.at[yy, core, :, xx]

    def hop(j, to, k, slot, landing):
        part = square(c, j).at[:, cut(k)]
        return remote(part, part, group_send.at[slot, k], group_recv.at[landing, k], to)

    def hop_in(landing, k):
        part = square(c, landing).at[:, cut(k)]
        return remote(part, part, group_send.at[0, k], group_recv.at[landing, k], twin)

    def share(j, k):
        part = square(c, j).at[:, cut(k)]
        yy, xx = ((y, x), (y2, x2), (y3, x3), (1 - y, 1 - x))[j]
        landing = (0, 2, 1, 3)[j]
        return remote(part, part, twin_send.at[j, k], twin_recv.at[landing, k], twin)

    def share_in(landing, k):
        yy, xx = ((y, x), (y2, x2), (y3, x3), (1 - y, 1 - x))[landing]
        part = all_ref.at[yy, 1 - c, :, xx, cut(k)]
        return remote(part, part, twin_send.at[0, k], twin_recv.at[landing, k], twin)

    keep = pltpu.make_async_copy(own_ref, all_ref.at[y, c, z, x], local_sem)
    keep.start()
    greet(around + [second, third, twin, partner])
    for k in range(NC):
        for d in (1, 2, 3):
            along(d, k).start()
    keep.wait()
    for step in range(NC + 2):
        k = step
        if k < NC:
            for d in (1, 2, 3):
                along_in(d, k).wait_recv()
            hop(0, third, k, 0, 2).start()
            hop(0, second, k, 1, 1).start()
            share(0, k).start()
        if step == NC - 3:

            @pl.when(moved)
            def _():
                head.start()

        k = step - 1
        if 0 <= k < NC:
            hop_in(1, k).wait_recv()
            hop(1, third, k, 2, 3).start()
            share(1, k).start()
        k = step - 2
        if 0 <= k < NC:
            hop_in(2, k).wait_recv()
            share(2, k).start()
            hop_in(3, k).wait_recv()
            share(3, k).start()
    for k in range(NC):
        for d in (1, 2, 3):
            along(d, k).wait_send()
        hop(0, third, k, 0, 2).wait_send()
        hop(0, second, k, 1, 1).wait_send()
        hop(1, third, k, 2, 3).wait_send()
        for j in range(4):
            share(j, k).wait_send()
            share_in(j, k).wait_recv()

    @pl.when(moved)
    def _():
        head.wait()


def gather_packed(own, pixels):
    rows = own.shape[0]
    dma = pltpu.SemaphoreType.DMA
    return pl.pallas_call(
        gather_kernel,
        out_shape=[
            jax.ShapeDtypeStruct((2, 2, 4, 2, rows, 128), own.dtype),
            jax.ShapeDtypeStruct((1, HEAD, pixels.shape[2]), pixels.dtype),
        ],
        in_specs=[pl.BlockSpec(memory_space=pltpu.VMEM), pl.BlockSpec(memory_space=pl.ANY)],
        out_specs=[pl.BlockSpec(memory_space=pl.ANY)] * 2,
        scratch_shapes=[dma((2,)), dma, dma((3, NC)), dma((3, NC)), dma((3, NC)), dma((4, NC)), dma((4, NC)), dma((4, NC))],
        compiler_params=pltpu.CompilerParams(collective_id=0, has_side_effects=True, vmem_limit_bytes=60 << 20),
        name="gather_packed",
    )(own, pixels)


def reduce_kernel(part_ref, sum_ref, own, twin_in, third_in, second_in, line_in, load_sem, twin_send, twin_recv, third_send, third_recv, second_send, second_recv, line_send, line_recv):
    f32, bf16 = jnp.float32, jnp.bfloat16
    y, c, z, x = spot()
    (x2, y2), (x3, y3), around, second, third, twin = partners()
    rows = sum_ref.shape[0] // NC

    def cut(k):
        return pl.ds(k * rows, rows)

    spots = ((1 - y, 1 - x), (y3, x3), (y2, x2), (y, x))
    turned = ((1 - y, 1 - x), (y2, x2), (y3, x3), (y, x))

    def load(j, k):
        yy, xx = spots[j]
        return pltpu.make_async_copy(part_ref.at[yy, c, :, xx, cut(k)], own.at[j, :, cut(k)], load_sem.at[j, k])

    def swap(j, k):
        yy, xx = turned[j]
        return remote(part_ref.at[yy, 1 - c, :, xx, cut(k)], twin_in.at[j, :, cut(k)], twin_send.at[j, k], twin_recv.at[j, k], twin)

    def to_third(j, k):
        return remote(own.at[j, :, cut(k)], third_in.at[j, :, cut(k)], third_send.at[j, k], third_recv.at[j, k], third)

    def to_second(k):
        return remote(own.at[2, :, cut(k)], second_in.at[:, cut(k)], second_send.at[k], second_recv.at[k], second)

    def to_line(d, k):
        return remote(own.at[3, (z + d) % 4, cut(k)], line_in.at[d - 1, cut(k)], line_send.at[d - 1, k], line_recv.at[d - 1, k], around[d - 1])

    for k in range(NC):
        for j in range(4):
            load(j, k).start()
    greet(around + [second, third, twin])
    for k in range(NC):
        for j in range(4):
            swap(j, k).start()

    def pair(j, k):
        load(j, k).wait()
        swap(j, k).wait_recv()
        return own[j, :, cut(k)].astype(f32) + twin_in[j, :, cut(k)].astype(f32)

    for step in range(NC + 3):
        k = step
        if k < NC:
            for j in (0, 1):
                own[j, :, cut(k)] = pair(j, k).astype(bf16)
                to_third(j, k).start()
        k = step - 1
        if 0 <= k < NC:
            held = pair(2, k)
            to_third(0, k).wait_recv()
            own[2, :, cut(k)] = (held + third_in[0, :, cut(k)].astype(f32)).astype(bf16)
            to_second(k).start()
        k = step - 2
        if 0 <= k < NC:
            held = pair(3, k)
            to_third(1, k).wait_recv()
            to_second(k).wait_recv()
            held += third_in[1, :, cut(k)].astype(f32) + second_in[:, cut(k)].astype(f32)
            own[3, :, cut(k)] = held.astype(bf16)
            for d in (1, 2, 3):
                to_line(d, k).start()
        k = step - 3
        if 0 <= k < NC:
            total = own[3, z, cut(k)].astype(f32)
            for d in (1, 2, 3):
                to_line(d, k).wait_recv()
                total += line_in[d - 1, cut(k)].astype(f32)
            sum_ref[cut(k)] = total
    for k in range(NC):
        for j in range(4):
            swap(j, k).wait_send()
        for j in (0, 1):
            to_third(j, k).wait_send()
        to_second(k).wait_send()
        for d in (1, 2, 3):
            to_line(d, k).wait_send()


def reduce_packed(part):
    rows = part.shape[-2]
    bf16 = jnp.bfloat16
    dma = pltpu.SemaphoreType.DMA
    return pl.pallas_call(
        reduce_kernel,
        out_shape=jax.ShapeDtypeStruct((rows, 128), jnp.float32),
        in_specs=[pl.BlockSpec(memory_space=pl.ANY)],
        out_specs=pl.BlockSpec(memory_space=pltpu.VMEM),
        scratch_shapes=[
            pltpu.VMEM((4, 4, rows, 128), bf16),
            pltpu.VMEM((4, 4, rows, 128), bf16),
            pltpu.VMEM((2, 4, rows, 128), bf16),
            pltpu.VMEM((4, rows, 128), bf16),
            pltpu.VMEM((3, rows, 128), bf16),
            dma((4, NC)), dma((4, NC)), dma((4, NC)), dma((2, NC)), dma((2, NC)), dma((NC,)), dma((NC,)), dma((3, NC)), dma((3, NC)),
        ],
        compiler_params=pltpu.CompilerParams(collective_id=1, has_side_effects=True, vmem_limit_bytes=56 << 20),
        name="reduce_packed",
    )(part)


CHUNK = 16


def over_x(k):
    return k % 2 == 0


def quad_peers():
    y, c, z, x = spot()
    low = z % 2
    side = place(y, c, z, 1 - x)
    along = place(y, c, z + 1 - 2 * low, x)
    twin = place(y, 1 - c, z, x)
    partner = place(y, 1 - c, (z + 2) % 4, x)
    moved = (c + z // 2) % 2 == 1
    return y, c, z, x, low, side, along, twin, partner, moved


def swap_images(value):
    pairs = []
    for y in range(2):
        for c in range(2):
            for z in range(4):
                for x in range(2):
                    other = (1 - c, (z + 2) % 4) if c != z // 2 else (c, z)
                    pairs.append((((y * 2 + c) * 4 + z) * 2 + x, ((y * 2 + other[0]) * 4 + other[1]) * 2 + x))
    return lax.ppermute(value, ("group", "img"), pairs)


def share_kernel(made_ref, mask_ref, pixel_ref, head_ref, rest_ref, all_ref, masked_ref, stream_ref,
                 held, top, bottom, tile, mixed, order, pixel_sem, store_sem, keep_sem, swap_send, swap_recv,
                 side_send, side_recv, along_send, along_recv, far_send, far_recv, twin_send, twin_recv):
    f32, bf16 = jnp.float32, jnp.bfloat16
    y, c, z, x, low, side, along, twin, partner, moved = quad_peers()
    dims, width = made_ref.shape
    count = dims // CHUNK
    group = 8 * CHUNK

    def cut(k):
        return pl.ds(k * CHUNK, CHUNK)

    def block(core, j, k):
        return held.at[2 * core + (low + j // 2) % 2, (x + j % 2) % 2, cut(k)]

    def keep(k):
        return pltpu.make_async_copy(made_ref.at[cut(k)], block(c, 0, k), keep_sem.at[k])

    def swap(k):
        return remote(made_ref.at[cut(k)], block(1 - c, 0, k), swap_send.at[k], swap_recv.at[k], partner)

    def swap_in(k):
        return remote(made_ref.at[cut(k)], block(c, 0, k), swap_send.at[k], swap_recv.at[k], partner)

    def to_side(k):
        return remote(block(c, 0, k), block(c, 0, k), side_send.at[k], side_recv.at[k], side)

    def from_side(k):
        return remote(block(c, 1, k), block(c, 1, k), side_send.at[k], side_recv.at[k], side)

    def to_along(k):
        return remote(block(c, 0, k), block(c, 0, k), along_send.at[k], along_recv.at[k], along)

    def from_along(k):
        return remote(block(c, 2, k), block(c, 2, k), along_send.at[k], along_recv.at[k], along)

    def pass_on(k):
        j, to = (2, side) if over_x(k) else (1, along)
        return remote(block(c, j, k), block(c, j, k), far_send.at[k], far_recv.at[k], to)

    def from_far(k):
        return remote(block(c, 3, k), block(c, 3, k), far_send.at[k], far_recv.at[k], twin)

    def give(j, k):
        return remote(block(c, j, k), block(c, j, k), twin_send.at[j, k], twin_recv.at[j, k], twin)

    def given(j, k):
        return remote(block(1 - c, j, k), block(1 - c, j, k), twin_send.at[j, k], twin_recv.at[j, k], twin)

    def store(k):
        return pltpu.make_async_copy(held.at[:, :, cut(k)], all_ref.at[:, :, cut(k)], store_sem.at[k])

    swapped = pltpu.make_async_copy(head_ref.at[0], top, pixel_sem.at[0])
    owned = pltpu.make_async_copy(pixel_ref.at[0, pl.ds(0, HEAD)], top, pixel_sem.at[0])
    lower = pltpu.make_async_copy(rest_ref.at[0], bottom, pixel_sem.at[1])

    @pl.when(jnp.logical_not(moved))
    def _():
        owned.start()
        for k in range(count):
            keep(k).start()

    lower.start()
    greet([side, along, twin, partner])

    @pl.when(moved)
    def _():
        swapped.start()
        for k in range(count):
            swap(k).start()

    def mask_pixels(part):
        @pl.when(part == 0)
        def _():
            lower.wait()
            owned.wait()

        def some(j, carry):
            lanes = pl.ds(pl.multiple_of(j * 1024, 1024), 1024)
            mask = mask_ref[:, lanes]
            masked_ref[0:HEAD, lanes] = (top[:, lanes].astype(f32) * mask).astype(bf16)
            tile[...] = jnp.zeros_like(tile)
            tile[0 : bottom.shape[0], :] = bottom[:, lanes].astype(f32) * mask
            masked_ref[HEAD:, lanes] = tile[...].astype(bf16)
            return carry

        cuts = width // 1024
        lax.fori_loop(part * (cuts // 2), (part + 1) * (cuts // 2), some, 0)

    def make_order():
        row = lax.broadcasted_iota(jnp.int32, order.shape, 0)
        column = lax.broadcasted_iota(jnp.int32, order.shape, 1)
        wanted = row % group // CHUNK * dims + row // group * CHUNK + row % CHUNK
        order[...] = jnp.where(column == wanted, 1.0, 0.0)

    for step in range(count + 3):
        k = step
        if k < count:

            @pl.when(moved)
            def _(k=k):
                swap_in(k).wait_recv()

            @pl.when(jnp.logical_not(moved))
            def _(k=k):
                keep(k).wait()

            to_side(k).start()
            to_along(k).start()
            give(0, k).start()
        if step < 2:
            mask_pixels(step)
        elif step == 2:
            make_order()
        k = step - 1
        if 0 <= k < count:
            if over_x(k):
                from_along(k).wait_recv()
                pass_on(k).start()
                from_side(k).wait_recv()
            else:
                from_side(k).wait_recv()
                pass_on(k).start()
                from_along(k).wait_recv()
            give(1, k).start()
            give(2, k).start()
        k = step - 2
        if 0 <= k < count:
            from_far(k).wait_recv()
            give(3, k).start()
        k = step - 3
        if 0 <= k < count:
            for j in range(4):
                given(j, k).wait_recv()
            store(k).start()
            part = held[:, :, cut(k), :].reshape(group, width)
            mixed[:, k * group : (k + 1) * group] = dot_nt(masked_ref[...], part)

    stream_ref[...] = exact(mixed[...], order[...], 1, 0)[0 : stream_ref.shape[0]]

    @pl.when(moved)
    def _():
        for k in range(count):
            swap(k).wait_send()

    for k in range(count):
        to_side(k).wait_send()
        to_along(k).wait_send()
        pass_on(k).wait_send()
        store(k).wait()
        for j in range(4):
            give(j, k).wait_send()


def share_kernels(made, mask, pixels, head, rest):
    dims, width = made.shape
    count = dims // CHUNK
    seq = pixels.shape[1]
    rows = tall(seq)
    f32 = jnp.float32
    dma = pltpu.SemaphoreType.DMA
    vmem, far = pl.BlockSpec(memory_space=pltpu.VMEM), pl.BlockSpec(memory_space=pl.ANY)
    shared, masked, stream = pl.pallas_call(
        share_kernel,
        out_shape=[
            jax.ShapeDtypeStruct((4, 2, dims, width), made.dtype),
            jax.ShapeDtypeStruct((rows, width), made.dtype),
            jax.ShapeDtypeStruct((seq, 8 * dims), f32),
        ],
        in_specs=[vmem, vmem, far, far, far],
        out_specs=[far, vmem, vmem],
        scratch_shapes=[
            pltpu.VMEM((4, 2, dims, width), made.dtype),
            pltpu.VMEM((HEAD, width), made.dtype),
            pltpu.VMEM((seq - HEAD, width), made.dtype),
            pltpu.VMEM((rows - HEAD, 1024), f32),
            pltpu.VMEM((rows, 8 * dims), f32),
            pltpu.VMEM((8 * dims, 8 * dims), f32),
            dma((2,)),
        ]
        + [dma((count,))] * 10
        + [dma((4, count))] * 2,
        compiler_params=pltpu.CompilerParams(collective_id=2, has_side_effects=True, vmem_limit_bytes=60 << 20),
        name="share_kernels",
    )(made, mask, pixels, head, rest)
    return shared.reshape(8 * dims, width), masked, stream


def fold_kernel(part_ref, all_ref, own, twin_in, relay_in, side_in, along_in, load_sem, keep_sem, twin_send, twin_recv, relay_send, relay_recv,
                side_send, side_recv, along_send, along_recv, swap_send, swap_recv, group_send, group_recv, give_send, give_recv):
    f32, bf16 = jnp.float32, jnp.bfloat16
    y, c, z, x, low, side, along, twin, partner, moved = quad_peers()
    over = place(1 - y, c, z, x)
    count = all_ref.shape[2] // CHUNK

    def cut(k):
        return pl.ds(k * CHUNK, CHUNK)

    def part(core, j, k):
        return part_ref.at[2 * core + (low + j // 2) % 2, (x + j % 2) % 2, cut(k)]

    def load(j, k):
        return pltpu.make_async_copy(part(c, j, k), own.at[j, cut(k)], load_sem.at[j, k])

    def swap(j, k):
        return remote(part(1 - c, j, k), twin_in.at[j, cut(k)], twin_send.at[j, k], twin_recv.at[j, k], twin)

    def relay(k):
        return remote(own.at[3, cut(k)], relay_in.at[cut(k)], relay_send.at[k], relay_recv.at[k], along if over_x(k) else side)

    def to_side(k):
        return remote(own.at[1, cut(k)], side_in.at[cut(k)], side_send.at[k], side_recv.at[k], side)

    def to_along(k):
        return remote(own.at[2, cut(k)], along_in.at[cut(k)], along_send.at[k], along_recv.at[k], along)

    def keep(k):
        return pltpu.make_async_copy(own.at[0, cut(k)], all_ref.at[y, c, cut(k)], keep_sem.at[k])

    def move(k):
        return remote(own.at[0, cut(k)], all_ref.at[y, 1 - c, cut(k)], swap_send.at[k], swap_recv.at[k], partner)

    def moved_in(k):
        return remote(own.at[0, cut(k)], all_ref.at[y, c, cut(k)], swap_send.at[k], swap_recv.at[k], partner)

    def cross(k):
        return remote(all_ref.at[y, c, cut(k)], all_ref.at[y, c, cut(k)], group_send.at[k], group_recv.at[k], over)

    def crossed(k):
        return remote(all_ref.at[1 - y, c, cut(k)], all_ref.at[1 - y, c, cut(k)], group_send.at[k], group_recv.at[k], over)

    def give(j, k):
        here = all_ref.at[(y + j) % 2, c, cut(k)]
        return remote(here, here, give_send.at[j, k], give_recv.at[j, k], twin)

    def given(j, k):
        here = all_ref.at[(y + j) % 2, 1 - c, cut(k)]
        return remote(here, here, give_send.at[j, k], give_recv.at[j, k], twin)

    def pair(j, k):
        load(j, k).wait()
        swap(j, k).wait_recv()
        return own[j, cut(k)].astype(f32) + twin_in[j, cut(k)].astype(f32)

    for k in range(count):
        for j in (3, 1, 2, 0):
            load(j, k).start()
    greet([side, along, twin, partner, over])
    for k in range(count):
        for j in (3, 1, 2, 0):
            swap(j, k).start()

    for step in range(count + 4):
        k = step
        if k < count:
            own[3, cut(k)] = pair(3, k).astype(bf16)
            relay(k).start()
        k = step - 1
        if 0 <= k < count:
            first, second = (to_along, to_side) if over_x(k) else (to_side, to_along)
            plain, summed = (2, 1) if over_x(k) else (1, 2)
            own[plain, cut(k)] = pair(plain, k).astype(bf16)
            first(k).start()
            held = pair(summed, k)
            relay(k).wait_recv()
            own[summed, cut(k)] = (held + relay_in[cut(k)].astype(f32)).astype(bf16)
            second(k).start()
        k = step - 2
        if 0 <= k < count:
            held = pair(0, k)
            to_side(k).wait_recv()
            to_along(k).wait_recv()
            held += side_in[cut(k)].astype(f32) + along_in[cut(k)].astype(f32)
            own[0, cut(k)] = held.astype(bf16)

            @pl.when(moved)
            def _(k=k):
                move(k).start()

            @pl.when(jnp.logical_not(moved))
            def _(k=k):
                keep(k).start()

        k = step - 3
        if 0 <= k < count:

            @pl.when(moved)
            def _(k=k):
                moved_in(k).wait_recv()

            @pl.when(jnp.logical_not(moved))
            def _(k=k):
                keep(k).wait()

            cross(k).start()
            give(0, k).start()
        k = step - 4
        if 0 <= k < count:
            crossed(k).wait_recv()
            give(1, k).start()

    @pl.when(moved)
    def _():
        for k in range(count):
            move(k).wait_send()

    for k in range(count):
        for j in range(4):
            swap(j, k).wait_send()
        relay(k).wait_send()
        to_side(k).wait_send()
        to_along(k).wait_send()
        cross(k).wait_send()
        for j in range(2):
            give(j, k).wait_send()
            given(j, k).wait_recv()


def fold_kernels(part):
    width = part.shape[1]
    dims = part.shape[0] // 8
    count = dims // CHUNK
    bf16 = jnp.bfloat16
    dma = pltpu.SemaphoreType.DMA
    folded = pl.pallas_call(
        fold_kernel,
        out_shape=jax.ShapeDtypeStruct((2, 2, dims, width), bf16),
        in_specs=[pl.BlockSpec(memory_space=pl.ANY)],
        out_specs=pl.BlockSpec(memory_space=pl.ANY),
        scratch_shapes=[
            pltpu.VMEM((4, dims, width), bf16),
            pltpu.VMEM((4, dims, width), bf16),
            pltpu.VMEM((dims, width), bf16),
            pltpu.VMEM((dims, width), bf16),
            pltpu.VMEM((dims, width), bf16),
            dma((4, count)),
            dma((count,)),
            dma((4, count)),
            dma((4, count)),
        ]
        + [dma((count,))] * 10
        + [dma((2, count))] * 2,
        compiler_params=pltpu.CompilerParams(collective_id=3, has_side_effects=True, vmem_limit_bytes=60 << 20),
        name="fold_kernels",
    )(part.reshape(4, 2, dims, width))
    return folded.reshape(4, dims, width)


def on_device(
    pixels,
    band_mask,
    wavelength,
    owner_order,
    rest_weight,
    rest_moment1,
    rest_moment2,
    fc_weight,
    fc_moment1,
    fc_moment2,
    cotangent,
):
    f32 = jnp.float32
    bf16 = jnp.bfloat16
    kernel_rate = float(E * PATCH * NB) ** (-0.5)
    groups = lax.axis_size("group")
    own_rows = rest_weight.shape[0]
    own_blocks = own_rows // 8
    fits = lax.axis_size("group") == 4 and lax.axis_size("img") == 8
    extra = -own_rows % 128
    slot_blocks = (own_rows + extra) // 8
    mask = band_mask.astype(f32)
    low_weight = fc_weight.astype(bf16)
    rest_low = jnp.pad(rest_weight.astype(bf16), ((0, extra), (0, 0)))
    if fits:
        mask = swap_images(mask)
        gathered, head = gather_packed(rest_low, pixels)
        gathered, rest, cotangent, low_weight = lax.optimization_barrier(
            (gathered, pixels[:, HEAD:], cotangent, low_weight)
        )
        rest, cotangent = swap_images(rest), swap_images(cotangent)
    else:
        gathered = lax.all_gather(rest_low, ("group", "img"), axis=0, tiled=True)
    shards = gathered.size // ((own_rows + extra) * 128)
    gathered = gathered.reshape(shards, own_rows + extra, 128)
    total_blocks = owner_order.shape[0]
    slots = jnp.pad(
        owner_order.reshape(shards, own_blocks),
        ((0, 0), (0, slot_blocks - own_blocks)),
        constant_values=total_blocks,
    ).reshape(-1)
    unpacked = spread_packed(gathered, slots, total_blocks)
    block_mats, wave_mats = unpacked[:4], unpacked[4:10]
    block_vectors, wave_vectors = unpacked[10:]
    embedded = embed_waves(wavelength).reshape(groups * NB, E)
    shaped_low, own_shaped, kept, slope = wave_layer(embedded, wave_mats, wave_vectors)
    master = lax.all_gather(low_weight, "group", axis=0, tiled=True)
    kernel_low = make_kernels(shaped_low, master)
    mask = jnp.repeat(mask, PATCH, axis=1)
    if fits:
        kernel_all, masked, stream = share_kernels(kernel_low, mask, pixels, head, rest)
    else:
        kernel_all = lax.all_gather(kernel_low, "img", axis=0, tiled=True)
        stream = embed_patches(pixels, mask, kernel_all)
        masked = jnp.pad((pixels[0] * mask).astype(bf16), ((0, tall(pixels.shape[1]) - pixels.shape[1]), (0, 0)))
    block_out, grad_low, block_vectors, *block_grads = block_pass(
        stream, cotangent, block_vectors, *block_mats
    )
    pixel_grad, kernel_grad = unembed_patches(masked, mask, kernel_all, grad_low, pixels.shape[1])
    if fits:
        all_groups = fold_kernels(kernel_grad)
        all_groups, block_out, pixel_grad = lax.optimization_barrier((all_groups, block_out, pixel_grad))
        block_out, pixel_grad = swap_images(block_out), swap_images(pixel_grad)
    else:
        kernel_grad_low = lax.psum_scatter(kernel_grad, "img", scatter_dimension=0, tiled=True)
        all_groups = lax.all_gather(kernel_grad_low[None], "group", axis=0, tiled=True)
    fc_new, fc_first, fc_second, shaped_part = master_update(
        all_groups,
        own_shaped,
        fc_weight,
        fc_moment1,
        fc_moment2,
        kernel_rate,
    )
    *wave_grads, wave_vectors = wave_back(shaped_part, embedded, kept, slope, wave_mats, wave_vectors)
    given = [*block_grads, *wave_grads, block_vectors, wave_vectors]
    joint_term = collect_packed(given, slots, total_blocks, shards, own_rows + extra)
    if fits:
        rest_grad = reduce_packed(joint_term.reshape(2, 2, 4, 2, own_rows + extra, 128))
    else:
        rest_grad = lax.psum_scatter(
            joint_term, ("group", "img"), scatter_dimension=0, tiled=False
        ).astype(f32)
    rest_grad = rest_grad[:own_rows]
    rest_new, rest_first, rest_second = adamw_step(
        rest_weight, rest_moment1, rest_moment2, rest_grad, rest_rate
    )
    return (block_out, pixel_grad, rest_new, rest_first, rest_second, fc_new, fc_first, fc_second)


def solution(mesh):
    placed = (
        P(("group", "img"), None, None),
        P(("group", "img"), None),
        P(),
        P(),
        P(("group", "img"), None),
        P(("group", "img"), None),
        P(("group", "img"), None),
        P("group", "img"),
        P("group", "img"),
        P("group", "img"),
        P(("group", "img"), None),
    )
    return jax.shard_map(
        on_device,
        mesh=mesh,
        in_specs=placed,
        out_specs=(
            P(("group", "img"), None),
            P(("group", "img"), None, None),
            P(("group", "img"), None),
            P(("group", "img"), None),
            P(("group", "img"), None),
            P("group", "img"),
            P("group", "img"),
            P("group", "img"),
        ),
        check_vma=False,
    )
```

```python
import functools
import math

import jax
import jax.numpy as jnp
from jax import lax
from jax.experimental import pallas as pl
from jax.experimental.pallas import tpu as pltpu
from jax.sharding import PartitionSpec as P

MESH = pl.DeviceIdType.MESH

D = 768
HEADS = 12
HD = 64
HID = 3072
E = 128
HH = 4
HFF = 2048
PATCH = 256
NB = 32
STEP = 5


beta_one = 0.5
beta_two = 0.75
decay_rate = 0.05
epsilon_add = 1e-08
rest_rate = 0.02


def layout():
    return [
        ("w_qkv", (D, 3 * D)),
        ("w_out", (D, D)),
        ("w_up", (D, HID)),
        ("w_down", (HID, D)),
        ("h_query", (E, E)),
        ("h_key", (E, E)),
        ("h_value", (E, E)),
        ("h_out", (E, E)),
        ("h_ffin", (E, HFF)),
        ("h_ffout", (HFF, E)),
        ("ln1_gain", (D,)),
        ("ln1_shift", (D,)),
        ("ln2_gain", (D,)),
        ("ln2_shift", (D,)),
        ("patch_bias", (D,)),
        ("hn1_gain", (E,)),
        ("hn1_shift", (E,)),
        ("hn2_gain", (E,)),
        ("hn2_shift", (E,)),
    ]


def embed_waves(wavelength):
    half_width = E // 2
    frequency = jnp.exp(-math.log(10000.0) * jnp.arange(half_width, dtype=jnp.float32) / half_width)
    angles = wavelength.astype(jnp.float32)[..., None] * frequency
    return jnp.concatenate([jnp.sin(angles), jnp.cos(angles)], axis=-1)


def matrices():
    listed, at = [], 0
    for name, extent in layout():
        if len(extent) == 2:
            listed.append((name, extent[0], extent[1], at))
        at += math.prod(extent) // 128
    return listed


def vector_places():
    listed, at = [], 0
    rows = [0, 0]
    for name, extent in layout():
        if len(extent) == 1:
            kind = 0 if extent[0] == D else 1
            for j in range(extent[0] // 128):
                listed.append((at + j, kind, rows[kind], j * 128))
            rows[kind] += 1
        at += math.prod(extent) // 128
    return listed


def vector_shapes():
    return [jax.ShapeDtypeStruct((8, D), jnp.float32), jax.ShapeDtypeStruct((8, E), jnp.float32)]


def shards_a_step(shards, wanted):
    return wanted if shards % wanted == 0 else 1


def spread_kernel(order_ref, low_ref, *refs):
    big, small = matrices()[:4], matrices()[4:]
    far, outs, linear, kept, sem = refs[:4], refs[4:12], refs[12], refs[13:17], refs[17]
    step = pl.program_id(0)
    shards, rows = low_ref.shape[0], low_ref.shape[1]

    for shard in range(shards):

        def two(j, carry, shard=shard):
            pair = low_ref[shard, pl.ds(pl.multiple_of(j * 16, 16), 16), :].astype(jnp.float32)
            for half in range(2):
                block = order_ref[(step * shards + shard) * (rows // 8) + j * 2 + half]
                linear[pl.ds(pl.multiple_of(block * 8, 8), 8), :] = pair[half * 8 : half * 8 + 8]
            return carry

        lax.fori_loop(0, rows // 16, two, 0, unroll=8)

    @pl.when(step == pl.num_programs(0) - 1)
    def _():
        def relay(height, width, first, out):
            lanes = width // 128

            def some(j, carry):
                top = pl.multiple_of(j * 128, 128)
                for lane in range(lanes):
                    part = linear[pl.ds(first + top * lanes + lane, 128, stride=lanes), :]
                    out[pl.ds(top, 128), lane * 128 : lane * 128 + 128] = part.astype(out.dtype)
                return carry

            lax.fori_loop(0, height // 128, some, 0)

        copies = []
        for j, (name, height, width, first) in enumerate(big):
            relay(height, width, first, kept[j])
            copies.append(pltpu.make_async_copy(kept[j], far[j], sem.at[j]))
            copies[-1].start()
        for (name, height, width, first), out in zip(small, outs):
            relay(height, width, first, out)
        for out in outs[-2:]:
            out[...] = jnp.zeros_like(out)
        for row, kind, top, lane in vector_places():
            outs[kind - 2][top : top + 1, lane : lane + 128] = linear[row : row + 1, :]
        for copy in copies:
            copy.wait()


def spread_packed(gathered, slots, blocks):
    shards, rows = gathered.shape[0], gathered.shape[1]
    some = shards_a_step(shards, 4)
    big = [jax.ShapeDtypeStruct((height, width), jnp.bfloat16) for name, height, width, first in matrices()[:4]]
    small = [jax.ShapeDtypeStruct((height, width), jnp.float32) for name, height, width, first in matrices()[4:]]
    small += vector_shapes()
    return pl.pallas_call(
        spread_kernel,
        out_shape=big + small,
        grid_spec=pltpu.PrefetchScalarGridSpec(
            num_scalar_prefetch=1,
            grid=(shards // some,),
            in_specs=[pl.BlockSpec((some, rows, 128), lambda s, order: (s, 0, 0))],
            out_specs=[pl.BlockSpec(memory_space=pl.ANY) for shape in big]
            + [pl.BlockSpec(shape.shape, lambda s, order: (0, 0), pipeline_mode=pl.Buffered(1)) for shape in small],
            scratch_shapes=[pltpu.VMEM(((blocks + 1) * 8, 128), jnp.float32)]
            + [pltpu.VMEM(shape.shape, shape.dtype) for shape in big]
            + [pltpu.SemaphoreType.DMA((4,))],
        ),
        compiler_params=pltpu.CompilerParams(vmem_limit_bytes=60 << 20),
        name="spread_packed",
    )(slots, gathered)


def collect_kernel(order_ref, *refs):
    big, small = matrices()[:4], matrices()[4:]
    far, ins, low_ref, linear, kept, sem = refs[:4], refs[4:12], refs[12], refs[13], refs[14:18], refs[18]
    step = pl.program_id(0)
    shards, rows = low_ref.shape[0], low_ref.shape[1]

    @pl.when(step == 0)
    def _():
        copies = [pltpu.make_async_copy(far[j], kept[j], sem.at[j]) for j in range(4)]
        for copy in copies:
            copy.start()

        def relay(height, width, first, given):
            lanes = width // 128

            def some(j, carry):
                top = pl.multiple_of(j * 128, 128)
                for lane in range(lanes):
                    part = given[pl.ds(top, 128), lane * 128 : lane * 128 + 128]
                    linear[pl.ds(first + top * lanes + lane, 128, stride=lanes), :] = part.astype(jnp.float32)
                return carry

            lax.fori_loop(0, height // 128, some, 0)

        for (name, height, width, first), given in zip(small, ins):
            relay(height, width, first, given)
        first = vector_places()[0][0]
        linear[first:, :] = jnp.zeros((linear.shape[0] - first, 128), jnp.float32)
        for row, kind, top, lane in vector_places():
            linear[row : row + 1, :] = ins[kind - 2][top : top + 1, lane : lane + 128]
        for j, (name, height, width, first) in enumerate(big):
            copies[j].wait()
            relay(height, width, first, kept[j])

    for shard in range(shards):

        def two(j, carry, shard=shard):
            parts = []
            for half in range(2):
                block = order_ref[(step * shards + shard) * (rows // 8) + j * 2 + half]
                parts.append(linear[pl.ds(pl.multiple_of(block * 8, 8), 8), :])
            low_ref[shard, pl.ds(pl.multiple_of(j * 16, 16), 16), :] = jnp.concatenate(parts, axis=0).astype(low_ref.dtype)
            return carry

        lax.fori_loop(0, rows // 16, two, 0, unroll=20)


def collect_packed(grads, slots, blocks, shards, rows):
    some = shards_a_step(shards, 2)
    whole = [pl.BlockSpec(grad.shape, lambda s, order: (0, 0), pipeline_mode=pl.Buffered(1)) for grad in grads[4:]]
    return pl.pallas_call(
        collect_kernel,
        out_shape=jax.ShapeDtypeStruct((shards, rows, 128), jnp.bfloat16),
        grid_spec=pltpu.PrefetchScalarGridSpec(
            num_scalar_prefetch=1,
            grid=(shards // some,),
            in_specs=[pl.BlockSpec(memory_space=pl.ANY)] * 4 + whole,
            out_specs=pl.BlockSpec((some, rows, 128), lambda s, order: (s, 0, 0)),
            scratch_shapes=[pltpu.VMEM(((blocks + 1) * 8, 128), jnp.float32)]
            + [pltpu.VMEM(grad.shape, grad.dtype) for grad in grads[:4]]
            + [pltpu.SemaphoreType.DMA((4,))],
        ),
        compiler_params=pltpu.CompilerParams(vmem_limit_bytes=60 << 20),
        name="collect_packed",
    )(slots, *grads)


def exact(a, b, left, right):
    return lax.dot_general(
        a, b, (((left,), (right,)), ((), ())), precision=lax.Precision.HIGHEST, preferred_element_type=jnp.float32
    )


def unit_scale(values):
    center = values - jnp.mean(values, axis=-1, keepdims=True)
    scale = lax.rsqrt(jnp.mean(center * center, axis=-1, keepdims=True) + 1e-06)
    return center * scale, scale


def unit_back(grad, unit, scale, gain):
    inner = grad * gain
    return scale * (
        inner - jnp.mean(inner, axis=-1, keepdims=True) - unit * jnp.mean(inner * unit, axis=-1, keepdims=True)
    )


def wave_kernel(embed_ref, wq_ref, wk_ref, wv_ref, wo_ref, win_ref, wout_ref, vec_ref, shaped_ref, own_ref, kept_ref, slope_ref):
    rows = embed_ref.shape[0]
    groups = rows // NB
    embedded = embed_ref[...]
    queries = exact(embedded, wq_ref[...], 1, 0)
    keys = exact(embedded, wk_ref[...], 1, 0)
    values = exact(embedded, wv_ref[...], 1, 0)
    size = E // HH
    across = lax.broadcasted_iota(jnp.int32, (rows, rows), 0) // NB == lax.broadcasted_iota(jnp.int32, (rows, rows), 1) // NB
    mixed = []
    for head in range(HH):
        lanes = slice(head * size, head * size + size)
        scores = exact(queries[:, lanes], keys[:, lanes], 1, 1) * size**-0.5
        scores = jnp.where(across, scores, -1e30)
        weight = jnp.exp(scores - jnp.max(scores, axis=-1, keepdims=True))
        weight = weight / jnp.sum(weight, axis=-1, keepdims=True)
        kept_ref[head] = weight
        mixed.append(exact(weight, values[:, lanes], 1, 0))
    mixed = jnp.concatenate(mixed, axis=1)
    unit_one, scale_one = unit_scale(embedded + exact(mixed, wo_ref[...], 1, 0))
    first = unit_one * vec_ref[0:1, :] + vec_ref[1:2, :]
    inner = exact(first, win_ref[...], 1, 0)
    half = 0.5 * (1.0 + lax.erf(inner * 0.5**0.5))
    slope_ref[0] = inner * half
    slope_ref[1] = half + inner * jnp.exp(-0.5 * inner * inner) * (2.0 * math.pi) ** -0.5
    unit_two, scale_two = unit_scale(first + exact(inner * half, wout_ref[...], 1, 0))
    shaped = (unit_two * vec_ref[2:3, :] + vec_ref[3:4, :] + embedded).astype(jnp.bfloat16)
    for j, part in enumerate((queries, keys, values, mixed, unit_one, unit_two)):
        kept_ref[HH + j] = part
    kept_ref[HH + 6] = jnp.broadcast_to(scale_one, (rows, E))
    kept_ref[HH + 7] = jnp.broadcast_to(scale_two, (rows, E))
    shaped_ref[...] = shaped
    wide = shaped.astype(jnp.float32)
    width = E // groups
    group = lax.axis_index("group")
    own = jnp.zeros((rows, width), jnp.float32)
    for j in range(groups):
        own = jnp.where(group == j, wide[:, j * width : (j + 1) * width], own)
    own_ref[...] = own.astype(jnp.bfloat16)


def wave_layer(embedded, mats, vectors):
    rows = embedded.shape[0]
    groups = rows // NB
    f32, bf16 = jnp.float32, jnp.bfloat16
    return pl.pallas_call(
        wave_kernel,
        out_shape=[
            jax.ShapeDtypeStruct((rows, E), bf16),
            jax.ShapeDtypeStruct((rows, E // groups), bf16),
            jax.ShapeDtypeStruct((HH + 8, rows, E), f32),
            jax.ShapeDtypeStruct((2, rows, HFF), f32),
        ],
        compiler_params=pltpu.CompilerParams(vmem_limit_bytes=60 << 20),
        name="wave_layer",
    )(embedded, *mats, vectors)


def wave_back_kernel(part_ref, embed_ref, kept_ref, slope_ref, wq_ref, wk_ref, wv_ref, wo_ref, win_ref, wout_ref, vec_ref,
                     gq_ref, gk_ref, gv_ref, go_ref, gin_ref, gout_ref, gvec_ref):
    rows = embed_ref.shape[0]
    groups = rows // NB
    width = E // groups
    size = E // HH
    group = lax.axis_index("group")
    spread = jnp.concatenate([part_ref[...]] * groups, axis=1)
    lane = lax.broadcasted_iota(jnp.int32, (rows, E), 1) // width
    grad = jnp.where(lane == group, spread, 0.0)
    embedded = embed_ref[...]
    queries, keys, values, mixed, unit_one, unit_two, scale_one, scale_two = (kept_ref[HH + j] for j in range(8))
    gvec_ref[...] = jnp.zeros_like(gvec_ref)
    gvec_ref[2:3, :] = jnp.sum(grad * unit_two, axis=0, keepdims=True)
    gvec_ref[3:4, :] = jnp.sum(grad, axis=0, keepdims=True)
    grad = unit_back(grad, unit_two, scale_two, vec_ref[2:3, :])
    gout_ref[...] = exact(slope_ref[0], grad, 0, 0)
    inner = exact(grad, wout_ref[...], 1, 1) * slope_ref[1]
    first = unit_one * vec_ref[0:1, :] + vec_ref[1:2, :]
    gin_ref[...] = exact(first, inner, 0, 0)
    grad = grad + exact(inner, win_ref[...], 1, 1)
    gvec_ref[0:1, :] = jnp.sum(grad * unit_one, axis=0, keepdims=True)
    gvec_ref[1:2, :] = jnp.sum(grad, axis=0, keepdims=True)
    grad = unit_back(grad, unit_one, scale_one, vec_ref[0:1, :])
    go_ref[...] = exact(mixed, grad, 0, 0)
    grad = exact(grad, wo_ref[...], 1, 1)
    parts = [[], [], []]
    for head in range(HH):
        lanes = slice(head * size, head * size + size)
        weight = kept_ref[head]
        grad_weight = exact(grad[:, lanes], values[:, lanes], 1, 1)
        parts[2].append(exact(weight, grad[:, lanes], 0, 0))
        score = weight * (grad_weight - jnp.sum(weight * grad_weight, axis=-1, keepdims=True)) * size**-0.5
        parts[0].append(exact(score, keys[:, lanes], 1, 0))
        parts[1].append(exact(score, queries[:, lanes], 0, 0))
    for out, part in zip((gq_ref, gk_ref, gv_ref), parts):
        out[...] = exact(embedded, jnp.concatenate(part, axis=1), 0, 0)


def wave_back(part, embedded, kept, slope, mats, vectors):
    f32 = jnp.float32
    return pl.pallas_call(
        wave_back_kernel,
        out_shape=[jax.ShapeDtypeStruct(mat.shape, f32) for mat in mats] + [jax.ShapeDtypeStruct((8, E), f32)],
        compiler_params=pltpu.CompilerParams(vmem_limit_bytes=60 << 20),
        name="wave_back",
    )(part, embedded, kept, slope, *mats, vectors)


def tall(count):
    return -(-count // 16) * 16


def dot_nn(a, b):
    return lax.dot_general(a, b, (((1,), (0,)), ((), ())), preferred_element_type=jnp.float32)


def dot_nt(a, b):
    return lax.dot_general(a, b, (((1,), (1,)), ((), ())), preferred_element_type=jnp.float32)


def dot_tn(a, b):
    return lax.dot_general(a, b, (((0,), (0,)), ((), ())), preferred_element_type=jnp.float32)


def block_kernel(stream_ref, up_ref, vec_ref, wqkv_hbm, wout_hbm, wup_hbm, wdown_hbm,
                 out_ref, low_ref, gvec_ref, gqkv_hbm, gout_hbm, gup_hbm, gdown_hbm,
                 wqkv, wout, wup, wdown, gqkv, gout, gup, gdown,
                 xs, ups, up_low, norm_one, qkv, att, probs, mid, norm_two, acc, hid_low, datt, dqkv, in_sem, out_sem):
    f32, bf16 = jnp.float32, jnp.bfloat16
    seq = stream_ref.shape[0]
    rows = xs.shape[0]
    loads = [
        pltpu.make_async_copy(src, dst, in_sem.at[j])
        for j, (src, dst) in enumerate(((wqkv_hbm, wqkv), (wout_hbm, wout), (wup_hbm, wup), (wdown_hbm, wdown)))
    ]
    for load in loads:
        load.start()
    stores = [
        pltpu.make_async_copy(src, dst, out_sem.at[j])
        for j, (src, dst) in enumerate(((gqkv, gqkv_hbm), (gout, gout_hbm), (gup, gup_hbm), (gdown, gdown_hbm)))
    ]
    gain_one, shift_one = vec_ref[0:1, :], vec_ref[1:2, :]
    gain_two, shift_two = vec_ref[2:3, :], vec_ref[3:4, :]
    xs[...] = jnp.zeros_like(xs)
    xs[0:seq, :] = stream_ref[...] + vec_ref[4:5, :]
    ups[...] = jnp.zeros_like(ups)
    ups[0:seq, :] = up_ref[...].astype(f32)
    up_low[...] = ups[...].astype(bf16)

    def normed(values):
        center = values - jnp.mean(values, axis=-1, keepdims=True)
        scale = lax.rsqrt(jnp.mean(center * center, axis=-1, keepdims=True) + 1e-06)
        return center * scale, scale

    def normed_back(grad, unit, scale, gain):
        inner = grad * gain
        return scale * (
            inner
            - jnp.mean(inner, axis=-1, keepdims=True)
            - unit * jnp.mean(inner * unit, axis=-1, keepdims=True)
        )

    unit, scale = normed(xs[...])
    norm_one[...] = (unit * gain_one + shift_one).astype(bf16)
    loads[0].wait()

    def tile(j, size=D):
        return pl.ds(pl.multiple_of(j * size, size), size)

    def each(count, body):
        lax.fori_loop(0, count, lambda j, carry: (body(j), carry)[1], 0)

    def qkv_part(j):
        qkv[:, tile(j)] = dot_nn(norm_one[...], wqkv[:, tile(j)]).astype(bf16)

    each(3, qkv_part)
    inside = lax.broadcasted_iota(jnp.int32, (rows, rows), 1) < seq

    def heads(p):
        pair = [qkv[:, pl.ds(pl.multiple_of(j * D + p * 128, 128), 128)] for j in range(3)]
        outs = []
        for h in range(2):
            query, key, value = (part[:, h * HD : h * HD + HD] for part in pair)
            scores = jnp.where(inside, dot_nt(query, key) * (HD**-0.5), -1e30)
            weight = jnp.exp(scores - jnp.max(scores, axis=-1, keepdims=True))
            weight = weight / jnp.sum(weight, axis=-1, keepdims=True)
            probs[p * 2 + h] = weight
            outs.append(dot_nn(weight.astype(bf16), value))
        att[:, pl.ds(pl.multiple_of(p * 128, 128), 128)] = jnp.concatenate(outs, axis=1).astype(bf16)

    each(HEADS // 2, heads)
    loads[1].wait()
    mid[...] = xs[...] + dot_nn(att[...], wout[...])
    unit, scale = normed(mid[...])
    norm_two[...] = (unit * gain_two + shift_two).astype(bf16)
    loads[2].wait()
    loads[3].wait()
    acc[...] = jnp.zeros_like(acc)

    def hidden_part(j):
        hidden = dot_nn(norm_two[...], wup[:, tile(j)])
        half = 0.5 * (1.0 + lax.erf(hidden * (0.5**0.5)))
        active = (hidden * half).astype(bf16)
        slope = half + hidden * jnp.exp(-0.5 * hidden * hidden) * (2.0 * math.pi) ** -0.5
        mid[...] += dot_nn(active, wdown[tile(j), :])
        gdown[tile(j), :] = dot_tn(active, up_low[...]).astype(bf16)
        grad_hidden = (dot_nt(up_low[...], wdown[tile(j), :]) * slope).astype(bf16)
        gup[:, tile(j)] = dot_tn(norm_two[...], grad_hidden).astype(bf16)
        acc[...] += dot_nt(grad_hidden, wup[:, tile(j)])

    kept_unit, kept_scale = unit, scale
    hid_low[...] = kept_unit
    each(HID // D, hidden_part)
    stores[2].start()
    stores[3].start()
    out_ref[...] = mid[0:seq, :].astype(bf16)
    grad = acc[...]
    unit = hid_low[...]
    gvec_ref[...] = jnp.zeros_like(gvec_ref)
    gvec_ref[2:3, :] = jnp.sum(grad * unit, axis=0, keepdims=True)
    gvec_ref[3:4, :] = jnp.sum(grad, axis=0, keepdims=True)
    ups[...] += normed_back(grad, unit, kept_scale, gain_two)
    up_low[...] = ups[...].astype(bf16)
    gout[...] = dot_tn(att[...], up_low[...]).astype(bf16)
    stores[1].start()
    datt[...] = dot_nt(up_low[...], wout[...]).astype(bf16)

    def heads_back(p):
        pair = [qkv[:, pl.ds(pl.multiple_of(j * D + p * 128, 128), 128)] for j in range(3)]
        grad_pair = datt[:, pl.ds(pl.multiple_of(p * 128, 128), 128)]
        grads = [[], [], []]
        for h in range(2):
            query, key, value = (part[:, h * HD : h * HD + HD] for part in pair)
            grad_out = grad_pair[:, h * HD : h * HD + HD]
            weight = probs[p * 2 + h]
            grad_weight = dot_nt(grad_out, value)
            grads[2].append(dot_tn(weight.astype(bf16), grad_out))
            grad_score = weight * (grad_weight - jnp.sum(weight * grad_weight, axis=-1, keepdims=True))
            grad_score = grad_score.astype(bf16)
            grads[0].append(dot_nn(grad_score, key) * (HD**-0.5))
            grads[1].append(dot_tn(grad_score, query) * (HD**-0.5))
        for j in range(3):
            dqkv[:, pl.ds(pl.multiple_of(j * D + p * 128, 128), 128)] = jnp.concatenate(grads[j], axis=1).astype(bf16)

    each(HEADS // 2, heads_back)
    acc[...] = jnp.zeros_like(acc)

    def qkv_back(j):
        gqkv[:, tile(j)] = dot_tn(norm_one[...], dqkv[:, tile(j)]).astype(bf16)
        acc[...] += dot_nt(dqkv[:, tile(j)], wqkv[:, tile(j)])

    each(3, qkv_back)
    stores[0].start()
    unit, scale = normed(xs[...])
    grad = acc[...]
    gvec_ref[0:1, :] = jnp.sum(grad * unit, axis=0, keepdims=True)
    gvec_ref[1:2, :] = jnp.sum(grad, axis=0, keepdims=True)
    total = ups[...] + normed_back(grad, unit, scale, gain_one)
    gvec_ref[4:5, :] = jnp.sum(total, axis=0, keepdims=True)
    low_ref[...] = total.astype(bf16)
    for store in stores:
        store.wait()


def block_pass(stream, upstream, vectors, wqkv, wout, wup, wdown):
    f32, bf16 = jnp.float32, jnp.bfloat16
    seq = stream.shape[0]
    rows = tall(seq)
    whole = pl.BlockSpec(memory_space=pltpu.VMEM)
    far = pl.BlockSpec(memory_space=pl.ANY)
    mats = [wqkv, wout, wup, wdown]
    kept = [pltpu.VMEM(mat.shape, bf16) for mat in mats]
    dma = pltpu.SemaphoreType.DMA
    return pl.pallas_call(
        block_kernel,
        out_shape=[
            jax.ShapeDtypeStruct((seq, D), bf16),
            jax.ShapeDtypeStruct((rows, D), bf16),
            jax.ShapeDtypeStruct((8, D), f32),
        ]
        + [jax.ShapeDtypeStruct(mat.shape, bf16) for mat in mats],
        in_specs=[whole] * 3 + [far] * 4,
        out_specs=[whole] * 3 + [far] * 4,
        scratch_shapes=kept
        + kept
        + [
            pltpu.VMEM((rows, D), f32),
            pltpu.VMEM((rows, D), f32),
            pltpu.VMEM((rows, D), bf16),
            pltpu.VMEM((rows, D), bf16),
            pltpu.VMEM((rows, 3 * D), bf16),
            pltpu.VMEM((rows, D), bf16),
            pltpu.VMEM((HEADS, rows, rows), f32),
            pltpu.VMEM((rows, D), f32),
            pltpu.VMEM((rows, D), bf16),
            pltpu.VMEM((rows, D), f32),
            pltpu.VMEM((rows, D), f32),
            pltpu.VMEM((rows, D), bf16),
            pltpu.VMEM((rows, 3 * D), bf16),
            dma((4,)),
            dma((4,)),
        ],
        compiler_params=pltpu.CompilerParams(vmem_limit_bytes=60 << 20),
        cost_estimate=pl.CostEstimate(flops=8_400_000_000, bytes_accessed=30_000_000, transcendentals=2_000_000),
        name="block_pass",
    )(stream, upstream, vectors, *mats)


def adamw_step(weight, moment_one, moment_two, grad, rate):
    first = beta_one * moment_one + (1.0 - beta_one) * grad
    second = beta_two * moment_two + (1.0 - beta_two) * grad * grad
    fix_one = 1.0 - beta_one**STEP
    fix_two = 1.0 - beta_two**STEP
    update = first / fix_one / (jnp.sqrt(second / fix_two) + epsilon_add) + decay_rate * weight
    return (weight - rate * update, first, second)


NC = 15
HEAD = 96


def dims_step(count):
    return 16 if count % 16 == 0 else count


def make_kernel(paired, shaped_ref, *refs):
    slabs, kernel_ref, master, turned = refs[:-3], refs[-3], refs[-2], refs[-1]
    dims = kernel_ref.shape[0]
    group = lax.axis_index("group")
    shaped = shaped_ref[pl.ds(pl.multiple_of(group * NB, NB), NB), :]
    for j, slab in enumerate(slabs):
        owner = (group + 2 * (j // 2)) % 4 + (j % 2) * (1 - 2 * (group % 2)) if paired else j
        master[pl.ds(pl.multiple_of(owner * slab.shape[0], slab.shape[0]), slab.shape[0]), :] = slab[...]
    for dim in range(dims):
        part = dot_nn(shaped, master[:, dim * PATCH : (dim + 1) * PATCH])
        turned[pl.ds(dim, NB, stride=dims), :] = part[:, :128]
        turned[pl.ds(NB * dims + dim, NB, stride=dims), :] = part[:, 128:]
    for band in range(NB):
        for half in range(2):
            row = half * NB * dims + band * dims
            lane = band * PATCH + half * 128
            kernel_ref[:, lane : lane + 128] = turned[row : row + dims, :].astype(kernel_ref.dtype)


def make_kernels(shaped, slabs, paired):
    dims = slabs[0].shape[1] // PATCH
    step = dims_step(dims)
    return pl.pallas_call(
        functools.partial(make_kernel, paired),
        out_shape=jax.ShapeDtypeStruct((dims, NB * PATCH), jnp.bfloat16),
        grid=(dims // step,),
        in_specs=[pl.BlockSpec(shaped.shape, lambda j: (0, 0))]
        + [pl.BlockSpec((slab.shape[0], step * PATCH), lambda j: (0, j)) for slab in slabs],
        out_specs=pl.BlockSpec((step, NB * PATCH), lambda j: (j, 0)),
        scratch_shapes=[
            pltpu.VMEM((E, step * PATCH), jnp.bfloat16),
            pltpu.VMEM((2 * NB * step, 128), jnp.float32),
        ],
        compiler_params=pltpu.CompilerParams(vmem_limit_bytes=60 << 20),
        name="make_kernels",
    )(shaped, *slabs)


def embed_kernel(pixel_ref, mask_ref, kernel_ref, stream_ref):
    masked = pixel_ref[...] * mask_ref[...].astype(jnp.bfloat16)
    part = dot_nt(masked, kernel_ref[...])

    @pl.when(pl.program_id(0) == 0)
    def _():
        stream_ref[...] = part

    @pl.when(pl.program_id(0) > 0)
    def _():
        stream_ref[...] += part


def embed_patches(pixels, mask, kernels):
    seq, width = pixels.shape[1], pixels.shape[2]
    cut = 1024
    return pl.pallas_call(
        embed_kernel,
        out_shape=jax.ShapeDtypeStruct((seq, D), jnp.float32),
        grid=(width // cut,),
        in_specs=[
            pl.BlockSpec((None, seq, cut), lambda j: (0, 0, j)),
            pl.BlockSpec((1, cut), lambda j: (0, j)),
            pl.BlockSpec((D, cut), lambda j: (0, j)),
        ],
        out_specs=pl.BlockSpec((seq, D), lambda j: (0, 0)),
        compiler_params=pltpu.CompilerParams(vmem_limit_bytes=60 << 20),
        name="embed_patches",
    )(pixels, mask, kernels)


def unembed_kernel(masked_ref, mask_ref, kernel_ref, low_ref, back_ref, grad_ref):
    seq = back_ref.shape[0]
    back_ref[...] = (dot_nn(low_ref[...], kernel_ref[...])[0:seq] * mask_ref[...]).astype(back_ref.dtype)
    grad_ref[...] = dot_tn(low_ref[...], masked_ref[...]).astype(grad_ref.dtype)


def unembed_patches(masked, mask, kernels, low, seq):
    rows, width = masked.shape
    cut = 1024
    return pl.pallas_call(
        unembed_kernel,
        out_shape=[
            jax.ShapeDtypeStruct((1, seq, width), jnp.bfloat16),
            jax.ShapeDtypeStruct((D, width), jnp.bfloat16),
        ],
        grid=(width // cut,),
        in_specs=[
            pl.BlockSpec((rows, cut), lambda j: (0, j)),
            pl.BlockSpec((1, cut), lambda j: (0, j)),
            pl.BlockSpec((D, cut), lambda j: (0, j)),
            pl.BlockSpec(low.shape, lambda j: (0, 0)),
        ],
        out_specs=[
            pl.BlockSpec((None, seq, cut), lambda j: (0, 0, j)),
            pl.BlockSpec((D, cut), lambda j: (0, j)),
        ],
        compiler_params=pltpu.CompilerParams(vmem_limit_bytes=60 << 20),
        name="unembed_patches",
    )(masked, mask, kernels, low)


def master_kernel(rate, grad_ref, shaped_ref, weight_ref, one_ref, two_ref, new_ref, first_ref, second_ref, back_ref, turned):
    groups, dims = grad_ref.shape[0], grad_ref.shape[1]
    bands = groups * NB
    for group in range(groups):
        for band in range(NB):
            for half in range(2):
                row = half * bands * dims + (group * NB + band) * dims
                lane = band * PATCH + half * 128
                turned[row : row + dims, :] = grad_ref[group, :, lane : lane + 128].astype(jnp.float32)
    total = jnp.zeros(back_ref.shape, jnp.float32)
    for dim in range(dims):
        part = jnp.concatenate(
            [turned[pl.ds(half * bands * dims + dim, bands, stride=dims), :] for half in range(2)], axis=1
        ).astype(jnp.bfloat16)
        lanes = slice(dim * PATCH, (dim + 1) * PATCH)
        weight = weight_ref[:, lanes]
        total += dot_nt(part, weight.astype(jnp.bfloat16))
        grad = dot_tn(shaped_ref[...], part)
        new_ref[:, lanes], first_ref[:, lanes], second_ref[:, lanes] = adamw_step(
            weight, one_ref[:, lanes], two_ref[:, lanes], grad, rate
        )

    @pl.when(pl.program_id(0) == 0)
    def _():
        back_ref[...] = total

    @pl.when(pl.program_id(0) > 0)
    def _():
        back_ref[...] += total


def master_update(grads, shaped, weight, one, two, rate):
    groups, dims = grads.shape[0], grads.shape[1]
    step = dims_step(dims)
    columns = pl.BlockSpec((weight.shape[0], step * PATCH), lambda j: (0, j))
    like = jax.ShapeDtypeStruct(weight.shape, jnp.float32)
    return pl.pallas_call(
        functools.partial(master_kernel, rate),
        out_shape=[like, like, like, jax.ShapeDtypeStruct(shaped.shape, jnp.float32)],
        grid=(dims // step,),
        in_specs=[
            pl.BlockSpec((groups, step, NB * PATCH), lambda j: (0, j, 0)),
            pl.BlockSpec(shaped.shape, lambda j: (0, 0)),
            columns,
            columns,
            columns,
        ],
        out_specs=[columns, columns, columns, pl.BlockSpec(shaped.shape, lambda j: (0, 0))],
        scratch_shapes=[pltpu.VMEM((2 * groups * NB * step, 128), jnp.float32)],
        compiler_params=pltpu.CompilerParams(vmem_limit_bytes=60 << 20),
        name="master_update",
    )(grads, shaped, weight, one, two)


def spot():
    group = lax.axis_index("group")
    image = lax.axis_index("img")
    return group // 2, group % 2, image // 2, image % 2


def place(y, c, z, x):
    return (y * 2 + c, z * 2 + x)


def partners():
    y, c, z, x = spot()
    x2, y2 = x + (1 - c) * (1 - 2 * x), y + c * (1 - 2 * y)
    x3, y3 = x + c * (1 - 2 * x), y + (1 - c) * (1 - 2 * y)
    around = [place(y, c, (z + d) % 4, x) for d in (1, 2, 3)]
    return (x2, y2), (x3, y3), around, place(y2, c, z, x2), place(y3, c, z, x3), place(y, 1 - c, z, x)


def greet(peers):
    barrier = pltpu.get_barrier_semaphore()
    for peer in peers:
        pl.semaphore_signal(barrier, inc=1, device_id=peer, device_id_type=MESH)
    pl.semaphore_wait(barrier, len(peers))


def remote(src, dst, send_sem, recv_sem, target):
    return pltpu.make_async_remote_copy(
        src_ref=src, dst_ref=dst, send_sem=send_sem, recv_sem=recv_sem, device_id=target, device_id_type=MESH
    )


def gather_kernel(own_ref, pixel_ref, all_ref, head_ref, head_sem, local_sem, line_send, line_recv, group_send, group_recv, twin_send, twin_recv):
    y, c, z, x = spot()
    (x2, y2), (x3, y3), around, second, third, twin = partners()
    partner = place(y, 1 - c, (z + 2) % 4, x)
    moved = (c + z // 2) % 2 == 1
    rows = own_ref.shape[0] // NC

    def cut(k):
        return pl.ds(k * rows, rows)

    head = remote(pixel_ref.at[0, pl.ds(0, HEAD)], head_ref.at[0], head_sem.at[0], head_sem.at[1], partner)

    def along(d, k):
        return remote(own_ref.at[cut(k)], all_ref.at[y, c, z, x, cut(k)], line_send.at[d - 1, k], line_recv.at[d - 1, k], around[d - 1])

    def along_in(d, k):
        return remote(own_ref.at[cut(k)], all_ref.at[y, c, (z + 4 - d) % 4, x, cut(k)], line_send.at[d - 1, k], line_recv.at[d - 1, k], around[d - 1])

    def square(core, j):
        yy, xx = ((y, x), (y2, x2), (y3, x3), (1 - y, 1 - x))[j]
        return all_ref.at[yy, core, :, xx]

    def hop(j, to, k, slot, landing):
        part = square(c, j).at[:, cut(k)]
        return remote(part, part, group_send.at[slot, k], group_recv.at[landing, k], to)

    def hop_in(landing, k):
        part = square(c, landing).at[:, cut(k)]
        return remote(part, part, group_send.at[0, k], group_recv.at[landing, k], twin)

    def share(j, k):
        part = square(c, j).at[:, cut(k)]
        yy, xx = ((y, x), (y2, x2), (y3, x3), (1 - y, 1 - x))[j]
        landing = (0, 2, 1, 3)[j]
        return remote(part, part, twin_send.at[j, k], twin_recv.at[landing, k], twin)

    def share_in(landing, k):
        yy, xx = ((y, x), (y2, x2), (y3, x3), (1 - y, 1 - x))[landing]
        part = all_ref.at[yy, 1 - c, :, xx, cut(k)]
        return remote(part, part, twin_send.at[0, k], twin_recv.at[landing, k], twin)

    keep = pltpu.make_async_copy(own_ref, all_ref.at[y, c, z, x], local_sem)
    keep.start()
    greet(around + [second, third, twin, partner])
    for k in range(NC):
        for d in (1, 2, 3):
            along(d, k).start()
    keep.wait()
    for step in range(NC + 2):
        k = step
        if k < NC:
            for d in (1, 2, 3):
                along_in(d, k).wait_recv()
            hop(0, third, k, 0, 2).start()
            hop(0, second, k, 1, 1).start()
            share(0, k).start()
        if step == NC - 3:

            @pl.when(moved)
            def _():
                head.start()

        k = step - 1
        if 0 <= k < NC:
            hop_in(1, k).wait_recv()
            hop(1, third, k, 2, 3).start()
            share(1, k).start()
        k = step - 2
        if 0 <= k < NC:
            hop_in(2, k).wait_recv()
            share(2, k).start()
            hop_in(3, k).wait_recv()
            share(3, k).start()
    for k in range(NC):
        for d in (1, 2, 3):
            along(d, k).wait_send()
        hop(0, third, k, 0, 2).wait_send()
        hop(0, second, k, 1, 1).wait_send()
        hop(1, third, k, 2, 3).wait_send()
        for j in range(4):
            share(j, k).wait_send()
            share_in(j, k).wait_recv()

    @pl.when(moved)
    def _():
        head.wait()


def gather_packed(own, pixels):
    rows = own.shape[0]
    dma = pltpu.SemaphoreType.DMA
    return pl.pallas_call(
        gather_kernel,
        out_shape=[
            jax.ShapeDtypeStruct((2, 2, 4, 2, rows, 128), own.dtype),
            jax.ShapeDtypeStruct((1, HEAD, pixels.shape[2]), pixels.dtype),
        ],
        in_specs=[pl.BlockSpec(memory_space=pltpu.VMEM), pl.BlockSpec(memory_space=pl.ANY)],
        out_specs=[pl.BlockSpec(memory_space=pl.ANY)] * 2,
        scratch_shapes=[dma((2,)), dma, dma((3, NC)), dma((3, NC)), dma((3, NC)), dma((4, NC)), dma((4, NC)), dma((4, NC))],
        compiler_params=pltpu.CompilerParams(collective_id=0, has_side_effects=True, vmem_limit_bytes=60 << 20),
        name="gather_packed",
    )(own, pixels)


def reduce_kernel(part_ref, sum_ref, own, twin_in, third_in, second_in, line_in, load_sem, twin_send, twin_recv, third_send, third_recv, second_send, second_recv, line_send, line_recv):
    f32, bf16 = jnp.float32, jnp.bfloat16
    y, c, z, x = spot()
    (x2, y2), (x3, y3), around, second, third, twin = partners()
    rows = sum_ref.shape[0] // NC

    def cut(k):
        return pl.ds(k * rows, rows)

    spots = ((1 - y, 1 - x), (y3, x3), (y2, x2), (y, x))
    turned = ((1 - y, 1 - x), (y2, x2), (y3, x3), (y, x))

    def load(j, k):
        yy, xx = spots[j]
        return pltpu.make_async_copy(part_ref.at[yy, c, :, xx, cut(k)], own.at[j, :, cut(k)], load_sem.at[j, k])

    def swap(j, k):
        yy, xx = turned[j]
        return remote(part_ref.at[yy, 1 - c, :, xx, cut(k)], twin_in.at[j, :, cut(k)], twin_send.at[j, k], twin_recv.at[j, k], twin)

    def to_third(j, k):
        return remote(own.at[j, :, cut(k)], third_in.at[j, :, cut(k)], third_send.at[j, k], third_recv.at[j, k], third)

    def to_second(k):
        return remote(own.at[2, :, cut(k)], second_in.at[:, cut(k)], second_send.at[k], second_recv.at[k], second)

    def to_line(d, k):
        return remote(own.at[3, (z + d) % 4, cut(k)], line_in.at[d - 1, cut(k)], line_send.at[d - 1, k], line_recv.at[d - 1, k], around[d - 1])

    for k in range(NC):
        for j in range(4):
            load(j, k).start()
    greet(around + [second, third, twin])
    for k in range(NC):
        for j in range(4):
            swap(j, k).start()

    def pair(j, k):
        load(j, k).wait()
        swap(j, k).wait_recv()
        return own[j, :, cut(k)].astype(f32) + twin_in[j, :, cut(k)].astype(f32)

    for step in range(NC + 3):
        k = step
        if k < NC:
            for j in (0, 1):
                own[j, :, cut(k)] = pair(j, k).astype(bf16)
                to_third(j, k).start()
        k = step - 1
        if 0 <= k < NC:
            held = pair(2, k)
            to_third(0, k).wait_recv()
            own[2, :, cut(k)] = (held + third_in[0, :, cut(k)].astype(f32)).astype(bf16)
            to_second(k).start()
        k = step - 2
        if 0 <= k < NC:
            held = pair(3, k)
            to_third(1, k).wait_recv()
            to_second(k).wait_recv()
            held += third_in[1, :, cut(k)].astype(f32) + second_in[:, cut(k)].astype(f32)
            own[3, :, cut(k)] = held.astype(bf16)
            for d in (1, 2, 3):
                to_line(d, k).start()
        k = step - 3
        if 0 <= k < NC:
            total = own[3, z, cut(k)].astype(f32)
            for d in (1, 2, 3):
                to_line(d, k).wait_recv()
                total += line_in[d - 1, cut(k)].astype(f32)
            sum_ref[cut(k)] = total
    for k in range(NC):
        for j in range(4):
            swap(j, k).wait_send()
        for j in (0, 1):
            to_third(j, k).wait_send()
        to_second(k).wait_send()
        for d in (1, 2, 3):
            to_line(d, k).wait_send()


def reduce_packed(part):
    rows = part.shape[-2]
    bf16 = jnp.bfloat16
    dma = pltpu.SemaphoreType.DMA
    return pl.pallas_call(
        reduce_kernel,
        out_shape=jax.ShapeDtypeStruct((rows, 128), jnp.float32),
        in_specs=[pl.BlockSpec(memory_space=pl.ANY)],
        out_specs=pl.BlockSpec(memory_space=pltpu.VMEM),
        scratch_shapes=[
            pltpu.VMEM((4, 4, rows, 128), bf16),
            pltpu.VMEM((4, 4, rows, 128), bf16),
            pltpu.VMEM((2, 4, rows, 128), bf16),
            pltpu.VMEM((4, rows, 128), bf16),
            pltpu.VMEM((3, rows, 128), bf16),
            dma((4, NC)), dma((4, NC)), dma((4, NC)), dma((2, NC)), dma((2, NC)), dma((NC,)), dma((NC,)), dma((3, NC)), dma((3, NC)),
        ],
        compiler_params=pltpu.CompilerParams(collective_id=1, has_side_effects=True, vmem_limit_bytes=56 << 20),
        name="reduce_packed",
    )(part)


CHUNK = 16


def over_x(k):
    return k % 2 == 0


def quad_peers():
    y, c, z, x = spot()
    low = z % 2
    side = place(y, c, z, 1 - x)
    along = place(y, c, z + 1 - 2 * low, x)
    twin = place(y, 1 - c, z, x)
    partner = place(y, 1 - c, (z + 2) % 4, x)
    moved = (c + z // 2) % 2 == 1
    return y, c, z, x, low, side, along, twin, partner, moved


def swap_group(value, flip):
    return lax.ppermute(value, "group", [(j, j ^ flip) for j in range(4)])


def swap_images(value):
    pairs = []
    for y in range(2):
        for c in range(2):
            for z in range(4):
                for x in range(2):
                    other = (1 - c, (z + 2) % 4) if c != z // 2 else (c, z)
                    pairs.append((((y * 2 + c) * 4 + z) * 2 + x, ((y * 2 + other[0]) * 4 + other[1]) * 2 + x))
    return lax.ppermute(value, ("group", "img"), pairs)


def share_kernel(made_ref, mask_ref, pixel_ref, head_ref, rest_ref, all_ref, masked_ref, stream_ref,
                 held, top, bottom, tile, mixed, order, pixel_sem, store_sem, keep_sem, swap_send, swap_recv,
                 side_send, side_recv, along_send, along_recv, far_send, far_recv, twin_send, twin_recv):
    f32, bf16 = jnp.float32, jnp.bfloat16
    y, c, z, x, low, side, along, twin, partner, moved = quad_peers()
    dims, width = made_ref.shape
    count = dims // CHUNK
    group = 8 * CHUNK

    def cut(k):
        return pl.ds(k * CHUNK, CHUNK)

    def block(core, j, k):
        return held.at[2 * core + (low + j // 2) % 2, (x + j % 2) % 2, cut(k)]

    def keep(k):
        return pltpu.make_async_copy(made_ref.at[cut(k)], block(c, 0, k), keep_sem.at[k])

    def swap(k):
        return remote(made_ref.at[cut(k)], block(1 - c, 0, k), swap_send.at[k], swap_recv.at[k], partner)

    def swap_in(k):
        return remote(made_ref.at[cut(k)], block(c, 0, k), swap_send.at[k], swap_recv.at[k], partner)

    def to_side(k):
        return remote(block(c, 0, k), block(c, 0, k), side_send.at[k], side_recv.at[k], side)

    def from_side(k):
        return remote(block(c, 1, k), block(c, 1, k), side_send.at[k], side_recv.at[k], side)

    def to_along(k):
        return remote(block(c, 0, k), block(c, 0, k), along_send.at[k], along_recv.at[k], along)

    def from_along(k):
        return remote(block(c, 2, k), block(c, 2, k), along_send.at[k], along_recv.at[k], along)

    def pass_on(k):
        j, to = (2, side) if over_x(k) else (1, along)
        return remote(block(c, j, k), block(c, j, k), far_send.at[k], far_recv.at[k], to)

    def from_far(k):
        return remote(block(c, 3, k), block(c, 3, k), far_send.at[k], far_recv.at[k], twin)

    def give(j, k):
        return remote(block(c, j, k), block(c, j, k), twin_send.at[j, k], twin_recv.at[j, k], twin)

    def given(j, k):
        return remote(block(1 - c, j, k), block(1 - c, j, k), twin_send.at[j, k], twin_recv.at[j, k], twin)

    def store(k):
        return pltpu.make_async_copy(held.at[:, :, cut(k)], all_ref.at[:, :, cut(k)], store_sem.at[k])

    swapped = pltpu.make_async_copy(head_ref.at[0], top, pixel_sem.at[0])
    owned = pltpu.make_async_copy(pixel_ref.at[0, pl.ds(0, HEAD)], top, pixel_sem.at[0])
    lower = pltpu.make_async_copy(rest_ref.at[0], bottom, pixel_sem.at[1])

    @pl.when(jnp.logical_not(moved))
    def _():
        owned.start()
        for k in range(count):
            keep(k).start()

    lower.start()
    greet([side, along, twin, partner])

    @pl.when(moved)
    def _():
        swapped.start()
        for k in range(count):
            swap(k).start()

    def mask_pixels(part):
        @pl.when(part == 0)
        def _():
            lower.wait()
            owned.wait()

        def some(j, carry):
            lanes = pl.ds(pl.multiple_of(j * 1024, 1024), 1024)
            mask = mask_ref[:, lanes]
            masked_ref[0:HEAD, lanes] = (top[:, lanes].astype(f32) * mask).astype(bf16)
            tile[...] = jnp.zeros_like(tile)
            tile[0 : bottom.shape[0], :] = bottom[:, lanes].astype(f32) * mask
            masked_ref[HEAD:, lanes] = tile[...].astype(bf16)
            return carry

        cuts = width // 1024
        lax.fori_loop(part * (cuts // 2), (part + 1) * (cuts // 2), some, 0)

    def make_order():
        row = lax.broadcasted_iota(jnp.int32, order.shape, 0)
        column = lax.broadcasted_iota(jnp.int32, order.shape, 1)
        wanted = row % group // CHUNK * dims + row // group * CHUNK + row % CHUNK
        order[...] = jnp.where(column == wanted, 1.0, 0.0)

    for step in range(count + 3):
        k = step
        if k < count:

            @pl.when(moved)
            def _(k=k):
                swap_in(k).wait_recv()

            @pl.when(jnp.logical_not(moved))
            def _(k=k):
                keep(k).wait()

            to_side(k).start()
            to_along(k).start()
            give(0, k).start()
        if step < 2:
            mask_pixels(step)
        elif step == 2:
            make_order()
        k = step - 1
        if 0 <= k < count:
            if over_x(k):
                from_along(k).wait_recv()
                pass_on(k).start()
                from_side(k).wait_recv()
            else:
                from_side(k).wait_recv()
                pass_on(k).start()
                from_along(k).wait_recv()
            give(1, k).start()
            give(2, k).start()
        k = step - 2
        if 0 <= k < count:
            from_far(k).wait_recv()
            give(3, k).start()
        k = step - 3
        if 0 <= k < count:
            for j in range(4):
                given(j, k).wait_recv()
            store(k).start()
            part = held[:, :, cut(k), :].reshape(group, width)
            mixed[:, k * group : (k + 1) * group] = dot_nt(masked_ref[...], part)

    stream_ref[...] = exact(mixed[...], order[...], 1, 0)[0 : stream_ref.shape[0]]

    @pl.when(moved)
    def _():
        for k in range(count):
            swap(k).wait_send()

    for k in range(count):
        to_side(k).wait_send()
        to_along(k).wait_send()
        pass_on(k).wait_send()
        store(k).wait()
        for j in range(4):
            give(j, k).wait_send()


def share_kernels(made, mask, pixels, head, rest):
    dims, width = made.shape
    count = dims // CHUNK
    seq = pixels.shape[1]
    rows = tall(seq)
    f32 = jnp.float32
    dma = pltpu.SemaphoreType.DMA
    vmem, far = pl.BlockSpec(memory_space=pltpu.VMEM), pl.BlockSpec(memory_space=pl.ANY)
    shared, masked, stream = pl.pallas_call(
        share_kernel,
        out_shape=[
            jax.ShapeDtypeStruct((4, 2, dims, width), made.dtype),
            jax.ShapeDtypeStruct((rows, width), made.dtype),
            jax.ShapeDtypeStruct((seq, 8 * dims), f32),
        ],
        in_specs=[vmem, vmem, far, far, far],
        out_specs=[far, vmem, vmem],
        scratch_shapes=[
            pltpu.VMEM((4, 2, dims, width), made.dtype),
            pltpu.VMEM((HEAD, width), made.dtype),
            pltpu.VMEM((seq - HEAD, width), made.dtype),
            pltpu.VMEM((rows - HEAD, 1024), f32),
            pltpu.VMEM((rows, 8 * dims), f32),
            pltpu.VMEM((8 * dims, 8 * dims), f32),
            dma((2,)),
        ]
        + [dma((count,))] * 10
        + [dma((4, count))] * 2,
        compiler_params=pltpu.CompilerParams(collective_id=2, has_side_effects=True, vmem_limit_bytes=60 << 20),
        name="share_kernels",
    )(made, mask, pixels, head, rest)
    return shared.reshape(8 * dims, width), masked, stream


def fold_kernel(masked_ref, mask_ref, low_ref, kernel_ref, all_ref, back_ref,
                gone, own, twin_in, relay_in, side_in, along_in, tiles, backs, tile_sem, back_sem, keep_sem, twin_send, twin_recv,
                relay_send, relay_recv, side_send, side_recv, along_send, along_recv, swap_send, swap_recv,
                group_send, group_recv, give_send, give_recv):
    f32, bf16 = jnp.float32, jnp.bfloat16
    y, c, z, x, low, side, along, twin, partner, moved = quad_peers()
    over = place(1 - y, c, z, x)
    dims, width = all_ref.shape[2], all_ref.shape[3]
    count = dims // CHUNK
    seq = back_ref.shape[1]
    lane = tiles.shape[2]

    def cut(k):
        return pl.ds(k * CHUNK, CHUNK)

    def spot_of(j):
        return (low + j // 2) % 2, (x + j % 2) % 2

    def mine(j, k):
        a, b = spot_of(j)
        return own.at[a, b, cut(k)]

    def swap(k):
        return remote(gone.at[:, :, cut(k)], twin_in.at[:, :, cut(k)], twin_send.at[k], twin_recv.at[k], twin)

    def relay(k):
        return remote(mine(3, k), relay_in.at[cut(k)], relay_send.at[k], relay_recv.at[k], along if over_x(k) else side)

    def to_side(k):
        return remote(mine(1, k), side_in.at[cut(k)], side_send.at[k], side_recv.at[k], side)

    def to_along(k):
        return remote(mine(2, k), along_in.at[cut(k)], along_send.at[k], along_recv.at[k], along)

    def keep(k):
        return pltpu.make_async_copy(mine(0, k), all_ref.at[y, c, cut(k)], keep_sem.at[k])

    def move(k):
        return remote(mine(0, k), all_ref.at[y, 1 - c, cut(k)], swap_send.at[k], swap_recv.at[k], partner)

    def moved_in(k):
        return remote(mine(0, k), all_ref.at[y, c, cut(k)], swap_send.at[k], swap_recv.at[k], partner)

    def cross(k):
        return remote(all_ref.at[y, c, cut(k)], all_ref.at[y, c, cut(k)], group_send.at[k], group_recv.at[k], over)

    def crossed(k):
        return remote(all_ref.at[1 - y, c, cut(k)], all_ref.at[1 - y, c, cut(k)], group_send.at[k], group_recv.at[k], over)

    def give(j, k):
        here = all_ref.at[(y + j) % 2, c, cut(k)]
        return remote(here, here, give_send.at[j, k], give_recv.at[j, k], twin)

    def given(j, k):
        here = all_ref.at[(y + j) % 2, 1 - c, cut(k)]
        return remote(here, here, give_send.at[j, k], give_recv.at[j, k], twin)

    def fetch(j):
        return pltpu.make_async_copy(kernel_ref.at[:, pl.ds(j * lane, lane)], tiles.at[j % 2], tile_sem.at[j % 2])

    def drain(j):
        return pltpu.make_async_copy(backs.at[j % 2], back_ref.at[0, :, pl.ds(j * lane, lane)], back_sem.at[j % 2])

    def half(core, out):
        chosen = low_ref[:, pl.ds(pl.multiple_of(core * 4 * dims, 128), 4 * dims)]

        def some(j, carry):
            lanes = pl.ds(pl.multiple_of(j * 1024, 1024), 1024)
            part = dot_tn(chosen, masked_ref[:, lanes]).astype(bf16)
            out[:, :, :, lanes] = part.reshape(2, 2, dims, 1024)
            return carry

        lax.fori_loop(0, width // 1024, some, 0)

    def pixels_back(j):
        fetch(j).wait()
        if j >= 2:
            drain(j - 2).wait()
        part = dot_nn(low_ref[...], tiles[j % 2])[0:seq] * mask_ref[:, j * lane : (j + 1) * lane]
        backs[j % 2] = part.astype(bf16)
        drain(j).start()
        if (j + 2) * lane < width:
            fetch(j + 2).start()

    def pair(j, k):
        a, b = spot_of(j)
        return own[a, b, cut(k)].astype(f32) + twin_in[a, b, cut(k)].astype(f32)

    def put(j, k, value):
        a, b = spot_of(j)
        own[a, b, cut(k)] = value.astype(bf16)

    fetch(0).start()
    fetch(1).start()
    greet([side, along, twin, partner, over])
    half(1 - c, gone)
    for k in range(count):
        swap(k).start()
    half(c, own)

    for step in range(count + 4):
        k = step
        if k < count:
            swap(k).wait_recv()
            put(3, k, pair(3, k))
            relay(k).start()
        k = step - 1
        if 0 <= k < count:
            first, second = (to_along, to_side) if over_x(k) else (to_side, to_along)
            plain, summed = (2, 1) if over_x(k) else (1, 2)
            put(plain, k, pair(plain, k))
            first(k).start()
            relay(k).wait_recv()
            put(summed, k, pair(summed, k) + relay_in[cut(k)].astype(f32))
            second(k).start()
        k = step - 2
        if 0 <= k < count:
            to_side(k).wait_recv()
            to_along(k).wait_recv()
            put(0, k, pair(0, k) + side_in[cut(k)].astype(f32) + along_in[cut(k)].astype(f32))

            @pl.when(moved)
            def _(k=k):
                move(k).start()

            @pl.when(jnp.logical_not(moved))
            def _(k=k):
                keep(k).start()

        k = step - 3
        if 0 <= k < count:

            @pl.when(moved)
            def _(k=k):
                moved_in(k).wait_recv()

            @pl.when(jnp.logical_not(moved))
            def _(k=k):
                keep(k).wait()

            cross(k).start()
            give(0, k).start()
        k = step - 4
        if 0 <= k < count:
            crossed(k).wait_recv()
            give(1, k).start()
        if step * lane < width:
            pixels_back(step)

    @pl.when(moved)
    def _():
        for k in range(count):
            move(k).wait_send()

    for j in (width // lane - 2, width // lane - 1):
        drain(j).wait()
    for k in range(count):
        swap(k).wait_send()
        relay(k).wait_send()
        to_side(k).wait_send()
        to_along(k).wait_send()
        cross(k).wait_send()
        for j in range(2):
            give(j, k).wait_send()
            given(j, k).wait_recv()


def fold_kernels(masked, mask, low, kernels, seq):
    width = masked.shape[1]
    dims = kernels.shape[0] // 8
    count = dims // CHUNK
    bf16 = jnp.bfloat16
    dma = pltpu.SemaphoreType.DMA
    vmem, far = pl.BlockSpec(memory_space=pltpu.VMEM), pl.BlockSpec(memory_space=pl.ANY)
    folded, back = pl.pallas_call(
        fold_kernel,
        out_shape=[
            jax.ShapeDtypeStruct((2, 2, dims, width), bf16),
            jax.ShapeDtypeStruct((1, seq, width), bf16),
        ],
        in_specs=[vmem, vmem, vmem, far],
        out_specs=[far, far],
        scratch_shapes=[
            pltpu.VMEM((2, 2, dims, width), bf16),
            pltpu.VMEM((2, 2, dims, width), bf16),
            pltpu.VMEM((2, 2, dims, width), bf16),
            pltpu.VMEM((dims, width), bf16),
            pltpu.VMEM((dims, width), bf16),
            pltpu.VMEM((dims, width), bf16),
            pltpu.VMEM((2, 8 * dims, 1024), bf16),
            pltpu.VMEM((2, seq, 1024), bf16),
            dma((2,)),
            dma((2,)),
            dma((count,)),
        ]
        + [dma((count,))] * 12
        + [dma((2, count))] * 2,
        compiler_params=pltpu.CompilerParams(collective_id=3, has_side_effects=True, vmem_limit_bytes=60 << 20),
        name="fold_kernels",
    )(masked, mask, low, kernels)
    return folded.reshape(4, dims, width), back


def on_device(
    pixels,
    band_mask,
    wavelength,
    owner_order,
    rest_weight,
    rest_moment1,
    rest_moment2,
    fc_weight,
    fc_moment1,
    fc_moment2,
    cotangent,
):
    f32 = jnp.float32
    bf16 = jnp.bfloat16
    kernel_rate = float(E * PATCH * NB) ** (-0.5)
    groups = lax.axis_size("group")
    own_rows = rest_weight.shape[0]
    own_blocks = own_rows // 8
    fits = lax.axis_size("group") == 4 and lax.axis_size("img") == 8
    extra = -own_rows % 128
    slot_blocks = (own_rows + extra) // 8
    mask = band_mask.astype(f32)
    low_weight = fc_weight.astype(bf16)
    rest_low = jnp.pad(rest_weight.astype(bf16), ((0, extra), (0, 0)))
    if fits:
        mask = swap_images(mask)
        gathered, head = gather_packed(rest_low, pixels)
        gathered, rest, cotangent, low_weight = lax.optimization_barrier(
            (gathered, pixels[:, HEAD:], cotangent, low_weight)
        )
        across = swap_group(low_weight, 2)
        rest, cotangent = swap_images(rest), swap_images(cotangent)
    else:
        gathered = lax.all_gather(rest_low, ("group", "img"), axis=0, tiled=True)
    shards = gathered.size // ((own_rows + extra) * 128)
    gathered = gathered.reshape(shards, own_rows + extra, 128)
    total_blocks = owner_order.shape[0]
    slots = jnp.pad(
        owner_order.reshape(shards, own_blocks),
        ((0, 0), (0, slot_blocks - own_blocks)),
        constant_values=total_blocks,
    ).reshape(-1)
    unpacked = spread_packed(gathered, slots, total_blocks)
    if fits:
        *unpacked, across = lax.optimization_barrier((*unpacked, across))
        slabs = [low_weight, swap_group(low_weight, 1), across, swap_group(across, 1)]
    else:
        master = lax.all_gather(low_weight, "group", axis=0, tiled=False)
        slabs = [master[j] for j in range(groups)]
    block_mats, wave_mats = unpacked[:4], unpacked[4:10]
    block_vectors, wave_vectors = unpacked[10:]
    embedded = embed_waves(wavelength).reshape(groups * NB, E)
    shaped_low, own_shaped, kept, slope = wave_layer(embedded, wave_mats, wave_vectors)
    kernel_low = make_kernels(shaped_low, slabs, fits)
    mask = jnp.repeat(mask, PATCH, axis=1)
    if fits:
        kernel_all, masked, stream = share_kernels(kernel_low, mask, pixels, head, rest)
    else:
        kernel_all = lax.all_gather(kernel_low, "img", axis=0, tiled=True)
        stream = embed_patches(pixels, mask, kernel_all)
        masked = jnp.pad((pixels[0] * mask).astype(bf16), ((0, tall(pixels.shape[1]) - pixels.shape[1]), (0, 0)))
    block_out, grad_low, block_vectors, *block_grads = block_pass(
        stream, cotangent, block_vectors, *block_mats
    )
    if fits:
        all_groups, pixel_grad = fold_kernels(masked, mask, grad_low, kernel_all, pixels.shape[1])
        all_groups, block_out, pixel_grad = lax.optimization_barrier((all_groups, block_out, pixel_grad))
        block_out, pixel_grad = swap_images(block_out), swap_images(pixel_grad)
    else:
        pixel_grad, kernel_grad = unembed_patches(masked, mask, kernel_all, grad_low, pixels.shape[1])
        kernel_grad_low = lax.psum_scatter(kernel_grad, "img", scatter_dimension=0, tiled=True)
        all_groups = lax.all_gather(kernel_grad_low[None], "group", axis=0, tiled=True)
    fc_new, fc_first, fc_second, shaped_part = master_update(
        all_groups,
        own_shaped,
        fc_weight,
        fc_moment1,
        fc_moment2,
        kernel_rate,
    )
    *wave_grads, wave_vectors = wave_back(shaped_part, embedded, kept, slope, wave_mats, wave_vectors)
    given = [*block_grads, *wave_grads, block_vectors, wave_vectors]
    joint_term = collect_packed(given, slots, total_blocks, shards, own_rows + extra)
    if fits:
        rest_grad = reduce_packed(joint_term.reshape(2, 2, 4, 2, own_rows + extra, 128))
    else:
        rest_grad = lax.psum_scatter(
            joint_term, ("group", "img"), scatter_dimension=0, tiled=False
        ).astype(f32)
    rest_grad = rest_grad[:own_rows]
    rest_new, rest_first, rest_second = adamw_step(
        rest_weight, rest_moment1, rest_moment2, rest_grad, rest_rate
    )
    return (block_out, pixel_grad, rest_new, rest_first, rest_second, fc_new, fc_first, fc_second)


def solution(mesh):
    placed = (
        P(("group", "img"), None, None),
        P(("group", "img"), None),
        P(),
        P(),
        P(("group", "img"), None),
        P(("group", "img"), None),
        P(("group", "img"), None),
        P("group", "img"),
        P("group", "img"),
        P("group", "img"),
        P(("group", "img"), None),
    )
    return jax.shard_map(
        on_device,
        mesh=mesh,
        in_specs=placed,
        out_specs=(
            P(("group", "img"), None),
            P(("group", "img"), None, None),
            P(("group", "img"), None),
            P(("group", "img"), None),
            P(("group", "img"), None),
            P("group", "img"),
            P("group", "img"),
            P("group", "img"),
        ),
        check_vma=False,
    )
```

```python
import functools
import math

import jax
import jax.numpy as jnp
from jax import lax
from jax.experimental import pallas as pl
from jax.experimental.pallas import tpu as pltpu
from jax.sharding import PartitionSpec as P

MESH = pl.DeviceIdType.MESH

D = 768
HEADS = 12
HD = 64
HID = 3072
E = 128
HH = 4
HFF = 2048
PATCH = 256
NB = 32
STEP = 5


beta_one = 0.5
beta_two = 0.75
decay_rate = 0.05
epsilon_add = 1e-08
rest_rate = 0.02


def layout():
    return [
        ("w_qkv", (D, 3 * D)),
        ("w_out", (D, D)),
        ("w_up", (D, HID)),
        ("w_down", (HID, D)),
        ("h_query", (E, E)),
        ("h_key", (E, E)),
        ("h_value", (E, E)),
        ("h_out", (E, E)),
        ("h_ffin", (E, HFF)),
        ("h_ffout", (HFF, E)),
        ("ln1_gain", (D,)),
        ("ln1_shift", (D,)),
        ("ln2_gain", (D,)),
        ("ln2_shift", (D,)),
        ("patch_bias", (D,)),
        ("hn1_gain", (E,)),
        ("hn1_shift", (E,)),
        ("hn2_gain", (E,)),
        ("hn2_shift", (E,)),
    ]


def embed_waves(wavelength):
    half_width = E // 2
    frequency = jnp.exp(-math.log(10000.0) * jnp.arange(half_width, dtype=jnp.float32) / half_width)
    angles = wavelength.astype(jnp.float32)[..., None] * frequency
    return jnp.concatenate([jnp.sin(angles), jnp.cos(angles)], axis=-1)


def matrices():
    listed, at = [], 0
    for name, extent in layout():
        if len(extent) == 2:
            listed.append((name, extent[0], extent[1], at))
        at += math.prod(extent) // 128
    return listed


def vector_places():
    listed, at = [], 0
    rows = [0, 0]
    for name, extent in layout():
        if len(extent) == 1:
            kind = 0 if extent[0] == D else 1
            for j in range(extent[0] // 128):
                listed.append((at + j, kind, rows[kind], j * 128))
            rows[kind] += 1
        at += math.prod(extent) // 128
    return listed


def vector_shapes():
    return [jax.ShapeDtypeStruct((8, D), jnp.float32), jax.ShapeDtypeStruct((8, E), jnp.float32)]


def shards_a_step(shards, wanted):
    return wanted if shards % wanted == 0 else 1


def spread_kernel(order_ref, low_ref, *refs):
    big, small = matrices()[:4], matrices()[4:]
    far, outs, linear, kept, sem = refs[:4], refs[4:12], refs[12], refs[13:17], refs[17]
    step = pl.program_id(0)
    shards, rows = low_ref.shape[0], low_ref.shape[1]

    for shard in range(shards):

        def two(j, carry, shard=shard):
            pair = low_ref[shard, pl.ds(pl.multiple_of(j * 16, 16), 16), :].astype(jnp.float32)
            for half in range(2):
                block = order_ref[(step * shards + shard) * (rows // 8) + j * 2 + half]
                linear[pl.ds(pl.multiple_of(block * 8, 8), 8), :] = pair[half * 8 : half * 8 + 8]
            return carry

        lax.fori_loop(0, rows // 16, two, 0, unroll=8)

    @pl.when(step == pl.num_programs(0) - 1)
    def _():
        def relay(height, width, first, out):
            lanes = width // 128

            def some(j, carry):
                top = pl.multiple_of(j * 128, 128)
                for lane in range(lanes):
                    part = linear[pl.ds(first + top * lanes + lane, 128, stride=lanes), :]
                    out[pl.ds(top, 128), lane * 128 : lane * 128 + 128] = part.astype(out.dtype)
                return carry

            lax.fori_loop(0, height // 128, some, 0)

        copies = []
        for j, (name, height, width, first) in enumerate(big):
            relay(height, width, first, kept[j])
            copies.append(pltpu.make_async_copy(kept[j], far[j], sem.at[j]))
            copies[-1].start()
        for (name, height, width, first), out in zip(small, outs):
            relay(height, width, first, out)
        for out in outs[-2:]:
            out[...] = jnp.zeros_like(out)
        for row, kind, top, lane in vector_places():
            outs[kind - 2][top : top + 1, lane : lane + 128] = linear[row : row + 1, :]
        for copy in copies:
            copy.wait()


def spread_packed(gathered, slots, blocks):
    shards, rows = gathered.shape[0], gathered.shape[1]
    some = shards_a_step(shards, 4)
    big = [jax.ShapeDtypeStruct((height, width), jnp.bfloat16) for name, height, width, first in matrices()[:4]]
    small = [jax.ShapeDtypeStruct((height, width), jnp.float32) for name, height, width, first in matrices()[4:]]
    small += vector_shapes()
    return pl.pallas_call(
        spread_kernel,
        out_shape=big + small,
        grid_spec=pltpu.PrefetchScalarGridSpec(
            num_scalar_prefetch=1,
            grid=(shards // some,),
            in_specs=[pl.BlockSpec((some, rows, 128), lambda s, order: (s, 0, 0))],
            out_specs=[pl.BlockSpec(memory_space=pl.ANY) for shape in big]
            + [pl.BlockSpec(shape.shape, lambda s, order: (0, 0), pipeline_mode=pl.Buffered(1)) for shape in small],
            scratch_shapes=[pltpu.VMEM(((blocks + 1) * 8, 128), jnp.float32)]
            + [pltpu.VMEM(shape.shape, shape.dtype) for shape in big]
            + [pltpu.SemaphoreType.DMA((4,))],
        ),
        compiler_params=pltpu.CompilerParams(vmem_limit_bytes=60 << 20),
        name="spread_packed",
    )(slots, gathered)


def collect_kernel(order_ref, *refs):
    big, small = matrices()[:4], matrices()[4:]
    far, ins, low_ref, linear, kept, sem = refs[:4], refs[4:12], refs[12], refs[13], refs[14:18], refs[18]
    step = pl.program_id(0)
    shards, rows = low_ref.shape[0], low_ref.shape[1]

    @pl.when(step == 0)
    def _():
        copies = [pltpu.make_async_copy(far[j], kept[j], sem.at[j]) for j in range(4)]
        for copy in copies:
            copy.start()

        def relay(height, width, first, given):
            lanes = width // 128

            def some(j, carry):
                top = pl.multiple_of(j * 128, 128)
                for lane in range(lanes):
                    part = given[pl.ds(top, 128), lane * 128 : lane * 128 + 128]
                    linear[pl.ds(first + top * lanes + lane, 128, stride=lanes), :] = part.astype(jnp.float32)
                return carry

            lax.fori_loop(0, height // 128, some, 0)

        for (name, height, width, first), given in zip(small, ins):
            relay(height, width, first, given)
        first = vector_places()[0][0]
        linear[first:, :] = jnp.zeros((linear.shape[0] - first, 128), jnp.float32)
        for row, kind, top, lane in vector_places():
            linear[row : row + 1, :] = ins[kind - 2][top : top + 1, lane : lane + 128]
        for j, (name, height, width, first) in enumerate(big):
            copies[j].wait()
            relay(height, width, first, kept[j])

    for shard in range(shards):

        def two(j, carry, shard=shard):
            parts = []
            for half in range(2):
                block = order_ref[(step * shards + shard) * (rows // 8) + j * 2 + half]
                parts.append(linear[pl.ds(pl.multiple_of(block * 8, 8), 8), :])
            low_ref[shard, pl.ds(pl.multiple_of(j * 16, 16), 16), :] = jnp.concatenate(parts, axis=0).astype(low_ref.dtype)
            return carry

        lax.fori_loop(0, rows // 16, two, 0, unroll=20)


def collect_packed(grads, slots, blocks, shards, rows):
    some = shards_a_step(shards, 2)
    whole = [pl.BlockSpec(grad.shape, lambda s, order: (0, 0), pipeline_mode=pl.Buffered(1)) for grad in grads[4:]]
    return pl.pallas_call(
        collect_kernel,
        out_shape=jax.ShapeDtypeStruct((shards, rows, 128), jnp.bfloat16),
        grid_spec=pltpu.PrefetchScalarGridSpec(
            num_scalar_prefetch=1,
            grid=(shards // some,),
            in_specs=[pl.BlockSpec(memory_space=pl.ANY)] * 4 + whole,
            out_specs=pl.BlockSpec((some, rows, 128), lambda s, order: (s, 0, 0)),
            scratch_shapes=[pltpu.VMEM(((blocks + 1) * 8, 128), jnp.float32)]
            + [pltpu.VMEM(grad.shape, grad.dtype) for grad in grads[:4]]
            + [pltpu.SemaphoreType.DMA((4,))],
        ),
        compiler_params=pltpu.CompilerParams(vmem_limit_bytes=60 << 20),
        name="collect_packed",
    )(slots, *grads)


def finer(a, b, left, right):
    return lax.dot_general(
        a, b, (((left,), (right,)), ((), ())), precision=lax.Precision.HIGH, preferred_element_type=jnp.float32
    )


def unit_scale(values):
    center = values - jnp.mean(values, axis=-1, keepdims=True)
    scale = lax.rsqrt(jnp.mean(center * center, axis=-1, keepdims=True) + 1e-06)
    return center * scale, scale


def unit_back(grad, unit, scale, gain):
    inner = grad * gain
    return scale * (
        inner - jnp.mean(inner, axis=-1, keepdims=True) - unit * jnp.mean(inner * unit, axis=-1, keepdims=True)
    )


def wave_kernel(embed_ref, wq_ref, wk_ref, wv_ref, wo_ref, win_ref, wout_ref, vec_ref, shaped_ref, own_ref, kept_ref, slope_ref):
    rows = embed_ref.shape[0]
    groups = rows // NB
    embedded = embed_ref[...]
    queries = finer(embedded, wq_ref[...], 1, 0)
    keys = finer(embedded, wk_ref[...], 1, 0)
    values = finer(embedded, wv_ref[...], 1, 0)
    size = E // HH
    across = lax.broadcasted_iota(jnp.int32, (rows, rows), 0) // NB == lax.broadcasted_iota(jnp.int32, (rows, rows), 1) // NB
    mixed = []
    for head in range(HH):
        lanes = slice(head * size, head * size + size)
        scores = finer(queries[:, lanes], keys[:, lanes], 1, 1) * size**-0.5
        scores = jnp.where(across, scores, -1e30)
        weight = jnp.exp(scores - jnp.max(scores, axis=-1, keepdims=True))
        weight = weight / jnp.sum(weight, axis=-1, keepdims=True)
        kept_ref[head] = weight
        mixed.append(finer(weight, values[:, lanes], 1, 0))
    mixed = jnp.concatenate(mixed, axis=1)
    unit_one, scale_one = unit_scale(embedded + finer(mixed, wo_ref[...], 1, 0))
    first = unit_one * vec_ref[0:1, :] + vec_ref[1:2, :]
    inner = finer(first, win_ref[...], 1, 0)
    half = 0.5 * (1.0 + lax.erf(inner * 0.5**0.5))
    slope_ref[0] = inner * half
    slope_ref[1] = half + inner * jnp.exp(-0.5 * inner * inner) * (2.0 * math.pi) ** -0.5
    unit_two, scale_two = unit_scale(first + finer(inner * half, wout_ref[...], 1, 0))
    shaped = (unit_two * vec_ref[2:3, :] + vec_ref[3:4, :] + embedded).astype(jnp.bfloat16)
    for j, part in enumerate((queries, keys, values, mixed, unit_one, unit_two)):
        kept_ref[HH + j] = part
    kept_ref[HH + 6] = jnp.broadcast_to(scale_one, (rows, E))
    kept_ref[HH + 7] = jnp.broadcast_to(scale_two, (rows, E))
    shaped_ref[...] = shaped
    wide = shaped.astype(jnp.float32)
    width = E // groups
    group = lax.axis_index("group")
    own = jnp.zeros((rows, width), jnp.float32)
    for j in range(groups):
        own = jnp.where(group == j, wide[:, j * width : (j + 1) * width], own)
    own_ref[...] = own.astype(jnp.bfloat16)


def wave_layer(embedded, mats, vectors):
    rows = embedded.shape[0]
    groups = rows // NB
    f32, bf16 = jnp.float32, jnp.bfloat16
    return pl.pallas_call(
        wave_kernel,
        out_shape=[
            jax.ShapeDtypeStruct((rows, E), bf16),
            jax.ShapeDtypeStruct((rows, E // groups), bf16),
            jax.ShapeDtypeStruct((HH + 8, rows, E), f32),
            jax.ShapeDtypeStruct((2, rows, HFF), f32),
        ],
        compiler_params=pltpu.CompilerParams(vmem_limit_bytes=60 << 20),
        name="wave_layer",
    )(embedded, *mats, vectors)


def wave_back_kernel(part_ref, embed_ref, kept_ref, slope_ref, wq_ref, wk_ref, wv_ref, wo_ref, win_ref, wout_ref, vec_ref,
                     gq_ref, gk_ref, gv_ref, go_ref, gin_ref, gout_ref, gvec_ref):
    rows = embed_ref.shape[0]
    groups = rows // NB
    width = E // groups
    size = E // HH
    group = lax.axis_index("group")
    spread = jnp.concatenate([part_ref[...]] * groups, axis=1)
    lane = lax.broadcasted_iota(jnp.int32, (rows, E), 1) // width
    grad = jnp.where(lane == group, spread, 0.0)
    embedded = embed_ref[...]
    queries, keys, values, mixed, unit_one, unit_two, scale_one, scale_two = (kept_ref[HH + j] for j in range(8))
    gvec_ref[...] = jnp.zeros_like(gvec_ref)
    gvec_ref[2:3, :] = jnp.sum(grad * unit_two, axis=0, keepdims=True)
    gvec_ref[3:4, :] = jnp.sum(grad, axis=0, keepdims=True)
    grad = unit_back(grad, unit_two, scale_two, vec_ref[2:3, :])
    gout_ref[...] = finer(slope_ref[0], grad, 0, 0)
    inner = finer(grad, wout_ref[...], 1, 1) * slope_ref[1]
    first = unit_one * vec_ref[0:1, :] + vec_ref[1:2, :]
    gin_ref[...] = finer(first, inner, 0, 0)
    grad = grad + finer(inner, win_ref[...], 1, 1)
    gvec_ref[0:1, :] = jnp.sum(grad * unit_one, axis=0, keepdims=True)
    gvec_ref[1:2, :] = jnp.sum(grad, axis=0, keepdims=True)
    grad = unit_back(grad, unit_one, scale_one, vec_ref[0:1, :])
    go_ref[...] = finer(mixed, grad, 0, 0)
    grad = finer(grad, wo_ref[...], 1, 1)
    parts = [[], [], []]
    for head in range(HH):
        lanes = slice(head * size, head * size + size)
        weight = kept_ref[head]
        grad_weight = finer(grad[:, lanes], values[:, lanes], 1, 1)
        parts[2].append(finer(weight, grad[:, lanes], 0, 0))
        score = weight * (grad_weight - jnp.sum(weight * grad_weight, axis=-1, keepdims=True)) * size**-0.5
        parts[0].append(finer(score, keys[:, lanes], 1, 0))
        parts[1].append(finer(score, queries[:, lanes], 0, 0))
    for out, part in zip((gq_ref, gk_ref, gv_ref), parts):
        out[...] = finer(embedded, jnp.concatenate(part, axis=1), 0, 0)


def wave_back(part, embedded, kept, slope, mats, vectors):
    f32 = jnp.float32
    return pl.pallas_call(
        wave_back_kernel,
        out_shape=[jax.ShapeDtypeStruct(mat.shape, f32) for mat in mats] + [jax.ShapeDtypeStruct((8, E), f32)],
        compiler_params=pltpu.CompilerParams(vmem_limit_bytes=60 << 20),
        name="wave_back",
    )(part, embedded, kept, slope, *mats, vectors)


def tall(count):
    return -(-count // 16) * 16


def dot_nn(a, b):
    return lax.dot_general(a, b, (((1,), (0,)), ((), ())), preferred_element_type=jnp.float32)


def dot_nt(a, b):
    return lax.dot_general(a, b, (((1,), (1,)), ((), ())), preferred_element_type=jnp.float32)


def dot_tn(a, b):
    return lax.dot_general(a, b, (((0,), (0,)), ((), ())), preferred_element_type=jnp.float32)


def block_kernel(stream_ref, up_ref, vec_ref, wqkv_hbm, wout_hbm, wup_hbm, wdown_hbm,
                 out_ref, low_ref, gvec_ref, gqkv_hbm, gout_hbm, gup_hbm, gdown_hbm,
                 wqkv, wout, wup, wdown, gqkv, gout, gup, gdown,
                 xs, ups, up_low, norm_one, qkv, att, probs, mid, norm_two, acc, hid_low, datt, dqkv, in_sem, out_sem):
    f32, bf16 = jnp.float32, jnp.bfloat16
    seq = stream_ref.shape[0]
    rows = xs.shape[0]
    loads = [
        pltpu.make_async_copy(src, dst, in_sem.at[j])
        for j, (src, dst) in enumerate(((wqkv_hbm, wqkv), (wout_hbm, wout), (wup_hbm, wup), (wdown_hbm, wdown)))
    ]
    for load in loads:
        load.start()
    stores = [
        pltpu.make_async_copy(src, dst, out_sem.at[j])
        for j, (src, dst) in enumerate(((gqkv, gqkv_hbm), (gout, gout_hbm), (gup, gup_hbm), (gdown, gdown_hbm)))
    ]
    gain_one, shift_one = vec_ref[0:1, :], vec_ref[1:2, :]
    gain_two, shift_two = vec_ref[2:3, :], vec_ref[3:4, :]
    xs[...] = jnp.zeros_like(xs)
    xs[0:seq, :] = stream_ref[...] + vec_ref[4:5, :]
    ups[...] = jnp.zeros_like(ups)
    ups[0:seq, :] = up_ref[...].astype(f32)
    up_low[...] = ups[...].astype(bf16)

    def normed(values):
        center = values - jnp.mean(values, axis=-1, keepdims=True)
        scale = lax.rsqrt(jnp.mean(center * center, axis=-1, keepdims=True) + 1e-06)
        return center * scale, scale

    def normed_back(grad, unit, scale, gain):
        inner = grad * gain
        return scale * (
            inner
            - jnp.mean(inner, axis=-1, keepdims=True)
            - unit * jnp.mean(inner * unit, axis=-1, keepdims=True)
        )

    unit, scale = normed(xs[...])
    norm_one[...] = (unit * gain_one + shift_one).astype(bf16)
    loads[0].wait()

    def tile(j, size=D):
        return pl.ds(pl.multiple_of(j * size, size), size)

    def each(count, body):
        lax.fori_loop(0, count, lambda j, carry: (body(j), carry)[1], 0)

    def qkv_part(j):
        qkv[:, tile(j)] = dot_nn(norm_one[...], wqkv[:, tile(j)]).astype(bf16)

    each(3, qkv_part)
    inside = lax.broadcasted_iota(jnp.int32, (rows, rows), 1) < seq

    def heads(p):
        pair = [qkv[:, pl.ds(pl.multiple_of(j * D + p * 128, 128), 128)] for j in range(3)]
        outs = []
        for h in range(2):
            query, key, value = (part[:, h * HD : h * HD + HD] for part in pair)
            scores = jnp.where(inside, dot_nt(query, key) * (HD**-0.5), -1e30)
            weight = jnp.exp(scores - jnp.max(scores, axis=-1, keepdims=True))
            weight = weight / jnp.sum(weight, axis=-1, keepdims=True)
            probs[p * 2 + h] = weight
            outs.append(dot_nn(weight.astype(bf16), value))
        att[:, pl.ds(pl.multiple_of(p * 128, 128), 128)] = jnp.concatenate(outs, axis=1).astype(bf16)

    each(HEADS // 2, heads)
    loads[1].wait()
    mid[...] = xs[...] + dot_nn(att[...], wout[...])
    unit, scale = normed(mid[...])
    norm_two[...] = (unit * gain_two + shift_two).astype(bf16)
    loads[2].wait()
    loads[3].wait()
    acc[...] = jnp.zeros_like(acc)

    def hidden_part(j):
        hidden = dot_nn(norm_two[...], wup[:, tile(j)])
        half = 0.5 * (1.0 + lax.erf(hidden * (0.5**0.5)))
        active = (hidden * half).astype(bf16)
        slope = half + hidden * jnp.exp(-0.5 * hidden * hidden) * (2.0 * math.pi) ** -0.5
        mid[...] += dot_nn(active, wdown[tile(j), :])
        gdown[tile(j), :] = dot_tn(active, up_low[...]).astype(bf16)
        grad_hidden = (dot_nt(up_low[...], wdown[tile(j), :]) * slope).astype(bf16)
        gup[:, tile(j)] = dot_tn(norm_two[...], grad_hidden).astype(bf16)
        acc[...] += dot_nt(grad_hidden, wup[:, tile(j)])

    kept_unit, kept_scale = unit, scale
    hid_low[...] = kept_unit
    each(HID // D, hidden_part)
    stores[2].start()
    stores[3].start()
    out_ref[...] = mid[0:seq, :].astype(bf16)
    grad = acc[...]
    unit = hid_low[...]
    gvec_ref[...] = jnp.zeros_like(gvec_ref)
    gvec_ref[2:3, :] = jnp.sum(grad * unit, axis=0, keepdims=True)
    gvec_ref[3:4, :] = jnp.sum(grad, axis=0, keepdims=True)
    ups[...] += normed_back(grad, unit, kept_scale, gain_two)
    up_low[...] = ups[...].astype(bf16)
    gout[...] = dot_tn(att[...], up_low[...]).astype(bf16)
    stores[1].start()
    datt[...] = dot_nt(up_low[...], wout[...]).astype(bf16)

    def heads_back(p):
        pair = [qkv[:, pl.ds(pl.multiple_of(j * D + p * 128, 128), 128)] for j in range(3)]
        grad_pair = datt[:, pl.ds(pl.multiple_of(p * 128, 128), 128)]
        grads = [[], [], []]
        for h in range(2):
            query, key, value = (part[:, h * HD : h * HD + HD] for part in pair)
            grad_out = grad_pair[:, h * HD : h * HD + HD]
            weight = probs[p * 2 + h]
            grad_weight = dot_nt(grad_out, value)
            grads[2].append(dot_tn(weight.astype(bf16), grad_out))
            grad_score = weight * (grad_weight - jnp.sum(weight * grad_weight, axis=-1, keepdims=True))
            grad_score = grad_score.astype(bf16)
            grads[0].append(dot_nn(grad_score, key) * (HD**-0.5))
            grads[1].append(dot_tn(grad_score, query) * (HD**-0.5))
        for j in range(3):
            dqkv[:, pl.ds(pl.multiple_of(j * D + p * 128, 128), 128)] = jnp.concatenate(grads[j], axis=1).astype(bf16)

    each(HEADS // 2, heads_back)
    acc[...] = jnp.zeros_like(acc)

    def qkv_back(j):
        gqkv[:, tile(j)] = dot_tn(norm_one[...], dqkv[:, tile(j)]).astype(bf16)
        acc[...] += dot_nt(dqkv[:, tile(j)], wqkv[:, tile(j)])

    each(3, qkv_back)
    stores[0].start()
    unit, scale = normed(xs[...])
    grad = acc[...]
    gvec_ref[0:1, :] = jnp.sum(grad * unit, axis=0, keepdims=True)
    gvec_ref[1:2, :] = jnp.sum(grad, axis=0, keepdims=True)
    total = ups[...] + normed_back(grad, unit, scale, gain_one)
    gvec_ref[4:5, :] = jnp.sum(total, axis=0, keepdims=True)
    low_ref[...] = total.astype(bf16)
    for store in stores:
        store.wait()


def block_pass(stream, upstream, vectors, wqkv, wout, wup, wdown):
    f32, bf16 = jnp.float32, jnp.bfloat16
    seq = stream.shape[0]
    rows = tall(seq)
    whole = pl.BlockSpec(memory_space=pltpu.VMEM)
    far = pl.BlockSpec(memory_space=pl.ANY)
    mats = [wqkv, wout, wup, wdown]
    kept = [pltpu.VMEM(mat.shape, bf16) for mat in mats]
    dma = pltpu.SemaphoreType.DMA
    return pl.pallas_call(
        block_kernel,
        out_shape=[
            jax.ShapeDtypeStruct((seq, D), bf16),
            jax.ShapeDtypeStruct((rows, D), bf16),
            jax.ShapeDtypeStruct((8, D), f32),
        ]
        + [jax.ShapeDtypeStruct(mat.shape, bf16) for mat in mats],
        in_specs=[whole] * 3 + [far] * 4,
        out_specs=[whole] * 3 + [far] * 4,
        scratch_shapes=kept
        + kept
        + [
            pltpu.VMEM((rows, D), f32),
            pltpu.VMEM((rows, D), f32),
            pltpu.VMEM((rows, D), bf16),
            pltpu.VMEM((rows, D), bf16),
            pltpu.VMEM((rows, 3 * D), bf16),
            pltpu.VMEM((rows, D), bf16),
            pltpu.VMEM((HEADS, rows, rows), f32),
            pltpu.VMEM((rows, D), f32),
            pltpu.VMEM((rows, D), bf16),
            pltpu.VMEM((rows, D), f32),
            pltpu.VMEM((rows, D), f32),
            pltpu.VMEM((rows, D), bf16),
            pltpu.VMEM((rows, 3 * D), bf16),
            dma((4,)),
            dma((4,)),
        ],
        compiler_params=pltpu.CompilerParams(vmem_limit_bytes=60 << 20),
        cost_estimate=pl.CostEstimate(flops=8_400_000_000, bytes_accessed=30_000_000, transcendentals=2_000_000),
        name="block_pass",
    )(stream, upstream, vectors, *mats)


def adamw_step(weight, moment_one, moment_two, grad, rate):
    first = beta_one * moment_one + (1.0 - beta_one) * grad
    second = beta_two * moment_two + (1.0 - beta_two) * grad * grad
    fix_one = 1.0 - beta_one**STEP
    fix_two = 1.0 - beta_two**STEP
    update = first / fix_one / (jnp.sqrt(second / fix_two) + epsilon_add) + decay_rate * weight
    return (weight - rate * update, first, second)


NC = 15
HEAD = 96


def dims_step(count):
    return 16 if count % 16 == 0 else count


def spread_bands(shaped, master, turned, out):
    dims = out.shape[0]
    for dim in range(dims):
        part = dot_nn(shaped, master[:, dim * PATCH : (dim + 1) * PATCH])
        turned[pl.ds(dim, NB, stride=dims), :] = part[:, :128]
        turned[pl.ds(NB * dims + dim, NB, stride=dims), :] = part[:, 128:]
    for band in range(NB):
        for half in range(2):
            row = half * NB * dims + band * dims
            lane = band * PATCH + half * 128
            out[:, lane : lane + 128] = turned[row : row + dims, :].astype(out.dtype)


def own_bands(shaped_ref):
    return shaped_ref[pl.ds(pl.multiple_of(lax.axis_index("group") * NB, NB), NB), :]


def make_kernel(shaped_ref, master_ref, kernel_ref, turned):
    spread_bands(own_bands(shaped_ref), master_ref, turned, kernel_ref)


def make_kernels(shaped, master):
    dims = master.shape[1] // PATCH
    step = dims_step(dims)
    return pl.pallas_call(
        make_kernel,
        out_shape=jax.ShapeDtypeStruct((dims, NB * PATCH), jnp.bfloat16),
        grid=(dims // step,),
        in_specs=[
            pl.BlockSpec(shaped.shape, lambda j: (0, 0)),
            pl.BlockSpec((E, step * PATCH), lambda j: (0, j)),
        ],
        out_specs=pl.BlockSpec((step, NB * PATCH), lambda j: (j, 0)),
        scratch_shapes=[pltpu.VMEM((2 * NB * step, 128), jnp.float32)],
        compiler_params=pltpu.CompilerParams(vmem_limit_bytes=60 << 20),
        name="make_kernels",
    )(shaped, master)


def embed_kernel(pixel_ref, mask_ref, kernel_ref, stream_ref):
    masked = pixel_ref[...] * mask_ref[...].astype(jnp.bfloat16)
    part = dot_nt(masked, kernel_ref[...])

    @pl.when(pl.program_id(0) == 0)
    def _():
        stream_ref[...] = part

    @pl.when(pl.program_id(0) > 0)
    def _():
        stream_ref[...] += part


def embed_patches(pixels, mask, kernels):
    seq, width = pixels.shape[1], pixels.shape[2]
    cut = 1024
    return pl.pallas_call(
        embed_kernel,
        out_shape=jax.ShapeDtypeStruct((seq, D), jnp.float32),
        grid=(width // cut,),
        in_specs=[
            pl.BlockSpec((None, seq, cut), lambda j: (0, 0, j)),
            pl.BlockSpec((1, cut), lambda j: (0, j)),
            pl.BlockSpec((D, cut), lambda j: (0, j)),
        ],
        out_specs=pl.BlockSpec((seq, D), lambda j: (0, 0)),
        compiler_params=pltpu.CompilerParams(vmem_limit_bytes=60 << 20),
        name="embed_patches",
    )(pixels, mask, kernels)


def unembed_kernel(masked_ref, mask_ref, kernel_ref, low_ref, back_ref, grad_ref):
    seq = back_ref.shape[0]
    back_ref[...] = (dot_nn(low_ref[...], kernel_ref[...])[0:seq] * mask_ref[...]).astype(back_ref.dtype)
    grad_ref[...] = dot_tn(low_ref[...], masked_ref[...]).astype(grad_ref.dtype)


def unembed_patches(masked, mask, kernels, low, seq):
    rows, width = masked.shape
    cut = 1024
    return pl.pallas_call(
        unembed_kernel,
        out_shape=[
            jax.ShapeDtypeStruct((1, seq, width), jnp.bfloat16),
            jax.ShapeDtypeStruct((D, width), jnp.bfloat16),
        ],
        grid=(width // cut,),
        in_specs=[
            pl.BlockSpec((rows, cut), lambda j: (0, j)),
            pl.BlockSpec((1, cut), lambda j: (0, j)),
            pl.BlockSpec((D, cut), lambda j: (0, j)),
            pl.BlockSpec(low.shape, lambda j: (0, 0)),
        ],
        out_specs=[
            pl.BlockSpec((None, seq, cut), lambda j: (0, 0, j)),
            pl.BlockSpec((D, cut), lambda j: (0, j)),
        ],
        compiler_params=pltpu.CompilerParams(vmem_limit_bytes=60 << 20),
        name="unembed_patches",
    )(masked, mask, kernels, low)


def master_kernel(rate, grad_ref, shaped_ref, weight_ref, one_ref, two_ref, new_ref, first_ref, second_ref, back_ref, turned):
    groups, dims = grad_ref.shape[0], grad_ref.shape[1]
    bands = groups * NB
    for group in range(groups):
        for band in range(NB):
            for half in range(2):
                row = half * bands * dims + (group * NB + band) * dims
                lane = band * PATCH + half * 128
                turned[row : row + dims, :] = grad_ref[group, :, lane : lane + 128].astype(jnp.float32)
    total = jnp.zeros(back_ref.shape, jnp.float32)
    for dim in range(dims):
        part = jnp.concatenate(
            [turned[pl.ds(half * bands * dims + dim, bands, stride=dims), :] for half in range(2)], axis=1
        ).astype(jnp.bfloat16)
        lanes = slice(dim * PATCH, (dim + 1) * PATCH)
        weight = weight_ref[:, lanes]
        total += dot_nt(part, weight.astype(jnp.bfloat16))
        grad = dot_tn(shaped_ref[...], part)
        new_ref[:, lanes], first_ref[:, lanes], second_ref[:, lanes] = adamw_step(
            weight, one_ref[:, lanes], two_ref[:, lanes], grad, rate
        )

    @pl.when(pl.program_id(0) == 0)
    def _():
        back_ref[...] = total

    @pl.when(pl.program_id(0) > 0)
    def _():
        back_ref[...] += total


def master_update(grads, shaped, weight, one, two, rate):
    groups, dims = grads.shape[0], grads.shape[1]
    step = dims_step(dims)
    columns = pl.BlockSpec((weight.shape[0], step * PATCH), lambda j: (0, j))
    like = jax.ShapeDtypeStruct(weight.shape, jnp.float32)
    return pl.pallas_call(
        functools.partial(master_kernel, rate),
        out_shape=[like, like, like, jax.ShapeDtypeStruct(shaped.shape, jnp.float32)],
        grid=(dims // step,),
        in_specs=[
            pl.BlockSpec((groups, step, NB * PATCH), lambda j: (0, j, 0)),
            pl.BlockSpec(shaped.shape, lambda j: (0, 0)),
            columns,
            columns,
            columns,
        ],
        out_specs=[columns, columns, columns, pl.BlockSpec(shaped.shape, lambda j: (0, 0))],
        scratch_shapes=[pltpu.VMEM((2 * groups * NB * step, 128), jnp.float32)],
        compiler_params=pltpu.CompilerParams(vmem_limit_bytes=60 << 20),
        name="master_update",
    )(grads, shaped, weight, one, two)


def spot():
    group = lax.axis_index("group")
    image = lax.axis_index("img")
    return group // 2, group % 2, image // 2, image % 2


def place(y, c, z, x):
    return (y * 2 + c, z * 2 + x)


def partners():
    y, c, z, x = spot()
    x2, y2 = x + (1 - c) * (1 - 2 * x), y + c * (1 - 2 * y)
    x3, y3 = x + c * (1 - 2 * x), y + (1 - c) * (1 - 2 * y)
    around = [place(y, c, (z + d) % 4, x) for d in (1, 2, 3)]
    return (x2, y2), (x3, y3), around, place(y2, c, z, x2), place(y3, c, z, x3), place(y, 1 - c, z, x)


def greet(peers):
    barrier = pltpu.get_barrier_semaphore()
    for peer in peers:
        pl.semaphore_signal(barrier, inc=1, device_id=peer, device_id_type=MESH)
    pl.semaphore_wait(barrier, len(peers))


def remote(src, dst, send_sem, recv_sem, target):
    return pltpu.make_async_remote_copy(
        src_ref=src, dst_ref=dst, send_sem=send_sem, recv_sem=recv_sem, device_id=target, device_id_type=MESH
    )


def gather_kernel(rest_ref, pixel_ref, weight_ref, all_ref, head_ref, low_ref, own_ref, wide, narrow, weight_sem, head_sem, local_sem, line_send, line_recv, group_send, group_recv, twin_send, twin_recv):
    y, c, z, x = spot()
    (x2, y2), (x3, y3), around, second, third, twin = partners()
    partner = place(y, 1 - c, (z + 2) % 4, x)
    moved = (c + z // 2) % 2 == 1
    rows = own_ref.shape[0] // NC

    def cut(k):
        return pl.ds(k * rows, rows)

    head = remote(pixel_ref.at[0, pl.ds(0, HEAD)], head_ref.at[0], head_sem.at[0], head_sem.at[1], partner)

    def along(d, k):
        return remote(own_ref.at[cut(k)], all_ref.at[y, c, z, x, cut(k)], line_send.at[d - 1, k], line_recv.at[d - 1, k], around[d - 1])

    def along_in(d, k):
        return remote(own_ref.at[cut(k)], all_ref.at[y, c, (z + 4 - d) % 4, x, cut(k)], line_send.at[d - 1, k], line_recv.at[d - 1, k], around[d - 1])

    def square(core, j):
        yy, xx = ((y, x), (y2, x2), (y3, x3), (1 - y, 1 - x))[j]
        return all_ref.at[yy, core, :, xx]

    def hop(j, to, k, slot, landing):
        part = square(c, j).at[:, cut(k)]
        return remote(part, part, group_send.at[slot, k], group_recv.at[landing, k], to)

    def hop_in(landing, k):
        part = square(c, landing).at[:, cut(k)]
        return remote(part, part, group_send.at[0, k], group_recv.at[landing, k], twin)

    def share(j, k):
        part = square(c, j).at[:, cut(k)]
        yy, xx = ((y, x), (y2, x2), (y3, x3), (1 - y, 1 - x))[j]
        landing = (0, 2, 1, 3)[j]
        return remote(part, part, twin_send.at[j, k], twin_recv.at[landing, k], twin)

    def share_in(landing, k):
        yy, xx = ((y, x), (y2, x2), (y3, x3), (1 - y, 1 - x))[landing]
        part = all_ref.at[yy, 1 - c, :, xx, cut(k)]
        return remote(part, part, twin_send.at[0, k], twin_recv.at[landing, k], twin)

    fetch = pltpu.make_async_copy(weight_ref, wide, weight_sem.at[0])
    store = pltpu.make_async_copy(narrow, low_ref, weight_sem.at[1])
    fetch.start()
    even = rest_ref.shape[0] // 16 * 16
    own_ref[0:even, :] = rest_ref[0:even, :].astype(jnp.bfloat16)
    if even < own_ref.shape[0]:
        left = rest_ref.shape[0] - even
        parts = [rest_ref[even:, :]] if left else []
        parts.append(jnp.zeros((own_ref.shape[0] - even - left, 128), jnp.float32))
        own_ref[even:, :] = jnp.concatenate(parts, axis=0).astype(jnp.bfloat16)
    keep = pltpu.make_async_copy(own_ref, all_ref.at[y, c, z, x], local_sem)
    keep.start()
    greet(around + [second, third, twin, partner])
    for k in range(NC):
        for d in (1, 2, 3):
            along(d, k).start()
    keep.wait()
    for step in range(NC + 2):
        k = step
        if k < NC:
            for d in (1, 2, 3):
                along_in(d, k).wait_recv()
            hop(0, third, k, 0, 2).start()
            hop(0, second, k, 1, 1).start()
            share(0, k).start()
        if step == 3:
            fetch.wait()
            narrow[...] = wide[...].astype(jnp.bfloat16)
            store.start()
        if step == NC - 3:

            @pl.when(moved)
            def _():
                head.start()

        k = step - 1
        if 0 <= k < NC:
            hop_in(1, k).wait_recv()
            hop(1, third, k, 2, 3).start()
            share(1, k).start()
        k = step - 2
        if 0 <= k < NC:
            hop_in(2, k).wait_recv()
            share(2, k).start()
            hop_in(3, k).wait_recv()
            share(3, k).start()
    for k in range(NC):
        for d in (1, 2, 3):
            along(d, k).wait_send()
        hop(0, third, k, 0, 2).wait_send()
        hop(0, second, k, 1, 1).wait_send()
        hop(1, third, k, 2, 3).wait_send()
        for j in range(4):
            share(j, k).wait_send()
            share_in(j, k).wait_recv()

    store.wait()

    @pl.when(moved)
    def _():
        head.wait()


def gather_packed(own, pixels, weight, rows):
    bf16 = jnp.bfloat16
    dma = pltpu.SemaphoreType.DMA
    return pl.pallas_call(
        gather_kernel,
        out_shape=[
            jax.ShapeDtypeStruct((2, 2, 4, 2, rows, 128), bf16),
            jax.ShapeDtypeStruct((1, HEAD, pixels.shape[2]), pixels.dtype),
            jax.ShapeDtypeStruct(weight.shape, bf16),
        ],
        in_specs=[pl.BlockSpec(memory_space=pltpu.VMEM)] + [pl.BlockSpec(memory_space=pl.ANY)] * 2,
        out_specs=[pl.BlockSpec(memory_space=pl.ANY)] * 3,
        scratch_shapes=[
            pltpu.VMEM((rows, 128), bf16),
            pltpu.VMEM(weight.shape, jnp.float32),
            pltpu.VMEM(weight.shape, bf16),
            dma((2,)),
            dma((2,)),
            dma, dma((3, NC)), dma((3, NC)), dma((3, NC)), dma((4, NC)), dma((4, NC)), dma((4, NC))],
        compiler_params=pltpu.CompilerParams(collective_id=0, has_side_effects=True, vmem_limit_bytes=60 << 20),
        name="gather_packed",
    )(own, pixels, weight)


def reduce_kernel(part_ref, sum_ref, own, twin_in, third_in, second_in, line_in, load_sem, twin_send, twin_recv, third_send, third_recv, second_send, second_recv, line_send, line_recv):
    f32, bf16 = jnp.float32, jnp.bfloat16
    y, c, z, x = spot()
    (x2, y2), (x3, y3), around, second, third, twin = partners()
    rows = sum_ref.shape[0] // NC

    def cut(k):
        return pl.ds(k * rows, rows)

    spots = ((1 - y, 1 - x), (y3, x3), (y2, x2), (y, x))
    turned = ((1 - y, 1 - x), (y2, x2), (y3, x3), (y, x))

    def load(j, k):
        yy, xx = spots[j]
        return pltpu.make_async_copy(part_ref.at[yy, c, :, xx, cut(k)], own.at[j, :, cut(k)], load_sem.at[j, k])

    def swap(j, k):
        yy, xx = turned[j]
        return remote(part_ref.at[yy, 1 - c, :, xx, cut(k)], twin_in.at[j, :, cut(k)], twin_send.at[j, k], twin_recv.at[j, k], twin)

    def to_third(j, k):
        return remote(own.at[j, :, cut(k)], third_in.at[j, :, cut(k)], third_send.at[j, k], third_recv.at[j, k], third)

    def to_second(k):
        return remote(own.at[2, :, cut(k)], second_in.at[:, cut(k)], second_send.at[k], second_recv.at[k], second)

    def to_line(d, k):
        return remote(own.at[3, (z + d) % 4, cut(k)], line_in.at[d - 1, cut(k)], line_send.at[d - 1, k], line_recv.at[d - 1, k], around[d - 1])

    for k in range(NC):
        for j in range(4):
            load(j, k).start()
    greet(around + [second, third, twin])
    for k in range(NC):
        for j in range(4):
            swap(j, k).start()

    def pair(j, k):
        load(j, k).wait()
        swap(j, k).wait_recv()
        return own[j, :, cut(k)].astype(f32) + twin_in[j, :, cut(k)].astype(f32)

    for step in range(NC + 3):
        k = step
        if k < NC:
            for j in (0, 1):
                own[j, :, cut(k)] = pair(j, k).astype(bf16)
                to_third(j, k).start()
        k = step - 1
        if 0 <= k < NC:
            held = pair(2, k)
            to_third(0, k).wait_recv()
            own[2, :, cut(k)] = (held + third_in[0, :, cut(k)].astype(f32)).astype(bf16)
            to_second(k).start()
        k = step - 2
        if 0 <= k < NC:
            held = pair(3, k)
            to_third(1, k).wait_recv()
            to_second(k).wait_recv()
            held += third_in[1, :, cut(k)].astype(f32) + second_in[:, cut(k)].astype(f32)
            own[3, :, cut(k)] = held.astype(bf16)
            for d in (1, 2, 3):
                to_line(d, k).start()
        k = step - 3
        if 0 <= k < NC:
            total = own[3, z, cut(k)].astype(f32)
            for d in (1, 2, 3):
                to_line(d, k).wait_recv()
                total += line_in[d - 1, cut(k)].astype(f32)
            sum_ref[cut(k)] = total
    for k in range(NC):
        for j in range(4):
            swap(j, k).wait_send()
        for j in (0, 1):
            to_third(j, k).wait_send()
        to_second(k).wait_send()
        for d in (1, 2, 3):
            to_line(d, k).wait_send()


def reduce_packed(part):
    rows = part.shape[-2]
    bf16 = jnp.bfloat16
    dma = pltpu.SemaphoreType.DMA
    return pl.pallas_call(
        reduce_kernel,
        out_shape=jax.ShapeDtypeStruct((rows, 128), jnp.float32),
        in_specs=[pl.BlockSpec(memory_space=pl.ANY)],
        out_specs=pl.BlockSpec(memory_space=pltpu.VMEM),
        scratch_shapes=[
            pltpu.VMEM((4, 4, rows, 128), bf16),
            pltpu.VMEM((4, 4, rows, 128), bf16),
            pltpu.VMEM((2, 4, rows, 128), bf16),
            pltpu.VMEM((4, rows, 128), bf16),
            pltpu.VMEM((3, rows, 128), bf16),
            dma((4, NC)), dma((4, NC)), dma((4, NC)), dma((2, NC)), dma((2, NC)), dma((NC,)), dma((NC,)), dma((3, NC)), dma((3, NC)),
        ],
        compiler_params=pltpu.CompilerParams(collective_id=1, has_side_effects=True, vmem_limit_bytes=56 << 20),
        name="reduce_packed",
    )(part)


CHUNK = 16


def over_x(k):
    return k % 2 == 0


def quad_peers():
    y, c, z, x = spot()
    low = z % 2
    side = place(y, c, z, 1 - x)
    along = place(y, c, z + 1 - 2 * low, x)
    twin = place(y, 1 - c, z, x)
    partner = place(y, 1 - c, (z + 2) % 4, x)
    moved = (c + z // 2) % 2 == 1
    return y, c, z, x, low, side, along, twin, partner, moved


def swap_group(value, flip):
    return lax.ppermute(value, "group", [(j, j ^ flip) for j in range(4)])


def swap_images(value):
    pairs = []
    for y in range(2):
        for c in range(2):
            for z in range(4):
                for x in range(2):
                    other = (1 - c, (z + 2) % 4) if c != z // 2 else (c, z)
                    pairs.append((((y * 2 + c) * 4 + z) * 2 + x, ((y * 2 + other[0]) * 4 + other[1]) * 2 + x))
    return lax.ppermute(value, ("group", "img"), pairs)


def share_kernel(shaped_ref, mask_ref, own_slab, twin_slab, over_slab, far_slab, pixel_ref, head_ref, rest_ref,
                 all_ref, masked_ref, stream_ref, made_ref, master, turned, held, top, bottom, tile, mixed, order, slab_sem, pixel_sem, store_sem, keep_sem, swap_send, swap_recv,
                 side_send, side_recv, along_send, along_recv, far_send, far_recv, twin_send, twin_recv):
    f32, bf16 = jnp.float32, jnp.bfloat16
    y, c, z, x, low, side, along, twin, partner, moved = quad_peers()
    dims, width = made_ref.shape
    count = dims // CHUNK
    group = 8 * CHUNK

    def cut(k):
        return pl.ds(k * CHUNK, CHUNK)

    def block(core, j, k):
        return held.at[2 * core + (low + j // 2) % 2, (x + j % 2) % 2, cut(k)]

    def keep(k):
        return pltpu.make_async_copy(made_ref.at[cut(k)], block(c, 0, k), keep_sem.at[k])

    def swap(k):
        return remote(made_ref.at[cut(k)], block(1 - c, 0, k), swap_send.at[k], swap_recv.at[k], partner)

    def swap_in(k):
        return remote(made_ref.at[cut(k)], block(c, 0, k), swap_send.at[k], swap_recv.at[k], partner)

    def to_side(k):
        return remote(block(c, 0, k), block(c, 0, k), side_send.at[k], side_recv.at[k], side)

    def from_side(k):
        return remote(block(c, 1, k), block(c, 1, k), side_send.at[k], side_recv.at[k], side)

    def to_along(k):
        return remote(block(c, 0, k), block(c, 0, k), along_send.at[k], along_recv.at[k], along)

    def from_along(k):
        return remote(block(c, 2, k), block(c, 2, k), along_send.at[k], along_recv.at[k], along)

    def pass_on(k):
        j, to = (2, side) if over_x(k) else (1, along)
        return remote(block(c, j, k), block(c, j, k), far_send.at[k], far_recv.at[k], to)

    def from_far(k):
        return remote(block(c, 3, k), block(c, 3, k), far_send.at[k], far_recv.at[k], twin)

    def give(j, k):
        return remote(block(c, j, k), block(c, j, k), twin_send.at[j, k], twin_recv.at[j, k], twin)

    def given(j, k):
        return remote(block(1 - c, j, k), block(1 - c, j, k), twin_send.at[j, k], twin_recv.at[j, k], twin)

    def slabs(k):
        lanes = pl.ds(k * CHUNK * PATCH, CHUNK * PATCH)
        copies = []
        for j, slab in enumerate((own_slab, twin_slab, over_slab, far_slab)):
            owner = (y + j // 2) % 2 * 2 + (c + j % 2) % 2
            place_rows = pl.ds(pl.multiple_of(owner * slab.shape[0], slab.shape[0]), slab.shape[0])
            copies.append(pltpu.make_async_copy(slab.at[:, lanes], master.at[k % 2, place_rows], slab_sem.at[k % 2, j]))
        return copies

    def make(k):
        for copy in slabs(k):
            copy.wait()
        spread_bands(own_bands(shaped_ref), master.at[k % 2], turned, made_ref.at[cut(k)])
        if k + 2 < count:
            for copy in slabs(k + 2):
                copy.start()

        @pl.when(moved)
        def _():
            swap(k).start()

        @pl.when(jnp.logical_not(moved))
        def _():
            keep(k).start()

    def store(k):
        return pltpu.make_async_copy(held.at[:, :, cut(k)], all_ref.at[:, :, cut(k)], store_sem.at[k])

    swapped = pltpu.make_async_copy(head_ref.at[0], top, pixel_sem.at[0])
    owned = pltpu.make_async_copy(pixel_ref.at[0, pl.ds(0, HEAD)], top, pixel_sem.at[0])
    lower = pltpu.make_async_copy(rest_ref.at[0], bottom, pixel_sem.at[1])

    for k in (0, 1):
        for copy in slabs(k):
            copy.start()

    @pl.when(jnp.logical_not(moved))
    def _():
        owned.start()

    @pl.when(moved)
    def _():
        swapped.start()

    lower.start()
    greet([side, along, twin, partner])
    make(0)

    def mask_pixels(part):
        @pl.when(part == 0)
        def _():
            lower.wait()
            owned.wait()

        def some(j, carry):
            lanes = pl.ds(pl.multiple_of(j * 1024, 1024), 1024)
            mask = mask_ref[:, lanes]
            masked_ref[0:HEAD, lanes] = (top[:, lanes].astype(f32) * mask).astype(bf16)
            tile[...] = jnp.zeros_like(tile)
            tile[0 : bottom.shape[0], :] = bottom[:, lanes].astype(f32) * mask
            masked_ref[HEAD:, lanes] = tile[...].astype(bf16)
            return carry

        cuts = width // 1024
        lax.fori_loop(part * (cuts // 2), (part + 1) * (cuts // 2), some, 0)

    def make_order():
        row = lax.broadcasted_iota(jnp.int32, order.shape, 0)
        column = lax.broadcasted_iota(jnp.int32, order.shape, 1)
        wanted = row % group // CHUNK * dims + row // group * CHUNK + row % CHUNK
        order[...] = jnp.where(column == wanted, 1.0, 0.0)

    for step in range(count + 3):
        k = step
        if k < count:

            @pl.when(moved)
            def _(k=k):
                swap_in(k).wait_recv()

            @pl.when(jnp.logical_not(moved))
            def _(k=k):
                keep(k).wait()

            to_side(k).start()
            to_along(k).start()
            give(0, k).start()
        if step + 1 < count:
            make(step + 1)
        if step in (1, 2):
            mask_pixels(step - 1)
        elif step == 3:
            make_order()
        k = step - 1
        if 0 <= k < count:
            if over_x(k):
                from_along(k).wait_recv()
                pass_on(k).start()
                from_side(k).wait_recv()
            else:
                from_side(k).wait_recv()
                pass_on(k).start()
                from_along(k).wait_recv()
            give(1, k).start()
            give(2, k).start()
        k = step - 2
        if 0 <= k < count:
            from_far(k).wait_recv()
            give(3, k).start()
        k = step - 3
        if 0 <= k < count:
            for j in range(4):
                given(j, k).wait_recv()
            store(k).start()
            part = held[:, :, cut(k), :].reshape(group, width)
            mixed[:, k * group : (k + 1) * group] = dot_nt(masked_ref[...], part)

    stream_ref[...] = finer(mixed[...], order[...], 1, 0)[0 : stream_ref.shape[0]]

    @pl.when(moved)
    def _():
        for k in range(count):
            swap(k).wait_send()

    for k in range(count):
        to_side(k).wait_send()
        to_along(k).wait_send()
        pass_on(k).wait_send()
        store(k).wait()
        for j in range(4):
            give(j, k).wait_send()


def share_kernels(shaped, mask, slabs, pixels, head, rest):
    dims, width = slabs[0].shape[1] // PATCH, mask.shape[1]
    bf16 = jnp.bfloat16
    count = dims // CHUNK
    seq = pixels.shape[1]
    rows = tall(seq)
    f32 = jnp.float32
    dma = pltpu.SemaphoreType.DMA
    vmem, far = pl.BlockSpec(memory_space=pltpu.VMEM), pl.BlockSpec(memory_space=pl.ANY)
    shared, masked, stream = pl.pallas_call(
        share_kernel,
        out_shape=[
            jax.ShapeDtypeStruct((4, 2, dims, width), bf16),
            jax.ShapeDtypeStruct((rows, width), bf16),
            jax.ShapeDtypeStruct((seq, 8 * dims), f32),
        ],
        in_specs=[vmem, vmem] + [far] * 7,
        out_specs=[far, vmem, vmem],
        scratch_shapes=[
            pltpu.VMEM((dims, width), bf16),
            pltpu.VMEM((2, E, CHUNK * PATCH), bf16),
            pltpu.VMEM((2 * NB * CHUNK, 128), f32),
            pltpu.VMEM((4, 2, dims, width), bf16),
            pltpu.VMEM((HEAD, width), bf16),
            pltpu.VMEM((seq - HEAD, width), bf16),
            pltpu.VMEM((rows - HEAD, 1024), f32),
            pltpu.VMEM((rows, 8 * dims), f32),
            pltpu.VMEM((8 * dims, 8 * dims), f32),
            dma((2, 4)),
            dma((2,)),
        ]
        + [dma((count,))] * 10
        + [dma((4, count))] * 2,
        compiler_params=pltpu.CompilerParams(collective_id=2, has_side_effects=True, vmem_limit_bytes=60 << 20),
        name="share_kernels",
    )(shaped, mask, *slabs, pixels, head, rest)
    return shared.reshape(8 * dims, width), masked, stream


def fold_kernel(masked_ref, mask_ref, low_ref, kernel_ref, all_ref, back_ref,
                gone, own, twin_in, relay_in, side_in, along_in, tiles, backs, tile_sem, back_sem, keep_sem, twin_send, twin_recv,
                relay_send, relay_recv, side_send, side_recv, along_send, along_recv, swap_send, swap_recv,
                group_send, group_recv, give_send, give_recv):
    f32, bf16 = jnp.float32, jnp.bfloat16
    y, c, z, x, low, side, along, twin, partner, moved = quad_peers()
    over = place(1 - y, c, z, x)
    dims, width = all_ref.shape[2], all_ref.shape[3]
    count = dims // CHUNK
    seq = back_ref.shape[1]
    lane = tiles.shape[2]

    def cut(k):
        return pl.ds(k * CHUNK, CHUNK)

    def spot_of(j):
        return (low + j // 2) % 2, (x + j % 2) % 2

    def mine(j, k):
        a, b = spot_of(j)
        return own.at[a, b, cut(k)]

    def swap(k):
        return remote(gone.at[:, :, cut(k)], twin_in.at[:, :, cut(k)], twin_send.at[k], twin_recv.at[k], twin)

    def relay(k):
        return remote(mine(3, k), relay_in.at[cut(k)], relay_send.at[k], relay_recv.at[k], along if over_x(k) else side)

    def to_side(k):
        return remote(mine(1, k), side_in.at[cut(k)], side_send.at[k], side_recv.at[k], side)

    def to_along(k):
        return remote(mine(2, k), along_in.at[cut(k)], along_send.at[k], along_recv.at[k], along)

    def keep(k):
        return pltpu.make_async_copy(mine(0, k), all_ref.at[y, c, cut(k)], keep_sem.at[k])

    def move(k):
        return remote(mine(0, k), all_ref.at[y, 1 - c, cut(k)], swap_send.at[k], swap_recv.at[k], partner)

    def moved_in(k):
        return remote(mine(0, k), all_ref.at[y, c, cut(k)], swap_send.at[k], swap_recv.at[k], partner)

    def cross(k):
        return remote(all_ref.at[y, c, cut(k)], all_ref.at[y, c, cut(k)], group_send.at[k], group_recv.at[k], over)

    def crossed(k):
        return remote(all_ref.at[1 - y, c, cut(k)], all_ref.at[1 - y, c, cut(k)], group_send.at[k], group_recv.at[k], over)

    def give(j, k):
        here = all_ref.at[(y + j) % 2, c, cut(k)]
        return remote(here, here, give_send.at[j, k], give_recv.at[j, k], twin)

    def given(j, k):
        here = all_ref.at[(y + j) % 2, 1 - c, cut(k)]
        return remote(here, here, give_send.at[j, k], give_recv.at[j, k], twin)

    def fetch(j):
        return pltpu.make_async_copy(kernel_ref.at[:, pl.ds(j * lane, lane)], tiles.at[j % 2], tile_sem.at[j % 2])

    def drain(j):
        return pltpu.make_async_copy(backs.at[j % 2], back_ref.at[0, :, pl.ds(j * lane, lane)], back_sem.at[j % 2])

    def half(core, out):
        chosen = low_ref[:, pl.ds(pl.multiple_of(core * 4 * dims, 128), 4 * dims)]

        def some(j, carry):
            lanes = pl.ds(pl.multiple_of(j * 1024, 1024), 1024)
            part = dot_tn(chosen, masked_ref[:, lanes]).astype(bf16)
            out[:, :, :, lanes] = part.reshape(2, 2, dims, 1024)
            return carry

        lax.fori_loop(0, width // 1024, some, 0)

    def pixels_back(j):
        fetch(j).wait()
        if j >= 2:
            drain(j - 2).wait()
        part = dot_nn(low_ref[...], tiles[j % 2])[0:seq] * mask_ref[:, j * lane : (j + 1) * lane]
        backs[j % 2] = part.astype(bf16)
        drain(j).start()
        if (j + 2) * lane < width:
            fetch(j + 2).start()

    def pair(j, k):
        a, b = spot_of(j)
        return own[a, b, cut(k)].astype(f32) + twin_in[a, b, cut(k)].astype(f32)

    def put(j, k, value):
        a, b = spot_of(j)
        own[a, b, cut(k)] = value.astype(bf16)

    fetch(0).start()
    fetch(1).start()
    greet([side, along, twin, partner, over])
    half(1 - c, gone)
    for k in range(count):
        swap(k).start()
    half(c, own)

    for step in range(count + 4):
        k = step
        if k < count:
            swap(k).wait_recv()
            put(3, k, pair(3, k))
            relay(k).start()
        k = step - 1
        if 0 <= k < count:
            first, second = (to_along, to_side) if over_x(k) else (to_side, to_along)
            plain, summed = (2, 1) if over_x(k) else (1, 2)
            put(plain, k, pair(plain, k))
            first(k).start()
            relay(k).wait_recv()
            put(summed, k, pair(summed, k) + relay_in[cut(k)].astype(f32))
            second(k).start()
        k = step - 2
        if 0 <= k < count:
            to_side(k).wait_recv()
            to_along(k).wait_recv()
            put(0, k, pair(0, k) + side_in[cut(k)].astype(f32) + along_in[cut(k)].astype(f32))

            @pl.when(moved)
            def _(k=k):
                move(k).start()

            @pl.when(jnp.logical_not(moved))
            def _(k=k):
                keep(k).start()

        k = step - 3
        if 0 <= k < count:

            @pl.when(moved)
            def _(k=k):
                moved_in(k).wait_recv()

            @pl.when(jnp.logical_not(moved))
            def _(k=k):
                keep(k).wait()

            cross(k).start()
            give(0, k).start()
        k = step - 4
        if 0 <= k < count:
            crossed(k).wait_recv()
            give(1, k).start()
        if step >= 2 and (step - 2) * lane < width:
            pixels_back(step - 2)

    @pl.when(moved)
    def _():
        for k in range(count):
            move(k).wait_send()

    for j in (width // lane - 2, width // lane - 1):
        drain(j).wait()
    for k in range(count):
        swap(k).wait_send()
        relay(k).wait_send()
        to_side(k).wait_send()
        to_along(k).wait_send()
        cross(k).wait_send()
        for j in range(2):
            give(j, k).wait_send()
            given(j, k).wait_recv()


def fold_kernels(masked, mask, low, kernels, seq):
    width = masked.shape[1]
    dims = kernels.shape[0] // 8
    count = dims // CHUNK
    bf16 = jnp.bfloat16
    dma = pltpu.SemaphoreType.DMA
    vmem, far = pl.BlockSpec(memory_space=pltpu.VMEM), pl.BlockSpec(memory_space=pl.ANY)
    folded, back = pl.pallas_call(
        fold_kernel,
        out_shape=[
            jax.ShapeDtypeStruct((2, 2, dims, width), bf16),
            jax.ShapeDtypeStruct((1, seq, width), bf16),
        ],
        in_specs=[vmem, vmem, vmem, far],
        out_specs=[far, far],
        scratch_shapes=[
            pltpu.VMEM((2, 2, dims, width), bf16),
            pltpu.VMEM((2, 2, dims, width), bf16),
            pltpu.VMEM((2, 2, dims, width), bf16),
            pltpu.VMEM((dims, width), bf16),
            pltpu.VMEM((dims, width), bf16),
            pltpu.VMEM((dims, width), bf16),
            pltpu.VMEM((2, 8 * dims, 1024), bf16),
            pltpu.VMEM((2, seq, 1024), bf16),
            dma((2,)),
            dma((2,)),
            dma((count,)),
        ]
        + [dma((count,))] * 12
        + [dma((2, count))] * 2,
        compiler_params=pltpu.CompilerParams(collective_id=3, has_side_effects=True, vmem_limit_bytes=60 << 20),
        name="fold_kernels",
    )(masked, mask, low, kernels)
    return folded.reshape(4, dims, width), back


def on_device(
    pixels,
    band_mask,
    wavelength,
    owner_order,
    rest_weight,
    rest_moment1,
    rest_moment2,
    fc_weight,
    fc_moment1,
    fc_moment2,
    cotangent,
):
    f32 = jnp.float32
    bf16 = jnp.bfloat16
    kernel_rate = float(E * PATCH * NB) ** (-0.5)
    groups = lax.axis_size("group")
    own_rows = rest_weight.shape[0]
    own_blocks = own_rows // 8
    fits = lax.axis_size("group") == 4 and lax.axis_size("img") == 8
    extra = -own_rows % 128
    slot_blocks = (own_rows + extra) // 8
    mask = band_mask.astype(f32)
    if fits:
        mask = swap_images(mask)
        gathered, head, low_weight = gather_packed(rest_weight, pixels, fc_weight, own_rows + extra)
        gathered, rest, cotangent, low_weight = lax.optimization_barrier(
            (gathered, pixels[:, HEAD:], cotangent, low_weight)
        )
        across = swap_group(low_weight, 2)
        rest, cotangent = swap_images(rest), swap_images(cotangent)
    else:
        low_weight = fc_weight.astype(bf16)
        rest_low = jnp.pad(rest_weight.astype(bf16), ((0, extra), (0, 0)))
        gathered = lax.all_gather(rest_low, ("group", "img"), axis=0, tiled=True)
    shards = gathered.size // ((own_rows + extra) * 128)
    gathered = gathered.reshape(shards, own_rows + extra, 128)
    total_blocks = owner_order.shape[0]
    slots = jnp.pad(
        owner_order.reshape(shards, own_blocks),
        ((0, 0), (0, slot_blocks - own_blocks)),
        constant_values=total_blocks,
    ).reshape(-1)
    unpacked = spread_packed(gathered, slots, total_blocks)
    if fits:
        *unpacked, across = lax.optimization_barrier((*unpacked, across))
        slabs = [low_weight, swap_group(low_weight, 1), across, swap_group(across, 1)]
    else:
        master = lax.all_gather(low_weight, "group", axis=0, tiled=True)
    block_mats, wave_mats = unpacked[:4], unpacked[4:10]
    block_vectors, wave_vectors = unpacked[10:]
    embedded = embed_waves(wavelength).reshape(groups * NB, E)
    shaped_low, own_shaped, kept, slope = wave_layer(embedded, wave_mats, wave_vectors)
    mask = jnp.repeat(mask, PATCH, axis=1)
    if fits:
        kernel_all, masked, stream = share_kernels(shaped_low, mask, slabs, pixels, head, rest)
    else:
        kernel_low = make_kernels(shaped_low, master)
        kernel_all = lax.all_gather(kernel_low, "img", axis=0, tiled=True)
        stream = embed_patches(pixels, mask, kernel_all)
        masked = jnp.pad((pixels[0] * mask).astype(bf16), ((0, tall(pixels.shape[1]) - pixels.shape[1]), (0, 0)))
    block_out, grad_low, block_vectors, *block_grads = block_pass(
        stream, cotangent, block_vectors, *block_mats
    )
    if fits:
        all_groups, pixel_grad = fold_kernels(masked, mask, grad_low, kernel_all, pixels.shape[1])
        all_groups, block_out, pixel_grad = lax.optimization_barrier((all_groups, block_out, pixel_grad))
        block_out, pixel_grad = swap_images(block_out), swap_images(pixel_grad)
    else:
        pixel_grad, kernel_grad = unembed_patches(masked, mask, kernel_all, grad_low, pixels.shape[1])
        kernel_grad_low = lax.psum_scatter(kernel_grad, "img", scatter_dimension=0, tiled=True)
        all_groups = lax.all_gather(kernel_grad_low[None], "group", axis=0, tiled=True)
    fc_new, fc_first, fc_second, shaped_part = master_update(
        all_groups,
        own_shaped,
        fc_weight,
        fc_moment1,
        fc_moment2,
        kernel_rate,
    )
    *wave_grads, wave_vectors = wave_back(shaped_part, embedded, kept, slope, wave_mats, wave_vectors)
    given = [*block_grads, *wave_grads, block_vectors, wave_vectors]
    joint_term = collect_packed(given, slots, total_blocks, shards, own_rows + extra)
    if fits:
        rest_grad = reduce_packed(joint_term.reshape(2, 2, 4, 2, own_rows + extra, 128))
    else:
        rest_grad = lax.psum_scatter(
            joint_term, ("group", "img"), scatter_dimension=0, tiled=False
        ).astype(f32)
    rest_grad = rest_grad[:own_rows]
    rest_new, rest_first, rest_second = adamw_step(
        rest_weight, rest_moment1, rest_moment2, rest_grad, rest_rate
    )
    return (block_out, pixel_grad, rest_new, rest_first, rest_second, fc_new, fc_first, fc_second)


def solution(mesh):
    placed = (
        P(("group", "img"), None, None),
        P(("group", "img"), None),
        P(),
        P(),
        P(("group", "img"), None),
        P(("group", "img"), None),
        P(("group", "img"), None),
        P("group", "img"),
        P("group", "img"),
        P("group", "img"),
        P(("group", "img"), None),
    )
    return jax.shard_map(
        on_device,
        mesh=mesh,
        in_specs=placed,
        out_specs=(
            P(("group", "img"), None),
            P(("group", "img"), None, None),
            P(("group", "img"), None),
            P(("group", "img"), None),
            P(("group", "img"), None),
            P("group", "img"),
            P("group", "img"),
            P("group", "img"),
        ),
        check_vma=False,
    )
```

```python
import functools
import math

import jax
import jax.numpy as jnp
from jax import lax
from jax.experimental import pallas as pl
from jax.experimental.pallas import tpu as pltpu
from jax.sharding import PartitionSpec as P

MESH = pl.DeviceIdType.MESH

D = 768
HEADS = 12
HD = 64
HID = 3072
E = 128
HH = 4
HFF = 2048
PATCH = 256
NB = 32
STEP = 5


beta_one = 0.5
beta_two = 0.75
decay_rate = 0.05
epsilon_add = 1e-08
rest_rate = 0.02


def layout():
    return [
        ("w_qkv", (D, 3 * D)),
        ("w_out", (D, D)),
        ("w_up", (D, HID)),
        ("w_down", (HID, D)),
        ("h_query", (E, E)),
        ("h_key", (E, E)),
        ("h_value", (E, E)),
        ("h_out", (E, E)),
        ("h_ffin", (E, HFF)),
        ("h_ffout", (HFF, E)),
        ("ln1_gain", (D,)),
        ("ln1_shift", (D,)),
        ("ln2_gain", (D,)),
        ("ln2_shift", (D,)),
        ("patch_bias", (D,)),
        ("hn1_gain", (E,)),
        ("hn1_shift", (E,)),
        ("hn2_gain", (E,)),
        ("hn2_shift", (E,)),
    ]


def embed_waves(wavelength):
    half_width = E // 2
    frequency = jnp.exp(-math.log(10000.0) * jnp.arange(half_width, dtype=jnp.float32) / half_width)
    angles = wavelength.astype(jnp.float32)[..., None] * frequency
    return jnp.concatenate([jnp.sin(angles), jnp.cos(angles)], axis=-1)


def matrices():
    listed, at = [], 0
    for name, extent in layout():
        if len(extent) == 2:
            listed.append((name, extent[0], extent[1], at))
        at += math.prod(extent) // 128
    return listed


def vector_places():
    listed, at = [], 0
    rows = [0, 0]
    for name, extent in layout():
        if len(extent) == 1:
            kind = 0 if extent[0] == D else 1
            for j in range(extent[0] // 128):
                listed.append((at + j, kind, rows[kind], j * 128))
            rows[kind] += 1
        at += math.prod(extent) // 128
    return listed


def vector_shapes():
    return [jax.ShapeDtypeStruct((8, D), jnp.float32), jax.ShapeDtypeStruct((8, E), jnp.float32)]


def shards_a_step(shards, wanted):
    return wanted if shards % wanted == 0 else 1


def spread_kernel(order_ref, low_ref, *refs):
    big, small = matrices()[:4], matrices()[4:]
    far, outs, linear, kept, sem = refs[:4], refs[4:12], refs[12], refs[13:17], refs[17]
    step = pl.program_id(0)
    shards, rows = low_ref.shape[0], low_ref.shape[1]

    for shard in range(shards):

        def two(j, carry, shard=shard):
            pair = low_ref[shard, pl.ds(pl.multiple_of(j * 16, 16), 16), :].astype(jnp.float32)
            for half in range(2):
                block = order_ref[(step * shards + shard) * (rows // 8) + j * 2 + half]
                linear[pl.ds(pl.multiple_of(block * 8, 8), 8), :] = pair[half * 8 : half * 8 + 8]
            return carry

        lax.fori_loop(0, rows // 16, two, 0, unroll=8)

    @pl.when(step == pl.num_programs(0) - 1)
    def _():
        def relay(height, width, first, out):
            lanes = width // 128

            def some(j, carry):
                top = pl.multiple_of(j * 128, 128)
                for lane in range(lanes):
                    part = linear[pl.ds(first + top * lanes + lane, 128, stride=lanes), :]
                    out[pl.ds(top, 128), lane * 128 : lane * 128 + 128] = part.astype(out.dtype)
                return carry

            lax.fori_loop(0, height // 128, some, 0)

        copies = []
        for j, (name, height, width, first) in enumerate(big):
            relay(height, width, first, kept[j])
            copies.append(pltpu.make_async_copy(kept[j], far[j], sem.at[j]))
            copies[-1].start()
        for (name, height, width, first), out in zip(small, outs):
            relay(height, width, first, out)
        for out in outs[-2:]:
            out[...] = jnp.zeros_like(out)
        for row, kind, top, lane in vector_places():
            outs[kind - 2][top : top + 1, lane : lane + 128] = linear[row : row + 1, :]
        for copy in copies:
            copy.wait()


def spread_packed(gathered, slots, blocks):
    shards, rows = gathered.shape[0], gathered.shape[1]
    some = shards_a_step(shards, 4)
    big = [jax.ShapeDtypeStruct((height, width), jnp.bfloat16) for name, height, width, first in matrices()[:4]]
    small = [jax.ShapeDtypeStruct((height, width), jnp.float32) for name, height, width, first in matrices()[4:]]
    small += vector_shapes()
    return pl.pallas_call(
        spread_kernel,
        out_shape=big + small,
        grid_spec=pltpu.PrefetchScalarGridSpec(
            num_scalar_prefetch=1,
            grid=(shards // some,),
            in_specs=[pl.BlockSpec((some, rows, 128), lambda s, order: (s, 0, 0))],
            out_specs=[pl.BlockSpec(memory_space=pl.ANY) for shape in big]
            + [pl.BlockSpec(shape.shape, lambda s, order: (0, 0), pipeline_mode=pl.Buffered(1)) for shape in small],
            scratch_shapes=[pltpu.VMEM(((blocks + 1) * 8, 128), jnp.float32)]
            + [pltpu.VMEM(shape.shape, shape.dtype) for shape in big]
            + [pltpu.SemaphoreType.DMA((4,))],
        ),
        compiler_params=pltpu.CompilerParams(vmem_limit_bytes=60 << 20),
        name="spread_packed",
    )(slots, gathered)


def collect_kernel(order_ref, *refs):
    big, small = matrices()[:4], matrices()[4:]
    far, ins, low_ref, linear, kept, sem = refs[:4], refs[4:12], refs[12], refs[13], refs[14:18], refs[18]
    step = pl.program_id(0)
    shards, rows = low_ref.shape[0], low_ref.shape[1]

    @pl.when(step == 0)
    def _():
        copies = [pltpu.make_async_copy(far[j], kept[j], sem.at[j]) for j in range(4)]
        for copy in copies:
            copy.start()

        def relay(height, width, first, given):
            lanes = width // 128

            def some(j, carry):
                top = pl.multiple_of(j * 128, 128)
                for lane in range(lanes):
                    part = given[pl.ds(top, 128), lane * 128 : lane * 128 + 128]
                    linear[pl.ds(first + top * lanes + lane, 128, stride=lanes), :] = part.astype(jnp.float32)
                return carry

            lax.fori_loop(0, height // 128, some, 0)

        for (name, height, width, first), given in zip(small, ins):
            relay(height, width, first, given)
        first = vector_places()[0][0]
        linear[first:, :] = jnp.zeros((linear.shape[0] - first, 128), jnp.float32)
        for row, kind, top, lane in vector_places():
            linear[row : row + 1, :] = ins[kind - 2][top : top + 1, lane : lane + 128]
        for j, (name, height, width, first) in enumerate(big):
            copies[j].wait()
            relay(height, width, first, kept[j])

    for shard in range(shards):

        def two(j, carry, shard=shard):
            parts = []
            for half in range(2):
                block = order_ref[(step * shards + shard) * (rows // 8) + j * 2 + half]
                parts.append(linear[pl.ds(pl.multiple_of(block * 8, 8), 8), :])
            low_ref[shard, pl.ds(pl.multiple_of(j * 16, 16), 16), :] = jnp.concatenate(parts, axis=0).astype(low_ref.dtype)
            return carry

        lax.fori_loop(0, rows // 16, two, 0, unroll=20)


def collect_packed(grads, slots, blocks, shards, rows):
    some = shards_a_step(shards, 2)
    whole = [pl.BlockSpec(grad.shape, lambda s, order: (0, 0), pipeline_mode=pl.Buffered(1)) for grad in grads[4:]]
    return pl.pallas_call(
        collect_kernel,
        out_shape=jax.ShapeDtypeStruct((shards, rows, 128), jnp.bfloat16),
        grid_spec=pltpu.PrefetchScalarGridSpec(
            num_scalar_prefetch=1,
            grid=(shards // some,),
            in_specs=[pl.BlockSpec(memory_space=pl.ANY)] * 4 + whole,
            out_specs=pl.BlockSpec((some, rows, 128), lambda s, order: (s, 0, 0)),
            scratch_shapes=[pltpu.VMEM(((blocks + 1) * 8, 128), jnp.float32)]
            + [pltpu.VMEM(grad.shape, grad.dtype) for grad in grads[:4]]
            + [pltpu.SemaphoreType.DMA((4,))],
        ),
        compiler_params=pltpu.CompilerParams(vmem_limit_bytes=60 << 20),
        name="collect_packed",
    )(slots, *grads)


def finer(a, b, left, right):
    return lax.dot_general(
        a, b, (((left,), (right,)), ((), ())), precision=lax.Precision.HIGH, preferred_element_type=jnp.float32
    )


def unit_scale(values):
    center = values - jnp.mean(values, axis=-1, keepdims=True)
    scale = lax.rsqrt(jnp.mean(center * center, axis=-1, keepdims=True) + 1e-06)
    return center * scale, scale


def unit_back(grad, unit, scale, gain):
    inner = grad * gain
    return scale * (
        inner - jnp.mean(inner, axis=-1, keepdims=True) - unit * jnp.mean(inner * unit, axis=-1, keepdims=True)
    )


def wave_kernel(embed_ref, wq_ref, wk_ref, wv_ref, wo_ref, win_ref, wout_ref, vec_ref, shaped_ref, own_ref, kept_ref, slope_ref):
    rows = embed_ref.shape[0]
    groups = rows // NB
    embedded = embed_ref[...]
    queries = finer(embedded, wq_ref[...], 1, 0)
    keys = finer(embedded, wk_ref[...], 1, 0)
    values = finer(embedded, wv_ref[...], 1, 0)
    size = E // HH
    across = lax.broadcasted_iota(jnp.int32, (rows, rows), 0) // NB == lax.broadcasted_iota(jnp.int32, (rows, rows), 1) // NB
    mixed = []
    for head in range(HH):
        lanes = slice(head * size, head * size + size)
        scores = finer(queries[:, lanes], keys[:, lanes], 1, 1) * size**-0.5
        scores = jnp.where(across, scores, -1e30)
        weight = jnp.exp(scores - jnp.max(scores, axis=-1, keepdims=True))
        weight = weight / jnp.sum(weight, axis=-1, keepdims=True)
        kept_ref[head] = weight
        mixed.append(finer(weight, values[:, lanes], 1, 0))
    mixed = jnp.concatenate(mixed, axis=1)
    unit_one, scale_one = unit_scale(embedded + finer(mixed, wo_ref[...], 1, 0))
    first = unit_one * vec_ref[0:1, :] + vec_ref[1:2, :]
    inner = finer(first, win_ref[...], 1, 0)
    half = 0.5 * (1.0 + lax.erf(inner * 0.5**0.5))
    slope_ref[0] = inner * half
    slope_ref[1] = half + inner * jnp.exp(-0.5 * inner * inner) * (2.0 * math.pi) ** -0.5
    unit_two, scale_two = unit_scale(first + finer(inner * half, wout_ref[...], 1, 0))
    shaped = (unit_two * vec_ref[2:3, :] + vec_ref[3:4, :] + embedded).astype(jnp.bfloat16)
    for j, part in enumerate((queries, keys, values, mixed, unit_one, unit_two)):
        kept_ref[HH + j] = part
    kept_ref[HH + 6] = jnp.broadcast_to(scale_one, (rows, E))
    kept_ref[HH + 7] = jnp.broadcast_to(scale_two, (rows, E))
    shaped_ref[...] = shaped
    wide = shaped.astype(jnp.float32)
    width = E // groups
    group = lax.axis_index("group")
    own = jnp.zeros((rows, width), jnp.float32)
    for j in range(groups):
        own = jnp.where(group == j, wide[:, j * width : (j + 1) * width], own)
    own_ref[...] = own.astype(jnp.bfloat16)


def wave_layer(embedded, mats, vectors):
    rows = embedded.shape[0]
    groups = rows // NB
    f32, bf16 = jnp.float32, jnp.bfloat16
    return pl.pallas_call(
        wave_kernel,
        out_shape=[
            jax.ShapeDtypeStruct((rows, E), bf16),
            jax.ShapeDtypeStruct((rows, E // groups), bf16),
            jax.ShapeDtypeStruct((HH + 8, rows, E), f32),
            jax.ShapeDtypeStruct((2, rows, HFF), f32),
        ],
        compiler_params=pltpu.CompilerParams(vmem_limit_bytes=60 << 20),
        name="wave_layer",
    )(embedded, *mats, vectors)


def wave_back_kernel(part_ref, embed_ref, kept_ref, slope_ref, wq_ref, wk_ref, wv_ref, wo_ref, win_ref, wout_ref, vec_ref,
                     gq_ref, gk_ref, gv_ref, go_ref, gin_ref, gout_ref, gvec_ref):
    rows = embed_ref.shape[0]
    groups = rows // NB
    width = E // groups
    size = E // HH
    group = lax.axis_index("group")
    spread = jnp.concatenate([part_ref[...]] * groups, axis=1)
    lane = lax.broadcasted_iota(jnp.int32, (rows, E), 1) // width
    grad = jnp.where(lane == group, spread, 0.0)
    embedded = embed_ref[...]
    queries, keys, values, mixed, unit_one, unit_two, scale_one, scale_two = (kept_ref[HH + j] for j in range(8))
    gvec_ref[...] = jnp.zeros_like(gvec_ref)
    gvec_ref[2:3, :] = jnp.sum(grad * unit_two, axis=0, keepdims=True)
    gvec_ref[3:4, :] = jnp.sum(grad, axis=0, keepdims=True)
    grad = unit_back(grad, unit_two, scale_two, vec_ref[2:3, :])
    gout_ref[...] = finer(slope_ref[0], grad, 0, 0)
    inner = finer(grad, wout_ref[...], 1, 1) * slope_ref[1]
    first = unit_one * vec_ref[0:1, :] + vec_ref[1:2, :]
    gin_ref[...] = finer(first, inner, 0, 0)
    grad = grad + finer(inner, win_ref[...], 1, 1)
    gvec_ref[0:1, :] = jnp.sum(grad * unit_one, axis=0, keepdims=True)
    gvec_ref[1:2, :] = jnp.sum(grad, axis=0, keepdims=True)
    grad = unit_back(grad, unit_one, scale_one, vec_ref[0:1, :])
    go_ref[...] = finer(mixed, grad, 0, 0)
    grad = finer(grad, wo_ref[...], 1, 1)
    parts = [[], [], []]
    for head in range(HH):
        lanes = slice(head * size, head * size + size)
        weight = kept_ref[head]
        grad_weight = finer(grad[:, lanes], values[:, lanes], 1, 1)
        parts[2].append(finer(weight, grad[:, lanes], 0, 0))
        score = weight * (grad_weight - jnp.sum(weight * grad_weight, axis=-1, keepdims=True)) * size**-0.5
        parts[0].append(finer(score, keys[:, lanes], 1, 0))
        parts[1].append(finer(score, queries[:, lanes], 0, 0))
    for out, part in zip((gq_ref, gk_ref, gv_ref), parts):
        out[...] = finer(embedded, jnp.concatenate(part, axis=1), 0, 0)


def wave_back(part, embedded, kept, slope, mats, vectors):
    f32 = jnp.float32
    return pl.pallas_call(
        wave_back_kernel,
        out_shape=[jax.ShapeDtypeStruct(mat.shape, f32) for mat in mats] + [jax.ShapeDtypeStruct((8, E), f32)],
        compiler_params=pltpu.CompilerParams(vmem_limit_bytes=60 << 20),
        name="wave_back",
    )(part, embedded, kept, slope, *mats, vectors)


def tall(count):
    return -(-count // 16) * 16


def dot_nn(a, b):
    return lax.dot_general(a, b, (((1,), (0,)), ((), ())), preferred_element_type=jnp.float32)


def dot_nt(a, b):
    return lax.dot_general(a, b, (((1,), (1,)), ((), ())), preferred_element_type=jnp.float32)


def dot_tn(a, b):
    return lax.dot_general(a, b, (((0,), (0,)), ((), ())), preferred_element_type=jnp.float32)


def block_kernel(stream_ref, up_ref, vec_ref, wqkv_hbm, wout_hbm, wup_hbm, wdown_hbm,
                 out_ref, low_ref, gvec_ref, gqkv_hbm, gout_hbm, gup_hbm, gdown_hbm,
                 wqkv, wout, wup, wdown, gqkv, gout, gup, gdown,
                 xs, ups, up_low, norm_one, qkv, att, probs, mid, norm_two, acc, hid_low, datt, dqkv, in_sem, out_sem):
    f32, bf16 = jnp.float32, jnp.bfloat16
    seq = stream_ref.shape[0]
    rows = xs.shape[0]
    loads = [
        pltpu.make_async_copy(src, dst, in_sem.at[j])
        for j, (src, dst) in enumerate(((wqkv_hbm, wqkv), (wout_hbm, wout), (wup_hbm, wup), (wdown_hbm, wdown)))
    ]
    for load in loads:
        load.start()
    stores = [
        pltpu.make_async_copy(src, dst, out_sem.at[j])
        for j, (src, dst) in enumerate(((gqkv, gqkv_hbm), (gout, gout_hbm), (gup, gup_hbm), (gdown, gdown_hbm)))
    ]
    gain_one, shift_one = vec_ref[0:1, :], vec_ref[1:2, :]
    gain_two, shift_two = vec_ref[2:3, :], vec_ref[3:4, :]
    xs[...] = jnp.zeros_like(xs)
    xs[0:seq, :] = stream_ref[...] + vec_ref[4:5, :]
    ups[...] = jnp.zeros_like(ups)
    ups[0:seq, :] = up_ref[...].astype(f32)
    up_low[...] = ups[...].astype(bf16)

    def normed(values):
        center = values - jnp.mean(values, axis=-1, keepdims=True)
        scale = lax.rsqrt(jnp.mean(center * center, axis=-1, keepdims=True) + 1e-06)
        return center * scale, scale

    def normed_back(grad, unit, scale, gain):
        inner = grad * gain
        return scale * (
            inner
            - jnp.mean(inner, axis=-1, keepdims=True)
            - unit * jnp.mean(inner * unit, axis=-1, keepdims=True)
        )

    unit, scale = normed(xs[...])
    norm_one[...] = (unit * gain_one + shift_one).astype(bf16)
    loads[0].wait()

    def tile(j, size=D):
        return pl.ds(pl.multiple_of(j * size, size), size)

    def each(count, body):
        lax.fori_loop(0, count, lambda j, carry: (body(j), carry)[1], 0)

    def qkv_part(j):
        qkv[:, tile(j)] = dot_nn(norm_one[...], wqkv[:, tile(j)]).astype(bf16)

    each(3, qkv_part)
    inside = lax.broadcasted_iota(jnp.int32, (rows, rows), 1) < seq

    def heads(p):
        pair = [qkv[:, pl.ds(pl.multiple_of(j * D + p * 128, 128), 128)] for j in range(3)]
        outs = []
        for h in range(2):
            query, key, value = (part[:, h * HD : h * HD + HD] for part in pair)
            scores = jnp.where(inside, dot_nt(query, key) * (HD**-0.5), -1e30)
            weight = jnp.exp(scores - jnp.max(scores, axis=-1, keepdims=True))
            weight = weight / jnp.sum(weight, axis=-1, keepdims=True)
            probs[p * 2 + h] = weight
            outs.append(dot_nn(weight.astype(bf16), value))
        att[:, pl.ds(pl.multiple_of(p * 128, 128), 128)] = jnp.concatenate(outs, axis=1).astype(bf16)

    each(HEADS // 2, heads)
    loads[1].wait()
    mid[...] = xs[...] + dot_nn(att[...], wout[...])
    unit, scale = normed(mid[...])
    norm_two[...] = (unit * gain_two + shift_two).astype(bf16)
    loads[2].wait()
    loads[3].wait()
    acc[...] = jnp.zeros_like(acc)

    def hidden_part(j):
        hidden = dot_nn(norm_two[...], wup[:, tile(j)])
        half = 0.5 * (1.0 + lax.erf(hidden * (0.5**0.5)))
        active = (hidden * half).astype(bf16)
        slope = half + hidden * jnp.exp(-0.5 * hidden * hidden) * (2.0 * math.pi) ** -0.5
        mid[...] += dot_nn(active, wdown[tile(j), :])
        gdown[tile(j), :] = dot_tn(active, up_low[...]).astype(bf16)
        grad_hidden = (dot_nt(up_low[...], wdown[tile(j), :]) * slope).astype(bf16)
        gup[:, tile(j)] = dot_tn(norm_two[...], grad_hidden).astype(bf16)
        acc[...] += dot_nt(grad_hidden, wup[:, tile(j)])

    kept_unit, kept_scale = unit, scale
    hid_low[...] = kept_unit
    each(HID // D, hidden_part)
    stores[2].start()
    stores[3].start()
    out_ref[...] = mid[0:seq, :].astype(bf16)
    grad = acc[...]
    unit = hid_low[...]
    gvec_ref[...] = jnp.zeros_like(gvec_ref)
    gvec_ref[2:3, :] = jnp.sum(grad * unit, axis=0, keepdims=True)
    gvec_ref[3:4, :] = jnp.sum(grad, axis=0, keepdims=True)
    ups[...] += normed_back(grad, unit, kept_scale, gain_two)
    up_low[...] = ups[...].astype(bf16)
    gout[...] = dot_tn(att[...], up_low[...]).astype(bf16)
    stores[1].start()
    datt[...] = dot_nt(up_low[...], wout[...]).astype(bf16)

    def heads_back(p):
        pair = [qkv[:, pl.ds(pl.multiple_of(j * D + p * 128, 128), 128)] for j in range(3)]
        grad_pair = datt[:, pl.ds(pl.multiple_of(p * 128, 128), 128)]
        grads = [[], [], []]
        for h in range(2):
            query, key, value = (part[:, h * HD : h * HD + HD] for part in pair)
            grad_out = grad_pair[:, h * HD : h * HD + HD]
            weight = probs[p * 2 + h]
            grad_weight = dot_nt(grad_out, value)
            grads[2].append(dot_tn(weight.astype(bf16), grad_out))
            grad_score = weight * (grad_weight - jnp.sum(weight * grad_weight, axis=-1, keepdims=True))
            grad_score = grad_score.astype(bf16)
            grads[0].append(dot_nn(grad_score, key) * (HD**-0.5))
            grads[1].append(dot_tn(grad_score, query) * (HD**-0.5))
        for j in range(3):
            dqkv[:, pl.ds(pl.multiple_of(j * D + p * 128, 128), 128)] = jnp.concatenate(grads[j], axis=1).astype(bf16)

    each(HEADS // 2, heads_back)
    acc[...] = jnp.zeros_like(acc)

    def qkv_back(j):
        gqkv[:, tile(j)] = dot_tn(norm_one[...], dqkv[:, tile(j)]).astype(bf16)
        acc[...] += dot_nt(dqkv[:, tile(j)], wqkv[:, tile(j)])

    each(3, qkv_back)
    stores[0].start()
    unit, scale = normed(xs[...])
    grad = acc[...]
    gvec_ref[0:1, :] = jnp.sum(grad * unit, axis=0, keepdims=True)
    gvec_ref[1:2, :] = jnp.sum(grad, axis=0, keepdims=True)
    total = ups[...] + normed_back(grad, unit, scale, gain_one)
    gvec_ref[4:5, :] = jnp.sum(total, axis=0, keepdims=True)
    low_ref[...] = total.astype(bf16)
    for store in stores:
        store.wait()


def block_pass(stream, upstream, vectors, wqkv, wout, wup, wdown):
    f32, bf16 = jnp.float32, jnp.bfloat16
    seq = stream.shape[0]
    rows = tall(seq)
    whole = pl.BlockSpec(memory_space=pltpu.VMEM)
    far = pl.BlockSpec(memory_space=pl.ANY)
    mats = [wqkv, wout, wup, wdown]
    kept = [pltpu.VMEM(mat.shape, bf16) for mat in mats]
    dma = pltpu.SemaphoreType.DMA
    return pl.pallas_call(
        block_kernel,
        out_shape=[
            jax.ShapeDtypeStruct((seq, D), bf16),
            jax.ShapeDtypeStruct((rows, D), bf16),
            jax.ShapeDtypeStruct((8, D), f32),
        ]
        + [jax.ShapeDtypeStruct(mat.shape, bf16) for mat in mats],
        in_specs=[whole] * 3 + [far] * 4,
        out_specs=[whole] * 3 + [far] * 4,
        scratch_shapes=kept
        + kept
        + [
            pltpu.VMEM((rows, D), f32),
            pltpu.VMEM((rows, D), f32),
            pltpu.VMEM((rows, D), bf16),
            pltpu.VMEM((rows, D), bf16),
            pltpu.VMEM((rows, 3 * D), bf16),
            pltpu.VMEM((rows, D), bf16),
            pltpu.VMEM((HEADS, rows, rows), f32),
            pltpu.VMEM((rows, D), f32),
            pltpu.VMEM((rows, D), bf16),
            pltpu.VMEM((rows, D), f32),
            pltpu.VMEM((rows, D), f32),
            pltpu.VMEM((rows, D), bf16),
            pltpu.VMEM((rows, 3 * D), bf16),
            dma((4,)),
            dma((4,)),
        ],
        compiler_params=pltpu.CompilerParams(vmem_limit_bytes=60 << 20),
        cost_estimate=pl.CostEstimate(flops=8_400_000_000, bytes_accessed=30_000_000, transcendentals=2_000_000),
        name="block_pass",
    )(stream, upstream, vectors, *mats)


def adamw_step(weight, moment_one, moment_two, grad, rate):
    first = beta_one * moment_one + (1.0 - beta_one) * grad
    second = beta_two * moment_two + (1.0 - beta_two) * grad * grad
    fix_one = 1.0 - beta_one**STEP
    fix_two = 1.0 - beta_two**STEP
    update = first / fix_one / (jnp.sqrt(second / fix_two) + epsilon_add) + decay_rate * weight
    return (weight - rate * update, first, second)


NC = 15
HEAD = 96


def dims_step(count):
    return 16 if count % 16 == 0 else count


def spread_bands(shaped, master, turned, out):
    dims = out.shape[0]
    for dim in range(dims):
        part = dot_nn(shaped, master[:, dim * PATCH : (dim + 1) * PATCH])
        turned[pl.ds(dim, NB, stride=dims), :] = part[:, :128]
        turned[pl.ds(NB * dims + dim, NB, stride=dims), :] = part[:, 128:]
    for band in range(NB):
        for half in range(2):
            row = half * NB * dims + band * dims
            lane = band * PATCH + half * 128
            out[:, lane : lane + 128] = turned[row : row + dims, :].astype(out.dtype)


def own_bands(shaped_ref):
    return shaped_ref[pl.ds(pl.multiple_of(lax.axis_index("group") * NB, NB), NB), :]


def make_kernel(shaped_ref, master_ref, kernel_ref, turned):
    spread_bands(own_bands(shaped_ref), master_ref, turned, kernel_ref)


def make_kernels(shaped, master):
    dims = master.shape[1] // PATCH
    step = dims_step(dims)
    return pl.pallas_call(
        make_kernel,
        out_shape=jax.ShapeDtypeStruct((dims, NB * PATCH), jnp.bfloat16),
        grid=(dims // step,),
        in_specs=[
            pl.BlockSpec(shaped.shape, lambda j: (0, 0)),
            pl.BlockSpec((E, step * PATCH), lambda j: (0, j)),
        ],
        out_specs=pl.BlockSpec((step, NB * PATCH), lambda j: (j, 0)),
        scratch_shapes=[pltpu.VMEM((2 * NB * step, 128), jnp.float32)],
        compiler_params=pltpu.CompilerParams(vmem_limit_bytes=60 << 20),
        name="make_kernels",
    )(shaped, master)


def embed_kernel(pixel_ref, mask_ref, kernel_ref, stream_ref):
    masked = pixel_ref[...] * mask_ref[...].astype(jnp.bfloat16)
    part = dot_nt(masked, kernel_ref[...])

    @pl.when(pl.program_id(0) == 0)
    def _():
        stream_ref[...] = part

    @pl.when(pl.program_id(0) > 0)
    def _():
        stream_ref[...] += part


def embed_patches(pixels, mask, kernels):
    seq, width = pixels.shape[1], pixels.shape[2]
    cut = 1024
    return pl.pallas_call(
        embed_kernel,
        out_shape=jax.ShapeDtypeStruct((seq, D), jnp.float32),
        grid=(width // cut,),
        in_specs=[
            pl.BlockSpec((None, seq, cut), lambda j: (0, 0, j)),
            pl.BlockSpec((1, cut), lambda j: (0, j)),
            pl.BlockSpec((D, cut), lambda j: (0, j)),
        ],
        out_specs=pl.BlockSpec((seq, D), lambda j: (0, 0)),
        compiler_params=pltpu.CompilerParams(vmem_limit_bytes=60 << 20),
        name="embed_patches",
    )(pixels, mask, kernels)


def unembed_kernel(masked_ref, mask_ref, kernel_ref, low_ref, back_ref, grad_ref):
    seq = back_ref.shape[0]
    back_ref[...] = (dot_nn(low_ref[...], kernel_ref[...])[0:seq] * mask_ref[...]).astype(back_ref.dtype)
    grad_ref[...] = dot_tn(low_ref[...], masked_ref[...]).astype(grad_ref.dtype)


def unembed_patches(masked, mask, kernels, low, seq):
    rows, width = masked.shape
    cut = 1024
    return pl.pallas_call(
        unembed_kernel,
        out_shape=[
            jax.ShapeDtypeStruct((1, seq, width), jnp.bfloat16),
            jax.ShapeDtypeStruct((D, width), jnp.bfloat16),
        ],
        grid=(width // cut,),
        in_specs=[
            pl.BlockSpec((rows, cut), lambda j: (0, j)),
            pl.BlockSpec((1, cut), lambda j: (0, j)),
            pl.BlockSpec((D, cut), lambda j: (0, j)),
            pl.BlockSpec(low.shape, lambda j: (0, 0)),
        ],
        out_specs=[
            pl.BlockSpec((None, seq, cut), lambda j: (0, 0, j)),
            pl.BlockSpec((D, cut), lambda j: (0, j)),
        ],
        compiler_params=pltpu.CompilerParams(vmem_limit_bytes=60 << 20),
        name="unembed_patches",
    )(masked, mask, kernels, low)


def master_kernel(rate, grad_ref, shaped_ref, weight_ref, one_ref, two_ref, new_ref, first_ref, second_ref, back_ref, turned):
    groups, dims = grad_ref.shape[0], grad_ref.shape[1]
    bands = groups * NB
    for group in range(groups):
        for band in range(NB):
            for half in range(2):
                row = half * bands * dims + (group * NB + band) * dims
                lane = band * PATCH + half * 128
                turned[row : row + dims, :] = grad_ref[group, :, lane : lane + 128].astype(jnp.float32)
    total = jnp.zeros(back_ref.shape, jnp.float32)
    for dim in range(dims):
        part = jnp.concatenate(
            [turned[pl.ds(half * bands * dims + dim, bands, stride=dims), :] for half in range(2)], axis=1
        ).astype(jnp.bfloat16)
        lanes = slice(dim * PATCH, (dim + 1) * PATCH)
        weight = weight_ref[:, lanes]
        total += dot_nt(part, weight.astype(jnp.bfloat16))
        grad = dot_tn(shaped_ref[...], part)
        new_ref[:, lanes], first_ref[:, lanes], second_ref[:, lanes] = adamw_step(
            weight, one_ref[:, lanes], two_ref[:, lanes], grad, rate
        )

    @pl.when(pl.program_id(0) == 0)
    def _():
        back_ref[...] = total

    @pl.when(pl.program_id(0) > 0)
    def _():
        back_ref[...] += total


def master_update(grads, shaped, weight, one, two, rate):
    groups, dims = grads.shape[0], grads.shape[1]
    step = dims_step(dims)
    columns = pl.BlockSpec((weight.shape[0], step * PATCH), lambda j: (0, j))
    like = jax.ShapeDtypeStruct(weight.shape, jnp.float32)
    return pl.pallas_call(
        functools.partial(master_kernel, rate),
        out_shape=[like, like, like, jax.ShapeDtypeStruct(shaped.shape, jnp.float32)],
        grid=(dims // step,),
        in_specs=[
            pl.BlockSpec((groups, step, NB * PATCH), lambda j: (0, j, 0)),
            pl.BlockSpec(shaped.shape, lambda j: (0, 0)),
            columns,
            columns,
            columns,
        ],
        out_specs=[columns, columns, columns, pl.BlockSpec(shaped.shape, lambda j: (0, 0))],
        scratch_shapes=[pltpu.VMEM((2 * groups * NB * step, 128), jnp.float32)],
        compiler_params=pltpu.CompilerParams(vmem_limit_bytes=60 << 20),
        name="master_update",
    )(grads, shaped, weight, one, two)


def spot():
    group = lax.axis_index("group")
    image = lax.axis_index("img")
    return group // 2, group % 2, image // 2, image % 2


def place(y, c, z, x):
    return (y * 2 + c, z * 2 + x)


def partners():
    y, c, z, x = spot()
    x2, y2 = x + (1 - c) * (1 - 2 * x), y + c * (1 - 2 * y)
    x3, y3 = x + c * (1 - 2 * x), y + (1 - c) * (1 - 2 * y)
    around = [place(y, c, (z + d) % 4, x) for d in (1, 2, 3)]
    return (x2, y2), (x3, y3), around, place(y2, c, z, x2), place(y3, c, z, x3), place(y, 1 - c, z, x)


def greet(peers):
    barrier = pltpu.get_barrier_semaphore()
    for peer in peers:
        pl.semaphore_signal(barrier, inc=1, device_id=peer, device_id_type=MESH)
    pl.semaphore_wait(barrier, len(peers))


def remote(src, dst, send_sem, recv_sem, target):
    return pltpu.make_async_remote_copy(
        src_ref=src, dst_ref=dst, send_sem=send_sem, recv_sem=recv_sem, device_id=target, device_id_type=MESH
    )


def gather_kernel(rest_ref, pixel_ref, weight_ref, up_ref, mask_ref, all_ref, head_ref, low_ref, up_in, mask_in, own_ref, wide, narrow, weight_sem, head_sem, local_sem, line_send, line_recv, group_send, group_recv, twin_send, twin_recv):
    y, c, z, x = spot()
    (x2, y2), (x3, y3), around, second, third, twin = partners()
    partner = place(y, 1 - c, (z + 2) % 4, x)
    moved = (c + z // 2) % 2 == 1
    rows = own_ref.shape[0] // NC

    def cut(k):
        return pl.ds(k * rows, rows)

    head = remote(pixel_ref.at[0, pl.ds(0, HEAD)], head_ref.at[0], head_sem.at[0], head_sem.at[1], partner)
    small = [
        remote(up_ref, up_in, head_sem.at[2], head_sem.at[3], partner),
        remote(mask_ref, mask_in, head_sem.at[4], head_sem.at[5], partner),
    ]

    def along(d, k):
        return remote(own_ref.at[cut(k)], all_ref.at[y, c, z, x, cut(k)], line_send.at[d - 1, k], line_recv.at[d - 1, k], around[d - 1])

    def along_in(d, k):
        return remote(own_ref.at[cut(k)], all_ref.at[y, c, (z + 4 - d) % 4, x, cut(k)], line_send.at[d - 1, k], line_recv.at[d - 1, k], around[d - 1])

    def square(core, j):
        yy, xx = ((y, x), (y2, x2), (y3, x3), (1 - y, 1 - x))[j]
        return all_ref.at[yy, core, :, xx]

    def hop(j, to, k, slot, landing):
        part = square(c, j).at[:, cut(k)]
        return remote(part, part, group_send.at[slot, k], group_recv.at[landing, k], to)

    def hop_in(landing, k):
        part = square(c, landing).at[:, cut(k)]
        return remote(part, part, group_send.at[0, k], group_recv.at[landing, k], twin)

    def share(j, k):
        part = square(c, j).at[:, cut(k)]
        yy, xx = ((y, x), (y2, x2), (y3, x3), (1 - y, 1 - x))[j]
        landing = (0, 2, 1, 3)[j]
        return remote(part, part, twin_send.at[j, k], twin_recv.at[landing, k], twin)

    def share_in(landing, k):
        yy, xx = ((y, x), (y2, x2), (y3, x3), (1 - y, 1 - x))[landing]
        part = all_ref.at[yy, 1 - c, :, xx, cut(k)]
        return remote(part, part, twin_send.at[0, k], twin_recv.at[landing, k], twin)

    fetch = pltpu.make_async_copy(weight_ref, wide, weight_sem.at[0])
    store = pltpu.make_async_copy(narrow, low_ref, weight_sem.at[1])
    fetch.start()
    even = rest_ref.shape[0] // 16 * 16
    own_ref[0:even, :] = rest_ref[0:even, :].astype(jnp.bfloat16)
    if even < own_ref.shape[0]:
        left = rest_ref.shape[0] - even
        parts = [rest_ref[even:, :]] if left else []
        parts.append(jnp.zeros((own_ref.shape[0] - even - left, 128), jnp.float32))
        own_ref[even:, :] = jnp.concatenate(parts, axis=0).astype(jnp.bfloat16)
    keep = pltpu.make_async_copy(own_ref, all_ref.at[y, c, z, x], local_sem)
    keep.start()
    greet(around + [second, third, twin, partner])
    for k in range(NC):
        for d in (1, 2, 3):
            along(d, k).start()
    keep.wait()
    for step in range(NC + 2):
        k = step
        if k < NC:
            for d in (1, 2, 3):
                along_in(d, k).wait_recv()
            hop(0, third, k, 0, 2).start()
            hop(0, second, k, 1, 1).start()
            share(0, k).start()
        if step == 3:
            fetch.wait()
            narrow[...] = wide[...].astype(jnp.bfloat16)
            store.start()
        if step == NC // 2 + 1:

            @pl.when(moved)
            def _():
                head.start()
                for copy in small:
                    copy.start()

        k = step - 1
        if 0 <= k < NC:
            hop_in(1, k).wait_recv()
            hop(1, third, k, 2, 3).start()
            share(1, k).start()
        k = step - 2
        if 0 <= k < NC:
            hop_in(2, k).wait_recv()
            share(2, k).start()
            hop_in(3, k).wait_recv()
            share(3, k).start()
    for k in range(NC):
        for d in (1, 2, 3):
            along(d, k).wait_send()
        hop(0, third, k, 0, 2).wait_send()
        hop(0, second, k, 1, 1).wait_send()
        hop(1, third, k, 2, 3).wait_send()
        for j in range(4):
            share(j, k).wait_send()
            share_in(j, k).wait_recv()

    store.wait()

    @pl.when(moved)
    def _():
        head.wait()
        for copy in small:
            copy.wait()


def gather_packed(own, pixels, weight, upstream, mask, rows):
    bf16 = jnp.bfloat16
    dma = pltpu.SemaphoreType.DMA
    return pl.pallas_call(
        gather_kernel,
        out_shape=[
            jax.ShapeDtypeStruct((2, 2, 4, 2, rows, 128), bf16),
            jax.ShapeDtypeStruct((1, HEAD, pixels.shape[2]), pixels.dtype),
            jax.ShapeDtypeStruct(weight.shape, bf16),
            jax.ShapeDtypeStruct(upstream.shape, upstream.dtype),
            jax.ShapeDtypeStruct(mask.shape, mask.dtype),
        ],
        in_specs=[pl.BlockSpec(memory_space=pltpu.VMEM)] + [pl.BlockSpec(memory_space=pl.ANY)] * 4,
        out_specs=[pl.BlockSpec(memory_space=pl.ANY)] * 5,
        scratch_shapes=[
            pltpu.VMEM((rows, 128), bf16),
            pltpu.VMEM(weight.shape, jnp.float32),
            pltpu.VMEM(weight.shape, bf16),
            dma((2,)),
            dma((6,)),
            dma, dma((3, NC)), dma((3, NC)), dma((3, NC)), dma((4, NC)), dma((4, NC)), dma((4, NC))],
        compiler_params=pltpu.CompilerParams(collective_id=0, has_side_effects=True, vmem_limit_bytes=60 << 20),
        name="gather_packed",
    )(own, pixels, weight, upstream, mask)


def reduce_kernel(part_ref, sum_ref, own, twin_in, third_in, second_in, line_in, load_sem, twin_send, twin_recv, third_send, third_recv, second_send, second_recv, line_send, line_recv):
    f32, bf16 = jnp.float32, jnp.bfloat16
    y, c, z, x = spot()
    (x2, y2), (x3, y3), around, second, third, twin = partners()
    rows = sum_ref.shape[0] // NC

    def cut(k):
        return pl.ds(k * rows, rows)

    spots = ((1 - y, 1 - x), (y3, x3), (y2, x2), (y, x))
    turned = ((1 - y, 1 - x), (y2, x2), (y3, x3), (y, x))

    def load(j, k):
        yy, xx = spots[j]
        return pltpu.make_async_copy(part_ref.at[yy, c, :, xx, cut(k)], own.at[j, :, cut(k)], load_sem.at[j, k])

    def swap(j, k):
        yy, xx = turned[j]
        return remote(part_ref.at[yy, 1 - c, :, xx, cut(k)], twin_in.at[j, :, cut(k)], twin_send.at[j, k], twin_recv.at[j, k], twin)

    def to_third(j, k):
        return remote(own.at[j, :, cut(k)], third_in.at[j, :, cut(k)], third_send.at[j, k], third_recv.at[j, k], third)

    def to_second(k):
        return remote(own.at[2, :, cut(k)], second_in.at[:, cut(k)], second_send.at[k], second_recv.at[k], second)

    def to_line(d, k):
        return remote(own.at[3, (z + d) % 4, cut(k)], line_in.at[d - 1, cut(k)], line_send.at[d - 1, k], line_recv.at[d - 1, k], around[d - 1])

    for k in range(NC):
        for j in range(4):
            load(j, k).start()
    greet(around + [second, third, twin])
    for k in range(NC):
        for j in range(4):
            swap(j, k).start()

    def pair(j, k):
        load(j, k).wait()
        swap(j, k).wait_recv()
        return own[j, :, cut(k)].astype(f32) + twin_in[j, :, cut(k)].astype(f32)

    for step in range(NC + 3):
        k = step
        if k < NC:
            for j in (0, 1):
                own[j, :, cut(k)] = pair(j, k).astype(bf16)
                to_third(j, k).start()
        k = step - 1
        if 0 <= k < NC:
            held = pair(2, k)
            to_third(0, k).wait_recv()
            own[2, :, cut(k)] = (held + third_in[0, :, cut(k)].astype(f32)).astype(bf16)
            to_second(k).start()
        k = step - 2
        if 0 <= k < NC:
            held = pair(3, k)
            to_third(1, k).wait_recv()
            to_second(k).wait_recv()
            held += third_in[1, :, cut(k)].astype(f32) + second_in[:, cut(k)].astype(f32)
            own[3, :, cut(k)] = held.astype(bf16)
            for d in (1, 2, 3):
                to_line(d, k).start()
        k = step - 3
        if 0 <= k < NC:
            total = own[3, z, cut(k)].astype(f32)
            for d in (1, 2, 3):
                to_line(d, k).wait_recv()
                total += line_in[d - 1, cut(k)].astype(f32)
            sum_ref[cut(k)] = total
    for k in range(NC):
        for j in range(4):
            swap(j, k).wait_send()
        for j in (0, 1):
            to_third(j, k).wait_send()
        to_second(k).wait_send()
        for d in (1, 2, 3):
            to_line(d, k).wait_send()


def reduce_packed(part):
    rows = part.shape[-2]
    bf16 = jnp.bfloat16
    dma = pltpu.SemaphoreType.DMA
    return pl.pallas_call(
        reduce_kernel,
        out_shape=jax.ShapeDtypeStruct((rows, 128), jnp.float32),
        in_specs=[pl.BlockSpec(memory_space=pl.ANY)],
        out_specs=pl.BlockSpec(memory_space=pltpu.VMEM),
        scratch_shapes=[
            pltpu.VMEM((4, 4, rows, 128), bf16),
            pltpu.VMEM((4, 4, rows, 128), bf16),
            pltpu.VMEM((2, 4, rows, 128), bf16),
            pltpu.VMEM((4, rows, 128), bf16),
            pltpu.VMEM((3, rows, 128), bf16),
            dma((4, NC)), dma((4, NC)), dma((4, NC)), dma((2, NC)), dma((2, NC)), dma((NC,)), dma((NC,)), dma((3, NC)), dma((3, NC)),
        ],
        compiler_params=pltpu.CompilerParams(collective_id=1, has_side_effects=True, vmem_limit_bytes=56 << 20),
        name="reduce_packed",
    )(part)


CHUNK = 16


def over_x(k):
    return k % 2 == 0


def quad_peers():
    y, c, z, x = spot()
    low = z % 2
    side = place(y, c, z, 1 - x)
    along = place(y, c, z + 1 - 2 * low, x)
    twin = place(y, 1 - c, z, x)
    partner = place(y, 1 - c, (z + 2) % 4, x)
    moved = (c + z // 2) % 2 == 1
    return y, c, z, x, low, side, along, twin, partner, moved


def swap_group(value, flip):
    return lax.ppermute(value, "group", [(j, j ^ flip) for j in range(4)])


def swap_images(value):
    pairs = []
    for y in range(2):
        for c in range(2):
            for z in range(4):
                for x in range(2):
                    other = (1 - c, (z + 2) % 4) if c != z // 2 else (c, z)
                    pairs.append((((y * 2 + c) * 4 + z) * 2 + x, ((y * 2 + other[0]) * 4 + other[1]) * 2 + x))
    return lax.ppermute(value, ("group", "img"), pairs)


def share_kernel(shaped_ref, mask_ref, own_slab, over_slab, pixel_ref, head_ref, rest_ref,
                 all_ref, masked_ref, stream_ref, made_ref, master, turned, held, top, bottom, tile, mixed, order, slab_sem, slab_send, slab_recv, pixel_sem, store_sem, keep_sem, swap_send, swap_recv,
                 side_send, side_recv, along_send, along_recv, far_send, far_recv, twin_send, twin_recv):
    f32, bf16 = jnp.float32, jnp.bfloat16
    y, c, z, x, low, side, along, twin, partner, moved = quad_peers()
    dims, width = made_ref.shape
    count = dims // CHUNK
    group = 8 * CHUNK

    def cut(k):
        return pl.ds(k * CHUNK, CHUNK)

    def block(core, j, k):
        return held.at[2 * core + (low + j // 2) % 2, (x + j % 2) % 2, cut(k)]

    def keep(k):
        return pltpu.make_async_copy(made_ref.at[cut(k)], block(c, 0, k), keep_sem.at[k])

    def swap(k):
        return remote(made_ref.at[cut(k)], block(1 - c, 0, k), swap_send.at[k], swap_recv.at[k], partner)

    def swap_in(k):
        return remote(made_ref.at[cut(k)], block(c, 0, k), swap_send.at[k], swap_recv.at[k], partner)

    def to_side(k):
        return remote(block(c, 0, k), block(c, 0, k), side_send.at[k], side_recv.at[k], side)

    def from_side(k):
        return remote(block(c, 1, k), block(c, 1, k), side_send.at[k], side_recv.at[k], side)

    def to_along(k):
        return remote(block(c, 0, k), block(c, 0, k), along_send.at[k], along_recv.at[k], along)

    def from_along(k):
        return remote(block(c, 2, k), block(c, 2, k), along_send.at[k], along_recv.at[k], along)

    def pass_on(k):
        j, to = (2, side) if over_x(k) else (1, along)
        return remote(block(c, j, k), block(c, j, k), far_send.at[k], far_recv.at[k], to)

    def from_far(k):
        return remote(block(c, 3, k), block(c, 3, k), far_send.at[k], far_recv.at[k], twin)

    def give(j, k):
        return remote(block(c, j, k), block(c, j, k), twin_send.at[j, k], twin_recv.at[j, k], twin)

    def given(j, k):
        return remote(block(1 - c, j, k), block(1 - c, j, k), twin_send.at[j, k], twin_recv.at[j, k], twin)

    def slab(core, j, k):
        owner = (y + j) % 2 * 2 + core
        size = own_slab.shape[0]
        return master.at[k, pl.ds(pl.multiple_of(owner * size, size), size)]

    def slab_here(j, k):
        lanes = pl.ds(k * CHUNK * PATCH, CHUNK * PATCH)
        return (own_slab, over_slab)[j].at[:, lanes]

    def load_slab(j, k):
        return pltpu.make_async_copy(slab_here(j, k), slab(c, j, k), slab_sem.at[j, k])

    def send_slab(j, k):
        return remote(slab_here(j, k), slab(c, j, k), slab_send.at[j, k], slab_recv.at[j, k], twin)

    def slab_in(j, k):
        return remote(slab_here(j, k), slab(1 - c, j, k), slab_send.at[j, k], slab_recv.at[j, k], twin)

    def make(k):
        for j in range(2):
            load_slab(j, k).wait()
            slab_in(j, k).wait_recv()
        spread_bands(own_bands(shaped_ref), master.at[k], turned, made_ref.at[cut(k)])

        @pl.when(moved)
        def _():
            swap(k).start()

        @pl.when(jnp.logical_not(moved))
        def _():
            keep(k).start()

    def store(k):
        return pltpu.make_async_copy(held.at[:, :, cut(k)], all_ref.at[:, :, cut(k)], store_sem.at[k])

    swapped = pltpu.make_async_copy(head_ref.at[0], top, pixel_sem.at[0])
    owned = pltpu.make_async_copy(pixel_ref.at[0, pl.ds(0, HEAD)], top, pixel_sem.at[0])
    lower = pltpu.make_async_copy(rest_ref.at[0], bottom, pixel_sem.at[1])

    for k in range(count):
        for j in range(2):
            load_slab(j, k).start()

    @pl.when(jnp.logical_not(moved))
    def _():
        owned.start()

    @pl.when(moved)
    def _():
        swapped.start()

    lower.start()
    greet([side, along, twin, partner])
    for k in range(count):
        for j in range(2):
            send_slab(j, k).start()
    make(0)

    def mask_pixels(part):
        @pl.when(part == 0)
        def _():
            lower.wait()
            owned.wait()

        def some(j, carry):
            lanes = pl.ds(pl.multiple_of(j * 1024, 1024), 1024)
            mask = mask_ref[:, lanes]
            masked_ref[0:HEAD, lanes] = (top[:, lanes].astype(f32) * mask).astype(bf16)
            tile[...] = jnp.zeros_like(tile)
            tile[0 : bottom.shape[0], :] = bottom[:, lanes].astype(f32) * mask
            masked_ref[HEAD:, lanes] = tile[...].astype(bf16)
            return carry

        cuts = width // 1024
        lax.fori_loop(part * (cuts // 2), (part + 1) * (cuts // 2), some, 0)

    def make_order():
        row = lax.broadcasted_iota(jnp.int32, order.shape, 0)
        column = lax.broadcasted_iota(jnp.int32, order.shape, 1)
        wanted = row % group // CHUNK * dims + row // group * CHUNK + row % CHUNK
        order[...] = jnp.where(column == wanted, 1.0, 0.0)

    for step in range(count + 3):
        k = step
        if k < count:

            @pl.when(moved)
            def _(k=k):
                swap_in(k).wait_recv()

            @pl.when(jnp.logical_not(moved))
            def _(k=k):
                keep(k).wait()

            to_side(k).start()
            to_along(k).start()
            give(0, k).start()
        if step + 1 < count:
            make(step + 1)
        if step in (1, 2):
            mask_pixels(step - 1)
        elif step == 3:
            make_order()
        k = step - 1
        if 0 <= k < count:
            if over_x(k):
                from_along(k).wait_recv()
                pass_on(k).start()
                from_side(k).wait_recv()
            else:
                from_side(k).wait_recv()
                pass_on(k).start()
                from_along(k).wait_recv()
            give(1, k).start()
            give(2, k).start()
        k = step - 2
        if 0 <= k < count:
            from_far(k).wait_recv()
            give(3, k).start()
        k = step - 3
        if 0 <= k < count:
            for j in range(4):
                given(j, k).wait_recv()
            store(k).start()
            part = held[:, :, cut(k), :].reshape(group, width)
            mixed[:, k * group : (k + 1) * group] = dot_nt(masked_ref[...], part)

    stream_ref[...] = finer(mixed[...], order[...], 1, 0)[0 : stream_ref.shape[0]]

    @pl.when(moved)
    def _():
        for k in range(count):
            swap(k).wait_send()

    for k in range(count):
        to_side(k).wait_send()
        to_along(k).wait_send()
        pass_on(k).wait_send()
        store(k).wait()
        for j in range(2):
            send_slab(j, k).wait_send()
        for j in range(4):
            give(j, k).wait_send()


def share_kernels(shaped, mask, slabs, pixels, head, rest):
    dims, width = slabs[0].shape[1] // PATCH, mask.shape[1]
    bf16 = jnp.bfloat16
    count = dims // CHUNK
    seq = pixels.shape[1]
    rows = tall(seq)
    f32 = jnp.float32
    dma = pltpu.SemaphoreType.DMA
    vmem, far = pl.BlockSpec(memory_space=pltpu.VMEM), pl.BlockSpec(memory_space=pl.ANY)
    shared, masked, stream = pl.pallas_call(
        share_kernel,
        out_shape=[
            jax.ShapeDtypeStruct((4, 2, dims, width), bf16),
            jax.ShapeDtypeStruct((rows, width), bf16),
            jax.ShapeDtypeStruct((seq, 8 * dims), f32),
        ],
        in_specs=[vmem, vmem] + [far] * 5,
        out_specs=[far, vmem, vmem],
        scratch_shapes=[
            pltpu.VMEM((dims, width), bf16),
            pltpu.VMEM((count, E, CHUNK * PATCH), bf16),
            pltpu.VMEM((2 * NB * CHUNK, 128), f32),
            pltpu.VMEM((4, 2, dims, width), bf16),
            pltpu.VMEM((HEAD, width), bf16),
            pltpu.VMEM((seq - HEAD, width), bf16),
            pltpu.VMEM((rows - HEAD, 1024), f32),
            pltpu.VMEM((rows, 8 * dims), f32),
            pltpu.VMEM((8 * dims, 8 * dims), f32),
            dma((2, count)),
            dma((2, count)),
            dma((2, count)),
            dma((2,)),
        ]
        + [dma((count,))] * 10
        + [dma((4, count))] * 2,
        compiler_params=pltpu.CompilerParams(collective_id=2, has_side_effects=True, vmem_limit_bytes=60 << 20),
        name="share_kernels",
    )(shaped, mask, *slabs, pixels, head, rest)
    return shared.reshape(8 * dims, width), masked, stream


def fold_kernel(masked_ref, mask_ref, low_ref, kernel_ref, out_ref, all_ref, back_ref, out_in,
                gone, own, twin_in, relay_in, side_in, along_in, tiles, backs, out_sem, tile_sem, back_sem, keep_sem, twin_send, twin_recv,
                relay_send, relay_recv, side_send, side_recv, along_send, along_recv, swap_send, swap_recv,
                group_send, group_recv, give_send, give_recv):
    f32, bf16 = jnp.float32, jnp.bfloat16
    y, c, z, x, low, side, along, twin, partner, moved = quad_peers()
    over = place(1 - y, c, z, x)
    dims, width = all_ref.shape[2], all_ref.shape[3]
    count = dims // CHUNK
    seq = back_ref.shape[1]
    lane = tiles.shape[2]

    def cut(k):
        return pl.ds(k * CHUNK, CHUNK)

    def spot_of(j):
        return (low + j // 2) % 2, (x + j % 2) % 2

    def mine(j, k):
        a, b = spot_of(j)
        return own.at[a, b, cut(k)]

    def swap(k):
        return remote(gone.at[:, :, cut(k)], twin_in.at[:, :, cut(k)], twin_send.at[k], twin_recv.at[k], twin)

    def relay(k):
        return remote(mine(3, k), relay_in.at[cut(k)], relay_send.at[k], relay_recv.at[k], along if over_x(k) else side)

    def to_side(k):
        return remote(mine(1, k), side_in.at[cut(k)], side_send.at[k], side_recv.at[k], side)

    def to_along(k):
        return remote(mine(2, k), along_in.at[cut(k)], along_send.at[k], along_recv.at[k], along)

    def keep(k):
        return pltpu.make_async_copy(mine(0, k), all_ref.at[y, c, cut(k)], keep_sem.at[k])

    def move(k):
        return remote(mine(0, k), all_ref.at[y, 1 - c, cut(k)], swap_send.at[k], swap_recv.at[k], partner)

    def moved_in(k):
        return remote(mine(0, k), all_ref.at[y, c, cut(k)], swap_send.at[k], swap_recv.at[k], partner)

    def cross(k):
        return remote(all_ref.at[y, c, cut(k)], all_ref.at[y, c, cut(k)], group_send.at[k], group_recv.at[k], over)

    def crossed(k):
        return remote(all_ref.at[1 - y, c, cut(k)], all_ref.at[1 - y, c, cut(k)], group_send.at[k], group_recv.at[k], over)

    def give(j, k):
        here = all_ref.at[(y + j) % 2, c, cut(k)]
        return remote(here, here, give_send.at[j, k], give_recv.at[j, k], twin)

    def given(j, k):
        here = all_ref.at[(y + j) % 2, 1 - c, cut(k)]
        return remote(here, here, give_send.at[j, k], give_recv.at[j, k], twin)

    def fetch(j):
        return pltpu.make_async_copy(kernel_ref.at[:, pl.ds(j * lane, lane)], tiles.at[j % 2], tile_sem.at[j % 2])

    def drain(j):
        return pltpu.make_async_copy(backs.at[j % 2], back_ref.at[0, :, pl.ds(j * lane, lane)], back_sem.at[j % 2])

    def half(core, out):
        chosen = low_ref[:, pl.ds(pl.multiple_of(core * 4 * dims, 128), 4 * dims)]

        def some(j, carry):
            lanes = pl.ds(pl.multiple_of(j * 1024, 1024), 1024)
            part = dot_tn(chosen, masked_ref[:, lanes]).astype(bf16)
            out[:, :, :, lanes] = part.reshape(2, 2, dims, 1024)
            return carry

        lax.fori_loop(0, width // 1024, some, 0)

    def pixels_back(j):
        fetch(j).wait()
        if j >= 2:
            drain(j - 2).wait()
        part = dot_nn(low_ref[...], tiles[j % 2])[0:seq] * mask_ref[:, j * lane : (j + 1) * lane]
        backs[j % 2] = part.astype(bf16)
        drain(j).start()
        if (j + 2) * lane < width:
            fetch(j + 2).start()

    def pair(j, k):
        a, b = spot_of(j)
        return own[a, b, cut(k)].astype(f32) + twin_in[a, b, cut(k)].astype(f32)

    def put(j, k, value):
        a, b = spot_of(j)
        own[a, b, cut(k)] = value.astype(bf16)

    output = remote(out_ref, out_in, out_sem.at[0], out_sem.at[1], partner)
    fetch(0).start()
    fetch(1).start()
    greet([side, along, twin, partner, over])

    @pl.when(moved)
    def _():
        output.start()

    half(1 - c, gone)
    for k in range(count):
        swap(k).start()
    half(c, own)

    for step in range(count + 4):
        k = step
        if k < count:
            swap(k).wait_recv()
            put(3, k, pair(3, k))
            relay(k).start()
        k = step - 1
        if 0 <= k < count:
            first, second = (to_along, to_side) if over_x(k) else (to_side, to_along)
            plain, summed = (2, 1) if over_x(k) else (1, 2)
            put(plain, k, pair(plain, k))
            first(k).start()
            relay(k).wait_recv()
            put(summed, k, pair(summed, k) + relay_in[cut(k)].astype(f32))
            second(k).start()
        k = step - 2
        if 0 <= k < count:
            to_side(k).wait_recv()
            to_along(k).wait_recv()
            put(0, k, pair(0, k) + side_in[cut(k)].astype(f32) + along_in[cut(k)].astype(f32))

            @pl.when(moved)
            def _(k=k):
                move(k).start()

            @pl.when(jnp.logical_not(moved))
            def _(k=k):
                keep(k).start()

        k = step - 3
        if 0 <= k < count:

            @pl.when(moved)
            def _(k=k):
                moved_in(k).wait_recv()

            @pl.when(jnp.logical_not(moved))
            def _(k=k):
                keep(k).wait()

            cross(k).start()
            give(0, k).start()
        k = step - 4
        if 0 <= k < count:
            crossed(k).wait_recv()
            give(1, k).start()
        if step >= 2 and (step - 2) * lane < width:
            pixels_back(step - 2)

    @pl.when(moved)
    def _():
        output.wait()
        for k in range(count):
            move(k).wait_send()

    for j in (width // lane - 2, width // lane - 1):
        drain(j).wait()
    for k in range(count):
        swap(k).wait_send()
        relay(k).wait_send()
        to_side(k).wait_send()
        to_along(k).wait_send()
        cross(k).wait_send()
        for j in range(2):
            give(j, k).wait_send()
            given(j, k).wait_recv()


def fold_kernels(masked, mask, low, kernels, out):
    seq = out.shape[0]
    width = masked.shape[1]
    dims = kernels.shape[0] // 8
    count = dims // CHUNK
    bf16 = jnp.bfloat16
    dma = pltpu.SemaphoreType.DMA
    vmem, far = pl.BlockSpec(memory_space=pltpu.VMEM), pl.BlockSpec(memory_space=pl.ANY)
    folded, back, out_in = pl.pallas_call(
        fold_kernel,
        out_shape=[
            jax.ShapeDtypeStruct((2, 2, dims, width), bf16),
            jax.ShapeDtypeStruct((1, seq, width), bf16),
            jax.ShapeDtypeStruct(out.shape, out.dtype),
        ],
        in_specs=[vmem, vmem, vmem, far, far],
        out_specs=[far, far, far],
        scratch_shapes=[
            pltpu.VMEM((2, 2, dims, width), bf16),
            pltpu.VMEM((2, 2, dims, width), bf16),
            pltpu.VMEM((2, 2, dims, width), bf16),
            pltpu.VMEM((dims, width), bf16),
            pltpu.VMEM((dims, width), bf16),
            pltpu.VMEM((dims, width), bf16),
            pltpu.VMEM((2, 8 * dims, 1024), bf16),
            pltpu.VMEM((2, seq, 1024), bf16),
            dma((2,)),
            dma((2,)),
            dma((2,)),
            dma((count,)),
        ]
        + [dma((count,))] * 12
        + [dma((2, count))] * 2,
        compiler_params=pltpu.CompilerParams(collective_id=3, has_side_effects=True, vmem_limit_bytes=60 << 20),
        name="fold_kernels",
    )(masked, mask, low, kernels, out)
    return folded.reshape(4, dims, width), back, out_in


def on_device(
    pixels,
    band_mask,
    wavelength,
    owner_order,
    rest_weight,
    rest_moment1,
    rest_moment2,
    fc_weight,
    fc_moment1,
    fc_moment2,
    cotangent,
):
    f32 = jnp.float32
    bf16 = jnp.bfloat16
    kernel_rate = float(E * PATCH * NB) ** (-0.5)
    groups = lax.axis_size("group")
    own_rows = rest_weight.shape[0]
    own_blocks = own_rows // 8
    fits = lax.axis_size("group") == 4 and lax.axis_size("img") == 8
    extra = -own_rows % 128
    slot_blocks = (own_rows + extra) // 8
    mask = band_mask.astype(f32)
    if fits:
        group, image = lax.axis_index("group"), lax.axis_index("img")
        moved = (group % 2 + image // 4) % 2 == 1
        wide_mask = jnp.pad(mask, ((0, 7), (0, 128 - NB)))
        gathered, head, low_weight, up_in, mask_in = gather_packed(
            rest_weight, pixels, fc_weight, cotangent, wide_mask, own_rows + extra
        )
        gathered, rest, low_weight = lax.optimization_barrier((gathered, pixels[:, HEAD:], low_weight))
        across = swap_group(low_weight, 2)
        rest = swap_images(rest)
        cotangent = jnp.where(moved, up_in, cotangent)
        mask = jnp.where(moved, mask_in[:1, :NB], mask)
    else:
        low_weight = fc_weight.astype(bf16)
        rest_low = jnp.pad(rest_weight.astype(bf16), ((0, extra), (0, 0)))
        gathered = lax.all_gather(rest_low, ("group", "img"), axis=0, tiled=True)
    shards = gathered.size // ((own_rows + extra) * 128)
    gathered = gathered.reshape(shards, own_rows + extra, 128)
    total_blocks = owner_order.shape[0]
    slots = jnp.pad(
        owner_order.reshape(shards, own_blocks),
        ((0, 0), (0, slot_blocks - own_blocks)),
        constant_values=total_blocks,
    ).reshape(-1)
    unpacked = spread_packed(gathered, slots, total_blocks)
    if not fits:
        master = lax.all_gather(low_weight, "group", axis=0, tiled=True)
    block_mats, wave_mats = unpacked[:4], unpacked[4:10]
    block_vectors, wave_vectors = unpacked[10:]
    embedded = embed_waves(wavelength).reshape(groups * NB, E)
    shaped_low, own_shaped, kept, slope = wave_layer(embedded, wave_mats, wave_vectors)
    mask = jnp.repeat(mask, PATCH, axis=1)
    if fits:
        kernel_all, masked, stream = share_kernels(shaped_low, mask, (low_weight, across), pixels, head, rest)
    else:
        kernel_low = make_kernels(shaped_low, master)
        kernel_all = lax.all_gather(kernel_low, "img", axis=0, tiled=True)
        stream = embed_patches(pixels, mask, kernel_all)
        masked = jnp.pad((pixels[0] * mask).astype(bf16), ((0, tall(pixels.shape[1]) - pixels.shape[1]), (0, 0)))
    block_out, grad_low, block_vectors, *block_grads = block_pass(
        stream, cotangent, block_vectors, *block_mats
    )
    if fits:
        all_groups, pixel_grad, out_in = fold_kernels(masked, mask, grad_low, kernel_all, block_out)
        all_groups, pixel_grad = lax.optimization_barrier((all_groups, pixel_grad))
        pixel_grad = swap_images(pixel_grad)
        block_out = jnp.where(moved, out_in, block_out)
    else:
        pixel_grad, kernel_grad = unembed_patches(masked, mask, kernel_all, grad_low, pixels.shape[1])
        kernel_grad_low = lax.psum_scatter(kernel_grad, "img", scatter_dimension=0, tiled=True)
        all_groups = lax.all_gather(kernel_grad_low[None], "group", axis=0, tiled=True)
    fc_new, fc_first, fc_second, shaped_part = master_update(
        all_groups,
        own_shaped,
        fc_weight,
        fc_moment1,
        fc_moment2,
        kernel_rate,
    )
    *wave_grads, wave_vectors = wave_back(shaped_part, embedded, kept, slope, wave_mats, wave_vectors)
    given = [*block_grads, *wave_grads, block_vectors, wave_vectors]
    joint_term = collect_packed(given, slots, total_blocks, shards, own_rows + extra)
    if fits:
        rest_grad = reduce_packed(joint_term.reshape(2, 2, 4, 2, own_rows + extra, 128))
    else:
        rest_grad = lax.psum_scatter(
            joint_term, ("group", "img"), scatter_dimension=0, tiled=False
        ).astype(f32)
    rest_grad = rest_grad[:own_rows]
    rest_new, rest_first, rest_second = adamw_step(
        rest_weight, rest_moment1, rest_moment2, rest_grad, rest_rate
    )
    return (block_out, pixel_grad, rest_new, rest_first, rest_second, fc_new, fc_first, fc_second)


def solution(mesh):
    placed = (
        P(("group", "img"), None, None),
        P(("group", "img"), None),
        P(),
        P(),
        P(("group", "img"), None),
        P(("group", "img"), None),
        P(("group", "img"), None),
        P("group", "img"),
        P("group", "img"),
        P("group", "img"),
        P(("group", "img"), None),
    )
    return jax.shard_map(
        on_device,
        mesh=mesh,
        in_specs=placed,
        out_specs=(
            P(("group", "img"), None),
            P(("group", "img"), None, None),
            P(("group", "img"), None),
            P(("group", "img"), None),
            P(("group", "img"), None),
            P("group", "img"),
            P("group", "img"),
            P("group", "img"),
        ),
        check_vma=False,
    )
```

```python
import functools
import math

import jax
import jax.numpy as jnp
from jax import lax
from jax.experimental import pallas as pl
from jax.experimental.pallas import tpu as pltpu
from jax.sharding import PartitionSpec as P

MESH = pl.DeviceIdType.MESH

D = 768
HEADS = 12
HD = 64
HID = 3072
E = 128
HH = 4
HFF = 2048
PATCH = 256
NB = 32
STEP = 5


beta_one = 0.5
beta_two = 0.75
decay_rate = 0.05
epsilon_add = 1e-08
rest_rate = 0.02


def layout():
    return [
        ("w_qkv", (D, 3 * D)),
        ("w_out", (D, D)),
        ("w_up", (D, HID)),
        ("w_down", (HID, D)),
        ("h_query", (E, E)),
        ("h_key", (E, E)),
        ("h_value", (E, E)),
        ("h_out", (E, E)),
        ("h_ffin", (E, HFF)),
        ("h_ffout", (HFF, E)),
        ("ln1_gain", (D,)),
        ("ln1_shift", (D,)),
        ("ln2_gain", (D,)),
        ("ln2_shift", (D,)),
        ("patch_bias", (D,)),
        ("hn1_gain", (E,)),
        ("hn1_shift", (E,)),
        ("hn2_gain", (E,)),
        ("hn2_shift", (E,)),
    ]


def embed_waves(wavelength):
    half_width = E // 2
    frequency = jnp.exp(-math.log(10000.0) * jnp.arange(half_width, dtype=jnp.float32) / half_width)
    angles = wavelength.astype(jnp.float32)[..., None] * frequency
    return jnp.concatenate([jnp.sin(angles), jnp.cos(angles)], axis=-1)


def matrices():
    listed, at = [], 0
    for name, extent in layout():
        if len(extent) == 2:
            listed.append((name, extent[0], extent[1], at))
        at += math.prod(extent) // 128
    return listed


def vector_places():
    listed, at = [], 0
    rows = [0, 0]
    for name, extent in layout():
        if len(extent) == 1:
            kind = 0 if extent[0] == D else 1
            for j in range(extent[0] // 128):
                listed.append((at + j, kind, rows[kind], j * 128))
            rows[kind] += 1
        at += math.prod(extent) // 128
    return listed


def vector_shapes():
    return [jax.ShapeDtypeStruct((8, D), jnp.float32), jax.ShapeDtypeStruct((8, E), jnp.float32)]


def shards_a_step(shards, wanted):
    return wanted if shards % wanted == 0 else 1


def spread_kernel(order_ref, low_ref, *refs):
    big, small = matrices()[:4], matrices()[4:]
    far, outs, linear, kept, sem = refs[:4], refs[4:12], refs[12], refs[13:17], refs[17]
    step = pl.program_id(0)
    shards, rows = low_ref.shape[0], low_ref.shape[1]

    for shard in range(shards):

        def two(j, carry, shard=shard):
            pair = low_ref[shard, pl.ds(pl.multiple_of(j * 16, 16), 16), :].astype(jnp.float32)
            for half in range(2):
                block = order_ref[(step * shards + shard) * (rows // 8) + j * 2 + half]
                linear[pl.ds(pl.multiple_of(block * 8, 8), 8), :] = pair[half * 8 : half * 8 + 8]
            return carry

        lax.fori_loop(0, rows // 16, two, 0, unroll=8)

    @pl.when(step == pl.num_programs(0) - 1)
    def _():
        def relay(height, width, first, out):
            lanes = width // 128

            def some(j, carry):
                top = pl.multiple_of(j * 128, 128)
                for lane in range(lanes):
                    part = linear[pl.ds(first + top * lanes + lane, 128, stride=lanes), :]
                    out[pl.ds(top, 128), lane * 128 : lane * 128 + 128] = part.astype(out.dtype)
                return carry

            lax.fori_loop(0, height // 128, some, 0)

        copies = []
        for j, (name, height, width, first) in enumerate(big):
            relay(height, width, first, kept[j])
            copies.append(pltpu.make_async_copy(kept[j], far[j], sem.at[j]))
            copies[-1].start()
        for (name, height, width, first), out in zip(small, outs):
            relay(height, width, first, out)
        for out in outs[-2:]:
            out[...] = jnp.zeros_like(out)
        for row, kind, top, lane in vector_places():
            outs[kind - 2][top : top + 1, lane : lane + 128] = linear[row : row + 1, :]
        for copy in copies:
            copy.wait()


def spread_packed(gathered, slots, blocks):
    shards, rows = gathered.shape[0], gathered.shape[1]
    some = shards_a_step(shards, 4)
    big = [jax.ShapeDtypeStruct((height, width), jnp.bfloat16) for name, height, width, first in matrices()[:4]]
    small = [jax.ShapeDtypeStruct((height, width), jnp.float32) for name, height, width, first in matrices()[4:]]
    small += vector_shapes()
    return pl.pallas_call(
        spread_kernel,
        out_shape=big + small,
        grid_spec=pltpu.PrefetchScalarGridSpec(
            num_scalar_prefetch=1,
            grid=(shards // some,),
            in_specs=[pl.BlockSpec((some, rows, 128), lambda s, order: (s, 0, 0))],
            out_specs=[pl.BlockSpec(memory_space=pl.ANY) for shape in big]
            + [pl.BlockSpec(shape.shape, lambda s, order: (0, 0), pipeline_mode=pl.Buffered(1)) for shape in small],
            scratch_shapes=[pltpu.VMEM(((blocks + 1) * 8, 128), jnp.float32)]
            + [pltpu.VMEM(shape.shape, shape.dtype) for shape in big]
            + [pltpu.SemaphoreType.DMA((4,))],
        ),
        compiler_params=pltpu.CompilerParams(vmem_limit_bytes=60 << 20),
        name="spread_packed",
    )(slots, gathered)


def collect_kernel(order_ref, *refs):
    big, small = matrices()[:4], matrices()[4:]
    far, ins, low_ref, linear, kept, sem = refs[:4], refs[4:12], refs[12], refs[13], refs[14:18], refs[18]
    step = pl.program_id(0)
    shards, rows = low_ref.shape[0], low_ref.shape[1]

    @pl.when(step == 0)
    def _():
        copies = [pltpu.make_async_copy(far[j], kept[j], sem.at[j]) for j in range(4)]
        for copy in copies:
            copy.start()

        def relay(height, width, first, given):
            lanes = width // 128

            def some(j, carry):
                top = pl.multiple_of(j * 128, 128)
                for lane in range(lanes):
                    part = given[pl.ds(top, 128), lane * 128 : lane * 128 + 128]
                    linear[pl.ds(first + top * lanes + lane, 128, stride=lanes), :] = part.astype(jnp.float32)
                return carry

            lax.fori_loop(0, height // 128, some, 0)

        for (name, height, width, first), given in zip(small, ins):
            relay(height, width, first, given)
        first = vector_places()[0][0]
        linear[first:, :] = jnp.zeros((linear.shape[0] - first, 128), jnp.float32)
        for row, kind, top, lane in vector_places():
            linear[row : row + 1, :] = ins[kind - 2][top : top + 1, lane : lane + 128]
        for j, (name, height, width, first) in enumerate(big):
            copies[j].wait()
            relay(height, width, first, kept[j])

    for shard in range(shards):

        def two(j, carry, shard=shard):
            parts = []
            for half in range(2):
                block = order_ref[(step * shards + shard) * (rows // 8) + j * 2 + half]
                parts.append(linear[pl.ds(pl.multiple_of(block * 8, 8), 8), :])
            low_ref[shard, pl.ds(pl.multiple_of(j * 16, 16), 16), :] = jnp.concatenate(parts, axis=0).astype(low_ref.dtype)
            return carry

        lax.fori_loop(0, rows // 16, two, 0, unroll=20)


def collect_packed(grads, slots, blocks, shards, rows):
    some = shards_a_step(shards, 2)
    whole = [pl.BlockSpec(grad.shape, lambda s, order: (0, 0), pipeline_mode=pl.Buffered(1)) for grad in grads[4:]]
    return pl.pallas_call(
        collect_kernel,
        out_shape=jax.ShapeDtypeStruct((shards, rows, 128), jnp.bfloat16),
        grid_spec=pltpu.PrefetchScalarGridSpec(
            num_scalar_prefetch=1,
            grid=(shards // some,),
            in_specs=[pl.BlockSpec(memory_space=pl.ANY)] * 4 + whole,
            out_specs=pl.BlockSpec((some, rows, 128), lambda s, order: (s, 0, 0)),
            scratch_shapes=[pltpu.VMEM(((blocks + 1) * 8, 128), jnp.float32)]
            + [pltpu.VMEM(grad.shape, grad.dtype) for grad in grads[:4]]
            + [pltpu.SemaphoreType.DMA((4,))],
        ),
        compiler_params=pltpu.CompilerParams(vmem_limit_bytes=60 << 20),
        name="collect_packed",
    )(slots, *grads)


def finer(a, b, left, right):
    return lax.dot_general(
        a, b, (((left,), (right,)), ((), ())), precision=lax.Precision.HIGH, preferred_element_type=jnp.float32
    )


def unit_scale(values):
    center = values - jnp.mean(values, axis=-1, keepdims=True)
    scale = lax.rsqrt(jnp.mean(center * center, axis=-1, keepdims=True) + 1e-06)
    return center * scale, scale


def unit_back(grad, unit, scale, gain):
    inner = grad * gain
    return scale * (
        inner - jnp.mean(inner, axis=-1, keepdims=True) - unit * jnp.mean(inner * unit, axis=-1, keepdims=True)
    )


def wave_kernel(embed_ref, wq_ref, wk_ref, wv_ref, wo_ref, win_ref, wout_ref, vec_ref, shaped_ref, own_ref, kept_ref, slope_ref):
    rows = embed_ref.shape[0]
    groups = rows // NB
    embedded = embed_ref[...]
    queries = finer(embedded, wq_ref[...], 1, 0)
    keys = finer(embedded, wk_ref[...], 1, 0)
    values = finer(embedded, wv_ref[...], 1, 0)
    size = E // HH
    across = lax.broadcasted_iota(jnp.int32, (rows, rows), 0) // NB == lax.broadcasted_iota(jnp.int32, (rows, rows), 1) // NB
    mixed = []
    for head in range(HH):
        lanes = slice(head * size, head * size + size)
        scores = finer(queries[:, lanes], keys[:, lanes], 1, 1) * size**-0.5
        scores = jnp.where(across, scores, -1e30)
        weight = jnp.exp(scores - jnp.max(scores, axis=-1, keepdims=True))
        weight = weight / jnp.sum(weight, axis=-1, keepdims=True)
        kept_ref[head] = weight
        mixed.append(finer(weight, values[:, lanes], 1, 0))
    mixed = jnp.concatenate(mixed, axis=1)
    unit_one, scale_one = unit_scale(embedded + finer(mixed, wo_ref[...], 1, 0))
    first = unit_one * vec_ref[0:1, :] + vec_ref[1:2, :]
    inner = finer(first, win_ref[...], 1, 0)
    half = 0.5 * (1.0 + lax.erf(inner * 0.5**0.5))
    slope_ref[0] = inner * half
    slope_ref[1] = half + inner * jnp.exp(-0.5 * inner * inner) * (2.0 * math.pi) ** -0.5
    unit_two, scale_two = unit_scale(first + finer(inner * half, wout_ref[...], 1, 0))
    shaped = (unit_two * vec_ref[2:3, :] + vec_ref[3:4, :] + embedded).astype(jnp.bfloat16)
    for j, part in enumerate((queries, keys, values, mixed, unit_one, unit_two)):
        kept_ref[HH + j] = part
    kept_ref[HH + 6] = jnp.broadcast_to(scale_one, (rows, E))
    kept_ref[HH + 7] = jnp.broadcast_to(scale_two, (rows, E))
    shaped_ref[...] = shaped
    wide = shaped.astype(jnp.float32)
    width = E // groups
    group = lax.axis_index("group")
    own = jnp.zeros((rows, width), jnp.float32)
    for j in range(groups):
        own = jnp.where(group == j, wide[:, j * width : (j + 1) * width], own)
    own_ref[...] = own.astype(jnp.bfloat16)


def wave_layer(embedded, mats, vectors):
    rows = embedded.shape[0]
    groups = rows // NB
    f32, bf16 = jnp.float32, jnp.bfloat16
    return pl.pallas_call(
        wave_kernel,
        out_shape=[
            jax.ShapeDtypeStruct((rows, E), bf16),
            jax.ShapeDtypeStruct((rows, E // groups), bf16),
            jax.ShapeDtypeStruct((HH + 8, rows, E), f32),
            jax.ShapeDtypeStruct((2, rows, HFF), f32),
        ],
        compiler_params=pltpu.CompilerParams(vmem_limit_bytes=60 << 20),
        name="wave_layer",
    )(embedded, *mats, vectors)


def wave_back_kernel(part_ref, embed_ref, kept_ref, slope_ref, wq_ref, wk_ref, wv_ref, wo_ref, win_ref, wout_ref, vec_ref,
                     gq_ref, gk_ref, gv_ref, go_ref, gin_ref, gout_ref, gvec_ref):
    rows = embed_ref.shape[0]
    groups = rows // NB
    width = E // groups
    size = E // HH
    group = lax.axis_index("group")
    spread = jnp.concatenate([part_ref[...]] * groups, axis=1)
    lane = lax.broadcasted_iota(jnp.int32, (rows, E), 1) // width
    grad = jnp.where(lane == group, spread, 0.0)
    embedded = embed_ref[...]
    queries, keys, values, mixed, unit_one, unit_two, scale_one, scale_two = (kept_ref[HH + j] for j in range(8))
    gvec_ref[...] = jnp.zeros_like(gvec_ref)
    gvec_ref[2:3, :] = jnp.sum(grad * unit_two, axis=0, keepdims=True)
    gvec_ref[3:4, :] = jnp.sum(grad, axis=0, keepdims=True)
    grad = unit_back(grad, unit_two, scale_two, vec_ref[2:3, :])
    gout_ref[...] = finer(slope_ref[0], grad, 0, 0)
    inner = finer(grad, wout_ref[...], 1, 1) * slope_ref[1]
    first = unit_one * vec_ref[0:1, :] + vec_ref[1:2, :]
    gin_ref[...] = finer(first, inner, 0, 0)
    grad = grad + finer(inner, win_ref[...], 1, 1)
    gvec_ref[0:1, :] = jnp.sum(grad * unit_one, axis=0, keepdims=True)
    gvec_ref[1:2, :] = jnp.sum(grad, axis=0, keepdims=True)
    grad = unit_back(grad, unit_one, scale_one, vec_ref[0:1, :])
    go_ref[...] = finer(mixed, grad, 0, 0)
    grad = finer(grad, wo_ref[...], 1, 1)
    parts = [[], [], []]
    for head in range(HH):
        lanes = slice(head * size, head * size + size)
        weight = kept_ref[head]
        grad_weight = finer(grad[:, lanes], values[:, lanes], 1, 1)
        parts[2].append(finer(weight, grad[:, lanes], 0, 0))
        score = weight * (grad_weight - jnp.sum(weight * grad_weight, axis=-1, keepdims=True)) * size**-0.5
        parts[0].append(finer(score, keys[:, lanes], 1, 0))
        parts[1].append(finer(score, queries[:, lanes], 0, 0))
    for out, part in zip((gq_ref, gk_ref, gv_ref), parts):
        out[...] = finer(embedded, jnp.concatenate(part, axis=1), 0, 0)


def wave_back(part, embedded, kept, slope, mats, vectors):
    f32 = jnp.float32
    return pl.pallas_call(
        wave_back_kernel,
        out_shape=[jax.ShapeDtypeStruct(mat.shape, f32) for mat in mats] + [jax.ShapeDtypeStruct((8, E), f32)],
        compiler_params=pltpu.CompilerParams(vmem_limit_bytes=60 << 20),
        name="wave_back",
    )(part, embedded, kept, slope, *mats, vectors)


def tall(count):
    return -(-count // 16) * 16


def dot_nn(a, b):
    return lax.dot_general(a, b, (((1,), (0,)), ((), ())), preferred_element_type=jnp.float32)


def dot_nt(a, b):
    return lax.dot_general(a, b, (((1,), (1,)), ((), ())), preferred_element_type=jnp.float32)


def dot_tn(a, b):
    return lax.dot_general(a, b, (((0,), (0,)), ((), ())), preferred_element_type=jnp.float32)


def block_kernel(stream_ref, up_ref, vec_ref, wqkv_hbm, wout_hbm, wup_hbm, wdown_hbm,
                 out_ref, low_ref, gvec_ref, gqkv_hbm, gout_hbm, gup_hbm, gdown_hbm,
                 wqkv, wout, wup, wdown, gqkv, gout, gup, gdown,
                 xs, ups, up_low, norm_one, qkv, att, probs, mid, norm_two, acc, hid_low, datt, dqkv, in_sem, out_sem):
    f32, bf16 = jnp.float32, jnp.bfloat16
    seq = stream_ref.shape[0]
    rows = xs.shape[0]
    loads = [
        pltpu.make_async_copy(src, dst, in_sem.at[j])
        for j, (src, dst) in enumerate(((wqkv_hbm, wqkv), (wout_hbm, wout), (wup_hbm, wup), (wdown_hbm, wdown)))
    ]
    for load in loads:
        load.start()
    stores = [
        pltpu.make_async_copy(src, dst, out_sem.at[j])
        for j, (src, dst) in enumerate(((gqkv, gqkv_hbm), (gout, gout_hbm), (gup, gup_hbm), (gdown, gdown_hbm)))
    ]
    gain_one, shift_one = vec_ref[0:1, :], vec_ref[1:2, :]
    gain_two, shift_two = vec_ref[2:3, :], vec_ref[3:4, :]
    xs[...] = jnp.zeros_like(xs)
    xs[0:seq, :] = stream_ref[...] + vec_ref[4:5, :]
    ups[...] = jnp.zeros_like(ups)
    ups[0:seq, :] = up_ref[...].astype(f32)
    up_low[...] = ups[...].astype(bf16)

    def normed(values):
        center = values - jnp.mean(values, axis=-1, keepdims=True)
        scale = lax.rsqrt(jnp.mean(center * center, axis=-1, keepdims=True) + 1e-06)
        return center * scale, scale

    def normed_back(grad, unit, scale, gain):
        inner = grad * gain
        return scale * (
            inner
            - jnp.mean(inner, axis=-1, keepdims=True)
            - unit * jnp.mean(inner * unit, axis=-1, keepdims=True)
        )

    unit, scale = normed(xs[...])
    norm_one[...] = (unit * gain_one + shift_one).astype(bf16)
    loads[0].wait()

    def tile(j, size=D):
        return pl.ds(pl.multiple_of(j * size, size), size)

    def each(count, body):
        lax.fori_loop(0, count, lambda j, carry: (body(j), carry)[1], 0)

    def qkv_part(j):
        qkv[:, tile(j)] = dot_nn(norm_one[...], wqkv[:, tile(j)]).astype(bf16)

    each(3, qkv_part)
    inside = lax.broadcasted_iota(jnp.int32, (rows, rows), 1) < seq

    def heads(p):
        pair = [qkv[:, pl.ds(pl.multiple_of(j * D + p * 128, 128), 128)] for j in range(3)]
        outs = []
        for h in range(2):
            query, key, value = (part[:, h * HD : h * HD + HD] for part in pair)
            scores = jnp.where(inside, dot_nt(query, key) * (HD**-0.5), -1e30)
            weight = jnp.exp(scores - jnp.max(scores, axis=-1, keepdims=True))
            weight = weight / jnp.sum(weight, axis=-1, keepdims=True)
            probs[p * 2 + h] = weight
            outs.append(dot_nn(weight.astype(bf16), value))
        att[:, pl.ds(pl.multiple_of(p * 128, 128), 128)] = jnp.concatenate(outs, axis=1).astype(bf16)

    each(HEADS // 2, heads)
    loads[1].wait()
    mid[...] = xs[...] + dot_nn(att[...], wout[...])
    unit, scale = normed(mid[...])
    norm_two[...] = (unit * gain_two + shift_two).astype(bf16)
    loads[2].wait()
    loads[3].wait()
    acc[...] = jnp.zeros_like(acc)

    def hidden_part(j):
        hidden = dot_nn(norm_two[...], wup[:, tile(j)])
        half = 0.5 * (1.0 + lax.erf(hidden * (0.5**0.5)))
        active = (hidden * half).astype(bf16)
        slope = half + hidden * jnp.exp(-0.5 * hidden * hidden) * (2.0 * math.pi) ** -0.5
        mid[...] += dot_nn(active, wdown[tile(j), :])
        gdown[tile(j), :] = dot_tn(active, up_low[...]).astype(bf16)
        grad_hidden = (dot_nt(up_low[...], wdown[tile(j), :]) * slope).astype(bf16)
        gup[:, tile(j)] = dot_tn(norm_two[...], grad_hidden).astype(bf16)
        acc[...] += dot_nt(grad_hidden, wup[:, tile(j)])

    kept_unit, kept_scale = unit, scale
    hid_low[...] = kept_unit
    each(HID // D, hidden_part)
    stores[2].start()
    stores[3].start()
    out_ref[...] = mid[0:seq, :].astype(bf16)
    grad = acc[...]
    unit = hid_low[...]
    gvec_ref[...] = jnp.zeros_like(gvec_ref)
    gvec_ref[2:3, :] = jnp.sum(grad * unit, axis=0, keepdims=True)
    gvec_ref[3:4, :] = jnp.sum(grad, axis=0, keepdims=True)
    ups[...] += normed_back(grad, unit, kept_scale, gain_two)
    up_low[...] = ups[...].astype(bf16)
    gout[...] = dot_tn(att[...], up_low[...]).astype(bf16)
    stores[1].start()
    datt[...] = dot_nt(up_low[...], wout[...]).astype(bf16)

    def heads_back(p):
        pair = [qkv[:, pl.ds(pl.multiple_of(j * D + p * 128, 128), 128)] for j in range(3)]
        grad_pair = datt[:, pl.ds(pl.multiple_of(p * 128, 128), 128)]
        grads = [[], [], []]
        for h in range(2):
            query, key, value = (part[:, h * HD : h * HD + HD] for part in pair)
            grad_out = grad_pair[:, h * HD : h * HD + HD]
            weight = probs[p * 2 + h]
            grad_weight = dot_nt(grad_out, value)
            grads[2].append(dot_tn(weight.astype(bf16), grad_out))
            grad_score = weight * (grad_weight - jnp.sum(weight * grad_weight, axis=-1, keepdims=True))
            grad_score = grad_score.astype(bf16)
            grads[0].append(dot_nn(grad_score, key) * (HD**-0.5))
            grads[1].append(dot_tn(grad_score, query) * (HD**-0.5))
        for j in range(3):
            dqkv[:, pl.ds(pl.multiple_of(j * D + p * 128, 128), 128)] = jnp.concatenate(grads[j], axis=1).astype(bf16)

    each(HEADS // 2, heads_back)
    acc[...] = jnp.zeros_like(acc)

    def qkv_back(j):
        gqkv[:, tile(j)] = dot_tn(norm_one[...], dqkv[:, tile(j)]).astype(bf16)
        acc[...] += dot_nt(dqkv[:, tile(j)], wqkv[:, tile(j)])

    each(3, qkv_back)
    stores[0].start()
    unit, scale = normed(xs[...])
    grad = acc[...]
    gvec_ref[0:1, :] = jnp.sum(grad * unit, axis=0, keepdims=True)
    gvec_ref[1:2, :] = jnp.sum(grad, axis=0, keepdims=True)
    total = ups[...] + normed_back(grad, unit, scale, gain_one)
    gvec_ref[4:5, :] = jnp.sum(total, axis=0, keepdims=True)
    low_ref[...] = total.astype(bf16)
    for store in stores:
        store.wait()


def block_pass(stream, upstream, vectors, wqkv, wout, wup, wdown):
    f32, bf16 = jnp.float32, jnp.bfloat16
    seq = stream.shape[0]
    rows = tall(seq)
    whole = pl.BlockSpec(memory_space=pltpu.VMEM)
    far = pl.BlockSpec(memory_space=pl.ANY)
    mats = [wqkv, wout, wup, wdown]
    kept = [pltpu.VMEM(mat.shape, bf16) for mat in mats]
    dma = pltpu.SemaphoreType.DMA
    return pl.pallas_call(
        block_kernel,
        out_shape=[
            jax.ShapeDtypeStruct((seq, D), bf16),
            jax.ShapeDtypeStruct((rows, D), bf16),
            jax.ShapeDtypeStruct((8, D), f32),
        ]
        + [jax.ShapeDtypeStruct(mat.shape, bf16) for mat in mats],
        in_specs=[whole] * 3 + [far] * 4,
        out_specs=[whole] * 3 + [far] * 4,
        scratch_shapes=kept
        + kept
        + [
            pltpu.VMEM((rows, D), f32),
            pltpu.VMEM((rows, D), f32),
            pltpu.VMEM((rows, D), bf16),
            pltpu.VMEM((rows, D), bf16),
            pltpu.VMEM((rows, 3 * D), bf16),
            pltpu.VMEM((rows, D), bf16),
            pltpu.VMEM((HEADS, rows, rows), f32),
            pltpu.VMEM((rows, D), f32),
            pltpu.VMEM((rows, D), bf16),
            pltpu.VMEM((rows, D), f32),
            pltpu.VMEM((rows, D), f32),
            pltpu.VMEM((rows, D), bf16),
            pltpu.VMEM((rows, 3 * D), bf16),
            dma((4,)),
            dma((4,)),
        ],
        compiler_params=pltpu.CompilerParams(vmem_limit_bytes=60 << 20),
        cost_estimate=pl.CostEstimate(flops=8_400_000_000, bytes_accessed=30_000_000, transcendentals=2_000_000),
        name="block_pass",
    )(stream, upstream, vectors, *mats)


def adamw_step(weight, moment_one, moment_two, grad, rate):
    first = beta_one * moment_one + (1.0 - beta_one) * grad
    second = beta_two * moment_two + (1.0 - beta_two) * grad * grad
    fix_one = 1.0 - beta_one**STEP
    fix_two = 1.0 - beta_two**STEP
    update = first / fix_one / (jnp.sqrt(second / fix_two) + epsilon_add) + decay_rate * weight
    return (weight - rate * update, first, second)


NC = 15
HEAD = 96


def dims_step(count):
    return 16 if count % 16 == 0 else count


def spread_bands(shaped, master, turned, out):
    dims = out.shape[0]
    for dim in range(dims):
        part = dot_nn(shaped, master[:, dim * PATCH : (dim + 1) * PATCH])
        turned[pl.ds(dim, NB, stride=dims), :] = part[:, :128]
        turned[pl.ds(NB * dims + dim, NB, stride=dims), :] = part[:, 128:]
    for band in range(NB):
        for half in range(2):
            row = half * NB * dims + band * dims
            lane = band * PATCH + half * 128
            out[:, lane : lane + 128] = turned[row : row + dims, :].astype(out.dtype)


def own_bands(shaped_ref):
    return shaped_ref[pl.ds(pl.multiple_of(lax.axis_index("group") * NB, NB), NB), :]


def make_kernel(shaped_ref, master_ref, kernel_ref, turned):
    spread_bands(own_bands(shaped_ref), master_ref, turned, kernel_ref)


def make_kernels(shaped, master):
    dims = master.shape[1] // PATCH
    step = dims_step(dims)
    return pl.pallas_call(
        make_kernel,
        out_shape=jax.ShapeDtypeStruct((dims, NB * PATCH), jnp.bfloat16),
        grid=(dims // step,),
        in_specs=[
            pl.BlockSpec(shaped.shape, lambda j: (0, 0)),
            pl.BlockSpec((E, step * PATCH), lambda j: (0, j)),
        ],
        out_specs=pl.BlockSpec((step, NB * PATCH), lambda j: (j, 0)),
        scratch_shapes=[pltpu.VMEM((2 * NB * step, 128), jnp.float32)],
        compiler_params=pltpu.CompilerParams(vmem_limit_bytes=60 << 20),
        name="make_kernels",
    )(shaped, master)


def embed_kernel(pixel_ref, mask_ref, kernel_ref, stream_ref):
    masked = pixel_ref[...] * mask_ref[...].astype(jnp.bfloat16)
    part = dot_nt(masked, kernel_ref[...])

    @pl.when(pl.program_id(0) == 0)
    def _():
        stream_ref[...] = part

    @pl.when(pl.program_id(0) > 0)
    def _():
        stream_ref[...] += part


def embed_patches(pixels, mask, kernels):
    seq, width = pixels.shape[1], pixels.shape[2]
    cut = 1024
    return pl.pallas_call(
        embed_kernel,
        out_shape=jax.ShapeDtypeStruct((seq, D), jnp.float32),
        grid=(width // cut,),
        in_specs=[
            pl.BlockSpec((None, seq, cut), lambda j: (0, 0, j)),
            pl.BlockSpec((1, cut), lambda j: (0, j)),
            pl.BlockSpec((D, cut), lambda j: (0, j)),
        ],
        out_specs=pl.BlockSpec((seq, D), lambda j: (0, 0)),
        compiler_params=pltpu.CompilerParams(vmem_limit_bytes=60 << 20),
        name="embed_patches",
    )(pixels, mask, kernels)


def unembed_kernel(masked_ref, mask_ref, kernel_ref, low_ref, back_ref, grad_ref):
    seq = back_ref.shape[0]
    back_ref[...] = (dot_nn(low_ref[...], kernel_ref[...])[0:seq] * mask_ref[...]).astype(back_ref.dtype)
    grad_ref[...] = dot_tn(low_ref[...], masked_ref[...]).astype(grad_ref.dtype)


def unembed_patches(masked, mask, kernels, low, seq):
    rows, width = masked.shape
    cut = 1024
    return pl.pallas_call(
        unembed_kernel,
        out_shape=[
            jax.ShapeDtypeStruct((1, seq, width), jnp.bfloat16),
            jax.ShapeDtypeStruct((D, width), jnp.bfloat16),
        ],
        grid=(width // cut,),
        in_specs=[
            pl.BlockSpec((rows, cut), lambda j: (0, j)),
            pl.BlockSpec((1, cut), lambda j: (0, j)),
            pl.BlockSpec((D, cut), lambda j: (0, j)),
            pl.BlockSpec(low.shape, lambda j: (0, 0)),
        ],
        out_specs=[
            pl.BlockSpec((None, seq, cut), lambda j: (0, 0, j)),
            pl.BlockSpec((D, cut), lambda j: (0, j)),
        ],
        compiler_params=pltpu.CompilerParams(vmem_limit_bytes=60 << 20),
        name="unembed_patches",
    )(masked, mask, kernels, low)


def master_kernel(rate, grad_ref, shaped_ref, weight_ref, one_ref, two_ref, new_ref, first_ref, second_ref, back_ref, turned):
    groups, dims = grad_ref.shape[0], grad_ref.shape[1]
    bands = groups * NB
    for group in range(groups):
        for band in range(NB):
            for half in range(2):
                row = half * bands * dims + (group * NB + band) * dims
                lane = band * PATCH + half * 128
                turned[row : row + dims, :] = grad_ref[group, :, lane : lane + 128].astype(jnp.float32)
    total = jnp.zeros(back_ref.shape, jnp.float32)
    for dim in range(dims):
        part = jnp.concatenate(
            [turned[pl.ds(half * bands * dims + dim, bands, stride=dims), :] for half in range(2)], axis=1
        ).astype(jnp.bfloat16)
        lanes = slice(dim * PATCH, (dim + 1) * PATCH)
        weight = weight_ref[:, lanes]
        total += dot_nt(part, weight.astype(jnp.bfloat16))
        grad = dot_tn(shaped_ref[...], part)
        new_ref[:, lanes], first_ref[:, lanes], second_ref[:, lanes] = adamw_step(
            weight, one_ref[:, lanes], two_ref[:, lanes], grad, rate
        )

    @pl.when(pl.program_id(0) == 0)
    def _():
        back_ref[...] = total

    @pl.when(pl.program_id(0) > 0)
    def _():
        back_ref[...] += total


def master_update(grads, shaped, weight, one, two, rate):
    groups, dims = grads.shape[0], grads.shape[1]
    step = dims_step(dims)
    columns = pl.BlockSpec((weight.shape[0], step * PATCH), lambda j: (0, j))
    like = jax.ShapeDtypeStruct(weight.shape, jnp.float32)
    return pl.pallas_call(
        functools.partial(master_kernel, rate),
        out_shape=[like, like, like, jax.ShapeDtypeStruct(shaped.shape, jnp.float32)],
        grid=(dims // step,),
        in_specs=[
            pl.BlockSpec((groups, step, NB * PATCH), lambda j: (0, j, 0)),
            pl.BlockSpec(shaped.shape, lambda j: (0, 0)),
            columns,
            columns,
            columns,
        ],
        out_specs=[columns, columns, columns, pl.BlockSpec(shaped.shape, lambda j: (0, 0))],
        scratch_shapes=[pltpu.VMEM((2 * groups * NB * step, 128), jnp.float32)],
        compiler_params=pltpu.CompilerParams(vmem_limit_bytes=60 << 20),
        name="master_update",
    )(grads, shaped, weight, one, two)


def spot():
    group = lax.axis_index("group")
    image = lax.axis_index("img")
    return group // 2, group % 2, image // 2, image % 2


def place(y, c, z, x):
    return (y * 2 + c, z * 2 + x)


def partners():
    y, c, z, x = spot()
    x2, y2 = x + (1 - c) * (1 - 2 * x), y + c * (1 - 2 * y)
    x3, y3 = x + c * (1 - 2 * x), y + (1 - c) * (1 - 2 * y)
    around = [place(y, c, (z + d) % 4, x) for d in (1, 2, 3)]
    return (x2, y2), (x3, y3), around, place(y2, c, z, x2), place(y3, c, z, x3), place(y, 1 - c, z, x)


def greet(peers):
    barrier = pltpu.get_barrier_semaphore()
    for peer in peers:
        pl.semaphore_signal(barrier, inc=1, device_id=peer, device_id_type=MESH)
    pl.semaphore_wait(barrier, len(peers))


def remote(src, dst, send_sem, recv_sem, target):
    return pltpu.make_async_remote_copy(
        src_ref=src, dst_ref=dst, send_sem=send_sem, recv_sem=recv_sem, device_id=target, device_id_type=MESH
    )


def gather_kernel(rest_ref, pixel_ref, weight_ref, up_ref, mask_ref, all_ref, head_ref, low_ref, up_in, mask_in, own_ref, wide, narrow, weight_sem, head_sem, local_sem, line_send, line_recv, group_send, group_recv, twin_send, twin_recv):
    y, c, z, x = spot()
    (x2, y2), (x3, y3), around, second, third, twin = partners()
    partner = place(y, 1 - c, (z + 2) % 4, x)
    moved = (c + z // 2) % 2 == 1
    rows = own_ref.shape[0] // NC

    def cut(k):
        return pl.ds(k * rows, rows)

    head = remote(pixel_ref.at[0, pl.ds(0, HEAD)], head_ref.at[0], head_sem.at[0], head_sem.at[1], partner)
    small = [
        remote(up_ref, up_in, head_sem.at[2], head_sem.at[3], partner),
        remote(mask_ref, mask_in, head_sem.at[4], head_sem.at[5], partner),
    ]

    def along(d, k):
        return remote(own_ref.at[cut(k)], all_ref.at[y, c, z, x, cut(k)], line_send.at[d - 1, k], line_recv.at[d - 1, k], around[d - 1])

    def along_in(d, k):
        return remote(own_ref.at[cut(k)], all_ref.at[y, c, (z + 4 - d) % 4, x, cut(k)], line_send.at[d - 1, k], line_recv.at[d - 1, k], around[d - 1])

    def square(core, j):
        yy, xx = ((y, x), (y2, x2), (y3, x3), (1 - y, 1 - x))[j]
        return all_ref.at[yy, core, :, xx]

    def hop(j, to, k, slot, landing):
        part = square(c, j).at[:, cut(k)]
        return remote(part, part, group_send.at[slot, k], group_recv.at[landing, k], to)

    def hop_in(landing, k):
        part = square(c, landing).at[:, cut(k)]
        return remote(part, part, group_send.at[0, k], group_recv.at[landing, k], twin)

    def share(j, k):
        part = square(c, j).at[:, cut(k)]
        yy, xx = ((y, x), (y2, x2), (y3, x3), (1 - y, 1 - x))[j]
        landing = (0, 2, 1, 3)[j]
        return remote(part, part, twin_send.at[j, k], twin_recv.at[landing, k], twin)

    def share_in(landing, k):
        yy, xx = ((y, x), (y2, x2), (y3, x3), (1 - y, 1 - x))[landing]
        part = all_ref.at[yy, 1 - c, :, xx, cut(k)]
        return remote(part, part, twin_send.at[0, k], twin_recv.at[landing, k], twin)

    fetch = pltpu.make_async_copy(weight_ref, wide, weight_sem.at[0])
    store = pltpu.make_async_copy(narrow, low_ref, weight_sem.at[1])
    fetch.start()
    even = rest_ref.shape[0] // 16 * 16
    own_ref[0:even, :] = rest_ref[0:even, :].astype(jnp.bfloat16)
    if even < own_ref.shape[0]:
        left = rest_ref.shape[0] - even
        parts = [rest_ref[even:, :]] if left else []
        parts.append(jnp.zeros((own_ref.shape[0] - even - left, 128), jnp.float32))
        own_ref[even:, :] = jnp.concatenate(parts, axis=0).astype(jnp.bfloat16)
    keep = pltpu.make_async_copy(own_ref, all_ref.at[y, c, z, x], local_sem)
    keep.start()
    greet(around + [second, third, twin, partner])
    for k in range(NC):
        for d in (1, 2, 3):
            along(d, k).start()
    keep.wait()
    for step in range(NC + 2):
        k = step
        if k < NC:
            for d in (1, 2, 3):
                along_in(d, k).wait_recv()
            hop(0, third, k, 0, 2).start()
            hop(0, second, k, 1, 1).start()
            share(0, k).start()
        if step == 3:
            fetch.wait()
            narrow[...] = wide[...].astype(jnp.bfloat16)
            store.start()
        if step == NC // 2 + 1:

            @pl.when(moved)
            def _():
                head.start()
                for copy in small:
                    copy.start()

        k = step - 1
        if 0 <= k < NC:
            hop_in(1, k).wait_recv()
            hop(1, third, k, 2, 3).start()
            share(1, k).start()
        k = step - 2
        if 0 <= k < NC:
            hop_in(2, k).wait_recv()
            share(2, k).start()
            hop_in(3, k).wait_recv()
            share(3, k).start()
    for k in range(NC):
        for d in (1, 2, 3):
            along(d, k).wait_send()
        hop(0, third, k, 0, 2).wait_send()
        hop(0, second, k, 1, 1).wait_send()
        hop(1, third, k, 2, 3).wait_send()
        for j in range(4):
            share(j, k).wait_send()
            share_in(j, k).wait_recv()

    store.wait()

    @pl.when(moved)
    def _():
        head.wait()
        for copy in small:
            copy.wait()


def gather_packed(own, pixels, weight, upstream, mask, rows):
    bf16 = jnp.bfloat16
    dma = pltpu.SemaphoreType.DMA
    return pl.pallas_call(
        gather_kernel,
        out_shape=[
            jax.ShapeDtypeStruct((2, 2, 4, 2, rows, 128), bf16),
            jax.ShapeDtypeStruct((1, HEAD, pixels.shape[2]), pixels.dtype),
            jax.ShapeDtypeStruct(weight.shape, bf16),
            jax.ShapeDtypeStruct(upstream.shape, upstream.dtype),
            jax.ShapeDtypeStruct(mask.shape, mask.dtype),
        ],
        in_specs=[pl.BlockSpec(memory_space=pltpu.VMEM)] + [pl.BlockSpec(memory_space=pl.ANY)] * 4,
        out_specs=[pl.BlockSpec(memory_space=pl.ANY)] * 5,
        scratch_shapes=[
            pltpu.VMEM((rows, 128), bf16),
            pltpu.VMEM(weight.shape, jnp.float32),
            pltpu.VMEM(weight.shape, bf16),
            dma((2,)),
            dma((6,)),
            dma, dma((3, NC)), dma((3, NC)), dma((3, NC)), dma((4, NC)), dma((4, NC)), dma((4, NC))],
        compiler_params=pltpu.CompilerParams(collective_id=0, has_side_effects=True, vmem_limit_bytes=60 << 20),
        name="gather_packed",
    )(own, pixels, weight, upstream, mask)


def reduce_kernel(part_ref, sum_ref, own, twin_in, third_in, second_in, line_in, load_sem, twin_send, twin_recv, third_send, third_recv, second_send, second_recv, line_send, line_recv):
    f32, bf16 = jnp.float32, jnp.bfloat16
    y, c, z, x = spot()
    (x2, y2), (x3, y3), around, second, third, twin = partners()
    rows = sum_ref.shape[0] // NC

    def cut(k):
        return pl.ds(k * rows, rows)

    spots = ((1 - y, 1 - x), (y3, x3), (y2, x2), (y, x))
    turned = ((1 - y, 1 - x), (y2, x2), (y3, x3), (y, x))

    def load(j, k):
        yy, xx = spots[j]
        return pltpu.make_async_copy(part_ref.at[yy, c, :, xx, cut(k)], own.at[j, :, cut(k)], load_sem.at[j, k])

    def swap(j, k):
        yy, xx = turned[j]
        return remote(part_ref.at[yy, 1 - c, :, xx, cut(k)], twin_in.at[j, :, cut(k)], twin_send.at[j, k], twin_recv.at[j, k], twin)

    def to_third(j, k):
        return remote(own.at[j, :, cut(k)], third_in.at[j, :, cut(k)], third_send.at[j, k], third_recv.at[j, k], third)

    def to_second(k):
        return remote(own.at[2, :, cut(k)], second_in.at[:, cut(k)], second_send.at[k], second_recv.at[k], second)

    def to_line(d, k):
        return remote(own.at[3, (z + d) % 4, cut(k)], line_in.at[d - 1, cut(k)], line_send.at[d - 1, k], line_recv.at[d - 1, k], around[d - 1])

    for k in range(NC):
        for j in range(4):
            load(j, k).start()
    greet(around + [second, third, twin])
    for k in range(NC):
        for j in range(4):
            swap(j, k).start()

    def pair(j, k):
        load(j, k).wait()
        swap(j, k).wait_recv()
        return own[j, :, cut(k)].astype(f32) + twin_in[j, :, cut(k)].astype(f32)

    for step in range(NC + 3):
        k = step
        if k < NC:
            for j in (0, 1):
                own[j, :, cut(k)] = pair(j, k).astype(bf16)
                to_third(j, k).start()
        k = step - 1
        if 0 <= k < NC:
            held = pair(2, k)
            to_third(0, k).wait_recv()
            own[2, :, cut(k)] = (held + third_in[0, :, cut(k)].astype(f32)).astype(bf16)
            to_second(k).start()
        k = step - 2
        if 0 <= k < NC:
            held = pair(3, k)
            to_third(1, k).wait_recv()
            to_second(k).wait_recv()
            held += third_in[1, :, cut(k)].astype(f32) + second_in[:, cut(k)].astype(f32)
            own[3, :, cut(k)] = held.astype(bf16)
            for d in (1, 2, 3):
                to_line(d, k).start()
        k = step - 3
        if 0 <= k < NC:
            total = own[3, z, cut(k)].astype(f32)
            for d in (1, 2, 3):
                to_line(d, k).wait_recv()
                total += line_in[d - 1, cut(k)].astype(f32)
            sum_ref[cut(k)] = total
    for k in range(NC):
        for j in range(4):
            swap(j, k).wait_send()
        for j in (0, 1):
            to_third(j, k).wait_send()
        to_second(k).wait_send()
        for d in (1, 2, 3):
            to_line(d, k).wait_send()


def reduce_packed(part):
    rows = part.shape[-2]
    bf16 = jnp.bfloat16
    dma = pltpu.SemaphoreType.DMA
    return pl.pallas_call(
        reduce_kernel,
        out_shape=jax.ShapeDtypeStruct((rows, 128), jnp.float32),
        in_specs=[pl.BlockSpec(memory_space=pl.ANY)],
        out_specs=pl.BlockSpec(memory_space=pltpu.VMEM),
        scratch_shapes=[
            pltpu.VMEM((4, 4, rows, 128), bf16),
            pltpu.VMEM((4, 4, rows, 128), bf16),
            pltpu.VMEM((2, 4, rows, 128), bf16),
            pltpu.VMEM((4, rows, 128), bf16),
            pltpu.VMEM((3, rows, 128), bf16),
            dma((4, NC)), dma((4, NC)), dma((4, NC)), dma((2, NC)), dma((2, NC)), dma((NC,)), dma((NC,)), dma((3, NC)), dma((3, NC)),
        ],
        compiler_params=pltpu.CompilerParams(collective_id=1, has_side_effects=True, vmem_limit_bytes=56 << 20),
        name="reduce_packed",
    )(part)


CHUNK = 16
CUTS = 2


def over_x(k):
    return k % 3 != 2


def over_z(k):
    return k % 3 == 0


def quad_peers():
    y, c, z, x = spot()
    low = z % 2
    side = place(y, c, z, 1 - x)
    along = place(y, c, z + 1 - 2 * low, x)
    twin = place(y, 1 - c, z, x)
    partner = place(y, 1 - c, (z + 2) % 4, x)
    moved = (c + z // 2) % 2 == 1
    return y, c, z, x, low, side, along, twin, partner, moved


def swap_group(value, flip):
    return lax.ppermute(value, "group", [(j, j ^ flip) for j in range(4)])


def swap_images(value):
    pairs = []
    for y in range(2):
        for c in range(2):
            for z in range(4):
                for x in range(2):
                    other = (1 - c, (z + 2) % 4) if c != z // 2 else (c, z)
                    pairs.append((((y * 2 + c) * 4 + z) * 2 + x, ((y * 2 + other[0]) * 4 + other[1]) * 2 + x))
    return lax.ppermute(value, ("group", "img"), pairs)


def share_kernel(shaped_ref, mask_ref, own_slab, over_slab, pixel_ref, head_ref, rest_ref,
                 all_ref, masked_ref, stream_ref, made_ref, master, turned, held, top, bottom, tile, mixed, order, slab_sem, slab_send, slab_recv, pixel_sem, store_sem, keep_sem, swap_send, swap_recv,
                 side_send, side_recv, along_send, along_recv, far_send, far_recv, twin_send, twin_recv):
    f32, bf16 = jnp.float32, jnp.bfloat16
    y, c, z, x, low, side, along, twin, partner, moved = quad_peers()
    dims, width = made_ref.shape
    chunks = dims // CHUNK
    count = chunks * CUTS
    group = 8 * CHUNK

    def cut(k):
        return pl.ds(k // CUTS * CHUNK, CHUNK), pl.ds(k % CUTS * (width // CUTS), width // CUTS)

    def rows_of(r):
        return pl.ds(r * CHUNK, CHUNK)

    def block(core, j, k):
        return held.at[2 * core + (low + j // 2) % 2, (x + j % 2) % 2, *cut(k)]

    def keep(k):
        return pltpu.make_async_copy(made_ref.at[*cut(k)], block(c, 0, k), keep_sem.at[k])

    def swap(k):
        return remote(made_ref.at[*cut(k)], block(1 - c, 0, k), swap_send.at[k], swap_recv.at[k], partner)

    def swap_in(k):
        return remote(made_ref.at[*cut(k)], block(c, 0, k), swap_send.at[k], swap_recv.at[k], partner)

    def to_side(k):
        return remote(block(c, 0, k), block(c, 0, k), side_send.at[k], side_recv.at[k], side)

    def from_side(k):
        return remote(block(c, 1, k), block(c, 1, k), side_send.at[k], side_recv.at[k], side)

    def to_along(k):
        return remote(block(c, 0, k), block(c, 0, k), along_send.at[k], along_recv.at[k], along)

    def from_along(k):
        return remote(block(c, 2, k), block(c, 2, k), along_send.at[k], along_recv.at[k], along)

    def pass_on(k):
        j, to = (2, side) if over_x(k) else (1, along)
        return remote(block(c, j, k), block(c, j, k), far_send.at[k], far_recv.at[k], to)

    def from_far(k):
        return remote(block(c, 3, k), block(c, 3, k), far_send.at[k], far_recv.at[k], twin)

    def give(j, k):
        return remote(block(c, j, k), block(c, j, k), twin_send.at[j, k], twin_recv.at[j, k], twin)

    def given(j, k):
        return remote(block(1 - c, j, k), block(1 - c, j, k), twin_send.at[j, k], twin_recv.at[j, k], twin)

    def slab(core, j, k):
        owner = (y + j) % 2 * 2 + core
        size = own_slab.shape[0]
        return master.at[k, pl.ds(pl.multiple_of(owner * size, size), size)]

    def slab_here(j, k):
        lanes = pl.ds(k * CHUNK * PATCH, CHUNK * PATCH)
        return (own_slab, over_slab)[j].at[:, lanes]

    def load_slab(j, k):
        return pltpu.make_async_copy(slab_here(j, k), slab(c, j, k), slab_sem.at[j, k])

    def send_slab(j, k):
        return remote(slab_here(j, k), slab(c, j, k), slab_send.at[j, k], slab_recv.at[j, k], twin)

    def slab_in(j, k):
        return remote(slab_here(j, k), slab(1 - c, j, k), slab_send.at[j, k], slab_recv.at[j, k], twin)

    def make(k):
        for j in range(2):
            load_slab(j, k).wait()
            slab_in(j, k).wait_recv()
        spread_bands(own_bands(shaped_ref), master.at[k], turned, made_ref.at[rows_of(k)])

        @pl.when(moved)
        def _():
            for cut_at in range(CUTS):
                swap(k * CUTS + cut_at).start()

        @pl.when(jnp.logical_not(moved))
        def _():
            for cut_at in range(CUTS):
                keep(k * CUTS + cut_at).start()

    def store(r):
        return pltpu.make_async_copy(held.at[:, :, rows_of(r)], all_ref.at[:, :, rows_of(r)], store_sem.at[r])

    swapped = pltpu.make_async_copy(head_ref.at[0], top, pixel_sem.at[0])
    owned = pltpu.make_async_copy(pixel_ref.at[0, pl.ds(0, HEAD)], top, pixel_sem.at[0])
    lower = pltpu.make_async_copy(rest_ref.at[0], bottom, pixel_sem.at[1])

    for k in range(chunks):
        for j in range(2):
            load_slab(j, k).start()

    @pl.when(jnp.logical_not(moved))
    def _():
        owned.start()

    @pl.when(moved)
    def _():
        swapped.start()

    lower.start()
    greet([side, along, twin, partner])
    for k in range(chunks):
        for j in range(2):
            send_slab(j, k).start()
    make(0)

    def mask_pixels(part):
        @pl.when(part == 0)
        def _():
            lower.wait()
            owned.wait()

        def some(j, carry):
            lanes = pl.ds(pl.multiple_of(j * 1024, 1024), 1024)
            mask = mask_ref[:, lanes]
            masked_ref[0:HEAD, lanes] = (top[:, lanes].astype(f32) * mask).astype(bf16)
            tile[...] = jnp.zeros_like(tile)
            tile[0 : bottom.shape[0], :] = bottom[:, lanes].astype(f32) * mask
            masked_ref[HEAD:, lanes] = tile[...].astype(bf16)
            return carry

        cuts = width // 1024
        lax.fori_loop(part * (cuts // 2), (part + 1) * (cuts // 2), some, 0)

    def make_order():
        row = lax.broadcasted_iota(jnp.int32, order.shape, 0)
        column = lax.broadcasted_iota(jnp.int32, order.shape, 1)
        wanted = row % group // CHUNK * dims + row // group * CHUNK + row % CHUNK
        order[...] = jnp.where(column == wanted, 1.0, 0.0)

    for step in range(count + 3):
        k = step
        if k < count:

            @pl.when(moved)
            def _(k=k):
                swap_in(k).wait_recv()

            @pl.when(jnp.logical_not(moved))
            def _(k=k):
                keep(k).wait()

            to_side(k).start()
            to_along(k).start()
            give(0, k).start()
        if step % CUTS == 0 and step // CUTS + 1 < chunks:
            make(step // CUTS + 1)
        if step in (1, 3):
            mask_pixels(step // 2)
        elif step == 5:
            make_order()
        k = step - 1
        if 0 <= k < count:
            if over_x(k):
                from_along(k).wait_recv()
                pass_on(k).start()
                from_side(k).wait_recv()
            else:
                from_side(k).wait_recv()
                pass_on(k).start()
                from_along(k).wait_recv()
            give(1, k).start()
            give(2, k).start()
        k = step - 2
        if 0 <= k < count:
            from_far(k).wait_recv()
            give(3, k).start()
        k = step - 3
        if 0 <= k < count:
            for j in range(4):
                given(j, k).wait_recv()
            if k % CUTS == CUTS - 1:
                r = k // CUTS
                store(r).start()
                part = held[:, :, rows_of(r), :].reshape(group, width)
                mixed[:, r * group : (r + 1) * group] = dot_nt(masked_ref[...], part)

    stream_ref[...] = finer(mixed[...], order[...], 1, 0)[0 : stream_ref.shape[0]]

    @pl.when(moved)
    def _():
        for k in range(count):
            swap(k).wait_send()

    for k in range(count):
        to_side(k).wait_send()
        to_along(k).wait_send()
        pass_on(k).wait_send()
        for j in range(4):
            give(j, k).wait_send()
    for k in range(chunks):
        store(k).wait()
        for j in range(2):
            send_slab(j, k).wait_send()


def share_kernels(shaped, mask, slabs, pixels, head, rest):
    dims, width = slabs[0].shape[1] // PATCH, mask.shape[1]
    bf16 = jnp.bfloat16
    chunks = dims // CHUNK
    count = chunks * CUTS
    seq = pixels.shape[1]
    rows = tall(seq)
    f32 = jnp.float32
    dma = pltpu.SemaphoreType.DMA
    vmem, far = pl.BlockSpec(memory_space=pltpu.VMEM), pl.BlockSpec(memory_space=pl.ANY)
    shared, masked, stream = pl.pallas_call(
        share_kernel,
        out_shape=[
            jax.ShapeDtypeStruct((4, 2, dims, width), bf16),
            jax.ShapeDtypeStruct((rows, width), bf16),
            jax.ShapeDtypeStruct((seq, 8 * dims), f32),
        ],
        in_specs=[vmem, vmem] + [far] * 5,
        out_specs=[far, vmem, vmem],
        scratch_shapes=[
            pltpu.VMEM((dims, width), bf16),
            pltpu.VMEM((chunks, E, CHUNK * PATCH), bf16),
            pltpu.VMEM((2 * NB * CHUNK, 128), f32),
            pltpu.VMEM((4, 2, dims, width), bf16),
            pltpu.VMEM((HEAD, width), bf16),
            pltpu.VMEM((seq - HEAD, width), bf16),
            pltpu.VMEM((rows - HEAD, 1024), f32),
            pltpu.VMEM((rows, 8 * dims), f32),
            pltpu.VMEM((8 * dims, 8 * dims), f32),
            dma((2, chunks)),
            dma((2, chunks)),
            dma((2, chunks)),
            dma((2,)),
        ]
        + [dma((count,))] * 10
        + [dma((4, count))] * 2,
        compiler_params=pltpu.CompilerParams(collective_id=2, has_side_effects=True, vmem_limit_bytes=60 << 20),
        name="share_kernels",
    )(shaped, mask, *slabs, pixels, head, rest)
    return shared.reshape(8 * dims, width), masked, stream


def fold_kernel(masked_ref, mask_ref, low_ref, kernel_ref, out_ref, all_ref, back_ref, out_in,
                gone, own, twin_in, relay_in, side_in, along_in, tiles, backs, out_sem, tile_sem, back_sem, keep_sem, twin_send, twin_recv,
                relay_send, relay_recv, side_send, side_recv, along_send, along_recv, swap_send, swap_recv,
                group_send, group_recv, give_send, give_recv):
    f32, bf16 = jnp.float32, jnp.bfloat16
    y, c, z, x, low, side, along, twin, partner, moved = quad_peers()
    over = place(1 - y, c, z, x)
    dims, width = all_ref.shape[2], all_ref.shape[3]
    count = dims // CHUNK * CUTS
    seq = back_ref.shape[1]
    lane = tiles.shape[2]

    def cut(k):
        return pl.ds(k // CUTS * CHUNK, CHUNK), pl.ds(k % CUTS * (width // CUTS), width // CUTS)

    def spot_of(j):
        return (low + j // 2) % 2, (x + j % 2) % 2

    def mine(j, k):
        a, b = spot_of(j)
        return own.at[a, b, *cut(k)]

    def swap(k):
        return remote(gone.at[:, :, *cut(k)], twin_in.at[:, :, *cut(k)], twin_send.at[k], twin_recv.at[k], twin)

    def relay(k):
        return remote(mine(3, k), relay_in.at[*cut(k)], relay_send.at[k], relay_recv.at[k], along if over_z(k) else side)

    def to_side(k):
        return remote(mine(1, k), side_in.at[*cut(k)], side_send.at[k], side_recv.at[k], side)

    def to_along(k):
        return remote(mine(2, k), along_in.at[*cut(k)], along_send.at[k], along_recv.at[k], along)

    def keep(k):
        return pltpu.make_async_copy(mine(0, k), all_ref.at[y, c, *cut(k)], keep_sem.at[k])

    def move(k):
        return remote(mine(0, k), all_ref.at[y, 1 - c, *cut(k)], swap_send.at[k], swap_recv.at[k], partner)

    def moved_in(k):
        return remote(mine(0, k), all_ref.at[y, c, *cut(k)], swap_send.at[k], swap_recv.at[k], partner)

    def cross(k):
        return remote(all_ref.at[y, c, *cut(k)], all_ref.at[y, c, *cut(k)], group_send.at[k], group_recv.at[k], over)

    def crossed(k):
        return remote(all_ref.at[1 - y, c, *cut(k)], all_ref.at[1 - y, c, *cut(k)], group_send.at[k], group_recv.at[k], over)

    def give(j, k):
        here = all_ref.at[(y + j) % 2, c, *cut(k)]
        return remote(here, here, give_send.at[j, k], give_recv.at[j, k], twin)

    def given(j, k):
        here = all_ref.at[(y + j) % 2, 1 - c, *cut(k)]
        return remote(here, here, give_send.at[j, k], give_recv.at[j, k], twin)

    def fetch(j):
        return pltpu.make_async_copy(kernel_ref.at[:, pl.ds(j * lane, lane)], tiles.at[j % 2], tile_sem.at[j % 2])

    def drain(j):
        return pltpu.make_async_copy(backs.at[j % 2], back_ref.at[0, :, pl.ds(j * lane, lane)], back_sem.at[j % 2])

    def half(core, out):
        chosen = low_ref[:, pl.ds(pl.multiple_of(core * 4 * dims, 128), 4 * dims)]

        def some(j, carry):
            lanes = pl.ds(pl.multiple_of(j * 1024, 1024), 1024)
            part = dot_tn(chosen, masked_ref[:, lanes]).astype(bf16)
            out[:, :, :, lanes] = part.reshape(2, 2, dims, 1024)
            return carry

        lax.fori_loop(0, width // 1024, some, 0)

    def pixels_back(j):
        fetch(j).wait()
        if j >= 2:
            drain(j - 2).wait()
        part = dot_nn(low_ref[...], tiles[j % 2])[0:seq] * mask_ref[:, j * lane : (j + 1) * lane]
        backs[j % 2] = part.astype(bf16)
        drain(j).start()
        if (j + 2) * lane < width:
            fetch(j + 2).start()

    def pair(j, k):
        a, b = spot_of(j)
        return own[a, b, *cut(k)].astype(f32) + twin_in[a, b, *cut(k)].astype(f32)

    def put(j, k, value):
        a, b = spot_of(j)
        own[a, b, *cut(k)] = value.astype(bf16)

    output = remote(out_ref, out_in, out_sem.at[0], out_sem.at[1], partner)
    fetch(0).start()
    fetch(1).start()
    greet([side, along, twin, partner, over])

    @pl.when(moved)
    def _():
        output.start()

    half(1 - c, gone)
    for k in range(count):
        swap(k).start()
    half(c, own)

    for step in range(count + 4):
        k = step
        if k < count:
            swap(k).wait_recv()
            put(3, k, pair(3, k))
            relay(k).start()
        k = step - 1
        if 0 <= k < count:
            first, second = (to_along, to_side) if over_z(k) else (to_side, to_along)
            plain, summed = (2, 1) if over_z(k) else (1, 2)
            put(plain, k, pair(plain, k))
            first(k).start()
            relay(k).wait_recv()
            put(summed, k, pair(summed, k) + relay_in[*cut(k)].astype(f32))
            second(k).start()
        k = step - 2
        if 0 <= k < count:
            to_side(k).wait_recv()
            to_along(k).wait_recv()
            put(0, k, pair(0, k) + side_in[*cut(k)].astype(f32) + along_in[*cut(k)].astype(f32))

            @pl.when(moved)
            def _(k=k):
                move(k).start()

            @pl.when(jnp.logical_not(moved))
            def _(k=k):
                keep(k).start()

        k = step - 3
        if 0 <= k < count:

            @pl.when(moved)
            def _(k=k):
                moved_in(k).wait_recv()

            @pl.when(jnp.logical_not(moved))
            def _(k=k):
                keep(k).wait()

            cross(k).start()
            give(0, k).start()
        k = step - 4
        if 0 <= k < count:
            crossed(k).wait_recv()
            give(1, k).start()
        if step >= 2 and (step - 2) * lane < width:
            pixels_back(step - 2)

    @pl.when(moved)
    def _():
        output.wait()
        for k in range(count):
            move(k).wait_send()

    for j in (width // lane - 2, width // lane - 1):
        drain(j).wait()
    for k in range(count):
        swap(k).wait_send()
        relay(k).wait_send()
        to_side(k).wait_send()
        to_along(k).wait_send()
        cross(k).wait_send()
        for j in range(2):
            give(j, k).wait_send()
            given(j, k).wait_recv()


def fold_kernels(masked, mask, low, kernels, out):
    seq = out.shape[0]
    width = masked.shape[1]
    dims = kernels.shape[0] // 8
    count = dims // CHUNK * CUTS
    bf16 = jnp.bfloat16
    dma = pltpu.SemaphoreType.DMA
    vmem, far = pl.BlockSpec(memory_space=pltpu.VMEM), pl.BlockSpec(memory_space=pl.ANY)
    folded, back, out_in = pl.pallas_call(
        fold_kernel,
        out_shape=[
            jax.ShapeDtypeStruct((2, 2, dims, width), bf16),
            jax.ShapeDtypeStruct((1, seq, width), bf16),
            jax.ShapeDtypeStruct(out.shape, out.dtype),
        ],
        in_specs=[vmem, vmem, vmem, far, far],
        out_specs=[far, far, far],
        scratch_shapes=[
            pltpu.VMEM((2, 2, dims, width), bf16),
            pltpu.VMEM((2, 2, dims, width), bf16),
            pltpu.VMEM((2, 2, dims, width), bf16),
            pltpu.VMEM((dims, width), bf16),
            pltpu.VMEM((dims, width), bf16),
            pltpu.VMEM((dims, width), bf16),
            pltpu.VMEM((2, 8 * dims, 1024), bf16),
            pltpu.VMEM((2, seq, 1024), bf16),
            dma((2,)),
            dma((2,)),
            dma((2,)),
            dma((count,)),
        ]
        + [dma((count,))] * 12
        + [dma((2, count))] * 2,
        compiler_params=pltpu.CompilerParams(collective_id=3, has_side_effects=True, vmem_limit_bytes=60 << 20),
        name="fold_kernels",
    )(masked, mask, low, kernels, out)
    return folded.reshape(4, dims, width), back, out_in


def on_device(
    pixels,
    band_mask,
    wavelength,
    owner_order,
    rest_weight,
    rest_moment1,
    rest_moment2,
    fc_weight,
    fc_moment1,
    fc_moment2,
    cotangent,
):
    f32 = jnp.float32
    bf16 = jnp.bfloat16
    kernel_rate = float(E * PATCH * NB) ** (-0.5)
    groups = lax.axis_size("group")
    own_rows = rest_weight.shape[0]
    own_blocks = own_rows // 8
    fits = lax.axis_size("group") == 4 and lax.axis_size("img") == 8
    extra = -own_rows % 128
    slot_blocks = (own_rows + extra) // 8
    mask = band_mask.astype(f32)
    if fits:
        group, image = lax.axis_index("group"), lax.axis_index("img")
        moved = (group % 2 + image // 4) % 2 == 1
        wide_mask = jnp.pad(mask, ((0, 7), (0, 128 - NB)))
        gathered, head, low_weight, up_in, mask_in = gather_packed(
            rest_weight, pixels, fc_weight, cotangent, wide_mask, own_rows + extra
        )
        gathered, rest, low_weight = lax.optimization_barrier((gathered, pixels[:, HEAD:], low_weight))
        across = swap_group(low_weight, 2)
        rest = swap_images(rest)
        cotangent = jnp.where(moved, up_in, cotangent)
        mask = jnp.where(moved, mask_in[:1, :NB], mask)
    else:
        low_weight = fc_weight.astype(bf16)
        rest_low = jnp.pad(rest_weight.astype(bf16), ((0, extra), (0, 0)))
        gathered = lax.all_gather(rest_low, ("group", "img"), axis=0, tiled=True)
    shards = gathered.size // ((own_rows + extra) * 128)
    gathered = gathered.reshape(shards, own_rows + extra, 128)
    total_blocks = owner_order.shape[0]
    slots = jnp.pad(
        owner_order.reshape(shards, own_blocks),
        ((0, 0), (0, slot_blocks - own_blocks)),
        constant_values=total_blocks,
    ).reshape(-1)
    unpacked = spread_packed(gathered, slots, total_blocks)
    if not fits:
        master = lax.all_gather(low_weight, "group", axis=0, tiled=True)
    block_mats, wave_mats = unpacked[:4], unpacked[4:10]
    block_vectors, wave_vectors = unpacked[10:]
    embedded = embed_waves(wavelength).reshape(groups * NB, E)
    shaped_low, own_shaped, kept, slope = wave_layer(embedded, wave_mats, wave_vectors)
    mask = jnp.repeat(mask, PATCH, axis=1)
    if fits:
        kernel_all, masked, stream = share_kernels(shaped_low, mask, (low_weight, across), pixels, head, rest)
    else:
        kernel_low = make_kernels(shaped_low, master)
        kernel_all = lax.all_gather(kernel_low, "img", axis=0, tiled=True)
        stream = embed_patches(pixels, mask, kernel_all)
        masked = jnp.pad((pixels[0] * mask).astype(bf16), ((0, tall(pixels.shape[1]) - pixels.shape[1]), (0, 0)))
    block_out, grad_low, block_vectors, *block_grads = block_pass(
        stream, cotangent, block_vectors, *block_mats
    )
    if fits:
        all_groups, pixel_grad, out_in = fold_kernels(masked, mask, grad_low, kernel_all, block_out)
        all_groups, pixel_grad = lax.optimization_barrier((all_groups, pixel_grad))
        pixel_grad = swap_images(pixel_grad)
        block_out = jnp.where(moved, out_in, block_out)
    else:
        pixel_grad, kernel_grad = unembed_patches(masked, mask, kernel_all, grad_low, pixels.shape[1])
        kernel_grad_low = lax.psum_scatter(kernel_grad, "img", scatter_dimension=0, tiled=True)
        all_groups = lax.all_gather(kernel_grad_low[None], "group", axis=0, tiled=True)
    fc_new, fc_first, fc_second, shaped_part = master_update(
        all_groups,
        own_shaped,
        fc_weight,
        fc_moment1,
        fc_moment2,
        kernel_rate,
    )
    *wave_grads, wave_vectors = wave_back(shaped_part, embedded, kept, slope, wave_mats, wave_vectors)
    given = [*block_grads, *wave_grads, block_vectors, wave_vectors]
    joint_term = collect_packed(given, slots, total_blocks, shards, own_rows + extra)
    if fits:
        rest_grad = reduce_packed(joint_term.reshape(2, 2, 4, 2, own_rows + extra, 128))
    else:
        rest_grad = lax.psum_scatter(
            joint_term, ("group", "img"), scatter_dimension=0, tiled=False
        ).astype(f32)
    rest_grad = rest_grad[:own_rows]
    rest_new, rest_first, rest_second = adamw_step(
        rest_weight, rest_moment1, rest_moment2, rest_grad, rest_rate
    )
    return (block_out, pixel_grad, rest_new, rest_first, rest_second, fc_new, fc_first, fc_second)


def solution(mesh):
    placed = (
        P(("group", "img"), None, None),
        P(("group", "img"), None),
        P(),
        P(),
        P(("group", "img"), None),
        P(("group", "img"), None),
        P(("group", "img"), None),
        P("group", "img"),
        P("group", "img"),
        P("group", "img"),
        P(("group", "img"), None),
    )
    return jax.shard_map(
        on_device,
        mesh=mesh,
        in_specs=placed,
        out_specs=(
            P(("group", "img"), None),
            P(("group", "img"), None, None),
            P(("group", "img"), None),
            P(("group", "img"), None),
            P(("group", "img"), None),
            P("group", "img"),
            P("group", "img"),
            P("group", "img"),
        ),
        check_vma=False,
    )
```

```python
import functools
import math

import jax
import jax.numpy as jnp
from jax import lax
from jax.experimental import pallas as pl
from jax.experimental.pallas import tpu as pltpu
from jax.sharding import PartitionSpec as P

MESH = pl.DeviceIdType.MESH

D = 768
HEADS = 12
HD = 64
HID = 3072
E = 128
HH = 4
HFF = 2048
PATCH = 256
NB = 32
STEP = 5


beta_one = 0.5
beta_two = 0.75
decay_rate = 0.05
epsilon_add = 1e-08
rest_rate = 0.02


def layout():
    return [
        ("w_qkv", (D, 3 * D)),
        ("w_out", (D, D)),
        ("w_up", (D, HID)),
        ("w_down", (HID, D)),
        ("h_query", (E, E)),
        ("h_key", (E, E)),
        ("h_value", (E, E)),
        ("h_out", (E, E)),
        ("h_ffin", (E, HFF)),
        ("h_ffout", (HFF, E)),
        ("ln1_gain", (D,)),
        ("ln1_shift", (D,)),
        ("ln2_gain", (D,)),
        ("ln2_shift", (D,)),
        ("patch_bias", (D,)),
        ("hn1_gain", (E,)),
        ("hn1_shift", (E,)),
        ("hn2_gain", (E,)),
        ("hn2_shift", (E,)),
    ]


def embed_waves(wavelength):
    half_width = E // 2
    frequency = jnp.exp(-math.log(10000.0) * jnp.arange(half_width, dtype=jnp.float32) / half_width)
    angles = wavelength.astype(jnp.float32)[..., None] * frequency
    return jnp.concatenate([jnp.sin(angles), jnp.cos(angles)], axis=-1)


def matrices():
    listed, at = [], 0
    for name, extent in layout():
        if len(extent) == 2:
            listed.append((name, extent[0], extent[1], at))
        at += math.prod(extent) // 128
    return listed


def vector_places():
    listed, at = [], 0
    rows = [0, 0]
    for name, extent in layout():
        if len(extent) == 1:
            kind = 0 if extent[0] == D else 1
            for j in range(extent[0] // 128):
                listed.append((at + j, kind, rows[kind], j * 128))
            rows[kind] += 1
        at += math.prod(extent) // 128
    return listed


def vector_shapes():
    return [jax.ShapeDtypeStruct((8, D), jnp.float32), jax.ShapeDtypeStruct((8, E), jnp.float32)]


def steps_together(count):
    return max(j for j in range(1, min(count, 60) + 1) if count % j == 0)


def shards_a_step(shards, wanted):
    return wanted if shards % wanted == 0 else 1


def spread_kernel(order_ref, low_ref, *refs):
    big, small = matrices()[:4], matrices()[4:]
    far, outs, linear, kept, sem = refs[:4], refs[4:12], refs[12], refs[13:17], refs[17]
    step = pl.program_id(0)
    shards, rows = low_ref.shape[0], low_ref.shape[1]

    for shard in range(shards):

        def two(j, carry, shard=shard):
            pair = low_ref[shard, pl.ds(pl.multiple_of(j * 16, 16), 16), :].astype(jnp.float32)
            for half in range(2):
                block = order_ref[(step * shards + shard) * (rows // 8) + j * 2 + half]
                linear[pl.ds(pl.multiple_of(block * 8, 8), 8), :] = pair[half * 8 : half * 8 + 8]
            return carry

        lax.fori_loop(0, rows // 16, two, 0, unroll=steps_together(rows // 16))

    @pl.when(step == pl.num_programs(0) - 1)
    def _():
        def relay(height, width, first, out):
            lanes = width // 128

            def some(j, carry):
                top = pl.multiple_of(j * 128, 128)
                for lane in range(lanes):
                    part = linear[pl.ds(first + top * lanes + lane, 128, stride=lanes), :]
                    out[pl.ds(top, 128), lane * 128 : lane * 128 + 128] = part.astype(out.dtype)
                return carry

            lax.fori_loop(0, height // 128, some, 0)

        copies = []
        for j, (name, height, width, first) in enumerate(big):
            relay(height, width, first, kept[j])
            copies.append(pltpu.make_async_copy(kept[j], far[j], sem.at[j]))
            copies[-1].start()
        for (name, height, width, first), out in zip(small, outs):
            relay(height, width, first, out)
        for out in outs[-2:]:
            out[...] = jnp.zeros_like(out)
        for row, kind, top, lane in vector_places():
            outs[kind - 2][top : top + 1, lane : lane + 128] = linear[row : row + 1, :]
        for copy in copies:
            copy.wait()


def spread_packed(gathered, slots, blocks):
    shards, rows = gathered.shape[0], gathered.shape[1]
    some = shards_a_step(shards, 4)
    big = [jax.ShapeDtypeStruct((height, width), jnp.bfloat16) for name, height, width, first in matrices()[:4]]
    small = [jax.ShapeDtypeStruct((height, width), jnp.float32) for name, height, width, first in matrices()[4:]]
    small += vector_shapes()
    return pl.pallas_call(
        spread_kernel,
        out_shape=big + small,
        grid_spec=pltpu.PrefetchScalarGridSpec(
            num_scalar_prefetch=1,
            grid=(shards // some,),
            in_specs=[pl.BlockSpec((some, rows, 128), lambda s, order: (s, 0, 0))],
            out_specs=[pl.BlockSpec(memory_space=pl.ANY) for shape in big]
            + [pl.BlockSpec(shape.shape, lambda s, order: (0, 0), pipeline_mode=pl.Buffered(1)) for shape in small],
            scratch_shapes=[pltpu.VMEM(((blocks + 1) * 8, 128), jnp.float32)]
            + [pltpu.VMEM(shape.shape, shape.dtype) for shape in big]
            + [pltpu.SemaphoreType.DMA((4,))],
        ),
        compiler_params=pltpu.CompilerParams(vmem_limit_bytes=60 << 20),
        name="spread_packed",
    )(slots, gathered)


def collect_kernel(order_ref, *refs):
    big, small = matrices()[:4], matrices()[4:]
    far, ins, low_ref, linear, kept, sem = refs[:4], refs[4:12], refs[12], refs[13], refs[14:18], refs[18]
    step = pl.program_id(0)
    shards, rows = low_ref.shape[0], low_ref.shape[1]

    @pl.when(step == 0)
    def _():
        copies = [pltpu.make_async_copy(far[j], kept[j], sem.at[j]) for j in range(4)]
        for copy in copies:
            copy.start()

        def relay(height, width, first, given):
            lanes = width // 128

            def some(j, carry):
                top = pl.multiple_of(j * 128, 128)
                for lane in range(lanes):
                    part = given[pl.ds(top, 128), lane * 128 : lane * 128 + 128]
                    linear[pl.ds(first + top * lanes + lane, 128, stride=lanes), :] = part.astype(jnp.float32)
                return carry

            lax.fori_loop(0, height // 128, some, 0)

        for (name, height, width, first), given in zip(small, ins):
            relay(height, width, first, given)
        first = vector_places()[0][0]
        linear[first:, :] = jnp.zeros((linear.shape[0] - first, 128), jnp.float32)
        for row, kind, top, lane in vector_places():
            linear[row : row + 1, :] = ins[kind - 2][top : top + 1, lane : lane + 128]
        for j, (name, height, width, first) in enumerate(big):
            copies[j].wait()
            relay(height, width, first, kept[j])

    for shard in range(shards):

        def two(j, carry, shard=shard):
            parts = []
            for half in range(2):
                block = order_ref[(step * shards + shard) * (rows // 8) + j * 2 + half]
                parts.append(linear[pl.ds(pl.multiple_of(block * 8, 8), 8), :])
            low_ref[shard, pl.ds(pl.multiple_of(j * 16, 16), 16), :] = jnp.concatenate(parts, axis=0).astype(low_ref.dtype)
            return carry

        lax.fori_loop(0, rows // 16, two, 0, unroll=steps_together(rows // 16))


def collect_packed(grads, slots, blocks, shards, rows):
    some = shards_a_step(shards, 2)
    whole = [pl.BlockSpec(grad.shape, lambda s, order: (0, 0), pipeline_mode=pl.Buffered(1)) for grad in grads[4:]]
    return pl.pallas_call(
        collect_kernel,
        out_shape=jax.ShapeDtypeStruct((shards, rows, 128), jnp.bfloat16),
        grid_spec=pltpu.PrefetchScalarGridSpec(
            num_scalar_prefetch=1,
            grid=(shards // some,),
            in_specs=[pl.BlockSpec(memory_space=pl.ANY)] * 4 + whole,
            out_specs=pl.BlockSpec((some, rows, 128), lambda s, order: (s, 0, 0)),
            scratch_shapes=[pltpu.VMEM(((blocks + 1) * 8, 128), jnp.float32)]
            + [pltpu.VMEM(grad.shape, grad.dtype) for grad in grads[:4]]
            + [pltpu.SemaphoreType.DMA((4,))],
        ),
        compiler_params=pltpu.CompilerParams(vmem_limit_bytes=60 << 20),
        name="collect_packed",
    )(slots, *grads)


def finer(a, b, left, right):
    return lax.dot_general(
        a, b, (((left,), (right,)), ((), ())), precision=lax.Precision.HIGH, preferred_element_type=jnp.float32
    )


def unit_scale(values):
    center = values - jnp.mean(values, axis=-1, keepdims=True)
    scale = lax.rsqrt(jnp.mean(center * center, axis=-1, keepdims=True) + 1e-06)
    return center * scale, scale


def unit_back(grad, unit, scale, gain):
    inner = grad * gain
    return scale * (
        inner - jnp.mean(inner, axis=-1, keepdims=True) - unit * jnp.mean(inner * unit, axis=-1, keepdims=True)
    )


def wave_kernel(embed_ref, wq_ref, wk_ref, wv_ref, wo_ref, win_ref, wout_ref, vec_ref, shaped_ref, own_ref, kept_ref, slope_ref):
    rows = embed_ref.shape[0]
    groups = rows // NB
    embedded = embed_ref[...]
    queries = finer(embedded, wq_ref[...], 1, 0)
    keys = finer(embedded, wk_ref[...], 1, 0)
    values = finer(embedded, wv_ref[...], 1, 0)
    size = E // HH
    across = lax.broadcasted_iota(jnp.int32, (rows, rows), 0) // NB == lax.broadcasted_iota(jnp.int32, (rows, rows), 1) // NB
    mixed = []
    for head in range(HH):
        lanes = slice(head * size, head * size + size)
        scores = finer(queries[:, lanes], keys[:, lanes], 1, 1) * size**-0.5
        scores = jnp.where(across, scores, -1e30)
        weight = jnp.exp(scores - jnp.max(scores, axis=-1, keepdims=True))
        weight = weight / jnp.sum(weight, axis=-1, keepdims=True)
        kept_ref[head] = weight
        mixed.append(finer(weight, values[:, lanes], 1, 0))
    mixed = jnp.concatenate(mixed, axis=1)
    unit_one, scale_one = unit_scale(embedded + finer(mixed, wo_ref[...], 1, 0))
    first = unit_one * vec_ref[0:1, :] + vec_ref[1:2, :]
    inner = finer(first, win_ref[...], 1, 0)
    half = 0.5 * (1.0 + lax.erf(inner * 0.5**0.5))
    slope_ref[0] = inner * half
    slope_ref[1] = half + inner * jnp.exp(-0.5 * inner * inner) * (2.0 * math.pi) ** -0.5
    unit_two, scale_two = unit_scale(first + finer(inner * half, wout_ref[...], 1, 0))
    shaped = (unit_two * vec_ref[2:3, :] + vec_ref[3:4, :] + embedded).astype(jnp.bfloat16)
    for j, part in enumerate((queries, keys, values, mixed, unit_one, unit_two)):
        kept_ref[HH + j] = part
    kept_ref[HH + 6] = jnp.broadcast_to(scale_one, (rows, E))
    kept_ref[HH + 7] = jnp.broadcast_to(scale_two, (rows, E))
    shaped_ref[...] = shaped
    wide = shaped.astype(jnp.float32)
    width = E // groups
    group = lax.axis_index("group")
    own = jnp.zeros((rows, width), jnp.float32)
    for j in range(groups):
        own = jnp.where(group == j, wide[:, j * width : (j + 1) * width], own)
    own_ref[...] = own.astype(jnp.bfloat16)


def wave_layer(embedded, mats, vectors):
    rows = embedded.shape[0]
    groups = rows // NB
    f32, bf16 = jnp.float32, jnp.bfloat16
    return pl.pallas_call(
        wave_kernel,
        out_shape=[
            jax.ShapeDtypeStruct((rows, E), bf16),
            jax.ShapeDtypeStruct((rows, E // groups), bf16),
            jax.ShapeDtypeStruct((HH + 8, rows, E), f32),
            jax.ShapeDtypeStruct((2, rows, HFF), f32),
        ],
        compiler_params=pltpu.CompilerParams(vmem_limit_bytes=60 << 20),
        name="wave_layer",
    )(embedded, *mats, vectors)


def wave_back_kernel(part_ref, embed_ref, kept_ref, slope_ref, wq_ref, wk_ref, wv_ref, wo_ref, win_ref, wout_ref, vec_ref,
                     gq_ref, gk_ref, gv_ref, go_ref, gin_ref, gout_ref, gvec_ref):
    rows = embed_ref.shape[0]
    groups = rows // NB
    width = E // groups
    size = E // HH
    group = lax.axis_index("group")
    spread = jnp.concatenate([part_ref[...]] * groups, axis=1)
    lane = lax.broadcasted_iota(jnp.int32, (rows, E), 1) // width
    grad = jnp.where(lane == group, spread, 0.0)
    embedded = embed_ref[...]
    queries, keys, values, mixed, unit_one, unit_two, scale_one, scale_two = (kept_ref[HH + j] for j in range(8))
    gvec_ref[...] = jnp.zeros_like(gvec_ref)
    gvec_ref[2:3, :] = jnp.sum(grad * unit_two, axis=0, keepdims=True)
    gvec_ref[3:4, :] = jnp.sum(grad, axis=0, keepdims=True)
    grad = unit_back(grad, unit_two, scale_two, vec_ref[2:3, :])
    gout_ref[...] = finer(slope_ref[0], grad, 0, 0)
    inner = finer(grad, wout_ref[...], 1, 1) * slope_ref[1]
    first = unit_one * vec_ref[0:1, :] + vec_ref[1:2, :]
    gin_ref[...] = finer(first, inner, 0, 0)
    grad = grad + finer(inner, win_ref[...], 1, 1)
    gvec_ref[0:1, :] = jnp.sum(grad * unit_one, axis=0, keepdims=True)
    gvec_ref[1:2, :] = jnp.sum(grad, axis=0, keepdims=True)
    grad = unit_back(grad, unit_one, scale_one, vec_ref[0:1, :])
    go_ref[...] = finer(mixed, grad, 0, 0)
    grad = finer(grad, wo_ref[...], 1, 1)
    parts = [[], [], []]
    for head in range(HH):
        lanes = slice(head * size, head * size + size)
        weight = kept_ref[head]
        grad_weight = finer(grad[:, lanes], values[:, lanes], 1, 1)
        parts[2].append(finer(weight, grad[:, lanes], 0, 0))
        score = weight * (grad_weight - jnp.sum(weight * grad_weight, axis=-1, keepdims=True)) * size**-0.5
        parts[0].append(finer(score, keys[:, lanes], 1, 0))
        parts[1].append(finer(score, queries[:, lanes], 0, 0))
    for out, part in zip((gq_ref, gk_ref, gv_ref), parts):
        out[...] = finer(embedded, jnp.concatenate(part, axis=1), 0, 0)


def wave_back(part, embedded, kept, slope, mats, vectors):
    f32 = jnp.float32
    return pl.pallas_call(
        wave_back_kernel,
        out_shape=[jax.ShapeDtypeStruct(mat.shape, f32) for mat in mats] + [jax.ShapeDtypeStruct((8, E), f32)],
        compiler_params=pltpu.CompilerParams(vmem_limit_bytes=60 << 20),
        name="wave_back",
    )(part, embedded, kept, slope, *mats, vectors)


def tall(count):
    return -(-count // 16) * 16


def dot_nn(a, b):
    return lax.dot_general(a, b, (((1,), (0,)), ((), ())), preferred_element_type=jnp.float32)


def dot_nt(a, b):
    return lax.dot_general(a, b, (((1,), (1,)), ((), ())), preferred_element_type=jnp.float32)


def dot_tn(a, b):
    return lax.dot_general(a, b, (((0,), (0,)), ((), ())), preferred_element_type=jnp.float32)


def block_kernel(stream_ref, up_ref, vec_ref, wqkv_hbm, wout_hbm, wup_hbm, wdown_hbm,
                 out_ref, low_ref, gvec_ref, gqkv_hbm, gout_hbm, gup_hbm, gdown_hbm,
                 wqkv, wout, wup, wdown, gqkv, gout, gup, gdown,
                 xs, ups, up_low, norm_one, qkv, att, probs, mid, norm_two, acc, hid_low, datt, dqkv, in_sem, out_sem):
    f32, bf16 = jnp.float32, jnp.bfloat16
    seq = stream_ref.shape[0]
    rows = xs.shape[0]
    loads = [
        pltpu.make_async_copy(src, dst, in_sem.at[j])
        for j, (src, dst) in enumerate(((wqkv_hbm, wqkv), (wout_hbm, wout), (wup_hbm, wup), (wdown_hbm, wdown)))
    ]
    for load in loads:
        load.start()
    stores = [
        pltpu.make_async_copy(src, dst, out_sem.at[j])
        for j, (src, dst) in enumerate(((gqkv, gqkv_hbm), (gout, gout_hbm), (gup, gup_hbm), (gdown, gdown_hbm)))
    ]
    gain_one, shift_one = vec_ref[0:1, :], vec_ref[1:2, :]
    gain_two, shift_two = vec_ref[2:3, :], vec_ref[3:4, :]
    xs[...] = jnp.zeros_like(xs)
    xs[0:seq, :] = stream_ref[...] + vec_ref[4:5, :]
    ups[...] = jnp.zeros_like(ups)
    ups[0:seq, :] = up_ref[...].astype(f32)
    up_low[...] = ups[...].astype(bf16)

    def normed(values):
        center = values - jnp.mean(values, axis=-1, keepdims=True)
        scale = lax.rsqrt(jnp.mean(center * center, axis=-1, keepdims=True) + 1e-06)
        return center * scale, scale

    def normed_back(grad, unit, scale, gain):
        inner = grad * gain
        return scale * (
            inner
            - jnp.mean(inner, axis=-1, keepdims=True)
            - unit * jnp.mean(inner * unit, axis=-1, keepdims=True)
        )

    unit, scale = normed(xs[...])
    norm_one[...] = (unit * gain_one + shift_one).astype(bf16)
    loads[0].wait()

    def tile(j, size=D):
        return pl.ds(pl.multiple_of(j * size, size), size)

    def each(count, body):
        lax.fori_loop(0, count, lambda j, carry: (body(j), carry)[1], 0)

    def qkv_part(j):
        qkv[:, tile(j)] = dot_nn(norm_one[...], wqkv[:, tile(j)]).astype(bf16)

    each(3, qkv_part)
    inside = lax.broadcasted_iota(jnp.int32, (rows, rows), 1) < seq

    def heads(p):
        pair = [qkv[:, pl.ds(pl.multiple_of(j * D + p * 128, 128), 128)] for j in range(3)]
        outs = []
        for h in range(2):
            query, key, value = (part[:, h * HD : h * HD + HD] for part in pair)
            scores = jnp.where(inside, dot_nt(query, key) * (HD**-0.5), -1e30)
            weight = jnp.exp(scores - jnp.max(scores, axis=-1, keepdims=True))
            weight = weight / jnp.sum(weight, axis=-1, keepdims=True)
            probs[p * 2 + h] = weight
            outs.append(dot_nn(weight.astype(bf16), value))
        att[:, pl.ds(pl.multiple_of(p * 128, 128), 128)] = jnp.concatenate(outs, axis=1).astype(bf16)

    each(HEADS // 2, heads)
    loads[1].wait()
    mid[...] = xs[...] + dot_nn(att[...], wout[...])
    unit, scale = normed(mid[...])
    norm_two[...] = (unit * gain_two + shift_two).astype(bf16)
    loads[2].wait()
    loads[3].wait()
    acc[...] = jnp.zeros_like(acc)

    def hidden_part(j):
        hidden = dot_nn(norm_two[...], wup[:, tile(j)])
        half = 0.5 * (1.0 + lax.erf(hidden * (0.5**0.5)))
        active = (hidden * half).astype(bf16)
        slope = half + hidden * jnp.exp(-0.5 * hidden * hidden) * (2.0 * math.pi) ** -0.5
        mid[...] += dot_nn(active, wdown[tile(j), :])
        gdown[tile(j), :] = dot_tn(active, up_low[...]).astype(bf16)
        grad_hidden = (dot_nt(up_low[...], wdown[tile(j), :]) * slope).astype(bf16)
        gup[:, tile(j)] = dot_tn(norm_two[...], grad_hidden).astype(bf16)
        acc[...] += dot_nt(grad_hidden, wup[:, tile(j)])

    kept_unit, kept_scale = unit, scale
    hid_low[...] = kept_unit
    each(HID // D, hidden_part)
    stores[2].start()
    stores[3].start()
    out_ref[...] = mid[0:seq, :].astype(bf16)
    grad = acc[...]
    unit = hid_low[...]
    gvec_ref[...] = jnp.zeros_like(gvec_ref)
    gvec_ref[2:3, :] = jnp.sum(grad * unit, axis=0, keepdims=True)
    gvec_ref[3:4, :] = jnp.sum(grad, axis=0, keepdims=True)
    ups[...] += normed_back(grad, unit, kept_scale, gain_two)
    up_low[...] = ups[...].astype(bf16)
    gout[...] = dot_tn(att[...], up_low[...]).astype(bf16)
    stores[1].start()
    datt[...] = dot_nt(up_low[...], wout[...]).astype(bf16)

    def heads_back(p):
        pair = [qkv[:, pl.ds(pl.multiple_of(j * D + p * 128, 128), 128)] for j in range(3)]
        grad_pair = datt[:, pl.ds(pl.multiple_of(p * 128, 128), 128)]
        grads = [[], [], []]
        for h in range(2):
            query, key, value = (part[:, h * HD : h * HD + HD] for part in pair)
            grad_out = grad_pair[:, h * HD : h * HD + HD]
            weight = probs[p * 2 + h]
            grad_weight = dot_nt(grad_out, value)
            grads[2].append(dot_tn(weight.astype(bf16), grad_out))
            grad_score = weight * (grad_weight - jnp.sum(weight * grad_weight, axis=-1, keepdims=True))
            grad_score = grad_score.astype(bf16)
            grads[0].append(dot_nn(grad_score, key) * (HD**-0.5))
            grads[1].append(dot_tn(grad_score, query) * (HD**-0.5))
        for j in range(3):
            dqkv[:, pl.ds(pl.multiple_of(j * D + p * 128, 128), 128)] = jnp.concatenate(grads[j], axis=1).astype(bf16)

    each(HEADS // 2, heads_back)
    acc[...] = jnp.zeros_like(acc)

    def qkv_back(j):
        gqkv[:, tile(j)] = dot_tn(norm_one[...], dqkv[:, tile(j)]).astype(bf16)
        acc[...] += dot_nt(dqkv[:, tile(j)], wqkv[:, tile(j)])

    each(3, qkv_back)
    stores[0].start()
    unit, scale = normed(xs[...])
    grad = acc[...]
    gvec_ref[0:1, :] = jnp.sum(grad * unit, axis=0, keepdims=True)
    gvec_ref[1:2, :] = jnp.sum(grad, axis=0, keepdims=True)
    total = ups[...] + normed_back(grad, unit, scale, gain_one)
    gvec_ref[4:5, :] = jnp.sum(total, axis=0, keepdims=True)
    low_ref[...] = total.astype(bf16)
    for store in stores:
        store.wait()


def block_pass(stream, upstream, vectors, wqkv, wout, wup, wdown):
    f32, bf16 = jnp.float32, jnp.bfloat16
    seq = stream.shape[0]
    rows = tall(seq)
    whole = pl.BlockSpec(memory_space=pltpu.VMEM)
    far = pl.BlockSpec(memory_space=pl.ANY)
    mats = [wqkv, wout, wup, wdown]
    kept = [pltpu.VMEM(mat.shape, bf16) for mat in mats]
    dma = pltpu.SemaphoreType.DMA
    return pl.pallas_call(
        block_kernel,
        out_shape=[
            jax.ShapeDtypeStruct((seq, D), bf16),
            jax.ShapeDtypeStruct((rows, D), bf16),
            jax.ShapeDtypeStruct((8, D), f32),
        ]
        + [jax.ShapeDtypeStruct(mat.shape, bf16) for mat in mats],
        in_specs=[whole] * 3 + [far] * 4,
        out_specs=[whole] * 3 + [far] * 4,
        scratch_shapes=kept
        + kept
        + [
            pltpu.VMEM((rows, D), f32),
            pltpu.VMEM((rows, D), f32),
            pltpu.VMEM((rows, D), bf16),
            pltpu.VMEM((rows, D), bf16),
            pltpu.VMEM((rows, 3 * D), bf16),
            pltpu.VMEM((rows, D), bf16),
            pltpu.VMEM((HEADS, rows, rows), f32),
            pltpu.VMEM((rows, D), f32),
            pltpu.VMEM((rows, D), bf16),
            pltpu.VMEM((rows, D), f32),
            pltpu.VMEM((rows, D), f32),
            pltpu.VMEM((rows, D), bf16),
            pltpu.VMEM((rows, 3 * D), bf16),
            dma((4,)),
            dma((4,)),
        ],
        compiler_params=pltpu.CompilerParams(vmem_limit_bytes=60 << 20),
        cost_estimate=pl.CostEstimate(flops=8_400_000_000, bytes_accessed=30_000_000, transcendentals=2_000_000),
        name="block_pass",
    )(stream, upstream, vectors, *mats)


def adamw_step(weight, moment_one, moment_two, grad, rate):
    first = beta_one * moment_one + (1.0 - beta_one) * grad
    second = beta_two * moment_two + (1.0 - beta_two) * grad * grad
    fix_one = 1.0 - beta_one**STEP
    fix_two = 1.0 - beta_two**STEP
    update = first / fix_one / (jnp.sqrt(second / fix_two) + epsilon_add) + decay_rate * weight
    return (weight - rate * update, first, second)


NC = 15
SPAN = 128
HEAD = 96


def dims_step(count):
    return 16 if count % 16 == 0 else count


def spread_bands(shaped, master, turned, out):
    dims = out.shape[0]
    for dim in range(dims):
        part = dot_nn(shaped, master[:, dim * PATCH : (dim + 1) * PATCH])
        turned[pl.ds(dim, NB, stride=dims), :] = part[:, :128]
        turned[pl.ds(NB * dims + dim, NB, stride=dims), :] = part[:, 128:]
    for band in range(NB):
        for half in range(2):
            row = half * NB * dims + band * dims
            lane = band * PATCH + half * 128
            out[:, lane : lane + 128] = turned[row : row + dims, :].astype(out.dtype)


def own_bands(shaped_ref):
    return shaped_ref[pl.ds(pl.multiple_of(lax.axis_index("group") * NB, NB), NB), :]


def make_kernel(shaped_ref, master_ref, kernel_ref, turned):
    spread_bands(own_bands(shaped_ref), master_ref, turned, kernel_ref)


def make_kernels(shaped, master):
    dims = master.shape[1] // PATCH
    step = dims_step(dims)
    return pl.pallas_call(
        make_kernel,
        out_shape=jax.ShapeDtypeStruct((dims, NB * PATCH), jnp.bfloat16),
        grid=(dims // step,),
        in_specs=[
            pl.BlockSpec(shaped.shape, lambda j: (0, 0)),
            pl.BlockSpec((E, step * PATCH), lambda j: (0, j)),
        ],
        out_specs=pl.BlockSpec((step, NB * PATCH), lambda j: (j, 0)),
        scratch_shapes=[pltpu.VMEM((2 * NB * step, 128), jnp.float32)],
        compiler_params=pltpu.CompilerParams(vmem_limit_bytes=60 << 20),
        name="make_kernels",
    )(shaped, master)


def embed_kernel(pixel_ref, mask_ref, kernel_ref, stream_ref):
    masked = pixel_ref[...] * mask_ref[...].astype(jnp.bfloat16)
    part = dot_nt(masked, kernel_ref[...])

    @pl.when(pl.program_id(0) == 0)
    def _():
        stream_ref[...] = part

    @pl.when(pl.program_id(0) > 0)
    def _():
        stream_ref[...] += part


def embed_patches(pixels, mask, kernels):
    seq, width = pixels.shape[1], pixels.shape[2]
    cut = 1024
    return pl.pallas_call(
        embed_kernel,
        out_shape=jax.ShapeDtypeStruct((seq, D), jnp.float32),
        grid=(width // cut,),
        in_specs=[
            pl.BlockSpec((None, seq, cut), lambda j: (0, 0, j)),
            pl.BlockSpec((1, cut), lambda j: (0, j)),
            pl.BlockSpec((D, cut), lambda j: (0, j)),
        ],
        out_specs=pl.BlockSpec((seq, D), lambda j: (0, 0)),
        compiler_params=pltpu.CompilerParams(vmem_limit_bytes=60 << 20),
        name="embed_patches",
    )(pixels, mask, kernels)


def unembed_kernel(masked_ref, mask_ref, kernel_ref, low_ref, back_ref, grad_ref):
    seq = back_ref.shape[0]
    back_ref[...] = (dot_nn(low_ref[...], kernel_ref[...])[0:seq] * mask_ref[...]).astype(back_ref.dtype)
    grad_ref[...] = dot_tn(low_ref[...], masked_ref[...]).astype(grad_ref.dtype)


def unembed_patches(masked, mask, kernels, low, seq):
    rows, width = masked.shape
    cut = 1024
    return pl.pallas_call(
        unembed_kernel,
        out_shape=[
            jax.ShapeDtypeStruct((1, seq, width), jnp.bfloat16),
            jax.ShapeDtypeStruct((D, width), jnp.bfloat16),
        ],
        grid=(width // cut,),
        in_specs=[
            pl.BlockSpec((rows, cut), lambda j: (0, j)),
            pl.BlockSpec((1, cut), lambda j: (0, j)),
            pl.BlockSpec((D, cut), lambda j: (0, j)),
            pl.BlockSpec(low.shape, lambda j: (0, 0)),
        ],
        out_specs=[
            pl.BlockSpec((None, seq, cut), lambda j: (0, 0, j)),
            pl.BlockSpec((D, cut), lambda j: (0, j)),
        ],
        compiler_params=pltpu.CompilerParams(vmem_limit_bytes=60 << 20),
        name="unembed_patches",
    )(masked, mask, kernels, low)


def master_kernel(rate, grad_ref, shaped_ref, weight_ref, one_ref, two_ref, new_ref, first_ref, second_ref, back_ref, turned):
    groups, dims = grad_ref.shape[0], grad_ref.shape[1]
    bands = groups * NB
    for group in range(groups):
        for band in range(NB):
            for half in range(2):
                row = half * bands * dims + (group * NB + band) * dims
                lane = band * PATCH + half * 128
                turned[row : row + dims, :] = grad_ref[group, :, lane : lane + 128].astype(jnp.float32)
    total = jnp.zeros(back_ref.shape, jnp.float32)
    for dim in range(dims):
        part = jnp.concatenate(
            [turned[pl.ds(half * bands * dims + dim, bands, stride=dims), :] for half in range(2)], axis=1
        ).astype(jnp.bfloat16)
        lanes = slice(dim * PATCH, (dim + 1) * PATCH)
        weight = weight_ref[:, lanes]
        total += dot_nt(part, weight.astype(jnp.bfloat16))
        grad = dot_tn(shaped_ref[...], part)
        new_ref[:, lanes], first_ref[:, lanes], second_ref[:, lanes] = adamw_step(
            weight, one_ref[:, lanes], two_ref[:, lanes], grad, rate
        )

    @pl.when(pl.program_id(0) == 0)
    def _():
        back_ref[...] = total

    @pl.when(pl.program_id(0) > 0)
    def _():
        back_ref[...] += total


def master_update(grads, shaped, weight, one, two, rate):
    groups, dims = grads.shape[0], grads.shape[1]
    step = dims_step(dims)
    columns = pl.BlockSpec((weight.shape[0], step * PATCH), lambda j: (0, j))
    like = jax.ShapeDtypeStruct(weight.shape, jnp.float32)
    return pl.pallas_call(
        functools.partial(master_kernel, rate),
        out_shape=[like, like, like, jax.ShapeDtypeStruct(shaped.shape, jnp.float32)],
        grid=(dims // step,),
        in_specs=[
            pl.BlockSpec((groups, step, NB * PATCH), lambda j: (0, j, 0)),
            pl.BlockSpec(shaped.shape, lambda j: (0, 0)),
            columns,
            columns,
            columns,
        ],
        out_specs=[columns, columns, columns, pl.BlockSpec(shaped.shape, lambda j: (0, 0))],
        scratch_shapes=[pltpu.VMEM((2 * groups * NB * step, 128), jnp.float32)],
        compiler_params=pltpu.CompilerParams(vmem_limit_bytes=60 << 20),
        name="master_update",
    )(grads, shaped, weight, one, two)


def spot():
    group = lax.axis_index("group")
    image = lax.axis_index("img")
    return group // 2, group % 2, image // 2, image % 2


def place(y, c, z, x):
    return (y * 2 + c, z * 2 + x)


def partners():
    y, c, z, x = spot()
    x2, y2 = x + (1 - c) * (1 - 2 * x), y + c * (1 - 2 * y)
    x3, y3 = x + c * (1 - 2 * x), y + (1 - c) * (1 - 2 * y)
    around = [place(y, c, (z + d) % 4, x) for d in (1, 2, 3)]
    return (x2, y2), (x3, y3), around, place(y2, c, z, x2), place(y3, c, z, x3), place(y, 1 - c, z, x)


def greet(peers):
    barrier = pltpu.get_barrier_semaphore()
    for peer in peers:
        pl.semaphore_signal(barrier, inc=1, device_id=peer, device_id_type=MESH)
    pl.semaphore_wait(barrier, len(peers))


def remote(src, dst, send_sem, recv_sem, target):
    return pltpu.make_async_remote_copy(
        src_ref=src, dst_ref=dst, send_sem=send_sem, recv_sem=recv_sem, device_id=target, device_id_type=MESH
    )


def gather_kernel(rest_ref, pixel_ref, weight_ref, up_ref, mask_ref, all_ref, head_ref, low_ref, up_in, mask_in, own_ref, wide, narrow, weight_sem, head_sem, local_sem, line_send, line_recv, group_send, group_recv, twin_send, twin_recv):
    y, c, z, x = spot()
    (x2, y2), (x3, y3), around, second, third, twin = partners()
    partner = place(y, 1 - c, (z + 2) % 4, x)
    moved = (c + z // 2) % 2 == 1
    rows = own_ref.shape[0]

    def cut(k):
        return pl.ds(k * SPAN, min(SPAN, rows - k * SPAN))

    head = remote(pixel_ref.at[0, pl.ds(0, HEAD)], head_ref.at[0], head_sem.at[0], head_sem.at[1], partner)
    small = [
        remote(up_ref, up_in, head_sem.at[2], head_sem.at[3], partner),
        remote(mask_ref, mask_in, head_sem.at[4], head_sem.at[5], partner),
    ]

    def along(d, k):
        return remote(own_ref.at[cut(k)], all_ref.at[y, c, z, x, cut(k)], line_send.at[d - 1, k], line_recv.at[d - 1, k], around[d - 1])

    def along_in(d, k):
        return remote(own_ref.at[cut(k)], all_ref.at[y, c, (z + 4 - d) % 4, x, cut(k)], line_send.at[d - 1, k], line_recv.at[d - 1, k], around[d - 1])

    def square(core, j):
        yy, xx = ((y, x), (y2, x2), (y3, x3), (1 - y, 1 - x))[j]
        return all_ref.at[yy, core, :, xx]

    def hop(j, to, k, slot, landing):
        part = square(c, j).at[:, cut(k)]
        return remote(part, part, group_send.at[slot, k], group_recv.at[landing, k], to)

    def hop_in(landing, k):
        part = square(c, landing).at[:, cut(k)]
        return remote(part, part, group_send.at[0, k], group_recv.at[landing, k], twin)

    def share(j, k):
        part = square(c, j).at[:, cut(k)]
        yy, xx = ((y, x), (y2, x2), (y3, x3), (1 - y, 1 - x))[j]
        landing = (0, 2, 1, 3)[j]
        return remote(part, part, twin_send.at[j, k], twin_recv.at[landing, k], twin)

    def share_in(landing, k):
        yy, xx = ((y, x), (y2, x2), (y3, x3), (1 - y, 1 - x))[landing]
        part = all_ref.at[yy, 1 - c, :, xx, cut(k)]
        return remote(part, part, twin_send.at[0, k], twin_recv.at[landing, k], twin)

    fetch = pltpu.make_async_copy(weight_ref, wide, weight_sem.at[0])
    store = pltpu.make_async_copy(narrow, low_ref, weight_sem.at[1])
    fetch.start()
    even = rest_ref.shape[0] // 16 * 16
    own_ref[0:even, :] = rest_ref[0:even, :].astype(jnp.bfloat16)
    if even < own_ref.shape[0]:
        left = rest_ref.shape[0] - even
        parts = [rest_ref[even:, :]] if left else []
        parts.append(jnp.zeros((own_ref.shape[0] - even - left, 128), jnp.float32))
        own_ref[even:, :] = jnp.concatenate(parts, axis=0).astype(jnp.bfloat16)
    keep = pltpu.make_async_copy(own_ref, all_ref.at[y, c, z, x], local_sem)
    keep.start()
    greet(around + [second, third, twin, partner])
    for k in range(NC):
        for d in (1, 2, 3):
            along(d, k).start()
    keep.wait()
    for step in range(NC + 2):
        k = step
        if k < NC:
            for d in (1, 2, 3):
                along_in(d, k).wait_recv()
            hop(0, third, k, 0, 2).start()
            hop(0, second, k, 1, 1).start()
            share(0, k).start()
        if step == 3:
            fetch.wait()
            narrow[...] = wide[...].astype(jnp.bfloat16)
            store.start()
        if step == NC // 2 + 1:

            @pl.when(moved)
            def _():
                head.start()
                for copy in small:
                    copy.start()

        k = step - 1
        if 0 <= k < NC:
            hop_in(1, k).wait_recv()
            hop(1, third, k, 2, 3).start()
            share(1, k).start()
        k = step - 2
        if 0 <= k < NC:
            hop_in(2, k).wait_recv()
            share(2, k).start()
            hop_in(3, k).wait_recv()
            share(3, k).start()
    for k in range(NC):
        for d in (1, 2, 3):
            along(d, k).wait_send()
        hop(0, third, k, 0, 2).wait_send()
        hop(0, second, k, 1, 1).wait_send()
        hop(1, third, k, 2, 3).wait_send()
        for j in range(4):
            share(j, k).wait_send()
            share_in(j, k).wait_recv()

    store.wait()

    @pl.when(moved)
    def _():
        head.wait()
        for copy in small:
            copy.wait()


def gather_packed(own, pixels, weight, upstream, mask, rows):
    bf16 = jnp.bfloat16
    dma = pltpu.SemaphoreType.DMA
    return pl.pallas_call(
        gather_kernel,
        out_shape=[
            jax.ShapeDtypeStruct((2, 2, 4, 2, rows, 128), bf16),
            jax.ShapeDtypeStruct((1, HEAD, pixels.shape[2]), pixels.dtype),
            jax.ShapeDtypeStruct(weight.shape, bf16),
            jax.ShapeDtypeStruct(upstream.shape, upstream.dtype),
            jax.ShapeDtypeStruct(mask.shape, mask.dtype),
        ],
        in_specs=[pl.BlockSpec(memory_space=pltpu.VMEM)] + [pl.BlockSpec(memory_space=pl.ANY)] * 4,
        out_specs=[pl.BlockSpec(memory_space=pl.ANY)] * 5,
        scratch_shapes=[
            pltpu.VMEM((rows, 128), bf16),
            pltpu.VMEM(weight.shape, jnp.float32),
            pltpu.VMEM(weight.shape, bf16),
            dma((2,)),
            dma((6,)),
            dma, dma((3, NC)), dma((3, NC)), dma((3, NC)), dma((4, NC)), dma((4, NC)), dma((4, NC))],
        compiler_params=pltpu.CompilerParams(collective_id=0, has_side_effects=True, vmem_limit_bytes=60 << 20),
        name="gather_packed",
    )(own, pixels, weight, upstream, mask)


def reduce_kernel(part_ref, sum_ref, own, twin_in, third_in, second_in, line_in, load_sem, twin_send, twin_recv, third_send, third_recv, second_send, second_recv, line_send, line_recv):
    f32, bf16 = jnp.float32, jnp.bfloat16
    y, c, z, x = spot()
    (x2, y2), (x3, y3), around, second, third, twin = partners()
    rows = sum_ref.shape[0]

    def cut(k):
        return pl.ds(k * SPAN, min(SPAN, rows - k * SPAN))

    spots = ((1 - y, 1 - x), (y3, x3), (y2, x2), (y, x))
    turned = ((1 - y, 1 - x), (y2, x2), (y3, x3), (y, x))

    def load(j, k):
        yy, xx = spots[j]
        return pltpu.make_async_copy(part_ref.at[yy, c, :, xx, cut(k)], own.at[j, :, cut(k)], load_sem.at[j, k])

    def swap(j, k):
        yy, xx = turned[j]
        return remote(part_ref.at[yy, 1 - c, :, xx, cut(k)], twin_in.at[j, :, cut(k)], twin_send.at[j, k], twin_recv.at[j, k], twin)

    def to_third(j, k):
        return remote(own.at[j, :, cut(k)], third_in.at[j, :, cut(k)], third_send.at[j, k], third_recv.at[j, k], third)

    def to_second(k):
        return remote(own.at[2, :, cut(k)], second_in.at[:, cut(k)], second_send.at[k], second_recv.at[k], second)

    def to_line(d, k):
        return remote(own.at[3, (z + d) % 4, cut(k)], line_in.at[d - 1, cut(k)], line_send.at[d - 1, k], line_recv.at[d - 1, k], around[d - 1])

    for k in range(NC):
        for j in range(4):
            load(j, k).start()
    greet(around + [second, third, twin])
    for k in range(NC):
        for j in range(4):
            swap(j, k).start()

    def pair(j, k):
        load(j, k).wait()
        swap(j, k).wait_recv()
        return own[j, :, cut(k)].astype(f32) + twin_in[j, :, cut(k)].astype(f32)

    for step in range(NC + 3):
        k = step
        if k < NC:
            for j in (0, 1):
                own[j, :, cut(k)] = pair(j, k).astype(bf16)
                to_third(j, k).start()
        k = step - 1
        if 0 <= k < NC:
            held = pair(2, k)
            to_third(0, k).wait_recv()
            own[2, :, cut(k)] = (held + third_in[0, :, cut(k)].astype(f32)).astype(bf16)
            to_second(k).start()
        k = step - 2
        if 0 <= k < NC:
            held = pair(3, k)
            to_third(1, k).wait_recv()
            to_second(k).wait_recv()
            held += third_in[1, :, cut(k)].astype(f32) + second_in[:, cut(k)].astype(f32)
            own[3, :, cut(k)] = held.astype(bf16)
            for d in (1, 2, 3):
                to_line(d, k).start()
        k = step - 3
        if 0 <= k < NC:
            total = own[3, z, cut(k)].astype(f32)
            for d in (1, 2, 3):
                to_line(d, k).wait_recv()
                total += line_in[d - 1, cut(k)].astype(f32)
            sum_ref[cut(k)] = total
    for k in range(NC):
        for j in range(4):
            swap(j, k).wait_send()
        for j in (0, 1):
            to_third(j, k).wait_send()
        to_second(k).wait_send()
        for d in (1, 2, 3):
            to_line(d, k).wait_send()


def reduce_packed(part):
    rows = part.shape[-2]
    bf16 = jnp.bfloat16
    dma = pltpu.SemaphoreType.DMA
    return pl.pallas_call(
        reduce_kernel,
        out_shape=jax.ShapeDtypeStruct((rows, 128), jnp.float32),
        in_specs=[pl.BlockSpec(memory_space=pl.ANY)],
        out_specs=pl.BlockSpec(memory_space=pltpu.VMEM),
        scratch_shapes=[
            pltpu.VMEM((4, 4, rows, 128), bf16),
            pltpu.VMEM((4, 4, rows, 128), bf16),
            pltpu.VMEM((2, 4, rows, 128), bf16),
            pltpu.VMEM((4, rows, 128), bf16),
            pltpu.VMEM((3, rows, 128), bf16),
            dma((4, NC)), dma((4, NC)), dma((4, NC)), dma((2, NC)), dma((2, NC)), dma((NC,)), dma((NC,)), dma((3, NC)), dma((3, NC)),
        ],
        compiler_params=pltpu.CompilerParams(collective_id=1, has_side_effects=True, vmem_limit_bytes=56 << 20),
        name="reduce_packed",
    )(part)


CHUNK = 16
CUTS = 2


def over_x(k):
    return k % 3 != 2


def over_z(k):
    return k % 3 == 0


def quad_peers():
    y, c, z, x = spot()
    low = z % 2
    side = place(y, c, z, 1 - x)
    along = place(y, c, z + 1 - 2 * low, x)
    twin = place(y, 1 - c, z, x)
    partner = place(y, 1 - c, (z + 2) % 4, x)
    moved = (c + z // 2) % 2 == 1
    return y, c, z, x, low, side, along, twin, partner, moved


def swap_group(value, flip):
    return lax.ppermute(value, "group", [(j, j ^ flip) for j in range(4)])


def swap_images(value):
    pairs = []
    for y in range(2):
        for c in range(2):
            for z in range(4):
                for x in range(2):
                    other = (1 - c, (z + 2) % 4) if c != z // 2 else (c, z)
                    pairs.append((((y * 2 + c) * 4 + z) * 2 + x, ((y * 2 + other[0]) * 4 + other[1]) * 2 + x))
    return lax.ppermute(value, ("group", "img"), pairs)


def share_kernel(shaped_ref, mask_ref, own_slab, over_slab, pixel_ref, head_ref, rest_ref,
                 all_ref, masked_ref, stream_ref, made_ref, master, turned, held, top, bottom, tile, mixed, order, slab_sem, slab_send, slab_recv, pixel_sem, store_sem, keep_sem, swap_send, swap_recv,
                 side_send, side_recv, along_send, along_recv, far_send, far_recv, twin_send, twin_recv):
    f32, bf16 = jnp.float32, jnp.bfloat16
    y, c, z, x, low, side, along, twin, partner, moved = quad_peers()
    dims, width = made_ref.shape
    chunks = dims // CHUNK
    count = chunks * CUTS
    group = 8 * CHUNK

    def cut(k):
        return pl.ds(k // CUTS * CHUNK, CHUNK), pl.ds(k % CUTS * (width // CUTS), width // CUTS)

    def rows_of(r):
        return pl.ds(r * CHUNK, CHUNK)

    def block(core, j, k):
        return held.at[2 * core + (low + j // 2) % 2, (x + j % 2) % 2, *cut(k)]

    def keep(k):
        return pltpu.make_async_copy(made_ref.at[*cut(k)], block(c, 0, k), keep_sem.at[k])

    def swap(k):
        return remote(made_ref.at[*cut(k)], block(1 - c, 0, k), swap_send.at[k], swap_recv.at[k], partner)

    def swap_in(k):
        return remote(made_ref.at[*cut(k)], block(c, 0, k), swap_send.at[k], swap_recv.at[k], partner)

    def to_side(k):
        return remote(block(c, 0, k), block(c, 0, k), side_send.at[k], side_recv.at[k], side)

    def from_side(k):
        return remote(block(c, 1, k), block(c, 1, k), side_send.at[k], side_recv.at[k], side)

    def to_along(k):
        return remote(block(c, 0, k), block(c, 0, k), along_send.at[k], along_recv.at[k], along)

    def from_along(k):
        return remote(block(c, 2, k), block(c, 2, k), along_send.at[k], along_recv.at[k], along)

    def pass_on(k):
        j, to = (2, side) if over_x(k) else (1, along)
        return remote(block(c, j, k), block(c, j, k), far_send.at[k], far_recv.at[k], to)

    def from_far(k):
        return remote(block(c, 3, k), block(c, 3, k), far_send.at[k], far_recv.at[k], twin)

    def give(j, k):
        return remote(block(c, j, k), block(c, j, k), twin_send.at[j, k], twin_recv.at[j, k], twin)

    def given(j, k):
        return remote(block(1 - c, j, k), block(1 - c, j, k), twin_send.at[j, k], twin_recv.at[j, k], twin)

    def slab(core, j, k):
        owner = (y + j) % 2 * 2 + core
        size = own_slab.shape[0]
        return master.at[k, pl.ds(pl.multiple_of(owner * size, size), size)]

    def slab_here(j, k):
        lanes = pl.ds(k * CHUNK * PATCH, CHUNK * PATCH)
        return (own_slab, over_slab)[j].at[:, lanes]

    def load_slab(j, k):
        return pltpu.make_async_copy(slab_here(j, k), slab(c, j, k), slab_sem.at[j, k])

    def send_slab(j, k):
        return remote(slab_here(j, k), slab(c, j, k), slab_send.at[j, k], slab_recv.at[j, k], twin)

    def slab_in(j, k):
        return remote(slab_here(j, k), slab(1 - c, j, k), slab_send.at[j, k], slab_recv.at[j, k], twin)

    def make(k):
        for j in range(2):
            load_slab(j, k).wait()
            slab_in(j, k).wait_recv()
        spread_bands(own_bands(shaped_ref), master.at[k], turned, made_ref.at[rows_of(k)])

        @pl.when(moved)
        def _():
            for cut_at in range(CUTS):
                swap(k * CUTS + cut_at).start()

        @pl.when(jnp.logical_not(moved))
        def _():
            for cut_at in range(CUTS):
                keep(k * CUTS + cut_at).start()

    def store(r):
        return pltpu.make_async_copy(held.at[:, :, rows_of(r)], all_ref.at[:, :, rows_of(r)], store_sem.at[r])

    swapped = pltpu.make_async_copy(head_ref.at[0], top, pixel_sem.at[0])
    owned = pltpu.make_async_copy(pixel_ref.at[0, pl.ds(0, HEAD)], top, pixel_sem.at[0])
    lower = pltpu.make_async_copy(rest_ref.at[0], bottom, pixel_sem.at[1])

    for k in range(chunks):
        for j in range(2):
            load_slab(j, k).start()

    @pl.when(jnp.logical_not(moved))
    def _():
        owned.start()

    @pl.when(moved)
    def _():
        swapped.start()

    lower.start()
    greet([side, along, twin, partner])
    for k in range(chunks):
        for j in range(2):
            send_slab(j, k).start()
    make(0)

    def mask_pixels(part):
        @pl.when(part == 0)
        def _():
            lower.wait()
            owned.wait()

        def some(j, carry):
            lanes = pl.ds(pl.multiple_of(j * 1024, 1024), 1024)
            mask = mask_ref[:, lanes]
            masked_ref[0:HEAD, lanes] = (top[:, lanes].astype(f32) * mask).astype(bf16)
            tile[...] = jnp.zeros_like(tile)
            tile[0 : bottom.shape[0], :] = bottom[:, lanes].astype(f32) * mask
            masked_ref[HEAD:, lanes] = tile[...].astype(bf16)
            return carry

        cuts = width // 1024
        lax.fori_loop(part * (cuts // 2), (part + 1) * (cuts // 2), some, 0)

    def make_order():
        row = lax.broadcasted_iota(jnp.int32, order.shape, 0)
        column = lax.broadcasted_iota(jnp.int32, order.shape, 1)
        wanted = row % group // CHUNK * dims + row // group * CHUNK + row % CHUNK
        order[...] = jnp.where(column == wanted, 1.0, 0.0)

    for step in range(count + 3):
        k = step
        if k < count:

            @pl.when(moved)
            def _(k=k):
                swap_in(k).wait_recv()

            @pl.when(jnp.logical_not(moved))
            def _(k=k):
                keep(k).wait()

            to_side(k).start()
            to_along(k).start()
            give(0, k).start()
        if step % CUTS == 0 and step // CUTS + 1 < chunks:
            make(step // CUTS + 1)
        if step in (1, 3):
            mask_pixels(step // 2)
        elif step == 5:
            make_order()
        k = step - 1
        if 0 <= k < count:
            if over_x(k):
                from_along(k).wait_recv()
                pass_on(k).start()
                from_side(k).wait_recv()
            else:
                from_side(k).wait_recv()
                pass_on(k).start()
                from_along(k).wait_recv()
            give(1, k).start()
            give(2, k).start()
        k = step - 2
        if 0 <= k < count:
            from_far(k).wait_recv()
            give(3, k).start()
        k = step - 3
        if 0 <= k < count:
            for j in range(4):
                given(j, k).wait_recv()
            if k % CUTS == CUTS - 1:
                r = k // CUTS
                store(r).start()
                part = held[:, :, rows_of(r), :].reshape(group, width)
                mixed[:, r * group : (r + 1) * group] = dot_nt(masked_ref[...], part)

    stream_ref[...] = finer(mixed[...], order[...], 1, 0)[0 : stream_ref.shape[0]]

    @pl.when(moved)
    def _():
        for k in range(count):
            swap(k).wait_send()

    for k in range(count):
        to_side(k).wait_send()
        to_along(k).wait_send()
        pass_on(k).wait_send()
        for j in range(4):
            give(j, k).wait_send()
    for k in range(chunks):
        store(k).wait()
        for j in range(2):
            send_slab(j, k).wait_send()


def share_kernels(shaped, mask, slabs, pixels, head, rest):
    dims, width = slabs[0].shape[1] // PATCH, mask.shape[1]
    bf16 = jnp.bfloat16
    chunks = dims // CHUNK
    count = chunks * CUTS
    seq = pixels.shape[1]
    rows = tall(seq)
    f32 = jnp.float32
    dma = pltpu.SemaphoreType.DMA
    vmem, far = pl.BlockSpec(memory_space=pltpu.VMEM), pl.BlockSpec(memory_space=pl.ANY)
    shared, masked, stream = pl.pallas_call(
        share_kernel,
        out_shape=[
            jax.ShapeDtypeStruct((4, 2, dims, width), bf16),
            jax.ShapeDtypeStruct((rows, width), bf16),
            jax.ShapeDtypeStruct((seq, 8 * dims), f32),
        ],
        in_specs=[vmem, vmem] + [far] * 5,
        out_specs=[far, vmem, vmem],
        scratch_shapes=[
            pltpu.VMEM((dims, width), bf16),
            pltpu.VMEM((chunks, E, CHUNK * PATCH), bf16),
            pltpu.VMEM((2 * NB * CHUNK, 128), f32),
            pltpu.VMEM((4, 2, dims, width), bf16),
            pltpu.VMEM((HEAD, width), bf16),
            pltpu.VMEM((seq - HEAD, width), bf16),
            pltpu.VMEM((rows - HEAD, 1024), f32),
            pltpu.VMEM((rows, 8 * dims), f32),
            pltpu.VMEM((8 * dims, 8 * dims), f32),
            dma((2, chunks)),
            dma((2, chunks)),
            dma((2, chunks)),
            dma((2,)),
        ]
        + [dma((count,))] * 10
        + [dma((4, count))] * 2,
        compiler_params=pltpu.CompilerParams(collective_id=2, has_side_effects=True, vmem_limit_bytes=60 << 20),
        name="share_kernels",
    )(shaped, mask, *slabs, pixels, head, rest)
    return shared.reshape(8 * dims, width), masked, stream


def fold_kernel(masked_ref, mask_ref, low_ref, kernel_ref, out_ref, all_ref, back_ref, out_in,
                gone, own, twin_in, relay_in, side_in, along_in, tiles, backs, out_sem, tile_sem, back_sem, keep_sem, twin_send, twin_recv,
                relay_send, relay_recv, side_send, side_recv, along_send, along_recv, swap_send, swap_recv,
                group_send, group_recv, give_send, give_recv):
    f32, bf16 = jnp.float32, jnp.bfloat16
    y, c, z, x, low, side, along, twin, partner, moved = quad_peers()
    over = place(1 - y, c, z, x)
    dims, width = all_ref.shape[2], all_ref.shape[3]
    count = dims // CHUNK * CUTS
    seq = back_ref.shape[1]
    lane = tiles.shape[2]

    def cut(k):
        return pl.ds(k // CUTS * CHUNK, CHUNK), pl.ds(k % CUTS * (width // CUTS), width // CUTS)

    def spot_of(j):
        return (low + j // 2) % 2, (x + j % 2) % 2

    def mine(j, k):
        a, b = spot_of(j)
        return own.at[a, b, *cut(k)]

    def swap(k):
        return remote(gone.at[:, :, *cut(k)], twin_in.at[:, :, *cut(k)], twin_send.at[k], twin_recv.at[k], twin)

    def relay(k):
        return remote(mine(3, k), relay_in.at[*cut(k)], relay_send.at[k], relay_recv.at[k], along if over_z(k) else side)

    def to_side(k):
        return remote(mine(1, k), side_in.at[*cut(k)], side_send.at[k], side_recv.at[k], side)

    def to_along(k):
        return remote(mine(2, k), along_in.at[*cut(k)], along_send.at[k], along_recv.at[k], along)

    def keep(k):
        return pltpu.make_async_copy(mine(0, k), all_ref.at[y, c, *cut(k)], keep_sem.at[k])

    def move(k):
        return remote(mine(0, k), all_ref.at[y, 1 - c, *cut(k)], swap_send.at[k], swap_recv.at[k], partner)

    def moved_in(k):
        return remote(mine(0, k), all_ref.at[y, c, *cut(k)], swap_send.at[k], swap_recv.at[k], partner)

    def cross(k):
        return remote(all_ref.at[y, c, *cut(k)], all_ref.at[y, c, *cut(k)], group_send.at[k], group_recv.at[k], over)

    def crossed(k):
        return remote(all_ref.at[1 - y, c, *cut(k)], all_ref.at[1 - y, c, *cut(k)], group_send.at[k], group_recv.at[k], over)

    def give(j, k):
        here = all_ref.at[(y + j) % 2, c, *cut(k)]
        return remote(here, here, give_send.at[j, k], give_recv.at[j, k], twin)

    def given(j, k):
        here = all_ref.at[(y + j) % 2, 1 - c, *cut(k)]
        return remote(here, here, give_send.at[j, k], give_recv.at[j, k], twin)

    def fetch(j):
        return pltpu.make_async_copy(kernel_ref.at[:, pl.ds(j * lane, lane)], tiles.at[j % 2], tile_sem.at[j % 2])

    def drain(j):
        return pltpu.make_async_copy(backs.at[j % 2], back_ref.at[0, :, pl.ds(j * lane, lane)], back_sem.at[j % 2])

    def half(core, out):
        chosen = low_ref[:, pl.ds(pl.multiple_of(core * 4 * dims, 128), 4 * dims)]

        def some(j, carry):
            lanes = pl.ds(pl.multiple_of(j * 1024, 1024), 1024)
            part = dot_tn(chosen, masked_ref[:, lanes]).astype(bf16)
            out[:, :, :, lanes] = part.reshape(2, 2, dims, 1024)
            return carry

        lax.fori_loop(0, width // 1024, some, 0)

    def pixels_back(j):
        fetch(j).wait()
        if j >= 2:
            drain(j - 2).wait()
        part = dot_nn(low_ref[...], tiles[j % 2])[0:seq] * mask_ref[:, j * lane : (j + 1) * lane]
        backs[j % 2] = part.astype(bf16)
        drain(j).start()
        if (j + 2) * lane < width:
            fetch(j + 2).start()

    def pair(j, k):
        a, b = spot_of(j)
        return own[a, b, *cut(k)].astype(f32) + twin_in[a, b, *cut(k)].astype(f32)

    def put(j, k, value):
        a, b = spot_of(j)
        own[a, b, *cut(k)] = value.astype(bf16)

    output = remote(out_ref, out_in, out_sem.at[0], out_sem.at[1], partner)
    fetch(0).start()
    fetch(1).start()
    greet([side, along, twin, partner, over])

    @pl.when(moved)
    def _():
        output.start()

    half(1 - c, gone)
    for k in range(count):
        swap(k).start()
    half(c, own)

    for step in range(count + 4):
        k = step
        if k < count:
            swap(k).wait_recv()
            put(3, k, pair(3, k))
            relay(k).start()
        k = step - 1
        if 0 <= k < count:
            first, second = (to_along, to_side) if over_z(k) else (to_side, to_along)
            plain, summed = (2, 1) if over_z(k) else (1, 2)
            put(plain, k, pair(plain, k))
            first(k).start()
            relay(k).wait_recv()
            put(summed, k, pair(summed, k) + relay_in[*cut(k)].astype(f32))
            second(k).start()
        k = step - 2
        if 0 <= k < count:
            to_side(k).wait_recv()
            to_along(k).wait_recv()
            put(0, k, pair(0, k) + side_in[*cut(k)].astype(f32) + along_in[*cut(k)].astype(f32))

            @pl.when(moved)
            def _(k=k):
                move(k).start()

            @pl.when(jnp.logical_not(moved))
            def _(k=k):
                keep(k).start()

        k = step - 3
        if 0 <= k < count:

            @pl.when(moved)
            def _(k=k):
                moved_in(k).wait_recv()

            @pl.when(jnp.logical_not(moved))
            def _(k=k):
                keep(k).wait()

            cross(k).start()
            give(0, k).start()
        k = step - 4
        if 0 <= k < count:
            crossed(k).wait_recv()
            give(1, k).start()
        if step >= 2 and (step - 2) * lane < width:
            pixels_back(step - 2)

    @pl.when(moved)
    def _():
        output.wait()
        for k in range(count):
            move(k).wait_send()

    for j in (width // lane - 2, width // lane - 1):
        drain(j).wait()
    for k in range(count):
        swap(k).wait_send()
        relay(k).wait_send()
        to_side(k).wait_send()
        to_along(k).wait_send()
        cross(k).wait_send()
        for j in range(2):
            give(j, k).wait_send()
            given(j, k).wait_recv()


def fold_kernels(masked, mask, low, kernels, out):
    seq = out.shape[0]
    width = masked.shape[1]
    dims = kernels.shape[0] // 8
    count = dims // CHUNK * CUTS
    bf16 = jnp.bfloat16
    dma = pltpu.SemaphoreType.DMA
    vmem, far = pl.BlockSpec(memory_space=pltpu.VMEM), pl.BlockSpec(memory_space=pl.ANY)
    folded, back, out_in = pl.pallas_call(
        fold_kernel,
        out_shape=[
            jax.ShapeDtypeStruct((2, 2, dims, width), bf16),
            jax.ShapeDtypeStruct((1, seq, width), bf16),
            jax.ShapeDtypeStruct(out.shape, out.dtype),
        ],
        in_specs=[vmem, vmem, vmem, far, far],
        out_specs=[far, far, far],
        scratch_shapes=[
            pltpu.VMEM((2, 2, dims, width), bf16),
            pltpu.VMEM((2, 2, dims, width), bf16),
            pltpu.VMEM((2, 2, dims, width), bf16),
            pltpu.VMEM((dims, width), bf16),
            pltpu.VMEM((dims, width), bf16),
            pltpu.VMEM((dims, width), bf16),
            pltpu.VMEM((2, 8 * dims, 1024), bf16),
            pltpu.VMEM((2, seq, 1024), bf16),
            dma((2,)),
            dma((2,)),
            dma((2,)),
            dma((count,)),
        ]
        + [dma((count,))] * 12
        + [dma((2, count))] * 2,
        compiler_params=pltpu.CompilerParams(collective_id=3, has_side_effects=True, vmem_limit_bytes=60 << 20),
        name="fold_kernels",
    )(masked, mask, low, kernels, out)
    return folded.reshape(4, dims, width), back, out_in


def on_device(
    pixels,
    band_mask,
    wavelength,
    owner_order,
    rest_weight,
    rest_moment1,
    rest_moment2,
    fc_weight,
    fc_moment1,
    fc_moment2,
    cotangent,
):
    f32 = jnp.float32
    bf16 = jnp.bfloat16
    kernel_rate = float(E * PATCH * NB) ** (-0.5)
    groups = lax.axis_size("group")
    own_rows = rest_weight.shape[0]
    own_blocks = own_rows // 8
    fits = lax.axis_size("group") == 4 and lax.axis_size("img") == 8
    extra = -own_rows % 16
    slot_blocks = (own_rows + extra) // 8
    mask = band_mask.astype(f32)
    if fits:
        group, image = lax.axis_index("group"), lax.axis_index("img")
        moved = (group % 2 + image // 4) % 2 == 1
        wide_mask = jnp.pad(mask, ((0, 7), (0, 128 - NB)))
        gathered, head, low_weight, up_in, mask_in = gather_packed(
            rest_weight, pixels, fc_weight, cotangent, wide_mask, own_rows + extra
        )
        gathered, rest, low_weight = lax.optimization_barrier((gathered, pixels[:, HEAD:], low_weight))
        across = swap_group(low_weight, 2)
        rest = swap_images(rest)
        cotangent = jnp.where(moved, up_in, cotangent)
        mask = jnp.where(moved, mask_in[:1, :NB], mask)
    else:
        low_weight = fc_weight.astype(bf16)
        rest_low = jnp.pad(rest_weight.astype(bf16), ((0, extra), (0, 0)))
        gathered = lax.all_gather(rest_low, ("group", "img"), axis=0, tiled=True)
    shards = gathered.size // ((own_rows + extra) * 128)
    gathered = gathered.reshape(shards, own_rows + extra, 128)
    total_blocks = owner_order.shape[0]
    slots = jnp.pad(
        owner_order.reshape(shards, own_blocks),
        ((0, 0), (0, slot_blocks - own_blocks)),
        constant_values=total_blocks,
    ).reshape(-1)
    unpacked = spread_packed(gathered, slots, total_blocks)
    if not fits:
        master = lax.all_gather(low_weight, "group", axis=0, tiled=True)
    block_mats, wave_mats = unpacked[:4], unpacked[4:10]
    block_vectors, wave_vectors = unpacked[10:]
    embedded = embed_waves(wavelength).reshape(groups * NB, E)
    shaped_low, own_shaped, kept, slope = wave_layer(embedded, wave_mats, wave_vectors)
    mask = jnp.repeat(mask, PATCH, axis=1)
    if fits:
        kernel_all, masked, stream = share_kernels(shaped_low, mask, (low_weight, across), pixels, head, rest)
    else:
        kernel_low = make_kernels(shaped_low, master)
        kernel_all = lax.all_gather(kernel_low, "img", axis=0, tiled=True)
        stream = embed_patches(pixels, mask, kernel_all)
        masked = jnp.pad((pixels[0] * mask).astype(bf16), ((0, tall(pixels.shape[1]) - pixels.shape[1]), (0, 0)))
    block_out, grad_low, block_vectors, *block_grads = block_pass(
        stream, cotangent, block_vectors, *block_mats
    )
    if fits:
        all_groups, pixel_grad, out_in = fold_kernels(masked, mask, grad_low, kernel_all, block_out)
        all_groups, pixel_grad = lax.optimization_barrier((all_groups, pixel_grad))
        pixel_grad = swap_images(pixel_grad)
        block_out = jnp.where(moved, out_in, block_out)
    else:
        pixel_grad, kernel_grad = unembed_patches(masked, mask, kernel_all, grad_low, pixels.shape[1])
        kernel_grad_low = lax.psum_scatter(kernel_grad, "img", scatter_dimension=0, tiled=True)
        all_groups = lax.all_gather(kernel_grad_low[None], "group", axis=0, tiled=True)
    fc_new, fc_first, fc_second, shaped_part = master_update(
        all_groups,
        own_shaped,
        fc_weight,
        fc_moment1,
        fc_moment2,
        kernel_rate,
    )
    *wave_grads, wave_vectors = wave_back(shaped_part, embedded, kept, slope, wave_mats, wave_vectors)
    given = [*block_grads, *wave_grads, block_vectors, wave_vectors]
    joint_term = collect_packed(given, slots, total_blocks, shards, own_rows + extra)
    if fits:
        rest_grad = reduce_packed(joint_term.reshape(2, 2, 4, 2, own_rows + extra, 128))
    else:
        rest_grad = lax.psum_scatter(
            joint_term, ("group", "img"), scatter_dimension=0, tiled=False
        ).astype(f32)
    rest_grad = rest_grad[:own_rows]
    rest_new, rest_first, rest_second = adamw_step(
        rest_weight, rest_moment1, rest_moment2, rest_grad, rest_rate
    )
    return (block_out, pixel_grad, rest_new, rest_first, rest_second, fc_new, fc_first, fc_second)


def solution(mesh):
    placed = (
        P(("group", "img"), None, None),
        P(("group", "img"), None),
        P(),
        P(),
        P(("group", "img"), None),
        P(("group", "img"), None),
        P(("group", "img"), None),
        P("group", "img"),
        P("group", "img"),
        P("group", "img"),
        P(("group", "img"), None),
    )
    return jax.shard_map(
        on_device,
        mesh=mesh,
        in_specs=placed,
        out_specs=(
            P(("group", "img"), None),
            P(("group", "img"), None, None),
            P(("group", "img"), None),
            P(("group", "img"), None),
            P(("group", "img"), None),
            P("group", "img"),
            P("group", "img"),
            P("group", "img"),
        ),
        check_vma=False,
    )
```
